32 devices in a mesh: ctx: 2 (over x), wshard: 16 (over z, y, core).
Axes of the slice: x: 2, y: 2, z: 4, core: 2. Of those that a mesh axis runs over, the one named last changes fastest.
Arguments:
- block_input: bfloat16 [32, 1024, 1024], P('wshard', 'ctx'), may hold values from -6 to 6
- block_order: int32 [32, 4], P('wshard'), may hold values from 0 to 3, as said below
- cotangent: bfloat16 [32, 1024, 1024], P('wshard', 'ctx'), may hold values from -6 to 6
- joint_weight: float32 [1024, 3072], P(('ctx', 'wshard')), may hold values from -0.1875 to 0.1875
- mixing_weight: float32 [1024, 1024], P(('ctx', 'wshard')), may hold values from -1 to 1
- expand_weight: float32 [1024, 4096], P(('ctx', 'wshard')), may hold values from -0.1875 to 0.1875
- shrink_weight: float32 [4096, 1024], P(('ctx', 'wshard')), may hold values from -0.09375 to 0.09375
- vectors: float32 [12, 1024], P(None, ('ctx', 'wshard')), may hold values from -0.5 to 1.4, as said below
- joint_first: float32 [1024, 3072], P(('ctx', 'wshard')), may hold values from -1086.116 to 1086.116
- mixing_first: float32 [1024, 1024], P(('ctx', 'wshard')), may hold values from -271.529 to 271.529
- expand_first: float32 [1024, 4096], P(('ctx', 'wshard')), may hold values from -325.8348 to 325.8348
- shrink_first: float32 [4096, 1024], P(('ctx', 'wshard')), may hold values from -651.6696 to 651.6696
- vectors_first: float32 [12, 1024], P(None, ('ctx', 'wshard')), may hold values from -1086.116 to 1086.116
- joint_second: float32 [1024, 3072], P(('ctx', 'wshard')), may hold values from 16384 to 131072
- mixing_second: float32 [1024, 1024], P(('ctx', 'wshard')), may hold values from 983.04 to 8192
- expand_second: float32 [1024, 4096], P(('ctx', 'wshard')), may hold values from 1474.56 to 11796.48
- shrink_second: float32 [4096, 1024], P(('ctx', 'wshard')), may hold values from 5898.24 to 47185.92
- vectors_second: float32 [12, 1024], P(None, ('ctx', 'wshard')), may hold values from 16384 to 131072
Outputs:
- block_output: bfloat16 [32, 1024, 1024], P('wshard', 'ctx')
- input_gradient: float32 [32, 1024, 1024], P('wshard', 'ctx')
- joint_updated: float32 [1024, 3072], P(('ctx', 'wshard'))
- mixing_updated: float32 [1024, 1024], P(('ctx', 'wshard'))
- expand_updated: float32 [1024, 4096], P(('ctx', 'wshard'))
- shrink_updated: float32 [4096, 1024], P(('ctx', 'wshard'))
- vectors_updated: float32 [12, 1024], P(None, ('ctx', 'wshard'))
- joint_moment: float32 [1024, 3072], P(('ctx', 'wshard'))
- mixing_moment: float32 [1024, 1024], P(('ctx', 'wshard'))
- expand_moment: float32 [1024, 4096], P(('ctx', 'wshard'))
- shrink_moment: float32 [4096, 1024], P(('ctx', 'wshard'))
- vectors_moment: float32 [12, 1024], P(None, ('ctx', 'wshard'))
- joint_square: float32 [1024, 3072], P(('ctx', 'wshard'))
- mixing_square: float32 [1024, 1024], P(('ctx', 'wshard'))
- expand_square: float32 [1024, 4096], P(('ctx', 'wshard'))
- shrink_square: float32 [4096, 1024], P(('ctx', 'wshard'))
- vectors_square: float32 [12, 1024], P(None, ('ctx', 'wshard'))
- joint_copy: bfloat16 [1024, 3072], P(('ctx', 'wshard'))
- mixing_copy: bfloat16 [1024, 1024], P(('ctx', 'wshard'))
- expand_copy: bfloat16 [1024, 4096], P(('ctx', 'wshard'))
- shrink_copy: bfloat16 [4096, 1024], P(('ctx', 'wshard'))
- vectors_copy: bfloat16 [12, 1024], P(None, ('ctx', 'wshard'))
The draws below stay inside these ranges and needn't reach their ends.
Inputs may be any that keep to these rules, and one draw needn't show every extreme that they name: `block_order`: each row lists every block number of its sequence once; the entries at places 2 c and 2 c + 1 add up to 3. `vectors`: rows 0 and 5 lie in 0.6 to 1.4, the others in -0.5 to 0.5.
All inputs are finite; a program needn't handle non-finite values.
Results may differ from the reference program's by a relative error of at most 0.012.
Values may be sent and summed in bfloat16 or wider, within the bound.
A program may use at most 640 MiB of HBM per device.

```python
import math
import jax
import jax.numpy as jnp
from jax import lax

D = 1024
H = 16
HD = 64
FF = 4096
BLK = 256
STEP = 10
LENGTH = 1024
BLOCKS = 4
SEQS = 32
TOKENS = 32768
VROWS = 12


def draw_block_order(key, part):
    key = jax.random.fold_in(key, 11)

    def one_row(row_key):
        pick_key, flip_key = jax.random.split(row_key)
        pair_count = BLOCKS // 2
        chosen = jax.random.permutation(pick_key, pair_count)
        flipped = jax.random.randint(flip_key, (pair_count,), 0, 2)
        upper_block = BLOCKS - 1 - chosen
        first_block = jnp.where(flipped == 1, upper_block, chosen)
        later_block = jnp.where(flipped == 1, chosen, upper_block)
        return jnp.stack([first_block, later_block], axis=1).reshape(BLOCKS).astype(jnp.int32)
    return jax.vmap(one_row)(jax.random.split(key, SEQS))


def draw_vectors(key, part):
    key = jax.random.fold_in(key, 5)
    base = jax.random.uniform(key, (VROWS, D), jnp.float32, -1.0, 1.0)
    row_index = lax.broadcasted_iota(jnp.int32, (VROWS, D), 0)
    gain_rows = (row_index == 0) | (row_index == 5)
    return jnp.where(gain_rows, 1.0 + 0.4 * base, 0.5 * base)


def levels(key, shape, cuts, smallest, high):
    def one(position, blocks):
        steps = jax.random.uniform(jax.random.fold_in(jax.random.fold_in(key, 6), position), (blocks,), jnp.float32, smallest / len(cuts), high / len(cuts))
        return jnp.repeat(jnp.exp(steps), shape[position] // blocks).reshape((-1,) + (1,) * (len(shape) - position - 1))

    gain = one(*cuts[0])
    for cut in cuts[1:]:
        gain = gain * one(*cut)
    return gain


def scatter_about(stream_key, dims, scale, reach, cuts=(), kind=jnp.bfloat16):
    drawn = jax.random.normal(stream_key, dims, jnp.float32) * scale
    if len(cuts) > 0:
        drawn = levels(stream_key, dims, cuts, -0.22, 0.18) * drawn
    return jnp.clip(drawn, min=-reach, max=reach).astype(kind)


def setup_inputs(seed: int = 0) -> dict:
    splits = jax.random.split(jax.random.key(seed), 19)
    block_input = scatter_about(splits[0], (SEQS, LENGTH, D), 1.0, 6.0, ((0, 16), (1, 2)))
    block_order = draw_block_order(jax.random.fold_in(splits[18], 71), 0)
    cotangent = scatter_about(splits[2], (SEQS, LENGTH, D), 1.0, 6.0, ((0, 16), (1, 2)))
    joint_weight = scatter_about(splits[3], (D, 3 * D), D ** -0.5, 0.1875, ((0, 32),), jnp.float32)
    mixing_weight = scatter_about(splits[4], (D, D), (D // 32) ** -0.5, 1.0, ((0, 32),), jnp.float32)
    expand_weight = scatter_about(splits[5], (D, FF), D ** -0.5, 0.1875, ((0, 32),), jnp.float32)
    shrink_weight = scatter_about(splits[6], (FF, D), FF ** -0.5, 0.09375, ((0, 32),), jnp.float32)
    vectors = draw_vectors(jax.random.fold_in(splits[18], 71), 0)
    joint_first = scatter_about(splits[8], (D, 3 * D), (TOKENS ** 0.5), 1086.116, ((0, 32),), jnp.float32)
    mixing_first = scatter_about(splits[9], (D, D), (0.25 * TOKENS ** 0.5), 271.529, ((0, 32),), jnp.float32)
    expand_first = scatter_about(splits[10], (D, FF), (0.3 * TOKENS ** 0.5), 325.8348, ((0, 32),), jnp.float32)
    shrink_first = scatter_about(splits[11], (FF, D), (0.6 * TOKENS ** 0.5), 651.6696, ((0, 32),), jnp.float32)
    vectors_first = scatter_about(splits[12], (VROWS, D), (TOKENS ** 0.5), 1086.116, ((1, 32),), jnp.float32)
    joint_second = jnp.clip(jnp.exp(math.log(131072.0) - 2.0794415 * jax.random.uniform(splits[13], (D, 3 * D), jnp.float32) ** levels(splits[13], (D, 3 * D), ((0, 32),), -0.2, 0.2)), 16384.0, 131072.0)
    mixing_second = jnp.clip(jnp.exp(math.log(8192.0) - 2.1202636 * jax.random.uniform(splits[14], (D, D), jnp.float32) ** levels(splits[14], (D, D), ((0, 32),), -0.2, 0.2)), 983.04, 8192.0)
    expand_second = jnp.clip(jnp.exp(math.log(11796.48) - 2.0794415 * jax.random.uniform(splits[15], (D, FF), jnp.float32) ** levels(splits[15], (D, FF), ((0, 32),), -0.2, 0.2)), 1474.56, 11796.48)
    shrink_second = jnp.clip(jnp.exp(math.log(47185.92) - 2.0794415 * jax.random.uniform(splits[16], (FF, D), jnp.float32) ** levels(splits[16], (FF, D), ((0, 32),), -0.2, 0.2)), 5898.24, 47185.92)
    vectors_second = jnp.clip(jnp.exp(math.log(131072.0) - 2.0794415 * jax.random.uniform(splits[17], (VROWS, D), jnp.float32) ** levels(splits[17], (VROWS, D), ((1, 32),), -0.2, 0.2)), 16384.0, 131072.0)
    return {"block_input": block_input, "block_order": block_order, "cotangent": cotangent, "joint_weight": joint_weight, "mixing_weight": mixing_weight, "expand_weight": expand_weight, "shrink_weight": shrink_weight, "vectors": vectors, "joint_first": joint_first, "mixing_first": mixing_first, "expand_first": expand_first, "shrink_first": shrink_first, "vectors_first": vectors_first, "joint_second": joint_second, "mixing_second": mixing_second, "expand_second": expand_second, "shrink_second": shrink_second, "vectors_second": vectors_second}


@jax.custom_vjp
def low(v):
    return lax.optimization_barrier(v.astype(jnp.bfloat16)).astype(jnp.float32)

@jax.custom_vjp
def low_back(v):
    return v

def low_keep(v):
    return (low(v), None)

def low_pass(kept, grad):
    return (grad,)

def back_keep(v):
    return (v, None)

def back_low(kept, grad):
    return (low(grad),)
low.defvjp(low_keep, low_pass)
low_back.defvjp(back_keep, back_low)
highest = lax.Precision.HIGHEST

def layer_norm(values, gain_row, shift_row):
    centered = values - lax.optimization_barrier(jnp.mean(values, axis=-1, keepdims=True))
    variance = lax.optimization_barrier(jnp.mean(centered * centered, axis=-1, keepdims=True))
    return centered * lax.rsqrt(variance + 1e-05) * gain_row + shift_row

def head_attend(triple, allowed):
    queries, key_rows, value_rows = triple
    products = jnp.dot(queries, key_rows.T, precision=highest)
    scores = low_back(products * 0.125)
    scores = jnp.where(allowed, scores, -1e+30)
    weights = jax.nn.softmax(scores, axis=-1)
    return jnp.dot(low(weights), value_rows, precision=highest)

def split_heads(matrix):
    return matrix.reshape(matrix.shape[0], H, HD).transpose(1, 0, 2)

def sequence_forward(parameters, inputs, blocks):
    joint_full, mixing, expand, shrink, vector_values = tuple((low(element) for element in parameters))
    width = inputs.shape[1]
    normed_first = low(layer_norm(inputs, vector_values[0], vector_values[1]))
    joint_out = jnp.dot(normed_first, joint_full, precision=highest)
    queries = low(low_back(joint_out[:, :width] + vector_values[2]))
    key_rows = low(low_back(joint_out[:, width:2 * width]))
    value_rows = low(low_back(joint_out[:, 2 * width:] + vector_values[3]))
    allowed = blocks[None, :] <= blocks[:, None]

    def attend_head(triple):
        return head_attend(triple, allowed)
    head_out = lax.map(jax.checkpoint(attend_head), (split_heads(queries), split_heads(key_rows), split_heads(value_rows)))
    merged = head_out.transpose(1, 0, 2).reshape(inputs.shape)
    merged = low(low_back(merged))
    branch = low_back(jnp.dot(merged, mixing, precision=highest) + vector_values[4])
    middle = inputs + branch
    second = low(layer_norm(middle, vector_values[5], vector_values[6]))
    hidden = low_back(jnp.dot(second, expand, precision=highest) + vector_values[8:].reshape(-1))
    active = low(jax.nn.gelu(hidden, approximate=True))
    return middle + jnp.dot(active, shrink, precision=highest) + vector_values[7]

def adam_update(weight, moment_one, moment_two, gradient, step_rate, decay_rate):
    first_new = 0.5 * moment_one + 0.5 * gradient
    second_new = 0.5 * moment_two + 0.5 * gradient * gradient
    correct = 1.0 - 0.5 ** STEP
    direction = first_new / correct / (jnp.sqrt(second_new / correct) + 1e-08)
    updated = weight - step_rate * (direction + decay_rate * weight)
    return (updated, first_new, second_new)

def reference(block_input, block_order, cotangent, joint_weight, mixing_weight, expand_weight, shrink_weight, vectors, joint_first, mixing_first, expand_first, shrink_first, vectors_first, joint_second, mixing_second, expand_second, shrink_second, vectors_second):
    parameters = (joint_weight, mixing_weight, expand_weight, shrink_weight, vectors)

    def one_step(carried, element):
        sequence, order_row, upstream = element
        blocks = jnp.repeat(order_row, BLK, total_repeat_length=sequence.shape[0])

        def forward(params_now, inputs):
            return sequence_forward(params_now, inputs, blocks)
        result, pull = jax.vjp(forward, parameters, sequence.astype(jnp.float32))
        param_grads, input_grad = pull(upstream.astype(jnp.float32))
        carried = tuple((total + extra for total, extra in zip(carried, param_grads)))
        return (carried, (result.astype(jnp.bfloat16), input_grad))
    zero_grads = tuple((jnp.zeros(element.shape, jnp.float32) for element in parameters))
    summed, (block_output, input_gradient) = lax.scan(one_step, zero_grads, (block_input, block_order, cotangent))
    firsts = (joint_first, mixing_first, expand_first, shrink_first, vectors_first)
    seconds = (joint_second, mixing_second, expand_second, shrink_second, vectors_second)
    updated, moments, squares = ([], [], [])
    for index_pos in range(5):
        step_rate = 0.5 if index_pos == 4 else 0.05
        decay_rate = 0.0 if index_pos == 4 else 0.1
        new_weight, new_first, new_second = adam_update(parameters[index_pos], firsts[index_pos], seconds[index_pos], summed[index_pos], step_rate, decay_rate)
        updated.append(new_weight)
        moments.append(new_first)
        squares.append(new_second)
    copies = [element.astype(jnp.bfloat16) for element in updated]
    return (block_output, input_gradient, updated[0], updated[1], updated[2], updated[3], updated[4], moments[0], moments[1], moments[2], moments[3], moments[4], squares[0], squares[1], squares[2], squares[3], squares[4], copies[0], copies[1], copies[2], copies[3], copies[4])
```

```python
import functools

import jax
import jax.numpy as jnp
from jax import lax
from jax.experimental import pallas as pl
from jax.experimental.pallas import tpu as pltpu
from jax.sharding import PartitionSpec as P

H = 16
HD = 64
BLK = 256
STEP = 10
PAIR = 2 * HD

norm_eps = 1e-05
adam_eps = 1e-08
group_heads = 4
score_scale = 0.125 * 1.4426950408889634
gelu_root = 0.7978845608028654
gelu_cubic = 0.044715
low = jnp.bfloat16
axes = ("ctx", "wshard")
small_cost = pl.CostEstimate(flops=1024, bytes_accessed=1024, transcendentals=0)


def nt(a,b):
    return lax.dot_general(a,b,(((1,),(1,)),((),())),preferred_element_type=jnp.float32)
def nn(a,b):
    return jnp.dot(a,b,preferred_element_type=jnp.float32)

def rows_of(place):
    return pl.ds(pl.multiple_of(place*BLK,BLK),BLK)

def attend_kernel(blocks, place_ref, q_ref, k_ref, v_ref, o_ref, lse_ref):
    seq=pl.program_id(0)
    lane=lax.broadcasted_iota(jnp.int32,(1,PAIR),1)
    masks=[lane<HD, lane>=HD]
    for i in range(blocks):
        rows=rows_of(place_ref[seq,i])
        qi=q_ref[rows,:]
        outs=[]
        for h in range(2):
            qh=jnp.where(masks[h],qi,jnp.zeros_like(qi))
            ss=[nt(qh,k_ref[rows_of(place_ref[seq,j]),:])*score_scale for j in range(i+1)]
            top=ss[0]
            for s in ss[1:]: top=jnp.maximum(top,s)
            top=jnp.max(top,axis=1,keepdims=True)
            ps=[jnp.exp2(s-top) for s in ss]
            tot=ps[0]
            for p in ps[1:]: tot=tot+p
            tot=jnp.sum(tot,axis=1,keepdims=True)
            acc=None
            for j in range(i+1):
                t=nn(ps[j].astype(jnp.bfloat16),v_ref[rows_of(place_ref[seq,j]),:])
                acc=t if acc is None else acc+t
            outs.append(acc*(1.0/tot))
            lse=top+jnp.log2(tot)
            lse_ref[h:h+1,rows]=jnp.transpose(jnp.broadcast_to(lse,(BLK,PAIR)))[0:1,:]
        o_ref[rows,:]=jnp.where(masks[0],outs[0],outs[1]).astype(o_ref.dtype)

def attend(place, qkv):
    tokens,width3=qkv.shape
    seqs,blocks=place.shape
    length=tokens//seqs
    width=width3//3
    pairs=width//PAIR
    spec=lambda part: pl.BlockSpec((length,PAIR),lambda s,p,place:(s,part*pairs+p))
    return pl.pallas_call(
        functools.partial(attend_kernel,blocks),
        grid_spec=pltpu.PrefetchScalarGridSpec(
            num_scalar_prefetch=1,grid=(seqs,pairs),
            in_specs=[spec(0),spec(1),spec(2)],
            out_specs=[pl.BlockSpec((length,PAIR),lambda s,p,place:(s,p)),
                       pl.BlockSpec((None,None,8,length),lambda s,p,place:(s,p,0,0))]),
        out_shape=[jax.ShapeDtypeStruct((tokens,width),jnp.bfloat16),
                   jax.ShapeDtypeStruct((seqs,pairs,8,length),jnp.float32)],
        compiler_params=pltpu.CompilerParams(vmem_limit_bytes=48<<20),
        cost_estimate=small_cost,
        name="attend",
    )(place,qkv,qkv,qkv)

def attend_back_kernel(blocks, place_ref, q_ref, k_ref, v_ref, do_ref, lse_ref, dq_ref, dk_ref, dv_ref, kt, dk_acc, dv_acc):
    seq=pl.program_id(0)
    lane=lax.broadcasted_iota(jnp.int32,(1,PAIR),1)
    masks=[lane<HD, lane>=HD]
    for j in range(blocks):
        kt[j]=jnp.transpose(k_ref[rows_of(place_ref[seq,j]),:])
    for i in range(blocks):
        rows=rows_of(place_ref[seq,i])
        qi=q_ref[rows,:]
        doi=do_ref[rows,:]
        dqts=[]
        for h in range(2):
            qh=jnp.where(masks[h],qi,jnp.zeros_like(qi))
            doh=jnp.where(masks[h],doi,jnp.zeros_like(doi))
            lse=lse_ref[h:h+1,rows]
            pts=[];dpts=[];delta=None
            for j in range(i+1):
                rj=rows_of(place_ref[seq,j])
                pt=jnp.exp2(nt(k_ref[rj,:],qh)*score_scale-lse)
                dpt=nt(v_ref[rj,:],doh)
                d=jnp.sum(pt*dpt,axis=0,keepdims=True)
                delta=d if delta is None else delta+d
                pts.append(pt);dpts.append(dpt)
            dqt=None
            for j in range(i+1):
                pb=pts[j].astype(jnp.bfloat16)
                ds=(pts[j]*(dpts[j]-delta)).astype(jnp.bfloat16)
                dv=nn(pb,doh)
                dk=nn(ds,qh)
                if i==j and h==0:
                    dv_acc[j]=dv; dk_acc[j]=dk
                else:
                    dv_acc[j]+=dv; dk_acc[j]+=dk
                t=nn(kt[j,h*HD:(h+1)*HD,:],ds)
                dqt=t if dqt is None else dqt+t
            dqts.append(dqt)
        dq_ref[rows,:]=(jnp.transpose(jnp.concatenate(dqts,axis=0))*0.125).astype(dq_ref.dtype)
    for j in range(blocks):
        rows=rows_of(place_ref[seq,j])
        dk_ref[rows,:]=(dk_acc[j]*0.125).astype(dk_ref.dtype)
        dv_ref[rows,:]=dv_acc[j].astype(dv_ref.dtype)

def attend_back(place, qkv, upstream, lse):
    tokens,width3=qkv.shape
    seqs,blocks=place.shape
    length=tokens//seqs
    width=width3//3
    pairs=width//PAIR
    spec=lambda part: pl.BlockSpec((length,PAIR),lambda s,p,place:(s,part*pairs+p))
    one=pl.BlockSpec((length,PAIR),lambda s,p,place:(s,p))
    return pl.pallas_call(
        functools.partial(attend_back_kernel,blocks),
        grid_spec=pltpu.PrefetchScalarGridSpec(
            num_scalar_prefetch=1,grid=(seqs,pairs),
            in_specs=[spec(0),spec(1),spec(2),one,pl.BlockSpec((None,None,8,length),lambda s,p,place:(s,p,0,0))],
            out_specs=[one,one,one],
            scratch_shapes=[pltpu.VMEM((blocks,PAIR,BLK),jnp.bfloat16),pltpu.VMEM((blocks,BLK,PAIR),jnp.float32),pltpu.VMEM((blocks,BLK,PAIR),jnp.float32)]),
        out_shape=[jax.ShapeDtypeStruct((tokens,width),jnp.bfloat16)]*3,
        compiler_params=pltpu.CompilerParams(vmem_limit_bytes=48<<20),
        cost_estimate=small_cost,
        name="attend_back",
    )(place,qkv,qkv,qkv,upstream,lse)


def mlp_kernel(first, rows_step, c_ref, dy_ref, we_ref, ws_ref, be_ref, *rest):
    if first:
        y_ref, dc_ref, gwe_ref, gws_ref, gbe_ref, ct, act_all, du_all = rest
    else:
        y_in, dc_in, y_ref, dc_ref, gwe_ref, gws_ref, gbe_ref, ct, act_all, du_all, sem = rest
    step=pl.program_id(0)
    tokens=c_ref.shape[0]
    @pl.when(step==0)
    def _():
        ct[...]=jnp.transpose(c_ref[...])
        if first:
            y_ref[...]=jnp.zeros_like(y_ref)
            dc_ref[...]=jnp.zeros_like(dc_ref)
        else:
            a=pltpu.make_async_copy(y_in,y_ref,sem.at[0]); b=pltpu.make_async_copy(dc_in,dc_ref,sem.at[1])
            a.start(); b.start(); a.wait(); b.wait()
    we=we_ref[...]; ws=ws_ref[...]
    total=None
    for r in range(tokens//rows_step):
        rows=pl.ds(r*rows_step,rows_step)
        u=nn(c_ref[rows,:],we)+be_ref[...]
        t2=u*u
        th=jnp.tanh(gelu_root*u*(1.0+gelu_cubic*t2))
        half=0.5+0.5*th
        act=(u*half).astype(jnp.bfloat16)
        slope=half+(0.5*gelu_root)*u*(1.0-th*th)*(1.0+(3*gelu_cubic)*t2)
        du=(nt(dy_ref[rows,:],ws)*slope).astype(jnp.bfloat16)
        act_all[rows,:]=act; du_all[rows,:]=du
        y_ref[rows,:]+=nn(act,ws)
        dc_ref[rows,:]+=nt(du,we)
        s=jnp.sum(du.astype(jnp.float32),axis=0,keepdims=True)
        total=s if total is None else total+s
    gbe_ref[...]=total
    gwe_ref[...]=nn(ct[...],du_all[...]).astype(gwe_ref.dtype)
    gws_ref[...]=lax.dot_general(act_all[...],dy_ref[...],(((0,),(0,)),((),())),preferred_element_type=jnp.float32).astype(gws_ref.dtype)

def mlp(c,dy,we,ws,be,before=None,tile=256,rows_step=256):
    tokens,width=c.shape
    hidden=we.shape[1]
    whole=pl.BlockSpec((tokens,width),lambda t:(0,0))
    specs=[whole,whole,pl.BlockSpec((width,tile),lambda t:(0,t)),pl.BlockSpec((tile,width),lambda t:(t,0)),pl.BlockSpec((1,tile),lambda t:(0,t))]
    args=[c,dy,we,ws,be]
    scratch=[pltpu.VMEM((width,tokens),jnp.bfloat16),pltpu.VMEM((tokens,tile),jnp.bfloat16),pltpu.VMEM((tokens,tile),jnp.bfloat16)]
    if before is not None:
        specs+=[pl.BlockSpec(memory_space=pl.ANY)]*2
        args+=list(before)
        scratch+=[pltpu.SemaphoreType.DMA((2,))]
    return pl.pallas_call(
        functools.partial(mlp_kernel,before is None,rows_step),
        grid=(hidden//tile,),
        in_specs=specs,
        out_specs=[whole,whole,pl.BlockSpec((width,tile),lambda t:(0,t)),pl.BlockSpec((tile,width),lambda t:(t,0)),pl.BlockSpec((1,tile),lambda t:(0,t))],
        out_shape=[jax.ShapeDtypeStruct((tokens,width),jnp.float32)]*2+[jax.ShapeDtypeStruct((width,hidden),jnp.bfloat16),jax.ShapeDtypeStruct((hidden,width),jnp.bfloat16),jax.ShapeDtypeStruct((1,hidden),jnp.float32)],
        scratch_shapes=scratch,
        compiler_params=pltpu.CompilerParams(vmem_limit_bytes=56<<20),
        cost_estimate=small_cost,
        name="mlp",
    )(*args)


def layer_norm(values, gain_row, shift_row):
    centered = values - jnp.mean(values, axis=-1, keepdims=True)
    variance = jnp.mean(centered * centered, axis=-1, keepdims=True)
    inverse = lax.rsqrt(variance + norm_eps)
    normal_part = centered * inverse
    return (normal_part * gain_row + shift_row, normal_part, inverse)


def norm_back(upstream, normal_part, inverse, gain_row):
    scaled = upstream * gain_row
    inner_sum = jnp.mean(scaled, axis=-1, keepdims=True)
    along_sum = jnp.mean(scaled * normal_part, axis=-1, keepdims=True)
    values_grad = inverse * (scaled - inner_sum - normal_part * along_sum)
    return (values_grad, jnp.sum(upstream * normal_part, axis=0), jnp.sum(upstream, axis=0))


def outer_sum(left_side, right_side):
    return lax.dot_general(
        left_side, right_side, (((0,), (0,)), ((), ())), preferred_element_type=jnp.float32
    )


def adam_update(weight, moment_one, moment_two, gradient, step_rate, decay_rate):
    first_new = 0.5 * moment_one + 0.5 * gradient
    second_new = 0.5 * moment_two + 0.5 * gradient * gradient
    correct = 1.0 - 0.5**STEP
    direction = first_new / correct / (jnp.sqrt(second_new / correct) + adam_eps)
    updated = weight - step_rate * (direction + decay_rate * weight)
    return (updated, first_new, second_new)


def to_groups(matrix):
    row_count = matrix.shape[0]
    return matrix.reshape(row_count, H // group_heads, group_heads, HD).transpose(1, 0, 2, 3)


def from_groups(stacked):
    return stacked.transpose(1, 0, 2, 3).reshape(stacked.shape[1], H * HD)


def tile_scores(queries, key_rows, allowed):
    products = jnp.einsum("rgd,lgd->grl", queries, key_rows, preferred_element_type=jnp.float32)
    return jnp.where(allowed[None], products * 0.125, -1e30)


def tile_forward(queries, key_rows, value_rows, allowed):
    scores = tile_scores(queries, key_rows, allowed)
    largest = jnp.max(scores, axis=-1, keepdims=True)
    exponent = jnp.exp(scores - largest)
    row_total = jnp.sum(exponent, axis=-1, keepdims=True)
    weights = (exponent / row_total).astype(low)
    mixed = jnp.einsum("grl,lgd->rgd", weights, value_rows, preferred_element_type=jnp.float32)
    return (mixed, (largest + jnp.log(row_total))[..., 0])


def tile_backward(queries, key_rows, value_rows, allowed, logsum, upstream):
    scores = tile_scores(queries, key_rows, allowed)
    recomputed = jnp.exp(scores - logsum[..., None])
    value_grad = jnp.einsum(
        "grl,rgd->lgd", recomputed.astype(low), upstream, preferred_element_type=jnp.float32
    )
    weight_grad = jnp.einsum(
        "rgd,lgd->grl", upstream, value_rows, preferred_element_type=jnp.float32
    )
    inner_sum = jnp.sum(recomputed * weight_grad, axis=-1, keepdims=True)
    score_grad = (recomputed * (weight_grad - inner_sum)).astype(low)
    query_grad = (
        jnp.einsum("grl,lgd->rgd", score_grad, key_rows, preferred_element_type=jnp.float32) * 0.125
    )
    key_grad = (
        jnp.einsum("grl,rgd->lgd", score_grad, queries, preferred_element_type=jnp.float32) * 0.125
    )
    return (query_grad, key_grad, value_grad)


def spread_forward(queries, key_value, allowed):
    def one_sequence(pieces):
        queries, key_value, allowed = pieces
        width = queries.shape[1]
        mixed, logsum = lax.map(
            lambda triple: tile_forward(triple[0], triple[1], triple[2], allowed),
            (to_groups(queries), to_groups(key_value[:, :width]), to_groups(key_value[:, width:])),
        )
        return (from_groups(mixed), logsum)

    return lax.map(one_sequence, (queries, key_value, allowed))


def spread_backward(queries, key_value, allowed, logsum, upstream):
    def one_sequence(pieces):
        queries, key_value, allowed, logsum, upstream = pieces
        width = queries.shape[1]
        query_grad, key_grad, value_grad = lax.map(
            lambda member: tile_backward(
                member[0], member[1], member[2], allowed, member[3], member[4]
            ),
            (
                to_groups(queries),
                to_groups(key_value[:, :width]),
                to_groups(key_value[:, width:]),
                logsum,
                to_groups(upstream),
            ),
        )
        return (
            from_groups(query_grad),
            jnp.concatenate([from_groups(key_grad), from_groups(value_grad)], axis=1),
        )

    return lax.map(one_sequence, (queries, key_value, allowed, logsum, upstream))


class Slice:
    def __init__(self, ctx_size, wshard_size):
        rest = wshard_size // 2
        self.sizes = {"c": ctx_size, "z": 4, "y": rest // 4, "k": 2}

    def here(self):
        flat = lax.axis_index(axes)
        found = {}
        for name in ("k", "y", "z", "c"):
            found[name] = flat % self.sizes[name]
            flat = flat // self.sizes[name]
        return found

    def shift(self, value, name, by):
        pairs = []
        sizes = self.sizes
        for c in range(sizes["c"]):
            for z in range(sizes["z"]):
                for y in range(sizes["y"]):
                    for k in range(sizes["k"]):
                        spot = {"c": c, "z": z, "y": y, "k": k}
                        goal = dict(spot)
                        goal[name] = (spot[name] + by) % sizes[name]
                        pairs.append((self.flat(spot), self.flat(goal)))
        return lax.ppermute(value, axes, pairs)

    def flat(self, spot):
        sizes = self.sizes
        return ((spot["c"] * sizes["z"] + spot["z"]) * sizes["y"] + spot["y"]) * sizes["k"] + spot[
            "k"
        ]

    def stack(self, array, name, here):
        size = self.sizes[name]
        parts = [array] + [self.shift(array, name, by) for by in range(1, size)]
        if size > 4:
            ordered = [parts[(-place) % size] for place in range(size)]
            return jnp.roll(jnp.stack(ordered), here[name], axis=0)
        return jnp.stack(
            [lax.select_n((here[name] - place) % size, *parts) if size > 2 else
             jnp.where(here[name] == place, parts[0], parts[1]) for place in range(size)]
        )

    def reach(self, pieces, name):
        grown = list(pieces)
        for by in range(1, self.sizes[name]):
            for array, place in pieces:
                moved = dict(place)
                moved[name] = (place[name] - by) % self.sizes[name]
                grown.append((self.shift(array, name, by), moved))
        return grown

    def gather_split(self, stacked, cut, here):
        sizes = self.sizes
        depth, rows, columns = stacked.shape
        out = jnp.zeros((sizes["c"], depth, sizes["y"], rows, columns), stacked.dtype)
        for low_column, high_column, order in ((0, cut, "cy"), (cut, columns, "yc")):
            pieces = [(stacked[:, :, low_column:high_column], here)]
            for name in order:
                pieces = self.reach(pieces, name)
            for array, place in pieces:
                out = lax.dynamic_update_slice(
                    out, array[None, :, None], (place["c"], 0, place["y"], 0, low_column)
                )
        return out.reshape(-1, columns)

    def gather_deep(self, block, here):
        sizes = self.sizes
        stacked = jnp.moveaxis(self.stack(self.stack(block, "c", here), "z", here), 0, 1)
        out = jnp.zeros(stacked.shape[:2] + (sizes["y"],) + block.shape, block.dtype)
        for array, place in self.reach([(stacked, here)], "y"):
            out = lax.dynamic_update_slice(
                out, array[:, :, None], (0, 0, place["y"], 0, 0)
            )
        return out.reshape(-1, block.shape[1])

    def send_terms(self, value, name, place, here):
        size = self.sizes[name]
        own = lax.dynamic_index_in_dim(value, here[name], place, False)
        moved = [
            self.shift(
                lax.dynamic_index_in_dim(value, (here[name] + by) % size, place, False), name, by
            )
            for by in range(1, size)
        ]
        return own, moved

    def add_terms(self, terms, kind=low):
        own, moved = terms
        total = own.astype(jnp.float32)
        for other in moved:
            total = total + other.astype(jnp.float32)
        return total.astype(kind)

    def everywhere(self, value):
        for name in ("k", "c", "y", "z"):
            total = value
            for by in range(1, self.sizes[name]):
                total = total + self.shift(value, name, by)
            value = total
        return value


def tie(value, *others):
    return lax.optimization_barrier((value, others))[0]


def by_core(core, first, second, axis):
    return jnp.where(
        core == 0,
        jnp.concatenate([first, second], axis=axis),
        jnp.concatenate([second, first], axis=axis),
    )


def pick(core, array, axis):
    return (
        lax.dynamic_index_in_dim(array, core, axis, False),
        lax.dynamic_index_in_dim(array, 1 - core, axis, False),
    )


def body(
    grid,
    block_input,
    block_order,
    cotangent,
    joint_weight,
    mixing_weight,
    expand_weight,
    shrink_weight,
    vectors,
    joint_first,
    mixing_first,
    expand_first,
    shrink_first,
    vectors_first,
    joint_second,
    mixing_second,
    expand_second,
    shrink_second,
    vectors_second,
):
    here = grid.here()
    core, ctx = here["k"], here["c"]
    ctx_size = grid.sizes["c"]
    seq_count, row_count, width = block_input.shape
    half = width // 2
    hidden_width = expand_weight.shape[1]
    slot = shrink_weight.shape[0]
    whole_sequences = ctx_size == seq_count
    tokens = seq_count * row_count
    row_blocks = row_count // BLK

    def to_sequence(rows):
        if not whole_sequences:
            return rows.reshape(tokens, width)
        parts = [lax.dynamic_index_in_dim(rows, ctx, 0, False)]
        for by in range(1, ctx_size):
            sent = lax.dynamic_index_in_dim(rows, (ctx + by) % ctx_size, 0, False)
            parts.append(grid.shift(sent, "c", by))
        return jnp.concatenate(parts, axis=0)

    def from_sequence(rows, kind):
        if not whole_sequences:
            return rows.astype(kind).reshape(seq_count, row_count, width)
        parts = [rows[:row_count].astype(kind)]
        for by in range(1, ctx_size):
            sent = rows[by * row_count : (by + 1) * row_count].astype(low)
            parts.append(grid.shift(sent, "c", -by).astype(kind))
        stacked = jnp.stack(parts)
        if ctx_size == 2:
            return jnp.where(ctx == 0, stacked, stacked[::-1])
        return jnp.roll(stacked, ctx, axis=0)

    def halves(shard, outer, inner):
        own, other = pick(core, shard.astype(low).reshape(shard.shape[0], outer, 2, inner), 2)
        return own.reshape(shard.shape[0], -1), other.reshape(shard.shape[0], -1)

    def rows_of_chip(own, other):
        return by_core(core, own, grid.shift(other, "k", 1), 0)

    part = vectors.shape[1]
    table = jnp.pad(vectors.T.astype(low), ((0, 0), (0, 128 - vectors.shape[0])))
    joint_halves = halves(joint_weight, 3, half)
    joint_block = rows_of_chip(
        *[jnp.concatenate([table, piece], axis=1) for piece in joint_halves]
    )
    joint_stack = grid.stack(joint_block, "z", here)
    input_rows = to_sequence(block_input).astype(jnp.float32)
    joint_and_table = grid.gather_split(joint_stack, 128 + 3 * half // 2, here)
    joint_own = joint_and_table[:, 128:]
    vector_values = joint_and_table[:, : vectors.shape[0]].T.astype(jnp.float32)
    joint_other = grid.shift(joint_own, "k", 1)

    mixing_shard, expand_shard, shrink_shard, cotangent = tie(
        (mixing_weight, expand_weight, shrink_weight, cotangent), joint_stack
    )
    mixing_own = grid.gather_split(
        grid.stack(rows_of_chip(*halves(mixing_shard, 1, half)), "z", here), half // 2, here
    )
    mixing_full = by_core(core, mixing_own, grid.shift(mixing_own, "k", 1), 1)
    expand_own = grid.gather_deep(
        rows_of_chip(*halves(expand_shard, hidden_width // (2 * slot), slot)), here
    )
    expand_other = grid.shift(expand_own, "k", 1)
    shrink_own = grid.gather_split(
        grid.stack(shrink_shard.astype(low), "z", here), half, here
    )
    shrink_other = grid.shift(shrink_own, "k", 1)
    upstream = to_sequence(cotangent)

    normed_first, normal_first, inverse_first = layer_norm(
        input_rows, vector_values[0], vector_values[1]
    )
    first_low = normed_first.astype(low)
    query_bias = pick(core, vector_values[2].reshape(2, half), 0)
    value_bias = pick(core, vector_values[3].reshape(2, half), 0)

    def project(weight, query_shift, value_shift):
        shift = jnp.concatenate([query_shift, jnp.zeros_like(query_shift), value_shift])
        return (jnp.dot(first_low, weight, preferred_element_type=jnp.float32) + shift).astype(low)

    joint_out_own = project(joint_own, query_bias[0], value_bias[0])
    joint_out_other = project(joint_other, query_bias[1], value_bias[1])
    if whole_sequences:
        order = lax.dynamic_slice_in_dim(block_order, ctx, 1, 0)[0]
        stored = jnp.arange(order.shape[0], dtype=jnp.int32)
        moved = ((ctx - stored // row_blocks) % ctx_size) * row_blocks + stored % row_blocks
        place = jnp.sum(
            jnp.where(order[None, :] == stored[:, None], moved[None, :], 0), axis=1
        )[None].astype(jnp.int32)
        mixed_own, logsum_own = attend(place, joint_out_own)
        mixed_other, logsum_other = attend(place, joint_out_other)
    else:
        joined = [
            by_core(
                core,
                joint_out_own[:, part * half : (part + 1) * half],
                joint_out_other[:, part * half : (part + 1) * half],
                1,
            ).reshape(seq_count, row_count, width)
            for part in range(3)
        ]
        queries = joined[0]
        key_value = lax.all_gather(
            jnp.concatenate(joined[1:], axis=2), "ctx", axis=1, tiled=True
        )
        own_blocks = lax.dynamic_slice_in_dim(block_order, ctx * row_blocks, row_blocks, 1)
        query_block = jnp.repeat(own_blocks, BLK, axis=1, total_repeat_length=row_count)
        key_block = jnp.repeat(block_order, BLK, axis=1, total_repeat_length=key_value.shape[1])
        allowed = key_block[:, None, :] <= query_block[:, :, None]
        mixed, logsum = spread_forward(queries, key_value, allowed)
        mixed_own, mixed_other = pick(core, mixed.astype(low).reshape(tokens, 2, half), 1)
    mixing_rows = pick(core, mixing_full.reshape(2, half, width), 0)
    branch = (
        jnp.dot(mixed_own, mixing_rows[0], preferred_element_type=jnp.float32)
        + jnp.dot(mixed_other, mixing_rows[1], preferred_element_type=jnp.float32)
        + vector_values[4]
    )
    middle = input_rows + branch
    normed_second, normal_second, inverse_second = layer_norm(
        middle, vector_values[5], vector_values[6]
    )
    second_low = normed_second.astype(low)

    hidden_bias = pick(core, vector_values[8:].reshape(hidden_width // (2 * slot), 2, slot), 1)
    result, second_grad, expand_grad_other, shrink_grad_other, hidden_bias_other = mlp(
        second_low, upstream, expand_other, shrink_other, hidden_bias[1].reshape(1, -1)
    )
    expand_moved = grid.shift(expand_grad_other, "k", 1)
    shrink_moved = grid.shift(shrink_grad_other, "k", 1)
    result, second_grad, expand_grad_own, shrink_grad_own, hidden_bias_own = mlp(
        second_low,
        upstream,
        expand_own,
        shrink_own,
        hidden_bias[0].reshape(1, -1),
        before=(result, second_grad),
    )

    def by_device(own, moved):
        sizes = grid.sizes
        total = grid.add_terms((own, [moved]))
        return total.reshape(sizes["c"], sizes["z"], sizes["y"], -1, own.shape[-1])

    def join_columns(part, outer, inner):
        rows = part.shape[0] // 2
        own, other = pick(core, part.reshape(2, rows, outer, inner), 0)
        return by_core(core, own[:, :, None], grid.shift(other, "k", 1)[:, :, None], 2).reshape(
            rows, 2 * outer * inner
        )

    def split_one(value, cut):
        return (
            grid.send_terms(value[..., :cut], "y", 2, here),
            grid.send_terms(value[..., cut:], "c", 0, here),
        )

    def split_two(terms):
        return (
            grid.send_terms(grid.add_terms(terms[0]), "c", 0, here),
            grid.send_terms(grid.add_terms(terms[1]), "y", 1, here),
        )

    def split_three(terms):
        joined = jnp.concatenate([grid.add_terms(terms[0]), grid.add_terms(terms[1])], axis=-1)
        return grid.send_terms(joined, "z", 0, here)

    shrink_terms = split_one(by_device(shrink_grad_own, shrink_moved), half)
    expand_terms = grid.send_terms(by_device(expand_grad_own, expand_moved), "y", 2, here)
    block_output = from_sequence(middle + result + vector_values[7], low)

    upstream_float = upstream.astype(jnp.float32)
    middle_part, gain_two, shift_two = norm_back(
        second_grad, normal_second, inverse_second, vector_values[5]
    )
    middle_grad = upstream_float + middle_part
    branch_low = middle_grad.astype(low)
    mixing_grad = by_core(
        core,
        outer_sum(mixed_own, branch_low).astype(low),
        outer_sum(mixed_other, branch_low).astype(low),
        0,
    )
    mixing_grad_own, mixing_grad_other = pick(core, mixing_grad.reshape(width, 2, half), 1)
    mixing_moved = grid.shift(mixing_grad_other, "k", 1)
    mixed_grad_other = nt(branch_low, mixing_rows[1]).astype(low)
    mixed_grad_own = nt(branch_low, mixing_rows[0]).astype(low)
    mixing_terms = split_one(by_device(mixing_grad_own, mixing_moved), half // 2)
    if whole_sequences:
        mixed_grad_other = tie(mixed_grad_other, mixing_moved)
        joint_back_other = jnp.concatenate(
            attend_back(place, joint_out_other, mixed_grad_other, logsum_other), axis=1
        )
        joint_grad_other = outer_sum(first_low, joint_back_other).astype(low)
        joint_moved = grid.shift(joint_grad_other, "k", 1)
        shrink_terms = split_two(shrink_terms)
        expand_terms = grid.send_terms(grid.add_terms(expand_terms), "z", 1, here)
        mixing_terms = split_two(mixing_terms)
        mixed_grad_own = tie(
            mixed_grad_own,
            joint_grad_other,
            block_output,
            [terms[0] for terms in shrink_terms + mixing_terms],
            expand_terms[0],
        )
        joint_back_own = jnp.concatenate(
            attend_back(place, joint_out_own, mixed_grad_own, logsum_own), axis=1
        )
    else:
        mixed_grad = by_core(core, mixed_grad_own, mixed_grad_other, 1)
        query_grad, key_value_grad = spread_backward(
            queries, key_value, allowed, logsum, mixed_grad.reshape(seq_count, row_count, width)
        )
        summed = lax.psum_scatter(
            key_value_grad.astype(low), "ctx", scatter_dimension=1, tiled=True
        )
        pieces = [query_grad.astype(low), summed[..., :width], summed[..., width:]]
        both = [pick(core, piece.reshape(tokens, 2, half), 1) for piece in pieces]
        joint_back_own = jnp.concatenate([piece[0] for piece in both], axis=1)
        joint_back_other = jnp.concatenate([piece[1] for piece in both], axis=1)
        joint_grad_other = outer_sum(first_low, joint_back_other).astype(low)
        joint_moved = grid.shift(joint_grad_other, "k", 1)
        shrink_terms = split_two(shrink_terms)
        expand_terms = grid.send_terms(grid.add_terms(expand_terms), "z", 1, here)
        mixing_terms = split_two(mixing_terms)
    joint_grad_own = outer_sum(first_low, joint_back_own).astype(low)
    joint_terms = split_one(by_device(joint_grad_own, joint_moved), 3 * half // 2)
    shrink_terms = split_three(shrink_terms)
    expand_terms = grid.send_terms(grid.add_terms(expand_terms), "c", 0, here)
    mixing_terms = split_three(mixing_terms)
    joint_back_own = tie(
        joint_back_own,
        [terms[0] for terms in joint_terms],
        shrink_terms[0],
        expand_terms[0],
        mixing_terms[0],
    )
    first_grad = nt(joint_back_other, joint_other) + nt(joint_back_own, joint_own)
    input_part, gain_one, shift_one = norm_back(
        first_grad, normal_first, inverse_first, vector_values[0]
    )
    input_gradient = from_sequence(middle_grad + input_part, jnp.float32)
    shrink_sum = grid.add_terms(shrink_terms, jnp.float32)
    expand_sum = join_columns(
        grid.add_terms(expand_terms, jnp.float32), hidden_width // (2 * slot), slot
    )
    mixing_sum = join_columns(grid.add_terms(mixing_terms, jnp.float32), 1, half)
    joint_terms = split_three(split_two(joint_terms))
    joint_sum = join_columns(grid.add_terms(joint_terms, jnp.float32), 3, half)

    def column_sum(rows):
        return jnp.sum(rows.astype(jnp.float32), axis=0)

    back_sums = [column_sum(joint_back_own), column_sum(joint_back_other)]
    query_bias_grad = by_core(core, back_sums[0][:half], back_sums[1][:half], 0)
    value_bias_grad = by_core(core, back_sums[0][2 * half :], back_sums[1][2 * half :], 0)
    hidden_bias_grad = by_core(
        core,
        hidden_bias_own.reshape(-1, 1, slot),
        hidden_bias_other.reshape(-1, 1, slot),
        1,
    ).reshape(-1, width)
    vector_grad = jnp.concatenate(
        [
            jnp.stack(
                [
                    gain_one,
                    shift_one,
                    query_bias_grad,
                    value_bias_grad,
                    column_sum(branch_low),
                    gain_two,
                    shift_two,
                    column_sum(upstream),
                ]
            ),
            hidden_bias_grad,
        ],
        axis=0,
    )
    vector_sum = lax.dynamic_slice_in_dim(
        grid.everywhere(vector_grad),
        lax.axis_index(axes) * part,
        part,
        1,
    )
    joint_new, joint_moment, joint_square = adam_update(
        joint_weight, joint_first, joint_second, joint_sum, 0.05, 0.1
    )
    mixing_new, mixing_moment, mixing_square = adam_update(
        mixing_weight, mixing_first, mixing_second, mixing_sum, 0.05, 0.1
    )
    expand_new, expand_moment, expand_square = adam_update(
        expand_weight, expand_first, expand_second, expand_sum, 0.05, 0.1
    )
    shrink_new, shrink_moment, shrink_square = adam_update(
        shrink_weight, shrink_first, shrink_second, shrink_sum, 0.05, 0.1
    )
    vectors_new, vectors_moment, vectors_square = adam_update(
        vectors, vectors_first, vectors_second, vector_sum, 0.5, 0.0
    )
    return (
        block_output,
        input_gradient,
        joint_new,
        mixing_new,
        expand_new,
        shrink_new,
        vectors_new,
        joint_moment,
        mixing_moment,
        expand_moment,
        shrink_moment,
        vectors_moment,
        joint_square,
        mixing_square,
        expand_square,
        shrink_square,
        vectors_square,
        joint_new.astype(low),
        mixing_new.astype(low),
        expand_new.astype(low),
        shrink_new.astype(low),
        vectors_new.astype(low),
    )


def solution(mesh):
    grid = Slice(mesh.shape["ctx"], mesh.shape["wshard"])
    rows = P("wshard", "ctx", None)
    matrix = P(axes, None)
    table = P(None, axes)
    parameters = (matrix, matrix, matrix, matrix, table)
    return jax.shard_map(
        functools.partial(body, grid),
        mesh=mesh,
        in_specs=(rows, P("wshard", None), rows) + parameters * 3,
        out_specs=(rows, rows) + parameters * 4,
        check_vma=False,
    )
```

```python
import functools

import jax
import jax.numpy as jnp
from jax import lax
from jax.experimental import pallas as pl
from jax.experimental.pallas import tpu as pltpu
from jax.sharding import PartitionSpec as P

H = 16
HD = 64
BLK = 256
STEP = 10
PAIR = 2 * HD

norm_eps = 1e-05
adam_eps = 1e-08
group_heads = 4
score_scale = 0.125 * 1.4426950408889634
gelu_root = 0.7978845608028654
gelu_cubic = 0.044715
low = jnp.bfloat16
axes = ("ctx", "wshard")
small_cost = pl.CostEstimate(flops=1024, bytes_accessed=1024, transcendentals=0)


def nt(a,b):
    return lax.dot_general(a,b,(((1,),(1,)),((),())),preferred_element_type=jnp.float32)
def nn(a,b):
    return jnp.dot(a,b,preferred_element_type=jnp.float32)

def arrange_kernel(place_ref, rows_ref, out_ref):
    out_ref[...] = rows_ref[...]


def arrange(place, rows):
    columns = rows.shape[1]
    return pl.pallas_call(
        arrange_kernel,
        grid_spec=pltpu.PrefetchScalarGridSpec(
            num_scalar_prefetch=1,
            grid=(place.shape[0],),
            in_specs=[pl.BlockSpec((BLK, columns), lambda i, place: (place[i], 0))],
            out_specs=pl.BlockSpec((BLK, columns), lambda i, place: (i, 0)),
        ),
        out_shape=jax.ShapeDtypeStruct(rows.shape, rows.dtype),
        cost_estimate=small_cost,
        name="arrange",
    )(place, rows)


def block_rows(block):
    return pl.ds(block * BLK, BLK)


def thirds(ref):
    return [ref.at[:, pl.ds(part * PAIR, PAIR)] for part in range(3)]


def attend_pair(blocks, projected, o_ref, lse_ref, between):
    q_ref, k_ref, v_ref = thirds(projected)
    lane = lax.broadcasted_iota(jnp.int32, (1, PAIR), 1)
    masks = [lane < HD, lane >= HD]
    for i in range(blocks):
        between(i)
        rows = block_rows(i)
        queries = q_ref[rows, :]
        outs = []
        for h in range(2):
            masked = jnp.where(masks[h], queries, jnp.zeros_like(queries))
            scores = [nt(masked, k_ref[block_rows(j), :]) * score_scale for j in range(i + 1)]
            top = scores[0]
            for score in scores[1:]:
                top = jnp.maximum(top, score)
            top = jnp.max(top, axis=1, keepdims=True)
            weights = [jnp.exp2(score - top) for score in scores]
            total = weights[0]
            for weight in weights[1:]:
                total = total + weight
            total = jnp.sum(total, axis=1, keepdims=True)
            mixed = nn(weights[0].astype(low), v_ref[block_rows(0), :])
            for j in range(1, i + 1):
                mixed = mixed + nn(weights[j].astype(low), v_ref[block_rows(j), :])
            outs.append(mixed * (1.0 / total))
            logsum = jnp.broadcast_to(top + jnp.log2(total), (BLK, PAIR))
            lse_ref[h : h + 1, rows] = jnp.transpose(logsum)[0:1, :]
        o_ref[rows, :] = jnp.where(masks[0], outs[0], outs[1]).astype(o_ref.dtype)


def attend_back_pair(
    blocks, projected, do_ref, lse_ref, back_ref, turned, key_sum, value_sum, between
):
    q_ref, k_ref, v_ref = thirds(projected)
    dq_ref, dk_ref, dv_ref = thirds(back_ref)
    lane = lax.broadcasted_iota(jnp.int32, (1, PAIR), 1)
    masks = [lane < HD, lane >= HD]
    for j in range(blocks):
        turned[j] = jnp.transpose(k_ref[block_rows(j), :])
    for i in range(blocks):
        between(i)
        rows = block_rows(i)
        queries, upstream = q_ref[rows, :], do_ref[rows, :]
        query_grads = []
        for h in range(2):
            masked = jnp.where(masks[h], queries, jnp.zeros_like(queries))
            pulled = jnp.where(masks[h], upstream, jnp.zeros_like(upstream))
            logsum = lse_ref[h : h + 1, rows]
            weights, pulls, inner = [], [], None
            for j in range(i + 1):
                weight = jnp.exp2(nt(k_ref[block_rows(j), :], masked) * score_scale - logsum)
                pull = nt(v_ref[block_rows(j), :], pulled)
                along = jnp.sum(weight * pull, axis=0, keepdims=True)
                inner = along if inner is None else inner + along
                weights.append(weight)
                pulls.append(pull)
            query_grad = None
            for j in range(i + 1):
                score_grad = (weights[j] * (pulls[j] - inner)).astype(low)
                value_grad = nn(weights[j].astype(low), pulled)
                key_grad = nn(score_grad, masked)
                if i == j and h == 0:
                    value_sum[j] = value_grad
                    key_sum[j] = key_grad
                else:
                    value_sum[j] += value_grad
                    key_sum[j] += key_grad
                piece = nn(turned[j, h * HD : (h + 1) * HD, :], score_grad)
                query_grad = piece if query_grad is None else query_grad + piece
            query_grads.append(query_grad)
        joined = jnp.transpose(jnp.concatenate(query_grads, axis=0))
        dq_ref[rows, :] = (joined * 0.125).astype(dq_ref.dtype)
    for j in range(blocks):
        dk_ref[block_rows(j), :] = (key_sum[j] * 0.125).astype(dk_ref.dtype)
        dv_ref[block_rows(j), :] = value_sum[j].astype(dv_ref.dtype)


def hooks(step, schedule):
    def between(block):
        for when, where, action in schedule:
            if where == block:
                pl.when(step == when)(action)

    return between


any_place = pl.BlockSpec(memory_space=pl.ANY)
whole_vmem = pl.BlockSpec(memory_space=pltpu.VMEM)


def mlp_kernel(first, rows_step, c_ref, dy_ref, we_ref, ws_ref, be_ref, *rest):
    if first:
        y_ref, dc_ref, gwe_ref, gws_ref, gbe_ref, ct, act_all, du_all = rest
    else:
        y_in, dc_in, y_ref, dc_ref, gwe_ref, gws_ref, gbe_ref, ct, act_all, du_all, sem = rest
    step=pl.program_id(0)
    tokens=c_ref.shape[0]
    @pl.when(step==0)
    def _():
        ct[...]=jnp.transpose(c_ref[...])
        if first:
            y_ref[...]=jnp.zeros_like(y_ref)
            dc_ref[...]=jnp.zeros_like(dc_ref)
        else:
            a=pltpu.make_async_copy(y_in,y_ref,sem.at[0]); b=pltpu.make_async_copy(dc_in,dc_ref,sem.at[1])
            a.start(); b.start(); a.wait(); b.wait()
    we=we_ref[...]; ws=ws_ref[...]
    total=None
    for r in range(tokens//rows_step):
        rows=pl.ds(r*rows_step,rows_step)
        u=nn(c_ref[rows,:],we)+be_ref[...]
        t2=u*u
        th=jnp.tanh(gelu_root*u*(1.0+gelu_cubic*t2))
        half=0.5+0.5*th
        act=(u*half).astype(jnp.bfloat16)
        slope=half+(0.5*gelu_root)*u*(1.0-th*th)*(1.0+(3*gelu_cubic)*t2)
        du=(nt(dy_ref[rows,:],ws)*slope).astype(jnp.bfloat16)
        act_all[rows,:]=act; du_all[rows,:]=du
        y_ref[rows,:]+=nn(act,ws)
        dc_ref[rows,:]+=nt(du,we)
        s=jnp.sum(du.astype(jnp.float32),axis=0,keepdims=True)
        total=s if total is None else total+s
    gbe_ref[...]=total
    gwe_ref[...]=nn(ct[...],du_all[...]).astype(gwe_ref.dtype)
    gws_ref[...]=lax.dot_general(act_all[...],dy_ref[...],(((0,),(0,)),((),())),preferred_element_type=jnp.float32).astype(gws_ref.dtype)

def mlp(c,dy,we,ws,be,before=None,tile=256,rows_step=256):
    tokens,width=c.shape
    hidden=we.shape[1]
    whole=pl.BlockSpec((tokens,width),lambda t:(0,0))
    specs=[whole,whole,pl.BlockSpec((width,tile),lambda t:(0,t)),pl.BlockSpec((tile,width),lambda t:(t,0)),pl.BlockSpec((1,tile),lambda t:(0,t))]
    args=[c,dy,we,ws,be]
    scratch=[pltpu.VMEM((width,tokens),jnp.bfloat16),pltpu.VMEM((tokens,tile),jnp.bfloat16),pltpu.VMEM((tokens,tile),jnp.bfloat16)]
    if before is not None:
        specs+=[pl.BlockSpec(memory_space=pl.ANY)]*2
        args+=list(before)
        scratch+=[pltpu.SemaphoreType.DMA((2,))]
    return pl.pallas_call(
        functools.partial(mlp_kernel,before is None,rows_step),
        grid=(hidden//tile,),
        in_specs=specs,
        out_specs=[whole,whole,pl.BlockSpec((width,tile),lambda t:(0,t)),pl.BlockSpec((tile,width),lambda t:(t,0)),pl.BlockSpec((1,tile),lambda t:(0,t))],
        out_shape=[jax.ShapeDtypeStruct((tokens,width),jnp.float32)]*2+[jax.ShapeDtypeStruct((width,hidden),jnp.bfloat16),jax.ShapeDtypeStruct((hidden,width),jnp.bfloat16),jax.ShapeDtypeStruct((1,hidden),jnp.float32)],
        scratch_shapes=scratch,
        compiler_params=pltpu.CompilerParams(vmem_limit_bytes=56<<20),
        cost_estimate=small_cost,
        name="mlp",
    )(*args)


MESH = pl.DeviceIdType.MESH


class Spot:
    def __init__(self, sizes):
        self.sizes = sizes
        ctx, shard = lax.axis_index("ctx"), lax.axis_index("wshard")
        self.c = ctx
        self.k = shard % 2
        self.y = (shard // 2) % 2
        self.z = shard // 4

    def device(self, name, by=1):
        c, z, y, k = self.c, self.z, self.y, self.k
        if name == "c":
            c = 1 - c
        if name == "y":
            y = 1 - y
        if name == "k":
            k = 1 - k
        if name == "z":
            z = (z + by) % self.sizes["z"]
        return (c, (z * 2 + y) * 2 + k)

    def meet(self, names):
        barrier = pltpu.get_barrier_semaphore()
        partners = []
        for name in names:
            for by in range(1, self.sizes[name]):
                partners.append(self.device(name, by))
        for partner in partners:
            pl.semaphore_signal(barrier, inc=1, device_id=partner, device_id_type=MESH)
        pl.semaphore_wait(barrier, len(partners))


class Mover:
    def __init__(self, spot, sems):
        self.spot, self.sems, self.count = spot, sems, 0

    def copy(self, source, target, name, by=1):
        number = self.count
        self.count += 1
        return pltpu.make_async_remote_copy(
            src_ref=source,
            dst_ref=target,
            send_sem=self.sems.at[0, number],
            recv_sem=self.sems.at[1, number],
            device_id=self.spot.device(name, by),
            device_id_type=MESH,
        )

    def local(self, source, target):
        number = self.count
        self.count += 1
        return pltpu.make_async_copy(source, target, self.sems.at[0, number])


def start(copies):
    for copy in copies:
        copy.start()


def wait(copies):
    for copy in copies:
        copy.wait()


def span(first, size):
    return pl.ds(pl.multiple_of(first, 128), size)


class GatherJob:
    def __init__(self, mover, half, offset, width, cut, core=True):
        spot = mover.spot
        c, z, y = spot.c, spot.z, spot.y

        def part(ci, zi, yi, first, size):
            return half.at[ci, zi, yi, :, span(offset + first, size)]

        every = slice(None)
        self.along_z = []
        for by in range(1, spot.sizes["z"]):
            block = part(c, z, y, 0, width)
            self.along_z.append(mover.copy(block, block, "z", by))
        self.near, self.far = [], []
        for first, size, one, two in ((0, cut, "c", "y"), (cut, width - cut, "y", "c")):
            if size == 0:
                continue
            block = part(c, every, y, first, size)
            self.near.append(mover.copy(block, block, one))
            self.near.append(mover.copy(block, block, two))
            block = part(1 - c if one == "c" else c, every, 1 - y if one == "y" else y, first, size)
            self.far.append(mover.copy(block, block, two))
        self.core = [[], [], []]
        if core:
            for stage, ci, yi in ((0, c, y), (1, 1 - c, y), (1, c, 1 - y), (2, 1 - c, 1 - y)):
                block = part(ci, every, yi, 0, width)
                self.core[stage].append(mover.copy(block, block, "k"))


def first_rows(mover, halves, out, width):
    spot = mover.spot
    rows = halves.shape[1]
    block = out.at[spot.c, spot.z, spot.y, pl.ds(pl.multiple_of(spot.k * rows, rows), rows)]
    return [
        mover.local(halves.at[spot.k], block.at[:, span(spot.k * width, width)]),
        mover.copy(halves.at[1 - spot.k], block.at[:, span((1 - spot.k) * width, width)], "k"),
    ]


class ReduceJob:
    def __init__(self, mover, mine, theirs, cut, scratch):
        self.spot = spot = mover.spot
        self.cut = cut
        (self.total, self.other, self.by_y, self.by_c, self.then_c, self.then_y, self.by_z) = scratch
        self.width = width = self.total.shape[-1]
        c, z, y = spot.c, spot.z, spot.y
        depth = spot.sizes["z"]
        every, left, right = slice(None), pl.ds(0, cut), pl.ds(cut, width - cut)
        total = self.total
        self.first = [mover.local(mine, total), mover.copy(theirs, self.other, "k")]
        self.near = [
            mover.copy(total.at[every, every, 1 - y, every, left], self.by_y, "y"),
            mover.copy(total.at[1 - c, every, every, every, right], self.by_c, "c"),
        ]
        self.far = [
            mover.copy(total.at[1 - c, every, y, every, left], self.then_c, "c"),
            mover.copy(total.at[c, every, 1 - y, every, right], self.then_y, "y"),
        ]
        self.along_z = [
            mover.copy(total.at[c, (z + by) % depth, y], self.by_z.at[by - 1], "z", by)
            for by in range(1, depth)
        ]

    @staticmethod
    def scratch(sizes, rows, width, cut):
        c, z, y = sizes["c"], sizes["z"], sizes["y"]
        shapes = [
            (c, z, y, rows, width),
            (c, z, y, rows, width),
            (c, z, rows, cut),
            (z, y, rows, width - cut),
            (z, rows, cut),
            (z, rows, width - cut),
            (z - 1, rows, width),
        ]
        return [pltpu.VMEM(shape, low) for shape in shapes]

    def add(self, where, extra):
        self.total[where] = (
            self.total[where].astype(jnp.float32) + extra.astype(jnp.float32)
        ).astype(low)

    def add_first(self):
        sizes = self.spot.sizes
        for c in range(sizes["c"]):
            for y in range(sizes["y"]):

                @pl.loop(0, sizes["z"])
                def _(z):
                    self.add((c, z, y), self.other[c, z, y])

    def add_near(self):
        spot, cut = self.spot, self.cut
        left, right = pl.ds(0, cut), pl.ds(cut, self.width - cut)

        @pl.loop(0, spot.sizes["z"])
        def _(z):
            for c in range(spot.sizes["c"]):
                self.add((c, z, spot.y, slice(None), left), self.by_y[c, z])
            for y in range(spot.sizes["y"]):
                self.add((spot.c, z, y, slice(None), right), self.by_c[z, y])

    def add_far(self):
        spot, cut = self.spot, self.cut
        left, right = pl.ds(0, cut), pl.ds(cut, self.width - cut)

        @pl.loop(0, spot.sizes["z"])
        def _(z):
            self.add((spot.c, z, spot.y, slice(None), left), self.then_c[z])
            self.add((spot.c, z, spot.y, slice(None), right), self.then_y[z])

    def result(self):
        spot = self.spot
        value = self.total[spot.c, spot.z, spot.y].astype(jnp.float32)
        for by in range(spot.sizes["z"] - 1):
            value = value + self.by_z[by].astype(jnp.float32)
        return value


def begin_kernel(sizes, *refs):
    (
        joint_halves, table, mixing_halves, expand_a, expand_b, shrink_a, shrink_b,
        joint, tables, mixing, grown_a, grown_b, shrunk_a, shrunk_b, sems,
    ) = refs
    spot = Spot(sizes)
    mover = Mover(spot, sems)
    c, z, y, k = spot.c, spot.z, spot.y, spot.k
    width, half = joint_halves.shape[2], mixing_halves.shape[2]
    rows = table.shape[0]
    joint_first = first_rows(mover, joint_halves, joint, width)
    spread = tables.at[c, z, y, pl.ds(pl.multiple_of(k * rows, rows), rows)]
    joint_first += [mover.local(table, spread), mover.copy(table, spread, "k")]
    later_first = first_rows(mover, mixing_halves, mixing, half)
    later_first += first_rows(mover, expand_a, grown_a, expand_a.shape[2])
    later_first += first_rows(mover, expand_b, grown_b, expand_b.shape[2])
    later_first += [
        mover.local(shrink_a, shrunk_a.at[k, c, z, y]),
        mover.local(shrink_b, shrunk_b.at[k, c, z, y]),
    ]
    job = GatherJob(mover, joint, k * width, width, width // 2)
    thin = GatherJob(mover, tables, 0, tables.shape[-1], tables.shape[-1], core=False)
    later = later_jobs(mover, mixing, grown_a, grown_b, shrunk_a, shrunk_b)[:3]
    spot.meet(("k", "c", "y", "z"))
    start(joint_first + later_first)
    wait(joint_first)
    start(thin.along_z + job.along_z)
    wait(later_first)
    wait(thin.along_z + job.along_z)
    start(thin.near + job.near + job.core[0])
    for each in later:
        start(each.along_z)
    wait(thin.near + job.near)
    start(thin.far + job.far + job.core[1])
    wait(thin.far + job.far)
    start(job.core[2])
    for each in later:
        wait(each.along_z)
    wait(job.core[0] + job.core[1] + job.core[2])


def later_jobs(mover, mixing, grown_a, grown_b, shrunk_a, shrunk_b):
    k = mover.spot.k
    half, grown, width = mixing.shape[-1] // 2, grown_a.shape[-1] // 2, shrunk_a.shape[-1]
    return [
        GatherJob(mover, mixing, k * half, half, half // 2),
        GatherJob(mover, shrunk_a.at[k], 0, width, width // 2),
        GatherJob(mover, grown_a, k * grown, grown, grown // 2),
        GatherJob(mover, shrunk_b.at[k], 0, width, width // 2),
        GatherJob(mover, grown_b, k * grown, grown, grown // 2),
    ]


def later_shapes(sizes, pieces):
    joint_halves, table, mixing_halves, expand_a, expand_b, shrink_a, shrink_b = pieces
    lead = (sizes["c"], sizes["z"], sizes["y"])
    rows = 2 * table.shape[0]

    def shape(*dims):
        return jax.ShapeDtypeStruct(dims, low)

    grown, shrunk = (*lead, rows, 2 * expand_a.shape[2]), (2, *lead, *shrink_a.shape)
    return [
        shape(*lead, rows, 2 * joint_halves.shape[2]),
        shape(*lead, rows, table.shape[1]),
        shape(*lead, rows, 2 * mixing_halves.shape[2]),
        shape(*grown),
        shape(*grown),
        shape(*shrunk),
        shape(*shrunk),
    ]


def begin(sizes, pieces):
    return pl.pallas_call(
        functools.partial(begin_kernel, sizes),
        in_specs=[whole_vmem] * 7,
        out_specs=[any_place] * 7,
        out_shape=later_shapes(sizes, pieces),
        scratch_shapes=[pltpu.SemaphoreType.DMA((2, 96))],
        compiler_params=pltpu.CompilerParams(
            collective_id=1, has_side_effects=True, vmem_limit_bytes=16 << 20
        ),
        cost_estimate=small_cost,
        name="begin",
    )(*pieces)


def attend_kernel(sizes, blocks, *refs):
    projected, o_ref, lse_ref = refs[0], refs[6], refs[7]
    outs, sems = refs[8:13], refs[13]
    spot = Spot(sizes)
    mover = Mover(spot, sems)
    mixing, shrink_a, expand_a, shrink_b, expand_b = later_jobs(mover, *outs)
    soon, then = [mixing, shrink_a, expand_a], [shrink_b, expand_b]

    def open_all():
        spot.meet(("k", "c", "y", "z"))
        for job in soon:
            start(job.near + job.core[0])
        for job in then:
            start(job.along_z)

    def soon_far():
        for job in soon:
            wait(job.near)
            start(job.far + job.core[1])

    def then_near():
        for job in then:
            wait(job.along_z)
            start(job.near + job.core[0])

    def soon_core():
        for job in soon:
            wait(job.far)
            start(job.core[2])

    def close_all():
        for job in then:
            wait(job.near)
            start(job.far + job.core[1])
        for job in then:
            wait(job.far)
            start(job.core[2])
        for job in soon + then:
            for stage in job.core:
                wait(stage)

    step = pl.program_id(0)
    schedule = [(0, 0, open_all), (5, 0, then_near), (6, 0, soon_far), (7, 3, soon_core)]
    attend_pair(blocks, projected, o_ref, lse_ref, hooks(step, schedule))
    pl.when(step == pl.num_programs(0) - 1)(close_all)


def attend(sizes, blocks, projected, outs):
    tokens, width = projected.shape[0], projected.shape[1] // 3
    pairs = width // PAIR
    return pl.pallas_call(
        functools.partial(attend_kernel, sizes, blocks),
        grid=(pairs,),
        in_specs=[pl.BlockSpec((tokens, 3 * PAIR), lambda g: (0, g))] + [any_place] * 5,
        out_specs=[
            pl.BlockSpec((tokens, PAIR), lambda g: (0, g)),
            pl.BlockSpec((None, 8, tokens), lambda g: (g, 0, 0)),
        ]
        + [any_place] * 5,
        out_shape=[
            jax.ShapeDtypeStruct((tokens, width), low),
            jax.ShapeDtypeStruct((pairs, 8, tokens), jnp.float32),
        ]
        + [jax.ShapeDtypeStruct(out.shape, out.dtype) for out in outs],
        input_output_aliases={1 + number: 2 + number for number in range(5)},
        scratch_shapes=[pltpu.SemaphoreType.DMA((2, 80))],
        compiler_params=pltpu.CompilerParams(
            collective_id=2, has_side_effects=True, vmem_limit_bytes=48 << 20
        ),
        cost_estimate=small_cost,
        name="attend",
    )(projected, *outs)


def core_halves(grad, k, width, first=0, size=None):
    size = width if size is None else size
    every = slice(None)
    return [
        grad.at[every, every, every, every, span(half * width + first, size)]
        for half in (k, 1 - k)
    ]


class Finish:
    def __init__(self, mover, summed, arrived):
        self.k = mover.spot.k
        self.summed, self.arrived = summed, arrived
        rows = arrived.shape[0]
        self.rows = rows
        away = summed.at[pl.ds(pl.multiple_of((1 - self.k) * rows, rows), rows)]
        self.copies = [mover.copy(away, arrived, "k")]

    def write(self, out, columns=slice(None)):
        rows = self.rows
        kept = pl.ds(pl.multiple_of(self.k * rows, rows), rows)
        out[self.k, :, columns] = self.summed[kept, :]
        out[1 - self.k, :, columns] = self.arrived[...]


def attend_back_kernel(sizes, blocks, *refs):
    projected, upstream, lse_ref = refs[:3]
    mixing, expand_a, shrink_a, expand_b, shrink_b = refs[3:8]
    back_ref = refs[8]
    mixing_out, expand_a_out, shrink_a_out, expand_b_out, shrink_b_out = refs[9:14]
    turned, key_sum, value_sum, sems = refs[14:18]
    scratch = [refs[18 + 7 * number : 25 + 7 * number] for number in range(5)]
    tails = [refs[53 + 2 * number : 55 + 2 * number] for number in range(3)]
    spot = Spot(sizes)
    mover = Mover(spot, sems)
    k = spot.k
    half, grown, width = mixing.shape[-1] // 2, expand_a.shape[-1] // 2, shrink_a.shape[-1]
    m = ReduceJob(mover, *core_halves(mixing, k, half), half // 2, scratch[0])
    ea = ReduceJob(mover, *core_halves(expand_a, k, grown), grown // 2, scratch[1])
    sa = ReduceJob(mover, shrink_a.at[k], shrink_a.at[1 - k], width // 2, scratch[2])
    eb = ReduceJob(mover, *core_halves(expand_b, k, grown), grown // 2, scratch[3])
    sb = ReduceJob(mover, shrink_b.at[k], shrink_b.at[1 - k], width // 2, scratch[4])
    ends = [Finish(mover, *tail) for tail in tails]

    def open_all():
        spot.meet(("k", "c", "y", "z"))
        for job in (sa, ea, m, sb, eb):
            start(job.first)

    def near(*jobs):
        for job in jobs:
            wait(job.first)
            job.add_first()
            start(job.near)

    def far(*jobs):
        for job in jobs:
            wait(job.near)
            job.add_near()
            start(job.far)

    def along_z(*jobs):
        for job in jobs:
            wait(job.far)
            job.add_far()
            start(job.along_z)

    def close_all():
        along_z(sa, ea)
        far(m, sb, eb)
        for job, end in ((ea, ends[1]),):
            wait(job.along_z)
            end.summed[...] = job.result()
            start(end.copies)
        wait(sa.along_z)
        shrink_a_out[...] = sa.result()
        along_z(m, sb, eb)
        for job, end in ((m, ends[0]), (eb, ends[2])):
            wait(job.along_z)
            end.summed[...] = job.result()
            start(end.copies)
        wait(sb.along_z)
        shrink_b_out[...] = sb.result()
        for end, out in zip(ends, (mixing_out, expand_a_out, expand_b_out)):
            wait(end.copies)
            end.write(out)

    step = pl.program_id(0)
    schedule = [
        (0, 0, open_all),
        (1, 3, lambda: near(sa, ea)),
        (4, 0, lambda: near(m, sb, eb)),
        (6, 3, lambda: far(sa, ea)),
    ]
    attend_back_pair(
        blocks, projected, upstream, lse_ref, back_ref, turned, key_sum, value_sum,
        hooks(step, schedule),
    )
    pl.when(step == pl.num_programs(0) - 1)(close_all)


def attend_back(sizes, blocks, projected, upstream, lse, grads):
    tokens, width = upstream.shape
    pairs = width // PAIR
    mixing, expand_a, shrink_a, expand_b, shrink_b = grads
    rows = mixing.shape[3]
    own = rows // 2
    half, grown, full = mixing.shape[-1] // 2, expand_a.shape[-1] // 2, shrink_a.shape[-1]
    triple = pl.BlockSpec((tokens, 3 * PAIR), lambda g: (0, g))
    finals = [(2, own, half), (2, own, grown), (rows, full), (2, own, grown), (rows, full)]
    scratch = [
        pltpu.VMEM((blocks, PAIR, BLK), low),
        pltpu.VMEM((blocks, BLK, PAIR), jnp.float32),
        pltpu.VMEM((blocks, BLK, PAIR), jnp.float32),
        pltpu.SemaphoreType.DMA((2, 48)),
    ]
    for columns in (half, grown, full, grown, full):
        scratch += ReduceJob.scratch(sizes, rows, columns, columns // 2)
    for columns in (half, grown, grown):
        scratch += [
            pltpu.VMEM((rows, columns), jnp.float32),
            pltpu.VMEM((own, columns), jnp.float32),
        ]
    return pl.pallas_call(
        functools.partial(attend_back_kernel, sizes, blocks),
        grid=(pairs,),
        in_specs=[
            triple,
            pl.BlockSpec((tokens, PAIR), lambda g: (0, g)),
            pl.BlockSpec((None, 8, tokens), lambda g: (g, 0, 0)),
        ]
        + [any_place] * 5,
        out_specs=[triple] + [whole_vmem] * 5,
        out_shape=[jax.ShapeDtypeStruct(projected.shape, low)]
        + [jax.ShapeDtypeStruct(final, jnp.float32) for final in finals],
        scratch_shapes=scratch,
        compiler_params=pltpu.CompilerParams(
            collective_id=3, has_side_effects=True, vmem_limit_bytes=56 << 20
        ),
        cost_estimate=small_cost,
        name="attend_back",
    )(projected, upstream, lse, *grads)


def end_kernel(sizes, joint, vector, out, vector_out, sems, steps, arrived, *scratch):
    spot = Spot(sizes)
    mover = Mover(spot, sems)
    width = joint.shape[-1] // 2
    part = width // 2
    jobs, ends = [], []
    for number in range(2):
        refs = scratch[9 * number : 9 * number + 9]
        halves = core_halves(joint, spot.k, width, number * part, part)
        jobs.append(ReduceJob(mover, *halves, part // 2, refs[:7]))
        ends.append(Finish(mover, *refs[7:]))
    hops = [
        mover.copy(steps.at[number], arrived.at[number], name)
        for number, name in enumerate(("k", "c", "y"))
    ]
    spread = [
        mover.copy(steps.at[3], arrived.at[2 + by], "z", by) for by in range(1, sizes["z"])
    ]
    spot.meet(("k", "c", "y", "z"))
    start(jobs[0].first)
    steps[0] = vector[...]
    start(hops[:1])
    start(jobs[1].first)

    def hop(number):
        wait([hops[number]])
        steps[number + 1] = steps[number] + arrived[number]
        start([hops[number + 1]] if number < 2 else spread)

    wait(jobs[0].first)
    jobs[0].add_first()
    start(jobs[0].near)
    hop(0)
    wait(jobs[1].first)
    jobs[1].add_first()
    start(jobs[1].near)
    hop(1)
    wait(jobs[0].near)
    jobs[0].add_near()
    start(jobs[0].far)
    hop(2)
    wait(jobs[1].near)
    jobs[1].add_near()
    start(jobs[1].far)
    for job in jobs:
        wait(job.far)
        job.add_far()
        start(job.along_z)
    wait(spread)
    total = steps[3]
    for by in range(1, sizes["z"]):
        total = total + arrived[2 + by]
    vector_out[...] = total
    for job, end in zip(jobs, ends):
        wait(job.along_z)
        end.summed[...] = job.result()
        start(end.copies)
    for number, end in enumerate(ends):
        wait(end.copies)
        end.write(out, pl.ds(number * part, part))


def end(sizes, joint, vector):
    rows, width = joint.shape[3], joint.shape[4] // 2
    part = width // 2
    scratch = [
        pltpu.SemaphoreType.DMA((2, 40)),
        pltpu.VMEM((4, *vector.shape), jnp.float32),
        pltpu.VMEM((2 + sizes["z"], *vector.shape), jnp.float32),
    ]
    for number in range(2):
        scratch += ReduceJob.scratch(sizes, rows, part, part // 2)
        scratch += [
            pltpu.VMEM((rows, part), jnp.float32),
            pltpu.VMEM((rows // 2, part), jnp.float32),
        ]
    return pl.pallas_call(
        functools.partial(end_kernel, sizes),
        in_specs=[any_place, whole_vmem],
        out_specs=[whole_vmem] * 2,
        out_shape=[
            jax.ShapeDtypeStruct((2, rows // 2, width), jnp.float32),
            jax.ShapeDtypeStruct(vector.shape, jnp.float32),
        ],
        scratch_shapes=scratch,
        compiler_params=pltpu.CompilerParams(
            collective_id=4, has_side_effects=True, vmem_limit_bytes=32 << 20
        ),
        cost_estimate=small_cost,
        name="end",
    )(joint, vector)


def layer_norm(values, gain_row, shift_row):
    centered = values - jnp.mean(values, axis=-1, keepdims=True)
    variance = jnp.mean(centered * centered, axis=-1, keepdims=True)
    inverse = lax.rsqrt(variance + norm_eps)
    normal_part = centered * inverse
    return (normal_part * gain_row + shift_row, normal_part, inverse)


def norm_back(upstream, normal_part, inverse, gain_row):
    scaled = upstream * gain_row
    inner_sum = jnp.mean(scaled, axis=-1, keepdims=True)
    along_sum = jnp.mean(scaled * normal_part, axis=-1, keepdims=True)
    values_grad = inverse * (scaled - inner_sum - normal_part * along_sum)
    return (values_grad, jnp.sum(upstream * normal_part, axis=0), jnp.sum(upstream, axis=0))


def outer_sum(left_side, right_side):
    return lax.dot_general(
        left_side, right_side, (((0,), (0,)), ((), ())), preferred_element_type=jnp.float32
    )


def adam_update(weight, moment_one, moment_two, gradient, step_rate, decay_rate):
    first_new = 0.5 * moment_one + 0.5 * gradient
    second_new = 0.5 * moment_two + 0.5 * gradient * gradient
    correct = 1.0 - 0.5**STEP
    direction = first_new / correct / (jnp.sqrt(second_new / correct) + adam_eps)
    updated = weight - step_rate * (direction + decay_rate * weight)
    return (updated, first_new, second_new)


def to_groups(matrix):
    row_count = matrix.shape[0]
    return matrix.reshape(row_count, H // group_heads, group_heads, HD).transpose(1, 0, 2, 3)


def from_groups(stacked):
    return stacked.transpose(1, 0, 2, 3).reshape(stacked.shape[1], H * HD)


def tile_scores(queries, key_rows, allowed):
    products = jnp.einsum("rgd,lgd->grl", queries, key_rows, preferred_element_type=jnp.float32)
    return jnp.where(allowed[None], products * 0.125, -1e30)


def tile_forward(queries, key_rows, value_rows, allowed):
    scores = tile_scores(queries, key_rows, allowed)
    largest = jnp.max(scores, axis=-1, keepdims=True)
    exponent = jnp.exp(scores - largest)
    row_total = jnp.sum(exponent, axis=-1, keepdims=True)
    weights = (exponent / row_total).astype(low)
    mixed = jnp.einsum("grl,lgd->rgd", weights, value_rows, preferred_element_type=jnp.float32)
    return (mixed, (largest + jnp.log(row_total))[..., 0])


def tile_backward(queries, key_rows, value_rows, allowed, logsum, upstream):
    scores = tile_scores(queries, key_rows, allowed)
    recomputed = jnp.exp(scores - logsum[..., None])
    value_grad = jnp.einsum(
        "grl,rgd->lgd", recomputed.astype(low), upstream, preferred_element_type=jnp.float32
    )
    weight_grad = jnp.einsum(
        "rgd,lgd->grl", upstream, value_rows, preferred_element_type=jnp.float32
    )
    inner_sum = jnp.sum(recomputed * weight_grad, axis=-1, keepdims=True)
    score_grad = (recomputed * (weight_grad - inner_sum)).astype(low)
    query_grad = (
        jnp.einsum("grl,lgd->rgd", score_grad, key_rows, preferred_element_type=jnp.float32) * 0.125
    )
    key_grad = (
        jnp.einsum("grl,rgd->lgd", score_grad, queries, preferred_element_type=jnp.float32) * 0.125
    )
    return (query_grad, key_grad, value_grad)


def spread_forward(queries, key_value, allowed):
    def one_sequence(pieces):
        queries, key_value, allowed = pieces
        width = queries.shape[1]
        mixed, logsum = lax.map(
            lambda triple: tile_forward(triple[0], triple[1], triple[2], allowed),
            (to_groups(queries), to_groups(key_value[:, :width]), to_groups(key_value[:, width:])),
        )
        return (from_groups(mixed), logsum)

    return lax.map(one_sequence, (queries, key_value, allowed))


def spread_backward(queries, key_value, allowed, logsum, upstream):
    def one_sequence(pieces):
        queries, key_value, allowed, logsum, upstream = pieces
        width = queries.shape[1]
        query_grad, key_grad, value_grad = lax.map(
            lambda member: tile_backward(
                member[0], member[1], member[2], allowed, member[3], member[4]
            ),
            (
                to_groups(queries),
                to_groups(key_value[:, :width]),
                to_groups(key_value[:, width:]),
                logsum,
                to_groups(upstream),
            ),
        )
        return (
            from_groups(query_grad),
            jnp.concatenate([from_groups(key_grad), from_groups(value_grad)], axis=1),
        )

    return lax.map(one_sequence, (queries, key_value, allowed, logsum, upstream))


class Slice:
    def __init__(self, ctx_size, wshard_size):
        rest = wshard_size // 2
        self.sizes = {"c": ctx_size, "z": 4, "y": rest // 4, "k": 2}

    def here(self):
        flat = lax.axis_index(axes)
        found = {}
        for name in ("k", "y", "z", "c"):
            found[name] = flat % self.sizes[name]
            flat = flat // self.sizes[name]
        return found

    def shift(self, value, name, by):
        pairs = []
        sizes = self.sizes
        for c in range(sizes["c"]):
            for z in range(sizes["z"]):
                for y in range(sizes["y"]):
                    for k in range(sizes["k"]):
                        spot = {"c": c, "z": z, "y": y, "k": k}
                        goal = dict(spot)
                        goal[name] = (spot[name] + by) % sizes[name]
                        pairs.append((self.flat(spot), self.flat(goal)))
        return lax.ppermute(value, axes, pairs)

    def flat(self, spot):
        sizes = self.sizes
        return ((spot["c"] * sizes["z"] + spot["z"]) * sizes["y"] + spot["y"]) * sizes["k"] + spot[
            "k"
        ]

    def stack(self, array, name, here):
        size = self.sizes[name]
        parts = [array] + [self.shift(array, name, by) for by in range(1, size)]
        if size > 4:
            ordered = [parts[(-place) % size] for place in range(size)]
            return jnp.roll(jnp.stack(ordered), here[name], axis=0)
        return jnp.stack(
            [lax.select_n((here[name] - place) % size, *parts) if size > 2 else
             jnp.where(here[name] == place, parts[0], parts[1]) for place in range(size)]
        )

    def reach(self, pieces, name):
        grown = list(pieces)
        for by in range(1, self.sizes[name]):
            for array, place in pieces:
                moved = dict(place)
                moved[name] = (place[name] - by) % self.sizes[name]
                grown.append((self.shift(array, name, by), moved))
        return grown

    def gather_split(self, stacked, cut, here):
        sizes = self.sizes
        depth, rows, columns = stacked.shape
        out = jnp.zeros((sizes["c"], depth, sizes["y"], rows, columns), stacked.dtype)
        for low_column, high_column, order in ((0, cut, "cy"), (cut, columns, "yc")):
            pieces = [(stacked[:, :, low_column:high_column], here)]
            for name in order:
                pieces = self.reach(pieces, name)
            for array, place in pieces:
                out = lax.dynamic_update_slice(
                    out, array[None, :, None], (place["c"], 0, place["y"], 0, low_column)
                )
        return out.reshape(-1, columns)

    def send_terms(self, value, name, place, here):
        size = self.sizes[name]
        own = lax.dynamic_index_in_dim(value, here[name], place, False)
        moved = [
            self.shift(
                lax.dynamic_index_in_dim(value, (here[name] + by) % size, place, False), name, by
            )
            for by in range(1, size)
        ]
        return own, moved

    def add_terms(self, terms, kind=low):
        own, moved = terms
        total = own.astype(jnp.float32)
        for other in moved:
            total = total + other.astype(jnp.float32)
        return total.astype(kind)

    def everywhere(self, value):
        for name in ("k", "c", "y", "z"):
            total = value
            for by in range(1, self.sizes[name]):
                total = total + self.shift(value, name, by)
            value = total
        return value


def tie(value, *others):
    return lax.optimization_barrier((value, others))[0]


def by_core(core, first, second, axis):
    return jnp.where(
        core == 0,
        jnp.concatenate([first, second], axis=axis),
        jnp.concatenate([second, first], axis=axis),
    )


def pick(core, array, axis):
    return (
        lax.dynamic_index_in_dim(array, core, axis, False),
        lax.dynamic_index_in_dim(array, 1 - core, axis, False),
    )


def gather_far(grid, here, pieces):
    joint_halves, table, mixing_halves, expand_a, expand_b, shrink_a, shrink_b = pieces
    core = here["k"]

    def chip_rows(halves):
        own, other = pick(core, halves, 0)
        return by_core(core, own, grid.shift(other, "k", 1), 0)

    def everyone(block):
        width = block.shape[1]
        return grid.gather_split(grid.stack(block, "z", here), width // 2, here)

    def both(block, axis):
        own = everyone(block)
        return by_core(core, own, grid.shift(own, "k", 1), axis)

    return (
        both(chip_rows(joint_halves), 1),
        everyone(by_core(core, table, grid.shift(table, "k", 1), 0)),
        both(chip_rows(mixing_halves), 1),
        both(chip_rows(expand_a), 1),
        both(chip_rows(expand_b), 1),
        both(shrink_a, 0),
        both(shrink_b, 0),
    )


def reduce_far(grid, here, gradient, by_rows):
    core = here["k"]
    sizes = grid.sizes
    if by_rows:
        own, other = pick(core, gradient.reshape(2, -1, gradient.shape[1]), 0)
    else:
        own, other = pick(core, gradient.reshape(gradient.shape[0], 2, -1), 1)
    total = grid.add_terms((own, [grid.shift(other, "k", 1)]))
    total = total.reshape(sizes["c"], sizes["z"], sizes["y"], -1, own.shape[-1])
    for name, place in (("y", 2), ("c", 0)):
        total = grid.add_terms(grid.send_terms(total, name, place, here))
    total = grid.add_terms(grid.send_terms(total, "z", 0, here), jnp.float32)
    if by_rows:
        return total
    kept, other = pick(core, total.reshape(2, -1, total.shape[1]), 0)
    return by_core(core, kept[None], grid.shift(other, "k", 1)[None], 0)


def body(
    grid,
    block_input,
    block_order,
    cotangent,
    joint_weight,
    mixing_weight,
    expand_weight,
    shrink_weight,
    vectors,
    joint_first,
    mixing_first,
    expand_first,
    shrink_first,
    vectors_first,
    joint_second,
    mixing_second,
    expand_second,
    shrink_second,
    vectors_second,
):
    here = grid.here()
    sizes = grid.sizes
    ctx, ctx_size = here["c"], sizes["c"]
    seq_count, row_count, width = block_input.shape
    half = width // 2
    pairs = H // 2
    hidden_width = expand_weight.shape[1]
    own_rows = joint_weight.shape[0]
    slot = shrink_weight.shape[0]
    sub = slot // 2
    chips = hidden_width // (2 * slot)
    tokens = seq_count * row_count
    row_blocks = row_count // BLK
    near = ctx_size == 2 and seq_count == 2 and sizes["y"] == 2 and own_rows % 32 == 0

    def to_sequence(rows):
        if not near:
            return rows.reshape(tokens, width)
        sent = lax.dynamic_index_in_dim(rows, 1 - ctx, 0, False)
        kept = lax.dynamic_index_in_dim(rows, ctx, 0, False)
        return jnp.concatenate([kept, grid.shift(sent, "c", 1)], axis=0)

    def from_sequence(rows, kind):
        if not near:
            return rows.astype(kind).reshape(seq_count, row_count, width)
        kept = rows[:row_count].astype(kind)
        arrived = grid.shift(rows[row_count:].astype(low), "c", 1).astype(kind)
        return by_core(ctx, kept[None], arrived[None], 0)

    def hidden_sets(shard):
        parts = shard.astype(low).reshape(own_rows, chips, 2, 2, sub)
        return [
            parts[:, :, :, number].transpose(2, 0, 1, 3).reshape(2, own_rows, chips * sub)
            for number in range(2)
        ]

    joint_halves = (
        joint_weight.astype(low)
        .reshape(own_rows, 3, 2, pairs // 2, PAIR)
        .transpose(2, 0, 3, 1, 4)
        .reshape(2, own_rows, 3 * half)
    )
    table = jnp.pad(vectors.T.astype(low), ((0, 0), (0, 128 - vectors.shape[0])))
    mixing_halves = mixing_weight.astype(low).reshape(own_rows, 2, half).transpose(1, 0, 2)
    shrink_low = shrink_weight.astype(low)
    pieces = [joint_halves, table, mixing_halves, *hidden_sets(expand_weight)]
    pieces += [shrink_low[:sub], shrink_low[sub:]]
    input_rows = to_sequence(block_input)
    upstream = to_sequence(cotangent)
    if near:
        joint, tables, *later = begin(sizes, pieces)
    else:
        joint, tables, mixing, expand_a, expand_b, shrink_a, shrink_b = gather_far(
            grid, here, pieces
        )
    joint = joint.reshape(width, 3 * width)
    vector_values = (
        tables.reshape(width, -1)[:, : vectors.shape[0]].T.astype(jnp.float32)
    )

    if near:
        order = lax.dynamic_slice_in_dim(block_order, ctx, 1, 0)[0]
        blocks = order.shape[0]
        stored = jnp.arange(blocks, dtype=jnp.int32)
        moved = jnp.where(stored // row_blocks == ctx, 0, row_blocks) + stored % row_blocks
        place = jnp.sum(jnp.where(order[None, :] == stored[:, None], moved[None, :], 0), axis=1)
        back = jnp.sum(jnp.where(moved[None, :] == stored[:, None], order[None, :], 0), axis=1)
        place, back = place.astype(jnp.int32), back.astype(jnp.int32)
        input_rows = arrange(place, input_rows)
        upstream = arrange(place, upstream)
    input_rows = input_rows.astype(jnp.float32)
    normed_first, normal_first, inverse_first = layer_norm(
        input_rows, vector_values[0], vector_values[1]
    )
    first_low = normed_first.astype(low)
    joint_shift = jnp.stack(
        [
            vector_values[2].reshape(pairs, PAIR),
            jnp.zeros((pairs, PAIR), jnp.float32),
            vector_values[3].reshape(pairs, PAIR),
        ],
        axis=1,
    ).reshape(-1)
    projected = (nn(first_low, joint) + joint_shift).astype(low)
    if near:
        mixed_low, logsum, mixing, expand_a, expand_b, shrink_a, shrink_b = attend(
            sizes, blocks, projected, later
        )
    else:
        by_part = projected.reshape(seq_count, row_count, pairs, 3, PAIR)
        queries, keys, values = [
            by_part[:, :, :, part].reshape(seq_count, row_count, width) for part in range(3)
        ]
        key_value = lax.all_gather(
            jnp.concatenate([keys, values], axis=2), "ctx", axis=1, tiled=True
        )
        own_blocks = lax.dynamic_slice_in_dim(block_order, ctx * row_blocks, row_blocks, 1)
        query_block = jnp.repeat(own_blocks, BLK, axis=1, total_repeat_length=row_count)
        key_block = jnp.repeat(block_order, BLK, axis=1, total_repeat_length=key_value.shape[1])
        allowed = key_block[:, None, :] <= query_block[:, :, None]
        mixed, logsum = spread_forward(queries, key_value, allowed)
        mixed_low = mixed.astype(low).reshape(tokens, width)
    mixing = mixing.reshape(width, width)
    expands = [expand.reshape(width, -1) for expand in (expand_a, expand_b)]
    shrinks = [shrink.reshape(-1, width) for shrink in (shrink_a, shrink_b)]
    middle = input_rows + (nn(mixed_low, mixing) + vector_values[4])
    normed_second, normal_second, inverse_second = layer_norm(
        middle, vector_values[5], vector_values[6]
    )
    second_low = normed_second.astype(low)

    hidden_bias = vector_values[8:].reshape(chips, 2, 2, sub)
    before, hidden_grads, hidden_bias_grads = None, [], []
    for number in range(2):
        bias = hidden_bias[:, :, number].transpose(1, 0, 2).reshape(1, -1)
        result, second_grad, expand_grad, shrink_grad, bias_grad = mlp(
            second_low, upstream, expands[number], shrinks[number], bias, before=before
        )
        before = (result, second_grad)
        hidden_grads += [expand_grad, shrink_grad]
        hidden_bias_grads.append(bias_grad.reshape(2, chips, 1, sub).transpose(1, 0, 2, 3))
    block_output = (middle + result + vector_values[7]).astype(low)
    if near:
        block_output = arrange(back, block_output)
    block_output = from_sequence(block_output, low)

    upstream_float = upstream.astype(jnp.float32)
    middle_part, gain_two, shift_two = norm_back(
        second_grad, normal_second, inverse_second, vector_values[5]
    )
    middle_grad = upstream_float + middle_part
    branch_low = middle_grad.astype(low)
    mixing_grad = outer_sum(mixed_low, branch_low).astype(low)
    mixed_grad = nt(branch_low, mixing).astype(low)
    if near:
        lead = (sizes["c"], sizes["z"], sizes["y"])
        grads = [mixing_grad.reshape(*lead, -1, width)]
        for number in range(2):
            expand_grad, shrink_grad = hidden_grads[2 * number : 2 * number + 2]
            grads.append(expand_grad.reshape(*lead, -1, expand_grad.shape[1]))
            grads.append(shrink_grad.reshape(2, *lead, -1, width))
        joint_back, mixing_part, *hidden_parts = attend_back(
            sizes, blocks, projected, mixed_grad, logsum, grads
        )
    else:
        query_grad, key_value_grad = spread_backward(
            queries, key_value, allowed, logsum, mixed_grad.reshape(seq_count, row_count, width)
        )
        summed = lax.psum_scatter(
            key_value_grad.astype(low), "ctx", scatter_dimension=1, tiled=True
        )
        parts = [query_grad.astype(low), summed[..., :width], summed[..., width:]]
        joint_back = jnp.stack(
            [part.reshape(tokens, pairs, PAIR) for part in parts], axis=2
        ).reshape(tokens, 3 * width)
        mixing_part = reduce_far(grid, here, mixing_grad, False)
        hidden_parts = [
            reduce_far(grid, here, grad, number % 2 == 1)
            for number, grad in enumerate(hidden_grads)
        ]
    joint_grad = outer_sum(first_low, joint_back).astype(low)
    first_grad = nt(joint_back, joint)
    input_part, gain_one, shift_one = norm_back(
        first_grad, normal_first, inverse_first, vector_values[0]
    )
    input_gradient = middle_grad + input_part
    if near:
        input_gradient = arrange(back, input_gradient)
    input_gradient = from_sequence(input_gradient, jnp.float32)

    def column_sum(rows):
        return jnp.sum(rows.astype(jnp.float32), axis=0)

    joint_sums = column_sum(joint_back).reshape(pairs, 3, PAIR)
    vector_grad = jnp.concatenate(
        [
            jnp.stack(
                [
                    gain_one,
                    shift_one,
                    joint_sums[:, 0].reshape(-1),
                    joint_sums[:, 2].reshape(-1),
                    column_sum(branch_low),
                    gain_two,
                    shift_two,
                    column_sum(upstream),
                ]
            ),
            jnp.concatenate(hidden_bias_grads, axis=2).reshape(-1, width),
        ],
        axis=0,
    )
    if near:
        joint_part, vector_sum = end(
            sizes,
            joint_grad.reshape(*lead, -1, 3 * width),
            jnp.pad(vector_grad, ((0, -vector_grad.shape[0] % 8), (0, 0))),
        )
    else:
        joint_part = reduce_far(grid, here, joint_grad, False)
        vector_sum = grid.everywhere(vector_grad)
    vector_sum = lax.dynamic_slice(
        vector_sum, (0, lax.axis_index(axes) * vectors.shape[1]), vectors.shape
    )
    joint_sum = (
        joint_part.reshape(2, own_rows, pairs // 2, 3, PAIR)
        .transpose(1, 3, 0, 2, 4)
        .reshape(joint_weight.shape)
    )
    mixing_sum = mixing_part.transpose(1, 0, 2).reshape(mixing_weight.shape)
    expand_sum = jnp.stack(
        [part.reshape(2, own_rows, chips, sub) for part in hidden_parts[0::2]], axis=0
    )
    expand_sum = expand_sum.transpose(2, 3, 1, 0, 4).reshape(expand_weight.shape)
    shrink_sum = jnp.concatenate(hidden_parts[1::2], axis=0)
    joint_new, joint_moment, joint_square = adam_update(
        joint_weight, joint_first, joint_second, joint_sum, 0.05, 0.1
    )
    mixing_new, mixing_moment, mixing_square = adam_update(
        mixing_weight, mixing_first, mixing_second, mixing_sum, 0.05, 0.1
    )
    expand_new, expand_moment, expand_square = adam_update(
        expand_weight, expand_first, expand_second, expand_sum, 0.05, 0.1
    )
    shrink_new, shrink_moment, shrink_square = adam_update(
        shrink_weight, shrink_first, shrink_second, shrink_sum, 0.05, 0.1
    )
    vectors_new, vectors_moment, vectors_square = adam_update(
        vectors, vectors_first, vectors_second, vector_sum, 0.5, 0.0
    )
    return (
        block_output,
        input_gradient,
        joint_new,
        mixing_new,
        expand_new,
        shrink_new,
        vectors_new,
        joint_moment,
        mixing_moment,
        expand_moment,
        shrink_moment,
        vectors_moment,
        joint_square,
        mixing_square,
        expand_square,
        shrink_square,
        vectors_square,
        joint_new.astype(low),
        mixing_new.astype(low),
        expand_new.astype(low),
        shrink_new.astype(low),
        vectors_new.astype(low),
    )


def solution(mesh):
    grid = Slice(mesh.shape["ctx"], mesh.shape["wshard"])
    rows = P("wshard", "ctx", None)
    matrix = P(axes, None)
    table = P(None, axes)
    parameters = (matrix, matrix, matrix, matrix, table)
    return jax.shard_map(
        functools.partial(body, grid),
        mesh=mesh,
        in_specs=(rows, P("wshard", None), rows) + parameters * 3,
        out_specs=(rows, rows) + parameters * 4,
        check_vma=False,
    )
```

```python
import functools

import jax
import jax.numpy as jnp
from jax import lax
from jax.experimental import pallas as pl
from jax.experimental.pallas import tpu as pltpu
from jax.sharding import PartitionSpec as P

H = 16
HD = 64
BLK = 256
STEP = 10
PAIR = 2 * HD

norm_eps = 1e-05
adam_eps = 1e-08
group_heads = 4
score_scale = 0.125 * 1.4426950408889634
gelu_root = 0.7978845608028654
gelu_cubic = 0.044715
low = jnp.bfloat16
axes = ("ctx", "wshard")
small_cost = pl.CostEstimate(flops=1024, bytes_accessed=1024, transcendentals=0)


def nt(left_side, right_side):
    return lax.dot_general(
        left_side, right_side, (((1,), (1,)), ((), ())), preferred_element_type=jnp.float32
    )


def nn(left_side, right_side):
    return jnp.dot(left_side, right_side, preferred_element_type=jnp.float32)


def outer_sum(left_side, right_side):
    return lax.dot_general(
        left_side, right_side, (((0,), (0,)), ((), ())), preferred_element_type=jnp.float32
    )


def block_rows(block):
    return pl.ds(block * BLK, BLK)


def thirds(ref):
    return [ref.at[:, pl.ds(part * PAIR, PAIR)] for part in range(3)]


def attend_pair(blocks, projected, o_ref, lse_ref, between):
    q_ref, k_ref, v_ref = thirds(projected)
    lane = lax.broadcasted_iota(jnp.int32, (1, PAIR), 1)
    masks = [lane < HD, lane >= HD]
    for i in range(blocks):
        between(i)
        rows = block_rows(i)
        queries = q_ref[rows, :]
        outs = []
        for h in range(2):
            masked = jnp.where(masks[h], queries, jnp.zeros_like(queries))
            scores = [nt(masked, k_ref[block_rows(j), :]) * score_scale for j in range(i + 1)]
            top = scores[0]
            for score in scores[1:]:
                top = jnp.maximum(top, score)
            top = jnp.max(top, axis=1, keepdims=True)
            weights = [jnp.exp2(score - top) for score in scores]
            total = weights[0]
            for weight in weights[1:]:
                total = total + weight
            total = jnp.sum(total, axis=1, keepdims=True)
            mixed = nn(weights[0].astype(low), v_ref[block_rows(0), :])
            for j in range(1, i + 1):
                mixed = mixed + nn(weights[j].astype(low), v_ref[block_rows(j), :])
            outs.append(mixed * (1.0 / total))
            logsum = jnp.broadcast_to(top + jnp.log2(total), (BLK, PAIR))
            lse_ref[h : h + 1, rows] = jnp.transpose(logsum)[0:1, :]
        o_ref[rows, :] = jnp.where(masks[0], outs[0], outs[1]).astype(o_ref.dtype)


def attend_back_pair(
    blocks, projected, do_ref, lse_ref, back_ref, turned, key_sum, value_sum, between
):
    q_ref, k_ref, v_ref = thirds(projected)
    dq_ref, dk_ref, dv_ref = thirds(back_ref)
    lane = lax.broadcasted_iota(jnp.int32, (1, PAIR), 1)
    masks = [lane < HD, lane >= HD]
    for j in range(blocks):
        turned[j] = jnp.transpose(k_ref[block_rows(j), :])
    for i in range(blocks):
        between(i)
        rows = block_rows(i)
        queries, upstream = q_ref[rows, :], do_ref[rows, :]
        query_grads = []
        for h in range(2):
            masked = jnp.where(masks[h], queries, jnp.zeros_like(queries))
            pulled = jnp.where(masks[h], upstream, jnp.zeros_like(upstream))
            logsum = lse_ref[h : h + 1, rows]
            weights, pulls, inner = [], [], None
            for j in range(i + 1):
                weight = jnp.exp2(nt(k_ref[block_rows(j), :], masked) * score_scale - logsum)
                pull = nt(v_ref[block_rows(j), :], pulled)
                along = jnp.sum(weight * pull, axis=0, keepdims=True)
                inner = along if inner is None else inner + along
                weights.append(weight)
                pulls.append(pull)
            query_grad = None
            for j in range(i + 1):
                score_grad = (weights[j] * (pulls[j] - inner)).astype(low)
                value_grad = nn(weights[j].astype(low), pulled)
                key_grad = nn(score_grad, masked)
                if i == j and h == 0:
                    value_sum[j] = value_grad
                    key_sum[j] = key_grad
                else:
                    value_sum[j] += value_grad
                    key_sum[j] += key_grad
                piece = nn(turned[j, h * HD : (h + 1) * HD, :], score_grad)
                query_grad = piece if query_grad is None else query_grad + piece
            query_grads.append(query_grad)
        joined = jnp.transpose(jnp.concatenate(query_grads, axis=0))
        dq_ref[rows, :] = (joined * 0.125).astype(dq_ref.dtype)
    for j in range(blocks):
        dk_ref[block_rows(j), :] = (key_sum[j] * 0.125).astype(dk_ref.dtype)
        dv_ref[block_rows(j), :] = value_sum[j].astype(dv_ref.dtype)


def hooks(step, schedule):
    def between(block):
        for when, where, action in schedule:
            if where == block:
                pl.when(step == when)(action)

    return between


any_place = pl.BlockSpec(memory_space=pl.ANY)
whole_vmem = pl.BlockSpec(memory_space=pltpu.VMEM)


MESH = pl.DeviceIdType.MESH


class Spot:
    def __init__(self, sizes):
        self.sizes = sizes
        ctx, shard = lax.axis_index("ctx"), lax.axis_index("wshard")
        self.c = ctx
        self.k = shard % 2
        self.y = (shard // 2) % 2
        self.z = shard // 4

    def device(self, name, by=1):
        c, z, y, k = self.c, self.z, self.y, self.k
        if name == "c":
            c = 1 - c
        if name == "y":
            y = 1 - y
        if name == "k":
            k = 1 - k
        if name == "z":
            z = (z + by) % self.sizes["z"]
        return (c, (z * 2 + y) * 2 + k)

    def meet(self, names):
        barrier = pltpu.get_barrier_semaphore()
        partners = []
        for name in names:
            for by in range(1, self.sizes[name]):
                partners.append(self.device(name, by))
        for partner in partners:
            pl.semaphore_signal(barrier, inc=1, device_id=partner, device_id_type=MESH)
        pl.semaphore_wait(barrier, len(partners))


class Mover:
    def __init__(self, spot, sems):
        self.spot, self.sems, self.count = spot, sems, 0

    def copy(self, source, target, name, by=1):
        number = self.count
        self.count += 1
        return pltpu.make_async_remote_copy(
            src_ref=source,
            dst_ref=target,
            send_sem=self.sems.at[0, number],
            recv_sem=self.sems.at[1, number],
            device_id=self.spot.device(name, by),
            device_id_type=MESH,
        )

    def local(self, source, target):
        number = self.count
        self.count += 1
        return pltpu.make_async_copy(source, target, self.sems.at[0, number])


class Refs:
    def __init__(self, refs):
        self.refs = list(refs)

    def take(self, count):
        taken, self.refs = self.refs[:count], self.refs[count:]
        return taken


def start(copies):
    for copy in copies:
        copy.start()


def wait(copies):
    for copy in copies:
        copy.wait()


def span(first, size):
    return pl.ds(pl.multiple_of(first, 128), size)


class Deep:
    def __init__(self, mover, quad):
        z = mover.spot.z
        self.copies = [
            mover.copy(quad.at[z], quad.at[z], "z", by) for by in range(1, mover.spot.sizes["z"])
        ]


def first_rows(mover, halves, quad):
    spot = mover.spot
    rows = halves.shape[1]
    block = quad.at[spot.z, pl.ds(pl.multiple_of(spot.k * rows, rows), rows)]
    return [
        mover.local(halves.at[spot.k], block),
        mover.copy(halves.at[1 - spot.k], block, "k"),
    ]


class Near:
    def __init__(self, mover, quad, half, offset, cut, core=True):
        spot = mover.spot
        c, z, y = spot.c, spot.z, spot.y
        width = quad.shape[-1]
        every = slice(None)

        def part(ci, yi, first, size):
            return half.at[ci, every, yi, :, span(offset + first, size)]

        self.near, self.far = [mover.local(quad, part(c, y, 0, width))], []
        for first, size, one, two in ((0, cut, "c", "y"), (cut, width - cut, "y", "c")):
            if size == 0:
                continue
            source = quad.at[every, every, pl.ds(first, size)]
            self.near.append(mover.copy(source, part(c, y, first, size), one))
            self.near.append(mover.copy(source, part(c, y, first, size), two))
            block = part(1 - c if one == "c" else c, 1 - y if one == "y" else y, first, size)
            self.far.append(mover.copy(block, block, two))
        self.core = [[], [], []]
        if core:
            self.core[0].append(mover.copy(quad, part(c, y, 0, width), "k"))
            for stage, ci, yi in ((1, 1 - c, y), (1, c, 1 - y), (2, 1 - c, 1 - y)):
                block = part(ci, yi, 0, width)
                self.core[stage].append(mover.copy(block, block, "k"))

    def close(self):
        wait(self.far)
        start(self.core[2])

    def close_core(self):
        for stage in self.core:
            wait(stage)


class ReduceNear:
    def __init__(self, mover, mine, theirs, cut, quad, scratch):
        self.spot = spot = mover.spot
        self.cut, self.quad = cut, quad
        self.total, self.other, self.by_y, self.by_c, self.then_c, self.then_y = scratch
        self.width = width = self.total.shape[-1]
        c, y = spot.c, spot.y
        every, left, right = slice(None), pl.ds(0, cut), pl.ds(cut, width - cut)
        total = self.total
        self.first = [mover.copy(theirs, self.other, "k")]
        if mine is not None:
            self.first.append(mover.local(mine, total))
        self.near = [
            mover.copy(total.at[every, every, 1 - y, every, left], self.by_y, "y"),
            mover.copy(total.at[1 - c, every, every, every, right], self.by_c, "c"),
        ]
        self.far = [
            mover.copy(total.at[1 - c, every, y, every, left], self.then_c, "c"),
            mover.copy(total.at[c, every, 1 - y, every, right], self.then_y, "y"),
        ]

    @staticmethod
    def scratch(sizes, rows, width, cut):
        c, z, y = sizes["c"], sizes["z"], sizes["y"]
        shapes = [
            (c, z, y, rows, width),
            (c, z, y, rows, width),
            (c, z, rows, cut),
            (z, y, rows, width - cut),
            (z, rows, cut),
            (z, rows, width - cut),
        ]
        return [pltpu.VMEM(shape, low) for shape in shapes]

    def add(self, where, extra):
        total = self.total[where].astype(jnp.float32) + extra.astype(jnp.float32)
        return total.astype(low)

    def go_near(self):
        wait(self.first)
        sizes = self.spot.sizes
        for c in range(sizes["c"]):
            for y in range(sizes["y"]):

                @pl.loop(0, sizes["z"])
                def _(z):
                    self.total[c, z, y] = self.add((c, z, y), self.other[c, z, y])

        start(self.near)

    def go_far(self):
        wait(self.near)
        spot, cut = self.spot, self.cut
        left, right = pl.ds(0, cut), pl.ds(cut, self.width - cut)

        @pl.loop(0, spot.sizes["z"])
        def _(z):
            for c in range(spot.sizes["c"]):
                where = (c, z, spot.y, slice(None), left)
                self.total[where] = self.add(where, self.by_y[c, z])
            for y in range(spot.sizes["y"]):
                where = (spot.c, z, y, slice(None), right)
                self.total[where] = self.add(where, self.by_c[z, y])

        start(self.far)

    def close(self):
        wait(self.far)
        spot, cut = self.spot, self.cut
        left, right = pl.ds(0, cut), pl.ds(cut, self.width - cut)

        @pl.loop(0, spot.sizes["z"])
        def _(z):
            for columns, extra in ((left, self.then_c), (right, self.then_y)):
                where = (spot.c, z, spot.y, slice(None), columns)
                self.quad[z, :, columns] = self.add(where, extra[z])


class ReduceDeep:
    def __init__(self, mover, quad, by_z):
        self.spot = spot = mover.spot
        self.quad, self.by_z = quad, by_z
        depth = spot.sizes["z"]
        self.copies = [
            mover.copy(quad.at[(spot.z + by) % depth], by_z.at[by - 1], "z", by)
            for by in range(1, depth)
        ]

    def result(self):
        spot = self.spot
        value = self.quad[spot.z].astype(jnp.float32)
        for by in range(spot.sizes["z"] - 1):
            value = value + self.by_z[by].astype(jnp.float32)
        return value


class Finish:
    def __init__(self, mover, summed, arrived):
        self.k = mover.spot.k
        self.summed, self.arrived = summed, arrived
        rows = arrived.shape[0]
        self.rows = rows
        away = summed.at[pl.ds(pl.multiple_of((1 - self.k) * rows, rows), rows)]
        self.copies = [mover.copy(away, arrived, "k")]

    @staticmethod
    def scratch(rows, width):
        return [pltpu.VMEM((rows, width), jnp.float32), pltpu.VMEM((rows // 2, width), jnp.float32)]

    def write(self, out, columns=slice(None)):
        rows = self.rows
        kept = pl.ds(pl.multiple_of(self.k * rows, rows), rows)
        out[self.k, :, columns] = self.summed[kept, :]
        out[1 - self.k, :, columns] = self.arrived[...]


def core_halves(grad, k, width, first=0, size=None):
    size = width if size is None else size
    every = slice(None)
    return [
        grad.at[every, every, every, every, span(half * width + first, size)]
        for half in (k, 1 - k)
    ]


all_axes = ("k", "c", "y", "z")


def params(number, megabytes):
    return pltpu.CompilerParams(
        collective_id=number, has_side_effects=True, vmem_limit_bytes=megabytes << 20
    )


def low_shape(*dims):
    return jax.ShapeDtypeStruct(dims, low)


def begin_kernel(sizes, *refs):
    refs = Refs(refs)
    joint_halves, table, mixing_halves, expand_halves, shrink = refs.take(5)
    joint, tables, mixing_quad, expand_quad, shrink_quad = refs.take(5)
    joint_quad, table_quad, sems = refs.take(3)
    spot = Spot(sizes)
    mover = Mover(spot, sems)
    width = joint_halves.shape[2]
    joint_first = first_rows(mover, joint_halves, joint_quad)
    rows = table.shape[0]
    spread = table_quad.at[spot.z, pl.ds(pl.multiple_of(spot.k * rows, rows), rows)]
    joint_first += [mover.local(table, spread), mover.copy(table, spread, "k")]
    later_first = first_rows(mover, mixing_halves, mixing_quad)
    later_first += first_rows(mover, expand_halves, expand_quad)
    later_first += [mover.local(shrink, shrink_quad.at[spot.z])]
    now = Deep(mover, joint_quad).copies + Deep(mover, table_quad).copies
    later = [Deep(mover, quad).copies for quad in (mixing_quad, shrink_quad, expand_quad)]
    job = Near(mover, joint_quad, joint, spot.k * width, width // 2)
    thin = Near(mover, table_quad, tables, 0, table.shape[1], core=False)
    spot.meet(all_axes)
    start(joint_first + later_first)
    wait(joint_first)
    start(now)
    wait(later_first)
    wait(now)
    start(thin.near + job.near + job.core[0])
    for copies in later:
        start(copies)
    wait(thin.near + job.near)
    start(thin.far + job.far + job.core[1])
    wait(thin.far)
    job.close()
    for copies in later:
        wait(copies)
    job.close_core()


def begin(sizes, joint_halves, table, mixing_halves, expand_halves, shrink):
    lead = (sizes["c"], sizes["z"], sizes["y"])
    depth, rows = sizes["z"], 2 * table.shape[0]
    width = joint_halves.shape[2]
    return pl.pallas_call(
        functools.partial(begin_kernel, sizes),
        in_specs=[whole_vmem] * 5,
        out_specs=[any_place] * 5,
        out_shape=[
            low_shape(*lead, rows, 2 * width),
            low_shape(*lead, rows, table.shape[1]),
            low_shape(depth, rows, mixing_halves.shape[2]),
            low_shape(depth, rows, expand_halves.shape[2]),
            low_shape(depth, *shrink.shape),
        ],
        scratch_shapes=[
            pltpu.VMEM((depth, rows, width), low),
            pltpu.VMEM((depth, rows, table.shape[1]), low),
            pltpu.SemaphoreType.DMA((2, 48)),
        ],
        compiler_params=params(1, 16),
        cost_estimate=small_cost,
        name="begin",
    )(joint_halves, table, mixing_halves, expand_halves, shrink)


def attend_kernel(sizes, blocks, *refs):
    refs = Refs(refs)
    projected, mixing_quad, expand_quad, shrink_quad, expand_halves, shrink = refs.take(6)
    o_ref, lse_ref, mixing, expand, shrunk, next_expand, next_shrink, sems = refs.take(8)
    spot = Spot(sizes)
    mover = Mover(spot, sems)
    k = spot.k
    half, grown, width = mixing_quad.shape[-1], expand_quad.shape[-1], shrink_quad.shape[-1]
    jobs = [
        Near(mover, mixing_quad, mixing, k * half, half // 2),
        Near(mover, shrink_quad, shrunk.at[k], 0, width // 2),
        Near(mover, expand_quad, expand, k * grown, grown // 2),
    ]
    next_first = first_rows(mover, expand_halves, next_expand)
    next_first += [mover.local(shrink, next_shrink.at[spot.z])]
    deep = Deep(mover, next_expand).copies + Deep(mover, next_shrink).copies

    def open_all():
        spot.meet(all_axes)
        start(next_first)
        for job in jobs:
            start(job.near + job.core[0])

    def next_deep():
        wait(next_first)
        start(deep)

    def far(*some):
        for job in some:
            wait(job.near)
            start(job.far + job.core[1])

    def close_all():
        for job in jobs:
            job.close()
        wait(deep)
        for job in jobs:
            job.close_core()

    step = pl.program_id(0)
    schedule = [
        (0, 0, open_all),
        (1, 0, next_deep),
        (2, 2, lambda: far(jobs[0])),
        (4, 2, lambda: far(jobs[1])),
        (7, 0, lambda: far(jobs[2])),
    ]
    attend_pair(blocks, projected, o_ref, lse_ref, hooks(step, schedule))
    pl.when(step == pl.num_programs(0) - 1)(close_all)


def attend(sizes, blocks, projected, quads, halves, shrink):
    tokens, width = projected.shape[0], projected.shape[1] // 3
    pairs = width // PAIR
    lead = (sizes["c"], sizes["z"], sizes["y"])
    depth, rows, half = quads[0].shape
    grown, full = quads[1].shape[2], quads[2].shape[2]
    return pl.pallas_call(
        functools.partial(attend_kernel, sizes, blocks),
        grid=(pairs,),
        in_specs=[pl.BlockSpec((tokens, 3 * PAIR), lambda g: (0, g))] + [whole_vmem] * 5,
        out_specs=[
            pl.BlockSpec((tokens, PAIR), lambda g: (0, g)),
            pl.BlockSpec((None, 8, tokens), lambda g: (g, 0, 0)),
        ]
        + [any_place] * 5,
        out_shape=[
            low_shape(tokens, width),
            jax.ShapeDtypeStruct((pairs, 8, tokens), jnp.float32),
            low_shape(*lead, rows, 2 * half),
            low_shape(*lead, rows, 2 * grown),
            low_shape(2, *lead, rows, full),
            low_shape(depth, rows, grown),
            low_shape(depth, rows, full),
        ],
        scratch_shapes=[pltpu.SemaphoreType.DMA((2, 64))],
        compiler_params=params(2, 48),
        cost_estimate=small_cost,
        name="attend",
    )(projected, *quads, halves, shrink)


def mlp_tile(first, rows_step, c_ref, dy_ref, we_ref, ws_ref, be_ref, before, outs, scratch, between):
    y_ref, dc_ref, gwe_ref, gws_ref, gbe_ref = outs
    turned, act_all, du_all = scratch[:3]
    tokens = c_ref.shape[0]

    @pl.when(pl.program_id(0) == 0)
    def _():
        turned[...] = jnp.transpose(c_ref[...])
        if first:
            y_ref[...] = jnp.zeros_like(y_ref)
            dc_ref[...] = jnp.zeros_like(dc_ref)
        else:
            sem = scratch[3]
            copies = [
                pltpu.make_async_copy(before[0], y_ref, sem.at[0]),
                pltpu.make_async_copy(before[1], dc_ref, sem.at[1]),
            ]
            start(copies)
            wait(copies)

    we, ws = we_ref[...], ws_ref[...]
    total = None
    for part in range(tokens // rows_step):
        between(part)
        rows = pl.ds(part * rows_step, rows_step)
        hidden = nn(c_ref[rows, :], we) + be_ref[...]
        squared = hidden * hidden
        bent = jnp.tanh(gelu_root * hidden * (1.0 + gelu_cubic * squared))
        gate = 0.5 + 0.5 * bent
        act = (hidden * gate).astype(low)
        slope = gate + (0.5 * gelu_root) * hidden * (1.0 - bent * bent) * (
            1.0 + (3 * gelu_cubic) * squared
        )
        du = (nt(dy_ref[rows, :], ws) * slope).astype(low)
        act_all[rows, :] = act
        du_all[rows, :] = du
        y_ref[rows, :] += nn(act, ws)
        dc_ref[rows, :] += nt(du, we)
        added = jnp.sum(du.astype(jnp.float32), axis=0, keepdims=True)
        total = added if total is None else total + added
    gbe_ref[...] = total
    gwe_ref[...] = nn(turned[...], du_all[...]).astype(gwe_ref.dtype)
    gws_ref[...] = outer_sum(act_all[...], dy_ref[...]).astype(gws_ref.dtype)


def mlp_parts(tokens, width, hidden, tile):
    whole = pl.BlockSpec((tokens, width), lambda t: (0, 0))
    down = pl.BlockSpec((width, tile), lambda t: (0, t))
    across = pl.BlockSpec((tile, width), lambda t: (t, 0))
    thin = pl.BlockSpec((1, tile), lambda t: (0, t))
    return (
        [whole, whole, down, across, thin],
        [whole, whole, down, across, thin],
        [
            jax.ShapeDtypeStruct((tokens, width), jnp.float32),
            jax.ShapeDtypeStruct((tokens, width), jnp.float32),
            low_shape(width, hidden),
            low_shape(hidden, width),
            jax.ShapeDtypeStruct((1, hidden), jnp.float32),
        ],
        [
            pltpu.VMEM((width, tokens), low),
            pltpu.VMEM((tokens, tile), low),
            pltpu.VMEM((tokens, tile), low),
        ],
    )


def mlp_plain_kernel(first, rows_step, *refs):
    refs = Refs(refs)
    inputs = refs.take(5)
    before = [] if first else refs.take(2)
    outs = refs.take(5)
    mlp_tile(first, rows_step, *inputs, before, outs, refs.refs, lambda part: None)


def mlp(c, dy, we, ws, be, before=(), tile=256, rows_step=256):
    in_specs, out_specs, out_shape, scratch = mlp_parts(*c.shape, we.shape[1], tile)
    if before:
        scratch = scratch + [pltpu.SemaphoreType.DMA((2,))]
    return pl.pallas_call(
        functools.partial(mlp_plain_kernel, not before, rows_step),
        grid=(we.shape[1] // tile,),
        in_specs=in_specs + [any_place] * len(before),
        out_specs=out_specs,
        out_shape=out_shape,
        scratch_shapes=scratch,
        compiler_params=pltpu.CompilerParams(vmem_limit_bytes=56 << 20),
        cost_estimate=small_cost,
        name="mlp",
    )(c, dy, we, ws, be, *before)


def mlp_gather_kernel(sizes, rows_step, *refs):
    refs = Refs(refs)
    inputs = refs.take(5)
    expand_quad, shrink_quad = refs.take(2)
    outs = refs.take(5)
    expand, shrunk = refs.take(2)
    scratch, (sems,) = refs.take(3), refs.take(1)
    spot = Spot(sizes)
    mover = Mover(spot, sems)
    grown, width = expand_quad.shape[-1], shrink_quad.shape[-1]
    jobs = [
        Near(mover, shrink_quad, shrunk.at[spot.k], 0, width // 2),
        Near(mover, expand_quad, expand, spot.k * grown, grown // 2),
    ]

    def open_all():
        spot.meet(all_axes)
        for job in jobs:
            start(job.near + job.core[0])

    def far(job):
        wait(job.near)
        start(job.far + job.core[1])

    def close_all():
        jobs[1].close()
        for job in jobs:
            job.close_core()

    step = pl.program_id(0)
    schedule = [
        (0, 0, open_all),
        (3, 0, lambda: far(jobs[0])),
        (5, 2, lambda: far(jobs[1])),
        (7, 0, jobs[0].close),
    ]
    mlp_tile(True, rows_step, *inputs, [], outs, scratch, hooks(step, schedule))
    pl.when(step == pl.num_programs(0) - 1)(close_all)


def mlp_gather(sizes, c, dy, we, ws, be, quads, tile=256, rows_step=256):
    in_specs, out_specs, out_shape, scratch = mlp_parts(*c.shape, we.shape[1], tile)
    lead = (sizes["c"], sizes["z"], sizes["y"])
    rows, grown, full = quads[0].shape[1], quads[0].shape[2], quads[1].shape[2]
    return pl.pallas_call(
        functools.partial(mlp_gather_kernel, sizes, rows_step),
        grid=(we.shape[1] // tile,),
        in_specs=in_specs + [whole_vmem] * 2,
        out_specs=out_specs + [any_place] * 2,
        out_shape=out_shape + [low_shape(*lead, rows, 2 * grown), low_shape(2, *lead, rows, full)],
        scratch_shapes=scratch + [pltpu.SemaphoreType.DMA((2, 32))],
        compiler_params=params(3, 56),
        cost_estimate=small_cost,
        name="mlp_gather",
    )(c, dy, we, ws, be, *quads)


def mlp_reduce_kernel(sizes, rows_step, *refs):
    refs = Refs(refs)
    inputs, before = refs.take(5), refs.take(2)
    expand, shrink = refs.take(2)
    outs = refs.take(5)
    expand_quad, shrink_quad = refs.take(2)
    scratch, (sems,) = refs.take(4), refs.take(1)
    spot = Spot(sizes)
    mover = Mover(spot, sems)
    grown, width = expand_quad.shape[-1], shrink_quad.shape[-1]
    jobs = [
        ReduceNear(
            mover, shrink.at[spot.k], shrink.at[1 - spot.k], width // 2, shrink_quad, refs.take(6)
        ),
        ReduceNear(
            mover, *core_halves(expand, spot.k, grown), grown // 2, expand_quad, refs.take(6)
        ),
    ]

    def open_all():
        spot.meet(all_axes)
        for job in jobs:
            start(job.first)

    def close_all():
        jobs[1].close()

    step = pl.program_id(0)
    schedule = [
        (0, 0, open_all),
        (1, 1, jobs[0].go_near),
        (2, 1, jobs[1].go_near),
        (4, 0, jobs[0].go_far),
        (6, 1, jobs[1].go_far),
        (7, 1, jobs[0].close),
    ]
    mlp_tile(False, rows_step, *inputs, before, outs, scratch, hooks(step, schedule))
    pl.when(step == pl.num_programs(0) - 1)(close_all)


def mlp_reduce(sizes, c, dy, we, ws, be, before, grads, tile=256, rows_step=256):
    in_specs, out_specs, out_shape, scratch = mlp_parts(*c.shape, we.shape[1], tile)
    expand, shrink = grads
    depth, rows = sizes["z"], expand.shape[3]
    grown, full = expand.shape[-1] // 2, shrink.shape[-1]
    scratch = scratch + [pltpu.SemaphoreType.DMA((2,)), pltpu.SemaphoreType.DMA((2, 16))]
    for columns in (full, grown):
        scratch += ReduceNear.scratch(sizes, rows, columns, columns // 2)
    return pl.pallas_call(
        functools.partial(mlp_reduce_kernel, sizes, rows_step),
        grid=(we.shape[1] // tile,),
        in_specs=in_specs + [any_place] * 4,
        out_specs=out_specs + [whole_vmem] * 2,
        out_shape=out_shape + [low_shape(depth, rows, grown), low_shape(depth, rows, full)],
        scratch_shapes=scratch,
        compiler_params=params(4, 60),
        cost_estimate=small_cost,
        name="mlp_reduce",
    )(c, dy, we, ws, be, *before, *grads)


def attend_back_kernel(sizes, blocks, *refs):
    refs = Refs(refs)
    projected, upstream, lse_ref, mixing, expand, shrink, done_expand, done_shrink = refs.take(8)
    back_ref, mixing_quad, expand_quad, shrink_quad, expand_out, shrink_out = refs.take(6)
    turned, key_sum, value_sum, sems = refs.take(4)
    spot = Spot(sizes)
    mover = Mover(spot, sems)
    k = spot.k
    half, grown, width = mixing_quad.shape[-1], expand_quad.shape[-1], shrink_quad.shape[-1]
    jobs = [
        ReduceNear(mover, shrink.at[k], shrink.at[1 - k], width // 2, shrink_quad, refs.take(6)),
        ReduceNear(mover, *core_halves(expand, k, grown), grown // 2, expand_quad, refs.take(6)),
        ReduceNear(mover, *core_halves(mixing, k, half), half // 2, mixing_quad, refs.take(6)),
    ]
    deep = [
        ReduceDeep(mover, done_expand, *refs.take(1)),
        ReduceDeep(mover, done_shrink, *refs.take(1)),
    ]
    ending = Finish(mover, *refs.take(2))

    def open_all():
        spot.meet(all_axes)
        for job in jobs:
            start(job.first)
        for job in deep:
            start(job.copies)

    def finish():
        wait(deep[0].copies)
        ending.summed[...] = deep[0].result()
        start(ending.copies)
        wait(deep[1].copies)
        shrink_out[...] = deep[1].result()

    def close_all():
        wait(ending.copies)
        ending.write(expand_out)
        jobs[1].close()
        jobs[2].close()

    step = pl.program_id(0)
    schedule = [
        (0, 0, open_all),
        (1, 1, jobs[0].go_near),
        (2, 1, jobs[1].go_near),
        (2, 3, jobs[2].go_near),
        (4, 0, jobs[0].go_far),
        (5, 3, finish),
        (6, 2, jobs[1].go_far),
        (7, 2, jobs[2].go_far),
        (7, 3, jobs[0].close),
    ]
    attend_back_pair(
        blocks, projected, upstream, lse_ref, back_ref, turned, key_sum, value_sum,
        hooks(step, schedule),
    )
    pl.when(step == pl.num_programs(0) - 1)(close_all)


def attend_back(sizes, blocks, projected, upstream, lse, grads, quads):
    tokens, width = upstream.shape
    pairs = width // PAIR
    mixing, expand, shrink = grads
    depth, rows = sizes["z"], mixing.shape[3]
    half, grown, full = mixing.shape[-1] // 2, expand.shape[-1] // 2, shrink.shape[-1]
    triple = pl.BlockSpec((tokens, 3 * PAIR), lambda g: (0, g))
    scratch = [
        pltpu.VMEM((blocks, PAIR, BLK), low),
        pltpu.VMEM((blocks, BLK, PAIR), jnp.float32),
        pltpu.VMEM((blocks, BLK, PAIR), jnp.float32),
        pltpu.SemaphoreType.DMA((2, 32)),
    ]
    for columns in (full, grown, half):
        scratch += ReduceNear.scratch(sizes, rows, columns, columns // 2)
    for columns in (grown, full):
        scratch += [pltpu.VMEM((depth - 1, rows, columns), low)]
    scratch += Finish.scratch(rows, grown)
    return pl.pallas_call(
        functools.partial(attend_back_kernel, sizes, blocks),
        grid=(pairs,),
        in_specs=[
            triple,
            pl.BlockSpec((tokens, PAIR), lambda g: (0, g)),
            pl.BlockSpec((None, 8, tokens), lambda g: (g, 0, 0)),
        ]
        + [any_place] * 3
        + [whole_vmem] * 2,
        out_specs=[triple] + [whole_vmem] * 5,
        out_shape=[
            low_shape(*projected.shape),
            low_shape(depth, rows, half),
            low_shape(depth, rows, grown),
            low_shape(depth, rows, full),
            jax.ShapeDtypeStruct((2, rows // 2, grown), jnp.float32),
            jax.ShapeDtypeStruct((rows, full), jnp.float32),
        ],
        scratch_shapes=scratch,
        compiler_params=params(5, 56),
        cost_estimate=small_cost,
        name="attend_back",
    )(projected, upstream, lse, *grads, *quads)


def normal_rows(rows):
    centered = rows - jnp.mean(rows, axis=-1, keepdims=True)
    inverse = lax.rsqrt(jnp.mean(centered * centered, axis=-1, keepdims=True) + norm_eps)
    return centered * inverse, inverse


def norm_pull(upstream, normal, inverse, gain):
    scaled = upstream * gain
    inner = jnp.mean(scaled, axis=-1, keepdims=True)
    along = jnp.mean(scaled * normal, axis=-1, keepdims=True)
    return inverse * (scaled - inner - normal * along)


def end_kernel(sizes, *refs):
    refs = Refs(refs)
    back_ref, back_far, low_far, joint_far, rows_far, middle_far = refs.take(6)
    gain_ref, vector, mixing_quad, expand_quad, shrink_quad = refs.take(5)
    out, vector_out, mixing_out, expand_out, shrink_out, kept, arrived_rows = refs.take(7)
    sems, steps, arrived = refs.take(3)
    grads, low_rows, turned, joint, rows_in, middle, sent = refs.take(7)
    spot = Spot(sizes)
    mover = Mover(spot, sems)
    width = joint.shape[-1] // 2
    part = width // 2
    tile = 256
    loads = [
        mover.local(far, near)
        for far, near in (
            (back_far, grads),
            (low_far, low_rows),
            (joint_far, joint),
            (rows_far, rows_in),
            (middle_far, middle),
        )
    ]
    jobs, deeps, ends, others_half = [], [], [], []
    for number in range(2):
        theirs, quad = refs.take(2)
        others_half.append(theirs)
        jobs.append(ReduceNear(mover, None, theirs, part // 2, quad, refs.take(6)))
        deeps.append(ReduceDeep(mover, quad, *refs.take(1)))
        ends.append(Finish(mover, *refs.take(2)))
    others = [
        ReduceDeep(mover, quad, *refs.take(1))
        for quad in (mixing_quad, expand_quad, shrink_quad)
    ]
    other_ends = [Finish(mover, *refs.take(2)) for _ in range(2)]
    hops = [
        mover.copy(steps.at[number], arrived.at[number], name)
        for number, name in enumerate(("k", "c", "y"))
    ]
    spread = [
        mover.copy(steps.at[3], arrived.at[2 + by], "z", by) for by in range(1, sizes["z"])
    ]
    rows_copy = mover.copy(sent, arrived_rows, "c")

    def gradient(core, number, target):
        @pl.loop(0, part // tile)
        def _(t):
            columns = span(core * width + number * part + t * tile, tile)
            piece = nn(turned[...], grads[:, columns]).astype(low)
            target[..., span(t * tile, tile)] = piece.reshape(*target.shape[:-1], tile)

    sums = {}

    def pull_block(number):
        rows = block_rows(number)
        pulled = grads[rows, :]
        upstream = nt(pulled, joint[...])
        normal, inverse = normal_rows(rows_in[rows, :].astype(jnp.float32))
        middle[rows, :] += norm_pull(upstream, normal, inverse, gain_ref[...])
        for name, value in (
            ("gain", upstream * normal),
            ("shift", upstream),
            ("back", pulled.astype(jnp.float32)),
        ):
            value = jnp.sum(value, axis=0, keepdims=True)
            sums[name] = sums[name] + value if name in sums else value

    def stored_block(place):
        number = jnp.full((1, middle.shape[1]), back_ref[place], jnp.int32)
        value = middle[block_rows(0), :]
        for other in range(1, middle.shape[0] // BLK):
            value = jnp.where(number == other, middle[block_rows(other), :], value)
        return value

    def hop(number):
        wait([hops[number]])
        steps[number + 1] = steps[number] + arrived[number]
        start([hops[number + 1]] if number < 2 else spread)

    start(loads)
    spot.meet(all_axes)
    for job in others:
        start(job.copies)
    wait(loads[:2])
    turned[...] = jnp.transpose(low_rows[...])
    for number, job in enumerate(jobs):
        gradient(1 - spot.k, number, others_half[number])
        start(job.first)
        gradient(spot.k, number, job.total)
        job.go_near()
    wait(loads[2:])
    pull_block(0)
    pull_block(1)
    jobs[0].go_far()
    pull_block(2)
    jobs[1].go_far()
    pull_block(3)
    for place in range(2):
        sent[block_rows(place), :] = stored_block(2 + place).astype(low)
    start([rows_copy])
    for place in range(2):
        kept[block_rows(place), :] = stored_block(place)
    steps[0] = vector[...]
    steps[0, 0:1, :] = sums["gain"]
    steps[0, 1:2, :] = sums["shift"]
    for pair in range(H // 2):
        for row, third in ((2, 0), (3, 2)):
            steps[0, row : row + 1, pair * PAIR : (pair + 1) * PAIR] = sums["back"][
                :, (3 * pair + third) * PAIR : (3 * pair + third + 1) * PAIR
            ]
    start(hops[:1])
    jobs[0].close()
    start(deeps[0].copies)
    hop(0)
    for job, ending in zip(others, other_ends):
        wait(job.copies)
        ending.summed[...] = job.result()
        start(ending.copies)
    wait(others[2].copies)
    shrink_out[...] = others[2].result()
    jobs[1].close()
    start(deeps[1].copies)
    hop(1)
    hop(2)
    for ending, target in zip(other_ends, (mixing_out, expand_out)):
        wait(ending.copies)
        ending.write(target)
    for deep, ending in zip(deeps, ends):
        wait(deep.copies)
        ending.summed[...] = deep.result()
        start(ending.copies)
    wait(spread)
    total = steps[3]
    for by in range(1, sizes["z"]):
        total = total + arrived[2 + by]
    vector_out[...] = total
    for number, ending in enumerate(ends):
        wait(ending.copies)
        ending.write(out, pl.ds(number * part, part))
    wait([rows_copy])


def end(sizes, back, joint_back, first_low, joint, rows_in, middle_grad, gain, vector, quads):
    tokens, model = rows_in.shape
    width = joint.shape[1] // 2
    lead = (sizes["c"], sizes["z"], sizes["y"])
    depth = sizes["z"]
    rows = model // (lead[0] * lead[1] * lead[2])
    part = width // 2
    half, grown, full = [quad.shape[-1] for quad in quads]
    scratch = [
        pltpu.SemaphoreType.DMA((2, 48)),
        pltpu.VMEM((4, *vector.shape), jnp.float32),
        pltpu.VMEM((2 + depth, *vector.shape), jnp.float32),
        pltpu.VMEM(joint_back.shape, low),
        pltpu.VMEM(first_low.shape, low),
        pltpu.VMEM(first_low.shape[::-1], low),
        pltpu.VMEM(joint.shape, low),
        pltpu.VMEM(rows_in.shape, low),
        pltpu.VMEM(middle_grad.shape, jnp.float32),
        pltpu.VMEM((tokens // 2, model), low),
    ]
    for number in range(2):
        scratch += [pltpu.VMEM((*lead, rows, part), low), pltpu.VMEM((depth, rows, part), low)]
        scratch += ReduceNear.scratch(sizes, rows, part, part // 2)
        scratch += [pltpu.VMEM((depth - 1, rows, part), low)]
        scratch += Finish.scratch(rows, part)
    scratch += [pltpu.VMEM((depth - 1, rows, columns), low) for columns in (half, grown, full)]
    for columns in (half, grown):
        scratch += Finish.scratch(rows, columns)
    own = rows // 2
    shapes = [(2, own, width), vector.shape, (2, own, half), (2, own, grown), (rows, full)]
    shapes.append((tokens // 2, model))
    return pl.pallas_call(
        functools.partial(end_kernel, sizes),
        in_specs=[pl.BlockSpec(memory_space=pltpu.SMEM)] + [any_place] * 5 + [whole_vmem] * 5,
        out_specs=[whole_vmem] * 6 + [any_place],
        out_shape=[jax.ShapeDtypeStruct(shape, jnp.float32) for shape in shapes]
        + [low_shape(tokens // 2, model)],
        scratch_shapes=scratch,
        compiler_params=params(6, 60),
        cost_estimate=small_cost,
        name="end",
    )(back, joint_back, first_low, joint, rows_in, middle_grad, gain, vector, *quads)


def give_kernel(back_ref, middle_ref, result_ref, shift_ref, kept_ref, sent_ref):
    value = (middle_ref[...] + result_ref[...] + shift_ref[...]).astype(low)
    step = pl.program_id(0)

    @pl.when(step < 2)
    def _():
        kept_ref[...] = value

    @pl.when(step >= 2)
    def _():
        sent_ref[...] = value


def give(back, middle, result, shift):
    width = middle.shape[1]
    block = pl.BlockSpec((BLK, width), lambda p, back: (back[p], 0))
    return pl.pallas_call(
        give_kernel,
        grid_spec=pltpu.PrefetchScalarGridSpec(
            num_scalar_prefetch=1,
            grid=(back.shape[0],),
            in_specs=[block, block, pl.BlockSpec((1, width), lambda p, back: (0, 0))],
            out_specs=[
                pl.BlockSpec((BLK, width), lambda p, back: (jnp.minimum(p, 1), 0)),
                pl.BlockSpec((BLK, width), lambda p, back: (jnp.maximum(p - 2, 0), 0)),
            ],
        ),
        out_shape=[low_shape(2 * BLK, width)] * 2,
        cost_estimate=small_cost,
        name="give",
    )(back, middle, result, shift)


def take_kernel(place_ref, kept_ref, arrived_ref, out_ref):
    here = place_ref[pl.program_id(0)] < 2

    @pl.when(here)
    def _():
        out_ref[...] = kept_ref[...]

    @pl.when(jnp.logical_not(here))
    def _():
        out_ref[...] = arrived_ref[...]


def take(place, kept, arrived):
    width = kept.shape[1]
    return pl.pallas_call(
        take_kernel,
        grid_spec=pltpu.PrefetchScalarGridSpec(
            num_scalar_prefetch=1,
            grid=(place.shape[0],),
            in_specs=[
                pl.BlockSpec((BLK, width), lambda i, place: (jnp.minimum(place[i], 1), 0)),
                pl.BlockSpec((BLK, width), lambda i, place: (jnp.maximum(place[i] - 2, 0), 0)),
            ],
            out_specs=pl.BlockSpec((BLK, width), lambda i, place: (i, 0)),
        ),
        out_shape=low_shape(4 * BLK, width),
        cost_estimate=small_cost,
        name="take",
    )(place, kept, arrived)


def last_kernel(ctx_ref, *refs):
    refs = Refs(refs)
    joint_part, mixing_part, expand_a, expand_b, shrink_a, shrink_b = refs.take(6)
    kept_grad, far_grad, kept_out, far_out = refs.take(4)
    states = [refs.take(3) for _ in range(4)]
    grad_out, block_out = refs.take(2)
    news = [refs.take(4) for _ in range(4)]
    here = ctx_ref[0]
    grad_out[here] = kept_grad[...]
    grad_out[1 - here] = far_grad[...].astype(jnp.float32)
    block_out[here] = kept_out[...]
    block_out[1 - here] = far_out[...]

    def update(number, where, gradient):
        weight, first, second = [ref[where] for ref in states[number]]
        results = adam_update(weight, first, second, gradient, 0.05, 0.1)
        for ref, value in zip(news[number], (*results, results[0].astype(low))):
            ref[where] = value

    every = slice(None)
    pairs = joint_part.shape[2] // (3 * PAIR)
    for core in range(2):
        for pair in range(pairs):
            for third in range(3):
                first = ((third * 2 + core) * pairs + pair) * PAIR
                source = (pair * 3 + third) * PAIR
                update(
                    0,
                    (every, pl.ds(first, PAIR)),
                    joint_part[core, :, source : source + PAIR],
                )
        half = mixing_part.shape[2]
        update(1, (every, pl.ds(core * half, half)), mixing_part[core])
        lane = lax.broadcasted_iota(jnp.int32, (1, PAIR), 1)
        for chip in range(0, expand_a.shape[2] // HD, 2):
            a = expand_a[core, :, chip * HD : chip * HD + PAIR]
            b = expand_b[core, :, chip * HD : chip * HD + PAIR]
            even = jnp.where(lane < HD, a, pltpu.roll(b, HD, 1))
            odd = jnp.where(lane < HD, pltpu.roll(a, HD, 1), b)
            for number, value in ((chip, even), (chip + 1, odd)):
                update(2, (every, pl.ds((number * 2 + core) * PAIR, PAIR)), value)
    rows = shrink_a.shape[0]
    update(3, (pl.ds(0, rows), every), shrink_a[...])
    update(3, (pl.ds(rows, rows), every), shrink_b[...])


def last(ctx, parts, kept_grad, far_grad, kept_out, far_out, states):
    shapes = [jax.ShapeDtypeStruct((2, *kept_grad.shape), jnp.float32), low_shape(2, *kept_out.shape)]
    for weight, _, _ in states:
        shapes += [jax.ShapeDtypeStruct(weight.shape, jnp.float32)] * 3
        shapes.append(low_shape(*weight.shape))
    flat = [array for state in states for array in state]
    return pl.pallas_call(
        last_kernel,
        in_specs=[pl.BlockSpec(memory_space=pltpu.SMEM)] + [whole_vmem] * (10 + len(flat)),
        out_specs=[whole_vmem] * len(shapes),
        out_shape=shapes,
        compiler_params=pltpu.CompilerParams(vmem_limit_bytes=56 << 20),
        cost_estimate=small_cost,
        name="last",
    )(ctx, *parts, kept_grad, far_grad, kept_out, far_out, *flat)


def layer_norm(values, gain_row, shift_row):
    centered = values - jnp.mean(values, axis=-1, keepdims=True)
    variance = jnp.mean(centered * centered, axis=-1, keepdims=True)
    inverse = lax.rsqrt(variance + norm_eps)
    normal_part = centered * inverse
    return (normal_part * gain_row + shift_row, normal_part, inverse)


def norm_back(upstream, normal_part, inverse, gain_row):
    scaled = upstream * gain_row
    inner_sum = jnp.mean(scaled, axis=-1, keepdims=True)
    along_sum = jnp.mean(scaled * normal_part, axis=-1, keepdims=True)
    values_grad = inverse * (scaled - inner_sum - normal_part * along_sum)
    return (values_grad, jnp.sum(upstream * normal_part, axis=0), jnp.sum(upstream, axis=0))


def adam_update(weight, moment_one, moment_two, gradient, step_rate, decay_rate):
    first_new = 0.5 * moment_one + 0.5 * gradient
    second_new = 0.5 * moment_two + 0.5 * gradient * gradient
    correct = 1.0 - 0.5**STEP
    direction = first_new / correct / (jnp.sqrt(second_new / correct) + adam_eps)
    updated = weight - step_rate * (direction + decay_rate * weight)
    return (updated, first_new, second_new)


def to_groups(matrix):
    row_count = matrix.shape[0]
    return matrix.reshape(row_count, H // group_heads, group_heads, HD).transpose(1, 0, 2, 3)


def from_groups(stacked):
    return stacked.transpose(1, 0, 2, 3).reshape(stacked.shape[1], H * HD)


def tile_scores(queries, key_rows, allowed):
    products = jnp.einsum("rgd,lgd->grl", queries, key_rows, preferred_element_type=jnp.float32)
    return jnp.where(allowed[None], products * 0.125, -1e30)


def tile_forward(queries, key_rows, value_rows, allowed):
    scores = tile_scores(queries, key_rows, allowed)
    largest = jnp.max(scores, axis=-1, keepdims=True)
    exponent = jnp.exp(scores - largest)
    row_total = jnp.sum(exponent, axis=-1, keepdims=True)
    weights = (exponent / row_total).astype(low)
    mixed = jnp.einsum("grl,lgd->rgd", weights, value_rows, preferred_element_type=jnp.float32)
    return (mixed, (largest + jnp.log(row_total))[..., 0])


def tile_backward(queries, key_rows, value_rows, allowed, logsum, upstream):
    scores = tile_scores(queries, key_rows, allowed)
    recomputed = jnp.exp(scores - logsum[..., None])
    value_grad = jnp.einsum(
        "grl,rgd->lgd", recomputed.astype(low), upstream, preferred_element_type=jnp.float32
    )
    weight_grad = jnp.einsum(
        "rgd,lgd->grl", upstream, value_rows, preferred_element_type=jnp.float32
    )
    inner_sum = jnp.sum(recomputed * weight_grad, axis=-1, keepdims=True)
    score_grad = (recomputed * (weight_grad - inner_sum)).astype(low)
    query_grad = (
        jnp.einsum("grl,lgd->rgd", score_grad, key_rows, preferred_element_type=jnp.float32) * 0.125
    )
    key_grad = (
        jnp.einsum("grl,rgd->lgd", score_grad, queries, preferred_element_type=jnp.float32) * 0.125
    )
    return (query_grad, key_grad, value_grad)


def spread_forward(queries, key_value, allowed):
    def one_sequence(pieces):
        queries, key_value, allowed = pieces
        width = queries.shape[1]
        mixed, logsum = lax.map(
            lambda triple: tile_forward(triple[0], triple[1], triple[2], allowed),
            (to_groups(queries), to_groups(key_value[:, :width]), to_groups(key_value[:, width:])),
        )
        return (from_groups(mixed), logsum)

    return lax.map(one_sequence, (queries, key_value, allowed))


def spread_backward(queries, key_value, allowed, logsum, upstream):
    def one_sequence(pieces):
        queries, key_value, allowed, logsum, upstream = pieces
        width = queries.shape[1]
        query_grad, key_grad, value_grad = lax.map(
            lambda member: tile_backward(
                member[0], member[1], member[2], allowed, member[3], member[4]
            ),
            (
                to_groups(queries),
                to_groups(key_value[:, :width]),
                to_groups(key_value[:, width:]),
                logsum,
                to_groups(upstream),
            ),
        )
        return (
            from_groups(query_grad),
            jnp.concatenate([from_groups(key_grad), from_groups(value_grad)], axis=1),
        )

    return lax.map(one_sequence, (queries, key_value, allowed, logsum, upstream))


class Slice:
    def __init__(self, ctx_size, wshard_size):
        rest = wshard_size // 2
        self.sizes = {"c": ctx_size, "z": 4, "y": rest // 4, "k": 2}

    def here(self):
        flat = lax.axis_index(axes)
        found = {}
        for name in ("k", "y", "z", "c"):
            found[name] = flat % self.sizes[name]
            flat = flat // self.sizes[name]
        return found

    def shift(self, value, name, by):
        pairs = []
        sizes = self.sizes
        for c in range(sizes["c"]):
            for z in range(sizes["z"]):
                for y in range(sizes["y"]):
                    for k in range(sizes["k"]):
                        spot = {"c": c, "z": z, "y": y, "k": k}
                        goal = dict(spot)
                        goal[name] = (spot[name] + by) % sizes[name]
                        pairs.append((self.flat(spot), self.flat(goal)))
        return lax.ppermute(value, axes, pairs)

    def flat(self, spot):
        sizes = self.sizes
        return ((spot["c"] * sizes["z"] + spot["z"]) * sizes["y"] + spot["y"]) * sizes["k"] + spot[
            "k"
        ]

    def stack(self, array, name, here):
        size = self.sizes[name]
        parts = [array] + [self.shift(array, name, by) for by in range(1, size)]
        if size > 4:
            ordered = [parts[(-place) % size] for place in range(size)]
            return jnp.roll(jnp.stack(ordered), here[name], axis=0)
        return jnp.stack(
            [lax.select_n((here[name] - place) % size, *parts) if size > 2 else
             jnp.where(here[name] == place, parts[0], parts[1]) for place in range(size)]
        )

    def reach(self, pieces, name):
        grown = list(pieces)
        for by in range(1, self.sizes[name]):
            for array, place in pieces:
                moved = dict(place)
                moved[name] = (place[name] - by) % self.sizes[name]
                grown.append((self.shift(array, name, by), moved))
        return grown

    def gather_split(self, stacked, cut, here):
        sizes = self.sizes
        depth, rows, columns = stacked.shape
        out = jnp.zeros((sizes["c"], depth, sizes["y"], rows, columns), stacked.dtype)
        for low_column, high_column, order in ((0, cut, "cy"), (cut, columns, "yc")):
            pieces = [(stacked[:, :, low_column:high_column], here)]
            for name in order:
                pieces = self.reach(pieces, name)
            for array, place in pieces:
                out = lax.dynamic_update_slice(
                    out, array[None, :, None], (place["c"], 0, place["y"], 0, low_column)
                )
        return out.reshape(-1, columns)

    def send_terms(self, value, name, place, here):
        size = self.sizes[name]
        own = lax.dynamic_index_in_dim(value, here[name], place, False)
        moved = [
            self.shift(
                lax.dynamic_index_in_dim(value, (here[name] + by) % size, place, False), name, by
            )
            for by in range(1, size)
        ]
        return own, moved

    def add_terms(self, terms, kind=low):
        own, moved = terms
        total = own.astype(jnp.float32)
        for other in moved:
            total = total + other.astype(jnp.float32)
        return total.astype(kind)

    def everywhere(self, value):
        for name in ("k", "c", "y", "z"):
            total = value
            for by in range(1, self.sizes[name]):
                total = total + self.shift(value, name, by)
            value = total
        return value


def tie(value, *others):
    return lax.optimization_barrier((value, others))[0]


def by_core(core, first, second, axis):
    return jnp.where(
        core == 0,
        jnp.concatenate([first, second], axis=axis),
        jnp.concatenate([second, first], axis=axis),
    )


def pick(core, array, axis):
    return (
        lax.dynamic_index_in_dim(array, core, axis, False),
        lax.dynamic_index_in_dim(array, 1 - core, axis, False),
    )


def gather_far(grid, here, pieces):
    joint_halves, table, mixing_halves, expand_a, expand_b, shrink_a, shrink_b = pieces
    core = here["k"]

    def chip_rows(halves):
        own, other = pick(core, halves, 0)
        return by_core(core, own, grid.shift(other, "k", 1), 0)

    def everyone(block):
        width = block.shape[1]
        return grid.gather_split(grid.stack(block, "z", here), width // 2, here)

    def both(block, axis):
        own = everyone(block)
        return by_core(core, own, grid.shift(own, "k", 1), axis)

    return (
        both(chip_rows(joint_halves), 1),
        everyone(by_core(core, table, grid.shift(table, "k", 1), 0)),
        both(chip_rows(mixing_halves), 1),
        both(chip_rows(expand_a), 1),
        both(chip_rows(expand_b), 1),
        both(shrink_a, 0),
        both(shrink_b, 0),
    )


def reduce_far(grid, here, gradient, by_rows):
    core = here["k"]
    sizes = grid.sizes
    if by_rows:
        own, other = pick(core, gradient.reshape(2, -1, gradient.shape[1]), 0)
    else:
        own, other = pick(core, gradient.reshape(gradient.shape[0], 2, -1), 1)
    total = grid.add_terms((own, [grid.shift(other, "k", 1)]))
    total = total.reshape(sizes["c"], sizes["z"], sizes["y"], -1, own.shape[-1])
    for name, place in (("y", 2), ("c", 0)):
        total = grid.add_terms(grid.send_terms(total, name, place, here))
    total = grid.add_terms(grid.send_terms(total, "z", 0, here), jnp.float32)
    if by_rows:
        return total
    kept, other = pick(core, total.reshape(2, -1, total.shape[1]), 0)
    return by_core(core, kept[None], grid.shift(other, "k", 1)[None], 0)


def body(
    grid,
    block_input,
    block_order,
    cotangent,
    joint_weight,
    mixing_weight,
    expand_weight,
    shrink_weight,
    vectors,
    joint_first,
    mixing_first,
    expand_first,
    shrink_first,
    vectors_first,
    joint_second,
    mixing_second,
    expand_second,
    shrink_second,
    vectors_second,
):
    here = grid.here()
    sizes = grid.sizes
    ctx, ctx_size = here["c"], sizes["c"]
    seq_count, row_count, width = block_input.shape
    half = width // 2
    pairs = H // 2
    hidden_width = expand_weight.shape[1]
    own_rows = joint_weight.shape[0]
    slot = shrink_weight.shape[0]
    sub = slot // 2
    chips = hidden_width // (2 * slot)
    tokens = seq_count * row_count
    row_blocks = row_count // BLK
    near = ctx_size == 2 and seq_count == 2 and sizes["y"] == 2 and own_rows % 32 == 0

    def exchange(rows):
        sent = lax.dynamic_index_in_dim(rows, 1 - ctx, 0, False)
        return lax.dynamic_index_in_dim(rows, ctx, 0, False), grid.shift(sent, "c", 1)

    def hidden_sets(shard):
        parts = shard.astype(low).reshape(own_rows, chips, 2, 2, sub)
        return [
            parts[:, :, :, number].transpose(2, 0, 1, 3).reshape(2, own_rows, chips * sub)
            for number in range(2)
        ]

    joint_halves = (
        joint_weight.astype(low)
        .reshape(own_rows, 3, 2, pairs // 2, PAIR)
        .transpose(2, 0, 3, 1, 4)
        .reshape(2, own_rows, 3 * half)
    )
    table = jnp.pad(vectors.T.astype(low), ((0, 0), (0, 128 - vectors.shape[0])))
    mixing_halves = mixing_weight.astype(low).reshape(own_rows, 2, half).transpose(1, 0, 2)
    shrink_low = shrink_weight.astype(low)
    pieces = [joint_halves, table, mixing_halves, *hidden_sets(expand_weight)]
    pieces += [shrink_low[:sub], shrink_low[sub:]]
    if near:
        input_parts = exchange(block_input)
        joint_halves, table, mixing_halves, expand_half, next_half, shrink, next_shrink = pieces
        joint, tables, *quads = begin(
            sizes, joint_halves, table, mixing_halves, expand_half, shrink
        )
    else:
        joint, tables, mixing, expand_a, expand_b, shrink_a, shrink_b = gather_far(
            grid, here, pieces
        )
    joint = joint.reshape(width, 3 * width)
    vector_values = (
        tables.reshape(width, -1)[:, : vectors.shape[0]].T.astype(jnp.float32)
    )

    if near:
        order = lax.dynamic_slice_in_dim(block_order, ctx, 1, 0)[0]
        blocks = order.shape[0]
        stored = jnp.arange(blocks, dtype=jnp.int32)
        moved = jnp.where(stored // row_blocks == ctx, 0, row_blocks) + stored % row_blocks
        place = jnp.sum(jnp.where(order[None, :] == stored[:, None], moved[None, :], 0), axis=1)
        back = jnp.sum(jnp.where(moved[None, :] == stored[:, None], order[None, :], 0), axis=1)
        place, back = place.astype(jnp.int32), back.astype(jnp.int32)
        input_low = take(place, *input_parts)
        upstream_parts = exchange(tie(cotangent, tables))
    else:
        input_low = block_input.reshape(tokens, width)
        upstream = cotangent.reshape(tokens, width)
    input_rows = input_low.astype(jnp.float32)
    normed_first, normal_first, inverse_first = layer_norm(
        input_rows, vector_values[0], vector_values[1]
    )
    first_low = normed_first.astype(low)
    joint_shift = jnp.stack(
        [
            vector_values[2].reshape(pairs, PAIR),
            jnp.zeros((pairs, PAIR), jnp.float32),
            vector_values[3].reshape(pairs, PAIR),
        ],
        axis=1,
    ).reshape(-1)
    projected = (nn(first_low, joint) + joint_shift).astype(low)
    if near:
        mixed_low, logsum, mixing, expand_a, shrink_a, *quads = attend(
            sizes, blocks, projected, quads, next_half, next_shrink
        )
    else:
        by_part = projected.reshape(seq_count, row_count, pairs, 3, PAIR)
        queries, keys, values = [
            by_part[:, :, :, part].reshape(seq_count, row_count, width) for part in range(3)
        ]
        key_value = lax.all_gather(
            jnp.concatenate([keys, values], axis=2), "ctx", axis=1, tiled=True
        )
        own_blocks = lax.dynamic_slice_in_dim(block_order, ctx * row_blocks, row_blocks, 1)
        query_block = jnp.repeat(own_blocks, BLK, axis=1, total_repeat_length=row_count)
        key_block = jnp.repeat(block_order, BLK, axis=1, total_repeat_length=key_value.shape[1])
        allowed = key_block[:, None, :] <= query_block[:, :, None]
        mixed, logsum = spread_forward(queries, key_value, allowed)
        mixed_low = mixed.astype(low).reshape(tokens, width)
    mixing = mixing.reshape(width, width)
    middle = input_rows + (nn(mixed_low, mixing) + vector_values[4])
    normed_second, normal_second, inverse_second = layer_norm(
        middle, vector_values[5], vector_values[6]
    )
    second_low = normed_second.astype(low)
    if near:
        upstream = take(place, *upstream_parts)

    lead = (sizes["c"], sizes["z"], sizes["y"])
    hidden_bias = vector_values[8:].reshape(chips, 2, 2, sub).transpose(2, 1, 0, 3).reshape(2, 1, -1)

    def operands(number, expand, shrink):
        return (
            second_low,
            upstream,
            expand.reshape(width, -1),
            shrink.reshape(-1, width),
            hidden_bias[number],
        )

    def by_device(expand_grad, shrink_grad):
        return (
            expand_grad.reshape(*lead, -1, expand_grad.shape[1]),
            shrink_grad.reshape(2, *lead, -1, width),
        )

    if near:
        *before, expand_grad_a, shrink_grad_a, bias_a, expand_b, shrink_b = mlp_gather(
            sizes, *operands(0, expand_a, shrink_a), quads
        )
        result, second_grad, expand_grad_b, shrink_grad_b, bias_b, *quads = mlp_reduce(
            sizes,
            *operands(1, expand_b, shrink_b),
            before,
            by_device(expand_grad_a, shrink_grad_a),
        )
    else:
        *before, expand_grad_a, shrink_grad_a, bias_a = mlp(*operands(0, expand_a, shrink_a))
        result, second_grad, expand_grad_b, shrink_grad_b, bias_b = mlp(
            *operands(1, expand_b, shrink_b), before=before
        )
    hidden_bias_grads = [
        bias.reshape(2, chips, 1, sub).transpose(1, 0, 2, 3) for bias in (bias_a, bias_b)
    ]
    if near:
        kept_out, sent_out = give(back, middle, result, vector_values[7:8])
        far_out = grid.shift(sent_out, "c", 1)
        second_grad = tie(second_grad, sent_out)
    else:
        block_output = (middle + result + vector_values[7]).astype(low).reshape(block_input.shape)

    upstream_float = upstream.astype(jnp.float32)
    middle_part, gain_two, shift_two = norm_back(
        second_grad, normal_second, inverse_second, vector_values[5]
    )
    middle_grad = upstream_float + middle_part
    branch_low = middle_grad.astype(low)
    mixing_grad = outer_sum(mixed_low, branch_low).astype(low)
    mixed_grad = nt(branch_low, mixing).astype(low)
    if near:
        joint_back, *last_quads, expand_part_a, shrink_part_a = attend_back(
            sizes,
            blocks,
            projected,
            mixed_grad,
            logsum,
            (
                mixing_grad.reshape(*lead, -1, width),
                *by_device(expand_grad_b, shrink_grad_b),
            ),
            quads,
        )
    else:
        query_grad, key_value_grad = spread_backward(
            queries, key_value, allowed, logsum, mixed_grad.reshape(seq_count, row_count, width)
        )
        summed = lax.psum_scatter(
            key_value_grad.astype(low), "ctx", scatter_dimension=1, tiled=True
        )
        parts = [query_grad.astype(low), summed[..., :width], summed[..., width:]]
        joint_back = jnp.stack(
            [part.reshape(tokens, pairs, PAIR) for part in parts], axis=2
        ).reshape(tokens, 3 * width)
        mixing_part = reduce_far(grid, here, mixing_grad, False)
        expand_part_a, shrink_part_a, expand_part_b, shrink_part_b = [
            reduce_far(grid, here, grad, number % 2 == 1)
            for number, grad in enumerate(
                (expand_grad_a, shrink_grad_a, expand_grad_b, shrink_grad_b)
            )
        ]

    def column_sum(rows):
        return jnp.sum(rows.astype(jnp.float32), axis=0)

    hidden_bias_grad = jnp.concatenate(hidden_bias_grads, axis=2).reshape(-1, width)
    vector_rows = [column_sum(branch_low), gain_two, shift_two, column_sum(upstream)]
    weights = (joint_weight, mixing_weight, expand_weight, shrink_weight)
    firsts = (joint_first, mixing_first, expand_first, shrink_first)
    seconds = (joint_second, mixing_second, expand_second, shrink_second)
    if near:
        rows = vectors.shape[0]
        vector_grad = jnp.concatenate(
            [jnp.zeros((4, width)), jnp.stack(vector_rows), hidden_bias_grad, jnp.zeros((-rows % 8, width))],
            axis=0,
        )
        joint_part, vector_sum, mixing_part, expand_part_b, shrink_part_b, kept_grad, far_grad = end(
            sizes,
            back,
            joint_back,
            first_low,
            joint,
            input_low,
            middle_grad,
            vector_values[0:1],
            vector_grad,
            last_quads,
        )
        input_gradient, block_output, *news = last(
            ctx.astype(jnp.int32).reshape(1),
            (joint_part, mixing_part, expand_part_a, expand_part_b, shrink_part_a, shrink_part_b),
            kept_grad,
            far_grad,
            kept_out,
            far_out,
            list(zip(weights, firsts, seconds)),
        )
        updated, moments, squares, copies = [news[number::4] for number in range(4)]
    else:
        joint_grad = outer_sum(first_low, joint_back).astype(low)
        first_grad = nt(joint_back, joint)
        input_part, gain_one, shift_one = norm_back(
            first_grad, normal_first, inverse_first, vector_values[0]
        )
        input_gradient = (middle_grad + input_part).reshape(block_input.shape)
        joint_sums = column_sum(joint_back).reshape(pairs, 3, PAIR)
        vector_rows = [
            gain_one,
            shift_one,
            joint_sums[:, 0].reshape(-1),
            joint_sums[:, 2].reshape(-1),
        ] + vector_rows
        joint_part = reduce_far(grid, here, joint_grad, False)
        vector_sum = grid.everywhere(
            jnp.concatenate([jnp.stack(vector_rows), hidden_bias_grad], axis=0)
        )
        joint_sum = (
            joint_part.reshape(2, own_rows, pairs // 2, 3, PAIR)
            .transpose(1, 3, 0, 2, 4)
            .reshape(joint_weight.shape)
        )
        mixing_sum = mixing_part.transpose(1, 0, 2).reshape(mixing_weight.shape)
        expand_sum = jnp.stack(
            [part.reshape(2, own_rows, chips, sub) for part in (expand_part_a, expand_part_b)]
        )
        expand_sum = expand_sum.transpose(2, 3, 1, 0, 4).reshape(expand_weight.shape)
        shrink_sum = jnp.concatenate([shrink_part_a, shrink_part_b], axis=0)
        updated, moments, squares = zip(
            *[
                adam_update(*terms, 0.05, 0.1)
                for terms in zip(
                    weights, firsts, seconds, (joint_sum, mixing_sum, expand_sum, shrink_sum)
                )
            ]
        )
        copies = [array.astype(low) for array in updated]
    vector_sum = lax.dynamic_slice(
        vector_sum, (0, lax.axis_index(axes) * vectors.shape[1]), vectors.shape
    )
    vectors_new, vectors_moment, vectors_square = adam_update(
        vectors, vectors_first, vectors_second, vector_sum, 0.5, 0.0
    )
    return (
        block_output,
        input_gradient,
        *updated,
        vectors_new,
        *moments,
        vectors_moment,
        *squares,
        vectors_square,
        *copies,
        vectors_new.astype(low),
    )


def solution(mesh):
    grid = Slice(mesh.shape["ctx"], mesh.shape["wshard"])
    rows = P("wshard", "ctx", None)
    matrix = P(axes, None)
    table = P(None, axes)
    parameters = (matrix, matrix, matrix, matrix, table)
    return jax.shard_map(
        functools.partial(body, grid),
        mesh=mesh,
        in_specs=(rows, P("wshard", None), rows) + parameters * 3,
        out_specs=(rows, rows) + parameters * 4,
        check_vma=False,
    )
```

```python
import functools

import jax
import jax.numpy as jnp
from jax import lax
from jax.experimental import pallas as pl
from jax.experimental.pallas import tpu as pltpu
from jax.sharding import PartitionSpec as P

H = 16
HD = 64
BLK = 256
STEP = 10
PAIR = 2 * HD

norm_eps = 1e-05
adam_eps = 1e-08
group_heads = 4
score_scale = 0.125 * 1.4426950408889634
gelu_root = 0.7978845608028654
gelu_cubic = 0.044715
low = jnp.bfloat16
axes = ("ctx", "wshard")
small_cost = pl.CostEstimate(flops=1024, bytes_accessed=1024, transcendentals=0)


def nt(left_side, right_side):
    return lax.dot_general(
        left_side, right_side, (((1,), (1,)), ((), ())), preferred_element_type=jnp.float32
    )


def nn(left_side, right_side):
    return jnp.dot(left_side, right_side, preferred_element_type=jnp.float32)


def outer_sum(left_side, right_side):
    return lax.dot_general(
        left_side, right_side, (((0,), (0,)), ((), ())), preferred_element_type=jnp.float32
    )


def block_rows(block):
    return pl.ds(block * BLK, BLK)


def thirds(ref):
    return [ref.at[:, pl.ds(part * PAIR, PAIR)] for part in range(3)]


def attend_pair(blocks, projected, o_ref, lse_ref, between):
    q_ref, k_ref, v_ref = thirds(projected)
    lane = lax.broadcasted_iota(jnp.int32, (1, PAIR), 1)
    masks = [lane < HD, lane >= HD]
    for i in range(blocks):
        between(i)
        rows = block_rows(i)
        queries = q_ref[rows, :]
        outs = []
        for h in range(2):
            masked = jnp.where(masks[h], queries, jnp.zeros_like(queries))
            scores = [nt(masked, k_ref[block_rows(j), :]) * score_scale for j in range(i + 1)]
            top = scores[0]
            for score in scores[1:]:
                top = jnp.maximum(top, score)
            top = jnp.max(top, axis=1, keepdims=True)
            weights = [jnp.exp2(score - top) for score in scores]
            total = weights[0]
            for weight in weights[1:]:
                total = total + weight
            total = jnp.sum(total, axis=1, keepdims=True)
            mixed = nn(weights[0].astype(low), v_ref[block_rows(0), :])
            for j in range(1, i + 1):
                mixed = mixed + nn(weights[j].astype(low), v_ref[block_rows(j), :])
            outs.append(mixed * (1.0 / total))
            logsum = jnp.broadcast_to(top + jnp.log2(total), (BLK, PAIR))
            lse_ref[h : h + 1, rows] = jnp.transpose(logsum)[0:1, :]
        o_ref[rows, :] = jnp.where(masks[0], outs[0], outs[1]).astype(o_ref.dtype)


def attend_back_pair(
    blocks, projected, do_ref, lse_ref, back_ref, turned, key_sum, value_sum, between
):
    q_ref, k_ref, v_ref = thirds(projected)
    dq_ref, dk_ref, dv_ref = thirds(back_ref)
    lane = lax.broadcasted_iota(jnp.int32, (1, PAIR), 1)
    masks = [lane < HD, lane >= HD]
    for j in range(blocks):
        turned[j] = jnp.transpose(k_ref[block_rows(j), :])
    for i in range(blocks):
        between(i)
        rows = block_rows(i)
        queries, upstream = q_ref[rows, :], do_ref[rows, :]
        query_grads = []
        for h in range(2):
            masked = jnp.where(masks[h], queries, jnp.zeros_like(queries))
            pulled = jnp.where(masks[h], upstream, jnp.zeros_like(upstream))
            logsum = lse_ref[h : h + 1, rows]
            weights, pulls, inner = [], [], None
            for j in range(i + 1):
                weight = jnp.exp2(nt(k_ref[block_rows(j), :], masked) * score_scale - logsum)
                pull = nt(v_ref[block_rows(j), :], pulled)
                along = jnp.sum(weight * pull, axis=0, keepdims=True)
                inner = along if inner is None else inner + along
                weights.append(weight)
                pulls.append(pull)
            query_grad = None
            for j in range(i + 1):
                score_grad = (weights[j] * (pulls[j] - inner)).astype(low)
                value_grad = nn(weights[j].astype(low), pulled)
                key_grad = nn(score_grad, masked)
                if i == j and h == 0:
                    value_sum[j] = value_grad
                    key_sum[j] = key_grad
                else:
                    value_sum[j] += value_grad
                    key_sum[j] += key_grad
                piece = nn(turned[j, h * HD : (h + 1) * HD, :], score_grad)
                query_grad = piece if query_grad is None else query_grad + piece
            query_grads.append(query_grad)
        joined = jnp.transpose(jnp.concatenate(query_grads, axis=0))
        dq_ref[rows, :] = (joined * 0.125).astype(dq_ref.dtype)
    for j in range(blocks):
        dk_ref[block_rows(j), :] = (key_sum[j] * 0.125).astype(dk_ref.dtype)
        dv_ref[block_rows(j), :] = value_sum[j].astype(dv_ref.dtype)


def hooks(step, schedule):
    def between(block):
        for when, where, action in schedule:
            if where == block:
                pl.when(step == when)(action)

    return between


any_place = pl.BlockSpec(memory_space=pl.ANY)
whole_vmem = pl.BlockSpec(memory_space=pltpu.VMEM)


MESH = pl.DeviceIdType.MESH


class Spot:
    def __init__(self, sizes):
        self.sizes = sizes
        ctx, shard = lax.axis_index("ctx"), lax.axis_index("wshard")
        self.c = ctx
        self.k = shard % 2
        self.y = (shard // 2) % 2
        self.z = shard // 4

    def device(self, name, by=1):
        c, z, y, k = self.c, self.z, self.y, self.k
        if name == "c":
            c = 1 - c
        if name == "y":
            y = 1 - y
        if name == "k":
            k = 1 - k
        if name == "z":
            z = (z + by) % self.sizes["z"]
        return (c, (z * 2 + y) * 2 + k)

    def meet(self, names):
        barrier = pltpu.get_barrier_semaphore()
        partners = []
        for name in names:
            for by in range(1, self.sizes[name]):
                partners.append(self.device(name, by))
        for partner in partners:
            pl.semaphore_signal(barrier, inc=1, device_id=partner, device_id_type=MESH)
        pl.semaphore_wait(barrier, len(partners))


class Mover:
    def __init__(self, spot, sems):
        self.spot, self.sems, self.count = spot, sems, 0

    def copy(self, source, target, name, by=1):
        number = self.count
        self.count += 1
        return pltpu.make_async_remote_copy(
            src_ref=source,
            dst_ref=target,
            send_sem=self.sems.at[0, number],
            recv_sem=self.sems.at[1, number],
            device_id=self.spot.device(name, by),
            device_id_type=MESH,
        )

    def local(self, source, target):
        number = self.count
        self.count += 1
        return pltpu.make_async_copy(source, target, self.sems.at[0, number])


class Refs:
    def __init__(self, refs):
        self.refs = list(refs)

    def take(self, count):
        taken, self.refs = self.refs[:count], self.refs[count:]
        return taken


def start(copies):
    for copy in copies:
        copy.start()


def wait(copies):
    for copy in copies:
        copy.wait()


def span(first, size):
    return pl.ds(pl.multiple_of(first, 128), size)


class Deep:
    def __init__(self, mover, quad):
        z = mover.spot.z
        self.copies = [
            mover.copy(quad.at[z], quad.at[z], "z", by) for by in range(1, mover.spot.sizes["z"])
        ]


def first_rows(mover, halves, quad):
    spot = mover.spot
    rows = halves.shape[1]
    block = quad.at[spot.z, pl.ds(pl.multiple_of(spot.k * rows, rows), rows)]
    return [
        mover.local(halves.at[spot.k], block),
        mover.copy(halves.at[1 - spot.k], block, "k"),
    ]


class Near:
    def __init__(self, mover, quad, half, offset, cut, core=True):
        spot = mover.spot
        c, z, y = spot.c, spot.z, spot.y
        width = quad.shape[-1]
        every = slice(None)

        def part(ci, yi, first, size):
            return half.at[ci, every, yi, :, span(offset + first, size)]

        self.near, self.far = [mover.local(quad, part(c, y, 0, width))], []
        for first, size, one, two in ((0, cut, "c", "y"), (cut, width - cut, "y", "c")):
            if size == 0:
                continue
            source = quad.at[every, every, pl.ds(first, size)]
            self.near.append(mover.copy(source, part(c, y, first, size), one))
            self.near.append(mover.copy(source, part(c, y, first, size), two))
            block = part(1 - c if one == "c" else c, 1 - y if one == "y" else y, first, size)
            self.far.append(mover.copy(block, block, two))
        self.core = [[], [], []]
        if core:
            self.core[0].append(mover.copy(quad, part(c, y, 0, width), "k"))
            for stage, ci, yi in ((1, 1 - c, y), (1, c, 1 - y), (2, 1 - c, 1 - y)):
                block = part(ci, yi, 0, width)
                self.core[stage].append(mover.copy(block, block, "k"))

    def close(self):
        wait(self.far)
        start(self.core[2])

    def close_core(self):
        for stage in self.core:
            wait(stage)


class ReduceNear:
    def __init__(self, mover, mine, theirs, cut, quad, scratch):
        self.spot = spot = mover.spot
        self.cut, self.quad = cut, quad
        self.total, self.other, self.by_y, self.by_c, self.then_c, self.then_y = scratch
        self.width = width = self.total.shape[-1]
        c, y = spot.c, spot.y
        every, left, right = slice(None), pl.ds(0, cut), pl.ds(cut, width - cut)
        total = self.total
        self.first = [mover.copy(theirs, self.other, "k")]
        if mine is not None:
            self.first.append(mover.local(mine, total))
        self.near = [
            mover.copy(total.at[every, every, 1 - y, every, left], self.by_y, "y"),
            mover.copy(total.at[1 - c, every, every, every, right], self.by_c, "c"),
        ]
        self.far = [
            mover.copy(total.at[1 - c, every, y, every, left], self.then_c, "c"),
            mover.copy(total.at[c, every, 1 - y, every, right], self.then_y, "y"),
        ]

    @staticmethod
    def scratch(sizes, rows, width, cut):
        c, z, y = sizes["c"], sizes["z"], sizes["y"]
        shapes = [
            (c, z, y, rows, width),
            (c, z, y, rows, width),
            (c, z, rows, cut),
            (z, y, rows, width - cut),
            (z, rows, cut),
            (z, rows, width - cut),
        ]
        return [pltpu.VMEM(shape, low) for shape in shapes]

    def add(self, where, extra):
        total = self.total[where].astype(jnp.float32) + extra.astype(jnp.float32)
        return total.astype(low)

    def go_near(self):
        wait(self.first)
        sizes = self.spot.sizes
        for c in range(sizes["c"]):
            for y in range(sizes["y"]):

                @pl.loop(0, sizes["z"])
                def _(z):
                    self.total[c, z, y] = self.add((c, z, y), self.other[c, z, y])

        start(self.near)

    def go_far(self):
        wait(self.near)
        spot, cut = self.spot, self.cut
        left, right = pl.ds(0, cut), pl.ds(cut, self.width - cut)

        @pl.loop(0, spot.sizes["z"])
        def _(z):
            for c in range(spot.sizes["c"]):
                where = (c, z, spot.y, slice(None), left)
                self.total[where] = self.add(where, self.by_y[c, z])
            for y in range(spot.sizes["y"]):
                where = (spot.c, z, y, slice(None), right)
                self.total[where] = self.add(where, self.by_c[z, y])

        start(self.far)

    def close(self):
        wait(self.far)
        spot, cut = self.spot, self.cut
        left, right = pl.ds(0, cut), pl.ds(cut, self.width - cut)

        @pl.loop(0, spot.sizes["z"])
        def _(z):
            for columns, extra in ((left, self.then_c), (right, self.then_y)):
                where = (spot.c, z, spot.y, slice(None), columns)
                self.quad[z, :, columns] = self.add(where, extra[z])


class ReduceDeep:
    def __init__(self, mover, quad, by_z):
        self.spot = spot = mover.spot
        self.quad, self.by_z = quad, by_z
        depth = spot.sizes["z"]
        self.copies = [
            mover.copy(quad.at[(spot.z + by) % depth], by_z.at[by - 1], "z", by)
            for by in range(1, depth)
        ]

    def result(self):
        spot = self.spot
        value = self.quad[spot.z].astype(jnp.float32)
        for by in range(spot.sizes["z"] - 1):
            value = value + self.by_z[by].astype(jnp.float32)
        return value


class Finish:
    def __init__(self, mover, summed, arrived):
        self.k = mover.spot.k
        self.summed, self.arrived = summed, arrived
        rows = arrived.shape[0]
        self.rows = rows
        away = summed.at[pl.ds(pl.multiple_of((1 - self.k) * rows, rows), rows)]
        self.copies = [mover.copy(away, arrived, "k")]

    @staticmethod
    def scratch(rows, width):
        return [pltpu.VMEM((rows, width), jnp.float32), pltpu.VMEM((rows // 2, width), jnp.float32)]

    def write(self, out, columns=slice(None)):
        rows = self.rows
        kept = pl.ds(pl.multiple_of(self.k * rows, rows), rows)
        out[self.k, :, columns] = self.summed[kept, :]
        out[1 - self.k, :, columns] = self.arrived[...]


def core_halves(grad, k, width, first=0, size=None):
    size = width if size is None else size
    every = slice(None)
    return [
        grad.at[every, every, every, every, span(half * width + first, size)]
        for half in (k, 1 - k)
    ]


all_axes = ("k", "c", "y", "z")


def params(number, megabytes):
    return pltpu.CompilerParams(
        collective_id=number, has_side_effects=True, vmem_limit_bytes=megabytes << 20
    )


def cut_of(width):
    return max(5 * width // 8 // 128, 1) * 128


def low_shape(*dims):
    return jax.ShapeDtypeStruct(dims, low)


def begin_kernel(sizes, *refs):
    refs = Refs(refs)
    joint_weight, table, mixing_weight, expand_weight, shrink_weight = refs.take(5)
    rows_in, upstream = refs.take(2)
    joint, tables, mixing_quad, expand_quad, shrink_quad, far_rows, far_upstream = refs.take(7)
    next_expand, next_shrink = refs.take(2)
    joint_quad, table_quad, sems, joint_halves, mixing_halves, expand_halves, shrink = refs.take(7)
    spot = Spot(sizes)
    mover = Mover(spot, sems)
    width = joint_halves.shape[2]
    joint_first = first_rows(mover, joint_halves, joint_quad)
    rows = table.shape[0]
    spread = table_quad.at[spot.z, pl.ds(pl.multiple_of(spot.k * rows, rows), rows)]
    joint_first += [mover.local(table, spread), mover.copy(table, spread, "k")]
    later_first = first_rows(mover, mixing_halves, mixing_quad)
    later_first += first_rows(mover, expand_halves, expand_quad)
    later_first += [mover.local(shrink, shrink_quad.at[spot.z])]
    now = Deep(mover, joint_quad).copies + Deep(mover, table_quad).copies
    later = [Deep(mover, quad).copies for quad in (mixing_quad, shrink_quad, expand_quad)]
    job = Near(mover, joint_quad, joint, spot.k * width, cut_of(width))
    thin = Near(mover, table_quad, tables, 0, table.shape[1], core=False)
    rows_copies = [
        mover.copy(rows_in.at[1 - spot.c], far_rows, "c"),
        mover.copy(upstream.at[1 - spot.c, block_rows(0)], far_upstream, "c"),
    ]
    pairs = width // (3 * PAIR)
    for core in range(2):
        for pair in range(pairs):
            for third in range(3):
                source = ((third * 2 + core) * pairs + pair) * PAIR
                target = (pair * 3 + third) * PAIR
                joint_halves[core, :, target : target + PAIR] = joint_weight[
                    :, source : source + PAIR
                ].astype(low)
    spot.meet(all_axes)
    start(joint_first)
    start(rows_copies[:1])
    half = mixing_halves.shape[2]
    for core in range(2):
        mixing_halves[core] = mixing_weight[:, core * half : (core + 1) * half].astype(low)
    sub = shrink.shape[0]
    shrink[...] = shrink_weight[:sub, :].astype(low)
    next_shrink[...] = shrink_weight[sub:, :].astype(low)
    lane = lax.broadcasted_iota(jnp.int32, (1, PAIR), 1)
    for core in range(2):
        for chip in range(0, expand_halves.shape[2] // HD, 2):
            one, two = [
                expand_weight[:, (number * 2 + core) * PAIR : (number * 2 + core + 1) * PAIR]
                for number in (chip, chip + 1)
            ]
            columns = pl.ds(chip * HD, PAIR)
            expand_halves[core, :, columns] = jnp.where(
                lane < HD, one, pltpu.roll(two, HD, 1)
            ).astype(low)
            next_expand[core, :, columns] = jnp.where(
                lane < HD, pltpu.roll(one, HD, 1), two
            ).astype(low)
    start(later_first)
    wait(joint_first)
    start(now)
    wait(later_first)
    wait(now)
    start(thin.near + job.near + job.core[0])
    for copies in later:
        start(copies)
    wait(thin.near + job.near)
    start(thin.far + job.far + job.core[1])
    start(rows_copies[1:])
    wait(thin.far)
    job.close()
    for copies in later:
        wait(copies)
    job.close_core()
    wait(rows_copies)


def begin(sizes, joint_weight, table, mixing_weight, expand_weight, shrink_weight, rows_in, upstream):
    lead = (sizes["c"], sizes["z"], sizes["y"])
    own, model = mixing_weight.shape
    depth, rows = sizes["z"], 2 * own
    width, half, grown = 3 * model // 2, model // 2, expand_weight.shape[1] // 4
    sub = shrink_weight.shape[0] // 2
    return pl.pallas_call(
        functools.partial(begin_kernel, sizes),
        in_specs=[whole_vmem] * 5 + [any_place] * 2,
        out_specs=[any_place] * 7 + [whole_vmem] * 2,
        out_shape=[
            low_shape(*lead, rows, 2 * width),
            low_shape(*lead, rows, table.shape[1]),
            low_shape(depth, rows, half),
            low_shape(depth, rows, grown),
            low_shape(depth, sub, model),
            low_shape(*rows_in.shape[1:]),
            low_shape(BLK, model),
            low_shape(2, own, grown),
            low_shape(sub, model),
        ],
        scratch_shapes=[
            pltpu.VMEM((depth, rows, width), low),
            pltpu.VMEM((depth, rows, table.shape[1]), low),
            pltpu.SemaphoreType.DMA((2, 48)),
            pltpu.VMEM((2, own, width), low),
            pltpu.VMEM((2, own, half), low),
            pltpu.VMEM((2, own, grown), low),
            pltpu.VMEM((sub, model), low),
        ],
        compiler_params=params(1, 60),
        cost_estimate=small_cost,
        name="begin",
    )(joint_weight, table, mixing_weight, expand_weight, shrink_weight, rows_in, upstream)


def normal_rows(rows):
    centered = rows - jnp.mean(rows, axis=-1, keepdims=True)
    inverse = lax.rsqrt(jnp.mean(centered * centered, axis=-1, keepdims=True) + norm_eps)
    return centered * inverse, inverse


def norm_pull(upstream, normal, inverse, gain):
    scaled = upstream * gain
    inner = jnp.mean(scaled, axis=-1, keepdims=True)
    along = jnp.mean(scaled * normal, axis=-1, keepdims=True)
    return inverse * (scaled - inner - normal * along)


def chosen_block(number, source):
    chosen = jnp.full((1, source.shape[1]), number, jnp.int32)
    value = source[block_rows(0), :].astype(jnp.float32)
    for other in range(1, source.shape[0] // BLK):
        value = jnp.where(chosen == other, source[block_rows(other), :].astype(jnp.float32), value)
    return value


def attend_kernel(sizes, blocks, *refs):
    refs = Refs(refs)
    place_ref, rows_in, far_rows, joint, norm_ref, shift_ref, upstream = refs.take(7)
    mixing_quad, expand_quad, shrink_quad, expand_halves, shrink = refs.take(5)
    o_ref, lse_ref, rows_ref, low_ref, projected_ref = refs.take(5)
    mixing, expand, shrunk, next_expand, next_shrink, far_upstream = refs.take(6)
    sems, rows_all, joint_all, projected = refs.take(4)
    spot = Spot(sizes)
    mover = Mover(spot, sems)
    k = spot.k
    half, grown, width = mixing_quad.shape[-1], expand_quad.shape[-1], shrink_quad.shape[-1]
    loads = [
        mover.local(rows_in.at[spot.c], rows_all.at[pl.ds(0, 2 * BLK)]),
        mover.local(far_rows, rows_all.at[pl.ds(2 * BLK, 2 * BLK)]),
        mover.local(joint, joint_all),
    ]
    jobs = [
        Near(mover, mixing_quad, mixing, k * half, cut_of(half)),
        Near(mover, shrink_quad, shrunk.at[k], 0, cut_of(width)),
        Near(mover, expand_quad, expand, k * grown, cut_of(grown)),
    ]
    next_first = first_rows(mover, expand_halves, next_expand)
    next_first += [mover.local(shrink, next_shrink.at[spot.z])]
    deep = Deep(mover, next_expand).copies + Deep(mover, next_shrink).copies
    upstream_copy = [mover.copy(upstream.at[1 - spot.c, block_rows(1)], far_upstream, "c")]

    def open_all():
        start(loads)
        spot.meet(all_axes)
        start(next_first)
        for job in jobs:
            start(job.near + job.core[0])
        wait(loads)

    def next_deep():
        wait(next_first)
        start(deep)
        start(upstream_copy)

    def far(job):
        wait(job.near)
        start(job.far + job.core[1])

    def close_all():
        for job in jobs:
            job.close()
        wait(deep)
        for job in jobs:
            job.close_core()
        wait(upstream_copy)

    step = pl.program_id(0)
    between = hooks(
        step,
        [
            (0, 0, open_all),
            (2, 0, next_deep),
            (4, 2, lambda: far(jobs[0])),
            (6, 2, lambda: far(jobs[1])),
            (9, 2, lambda: far(jobs[2])),
        ],
    )
    between(0)

    @pl.when(step < blocks)
    def _():
        value = chosen_block(place_ref[step], rows_all)
        rows_ref[...] = value.astype(low)
        normal, _ = normal_rows(value)
        normed = (normal * norm_ref[0:1, :] + norm_ref[1:2, :]).astype(low)
        low_ref[...] = normed
        rows = pl.ds(pl.multiple_of(step * BLK, BLK), BLK)
        for first in range(0, joint_all.shape[1], 512):
            columns = pl.ds(first, 512)
            projected[rows, columns] = (nn(normed, joint_all[:, columns]) + shift_ref[:, columns]).astype(low)

    @pl.when(step >= blocks)
    def _():
        columns = span((step - blocks) * 3 * PAIR, 3 * PAIR)
        projected_ref[...] = projected[:, columns]
        attend_pair(blocks, projected_ref, o_ref, lse_ref, lambda block: block > 0 and between(block))

    pl.when(step == pl.num_programs(0) - 1)(close_all)


def attend(sizes, place, rows_in, far_rows, joint, norm, shift, upstream, quads, halves, shrink):
    model = rows_in.shape[2]
    blocks = place.shape[0]
    tokens = blocks * BLK
    pairs = model // PAIR
    lead = (sizes["c"], sizes["z"], sizes["y"])
    depth, rows, half = quads[0].shape
    grown, full = quads[1].shape[2], quads[2].shape[2]
    by_rows = pl.BlockSpec((BLK, model), lambda g: (jnp.minimum(g, blocks - 1), 0))

    def pair(g):
        return jnp.maximum(g - blocks, 0)

    return pl.pallas_call(
        functools.partial(attend_kernel, sizes, blocks),
        grid=(blocks + pairs,),
        in_specs=[pl.BlockSpec(memory_space=pltpu.SMEM)]
        + [any_place] * 3
        + [whole_vmem] * 2
        + [any_place]
        + [whole_vmem] * 5,
        out_specs=[
            pl.BlockSpec((tokens, PAIR), lambda g: (0, pair(g))),
            pl.BlockSpec((None, 8, tokens), lambda g: (pair(g), 0, 0)),
            by_rows,
            by_rows,
            pl.BlockSpec((tokens, 3 * PAIR), lambda g: (0, pair(g))),
        ]
        + [any_place] * 6,
        out_shape=[
            low_shape(tokens, model),
            jax.ShapeDtypeStruct((pairs, 8, tokens), jnp.float32),
            low_shape(tokens, model),
            low_shape(tokens, model),
            low_shape(tokens, 3 * model),
            low_shape(*lead, rows, 2 * half),
            low_shape(*lead, rows, 2 * grown),
            low_shape(2, *lead, rows, full),
            low_shape(depth, rows, grown),
            low_shape(depth, rows, full),
            low_shape(BLK, model),
        ],
        scratch_shapes=[
            pltpu.SemaphoreType.DMA((2, 64)),
            pltpu.VMEM((tokens, model), low),
            pltpu.VMEM((model, 3 * model), low),
            pltpu.VMEM((tokens, 3 * model), low),
        ],
        compiler_params=params(2, 56),
        cost_estimate=small_cost,
        name="attend",
    )(place, rows_in, far_rows, joint, norm, shift, upstream, *quads, halves, shrink)


def mlp_tile(rows_step, c_ref, dy_ref, we_ref, ws_ref, be_ref, outs, scratch, between):
    y_ref, dc_ref, gwe_ref, gws_ref, gbe_ref = outs
    turned, act_all, du_all = scratch
    tokens = c_ref.shape[0]
    we, ws = we_ref[...], ws_ref[...]
    total = None
    for part in range(tokens // rows_step):
        between(part)
        rows = pl.ds(part * rows_step, rows_step)
        hidden = nn(c_ref[rows, :], we) + be_ref[...]
        squared = hidden * hidden
        bent = jnp.tanh(gelu_root * hidden * (1.0 + gelu_cubic * squared))
        gate = 0.5 + 0.5 * bent
        act = (hidden * gate).astype(low)
        slope = gate + (0.5 * gelu_root) * hidden * (1.0 - bent * bent) * (
            1.0 + (3 * gelu_cubic) * squared
        )
        du = (nt(dy_ref[rows, :], ws) * slope).astype(low)
        act_all[rows, :] = act
        du_all[rows, :] = du
        y_ref[rows, :] += nn(act, ws)
        dc_ref[rows, :] += nt(du, we)
        added = jnp.sum(du.astype(jnp.float32), axis=0, keepdims=True)
        total = added if total is None else total + added
    gbe_ref[...] = total
    gwe_ref[...] = nn(turned[...], du_all[...]).astype(gwe_ref.dtype)
    gws_ref[...] = outer_sum(act_all[...], dy_ref[...]).astype(gws_ref.dtype)


def mlp_parts(tokens, width, hidden, tile):
    whole = pl.BlockSpec((tokens, width), lambda t: (0, 0))
    down = pl.BlockSpec((width, tile), lambda t: (0, t))
    across = pl.BlockSpec((tile, width), lambda t: (t, 0))
    thin = pl.BlockSpec((1, tile), lambda t: (0, t))
    return (
        [whole, whole, down, across, thin],
        [whole, whole, down, across, thin],
        [
            jax.ShapeDtypeStruct((tokens, width), jnp.float32),
            jax.ShapeDtypeStruct((tokens, width), jnp.float32),
            low_shape(width, hidden),
            low_shape(hidden, width),
            jax.ShapeDtypeStruct((1, hidden), jnp.float32),
        ],
        [
            pltpu.VMEM((width, tokens), low),
            pltpu.VMEM((tokens, tile), low),
            pltpu.VMEM((tokens, tile), low),
        ],
    )


def mlp_plain_kernel(rows_step, *refs):
    refs = Refs(refs)
    c_ref, dy_ref, we_ref, ws_ref, be_ref, y_in, dc_in = refs.take(7)
    outs, scratch, (sem,) = refs.take(5), refs.take(3), refs.take(1)

    @pl.when(pl.program_id(0) == 0)
    def _():
        scratch[0][...] = jnp.transpose(c_ref[...])
        copies = [
            pltpu.make_async_copy(y_in, outs[0], sem.at[0]),
            pltpu.make_async_copy(dc_in, outs[1], sem.at[1]),
        ]
        start(copies)
        wait(copies)

    mlp_tile(rows_step, c_ref, dy_ref, we_ref, ws_ref, be_ref, outs, scratch, lambda part: None)


def mlp(c, dy, we, ws, be, before, tile=256, rows_step=256):
    in_specs, out_specs, out_shape, scratch = mlp_parts(*c.shape, we.shape[1], tile)
    return pl.pallas_call(
        functools.partial(mlp_plain_kernel, rows_step),
        grid=(we.shape[1] // tile,),
        in_specs=in_specs + [any_place] * 2,
        out_specs=out_specs,
        out_shape=out_shape,
        scratch_shapes=scratch + [pltpu.SemaphoreType.DMA((2,))],
        compiler_params=pltpu.CompilerParams(vmem_limit_bytes=56 << 20),
        cost_estimate=small_cost,
        name="mlp",
    )(c, dy, we, ws, be, *before)


def mlp_gather_kernel(sizes, blocks, rows_step, *refs):
    refs = Refs(refs)
    place_ref, mixed_ref, rows_ref, mixing, vector_ref, we_ref, ws_ref, be_ref = refs.take(8)
    upstream, far_a, far_b, expand_quad, shrink_quad = refs.take(5)
    outs, (middle_ref, low_ref, upstream_ref) = refs.take(5), refs.take(3)
    expand, shrunk = refs.take(2)
    scratch, (sems, raw, c_all, dy_all) = refs.take(3), refs.take(4)
    spot = Spot(sizes)
    mover = Mover(spot, sems)
    grown, width = expand_quad.shape[-1], shrink_quad.shape[-1]
    loads = [
        mover.local(upstream.at[spot.c], raw.at[pl.ds(0, 2 * BLK)]),
        mover.local(far_a, raw.at[pl.ds(2 * BLK, BLK)]),
        mover.local(far_b, raw.at[pl.ds(3 * BLK, BLK)]),
    ]
    jobs = [
        Near(mover, shrink_quad, shrunk.at[spot.k], 0, width // 2),
        Near(mover, expand_quad, expand, spot.k * grown, grown // 2),
    ]

    def open_all():
        start(loads)
        spot.meet(all_axes)
        for job in jobs:
            start(job.near + job.core[0])
        wait(loads)

    def far(job):
        wait(job.near)
        start(job.far + job.core[1])

    def close_all():
        jobs[1].close()
        for job in jobs:
            job.close_core()

    step = pl.program_id(0)
    between = hooks(
        step,
        [
            (0, 0, open_all),
            (6, 0, lambda: far(jobs[0])),
            (8, 2, lambda: far(jobs[1])),
            (10, 0, jobs[0].close),
        ],
    )
    between(0)

    @pl.when(step < blocks)
    def _():
        rows = pl.ds(pl.multiple_of(step * BLK, BLK), BLK)
        dy = chosen_block(place_ref[step], raw).astype(low)
        upstream_ref[...] = dy
        dy_all[rows, :] = dy
        branch = nn(mixed_ref[...], mixing[...]) + vector_ref[4:5, :]
        middle = rows_ref[...].astype(jnp.float32) + branch
        middle_ref[...] = middle
        normal, _ = normal_rows(middle)
        second = (normal * vector_ref[5:6, :] + vector_ref[6:7, :]).astype(low)
        low_ref[...] = second
        c_all[rows, :] = second
        outs[0][rows, :] = middle + vector_ref[7:8, :]
        outs[1][rows, :] = jnp.zeros(middle.shape, jnp.float32)

    @pl.when(step == blocks)
    def _():
        scratch[0][...] = jnp.transpose(c_all[...])

    @pl.when(step >= blocks)
    def _():
        mlp_tile(
            rows_step, c_all, dy_all, we_ref, ws_ref, be_ref, outs, scratch,
            lambda part: part > 0 and between(part),
        )

    pl.when(step == pl.num_programs(0) - 1)(close_all)


def mlp_gather(sizes, place, mixed, rows_in, mixing, vectors, we, ws, be, upstream, far_a, far_b, quads, tile=256, rows_step=256):
    tokens, model = mixed.shape
    blocks = place.shape[0]
    hidden = we.shape[1]
    lead = (sizes["c"], sizes["z"], sizes["y"])
    rows, grown, full = quads[0].shape[1], quads[0].shape[2], quads[1].shape[2]
    by_rows = pl.BlockSpec((BLK, model), lambda g: (jnp.minimum(g, blocks - 1), 0))
    whole = pl.BlockSpec((tokens, model), lambda g: (0, 0))

    def at(g):
        return jnp.maximum(g - blocks, 0)

    down = pl.BlockSpec((model, tile), lambda g: (0, at(g)))
    across = pl.BlockSpec((tile, model), lambda g: (at(g), 0))
    thin = pl.BlockSpec((1, tile), lambda g: (0, at(g)))
    _, _, out_shape, scratch = mlp_parts(tokens, model, hidden, tile)
    return pl.pallas_call(
        functools.partial(mlp_gather_kernel, sizes, blocks, rows_step),
        grid=(blocks + hidden // tile,),
        in_specs=[pl.BlockSpec(memory_space=pltpu.SMEM), by_rows, by_rows, whole_vmem, whole_vmem]
        + [down, across, thin]
        + [any_place] * 3
        + [whole_vmem] * 2,
        out_specs=[whole, whole, down, across, thin] + [by_rows] * 3 + [any_place] * 2,
        out_shape=out_shape
        + [
            jax.ShapeDtypeStruct((tokens, model), jnp.float32),
            low_shape(tokens, model),
            low_shape(tokens, model),
            low_shape(*lead, rows, 2 * grown),
            low_shape(2, *lead, rows, full),
        ],
        scratch_shapes=scratch
        + [pltpu.SemaphoreType.DMA((2, 32))]
        + [pltpu.VMEM((tokens, model), low)] * 3,
        compiler_params=params(3, 60),
        cost_estimate=small_cost,
        name="mlp_gather",
    )(place, mixed, rows_in, mixing, vectors, we, ws, be, upstream, far_a, far_b, *quads)


def mlp_reduce_kernel(sizes, rows_step, *refs):
    refs = Refs(refs)
    back_ref, c_ref, dy_ref, we_ref, ws_ref, be_ref, y_in, dc_in, expand, shrink = refs.take(10)
    outs = refs.take(4)
    expand_quad, shrink_quad, kept, sent = refs.take(4)
    scratch, (sems, y_all) = refs.take(3), refs.take(2)
    outs = [y_all] + outs
    spot = Spot(sizes)
    mover = Mover(spot, sems)
    grown, width = expand_quad.shape[-1], shrink_quad.shape[-1]
    loads = [mover.local(y_in, y_all), mover.local(dc_in, outs[1])]
    jobs = [
        ReduceNear(
            mover, shrink.at[spot.k], shrink.at[1 - spot.k], width // 2, shrink_quad, refs.take(6)
        ),
        ReduceNear(
            mover, *core_halves(expand, spot.k, grown), grown // 2, expand_quad, refs.take(6)
        ),
    ]

    def open_all():
        start(loads)
        spot.meet(all_axes)
        for job in jobs:
            start(job.first)
        scratch[0][...] = jnp.transpose(c_ref[...])
        wait(loads)

    def close_all():
        for place in range(2):
            kept[block_rows(place), :] = chosen_block(back_ref[place], y_all).astype(low)
            sent[block_rows(place), :] = chosen_block(back_ref[2 + place], y_all).astype(low)
        jobs[1].close()

    step = pl.program_id(0)
    schedule = [
        (0, 0, open_all),
        (1, 1, jobs[0].go_near),
        (2, 1, jobs[1].go_near),
        (4, 0, jobs[0].go_far),
        (6, 1, jobs[1].go_far),
        (7, 1, jobs[0].close),
    ]
    mlp_tile(
        rows_step, c_ref, dy_ref, we_ref, ws_ref, be_ref, outs, scratch, hooks(step, schedule)
    )
    pl.when(step == pl.num_programs(0) - 1)(close_all)


def mlp_reduce(sizes, back, c, dy, we, ws, be, before, grads, tile=256, rows_step=256):
    tokens, model = c.shape
    in_specs, out_specs, out_shape, scratch = mlp_parts(tokens, model, we.shape[1], tile)
    expand, shrink = grads
    depth, rows = sizes["z"], expand.shape[3]
    grown, full = expand.shape[-1] // 2, shrink.shape[-1]
    scratch = scratch + [pltpu.SemaphoreType.DMA((2, 16)), pltpu.VMEM((tokens, model), jnp.float32)]
    for columns in (full, grown):
        scratch += ReduceNear.scratch(sizes, rows, columns, columns // 2)
    return pl.pallas_call(
        functools.partial(mlp_reduce_kernel, sizes, rows_step),
        grid=(we.shape[1] // tile,),
        in_specs=[pl.BlockSpec(memory_space=pltpu.SMEM)] + in_specs + [any_place] * 4,
        out_specs=out_specs[1:] + [whole_vmem] * 4,
        out_shape=out_shape[1:]
        + [low_shape(depth, rows, grown), low_shape(depth, rows, full)]
        + [low_shape(tokens // 2, model)] * 2,
        scratch_shapes=scratch,
        compiler_params=params(4, 60),
        cost_estimate=small_cost,
        name="mlp_reduce",
    )(back, c, dy, we, ws, be, *before, *grads)


def attend_back_kernel(sizes, blocks, *refs):
    refs = Refs(refs)
    pulled_ref, middle_ref, upstream_ref, mixed, mixing, gain_ref = refs.take(6)
    projected, lse_ref, expand, shrink, done_expand, done_shrink, sent = refs.take(7)
    back_ref, grad_ref, sums_ref, mixing_quad, expand_quad, shrink_quad = refs.take(6)
    expand_out, shrink_out, far_out = refs.take(3)
    turned, key_sum, value_sum, sems, branch_all, mixed_grad, theirs = refs.take(7)
    spot = Spot(sizes)
    mover = Mover(spot, sems)
    k = spot.k
    half, grown, width = mixing_quad.shape[-1], expand_quad.shape[-1], shrink_quad.shape[-1]
    jobs = [
        ReduceNear(mover, shrink.at[k], shrink.at[1 - k], width // 2, shrink_quad, refs.take(6)),
        ReduceNear(mover, *core_halves(expand, k, grown), grown // 2, expand_quad, refs.take(6)),
        ReduceNear(mover, None, theirs, half // 2, mixing_quad, refs.take(6)),
    ]
    deep = [
        ReduceDeep(mover, done_expand, *refs.take(1)),
        ReduceDeep(mover, done_shrink, *refs.take(1)),
    ]
    ending = Finish(mover, *refs.take(2))
    rows_copy = [mover.copy(sent.at[block_rows(0)], far_out, "c")]

    def open_all():
        spot.meet(all_axes)
        for job in jobs[:2]:
            start(job.first)
        start(rows_copy)
        for job in deep:
            start(job.copies)

    def finish():
        wait(deep[0].copies)
        ending.summed[...] = deep[0].result()
        start(ending.copies)
        wait(deep[1].copies)
        shrink_out[...] = deep[1].result()

    def close_all():
        wait(ending.copies)
        ending.write(expand_out)
        jobs[1].close()
        jobs[2].close()
        wait(rows_copy)

    step = pl.program_id(0)
    between = hooks(
        step,
        [
            (0, 0, open_all),
            (3, 0, jobs[0].go_near),
            (4, 0, jobs[1].go_near),
            (4, 2, jobs[2].go_near),
            (6, 2, jobs[0].go_far),
            (7, 2, finish),
            (9, 0, jobs[1].go_far),
            (10, 0, jobs[2].go_far),
            (11, 1, jobs[0].close),
        ],
    )
    between(0)

    @pl.when(step < blocks)
    def _():
        rows = pl.ds(pl.multiple_of(step * BLK, BLK), BLK)
        pulled = pulled_ref[...]
        upstream = upstream_ref[...].astype(jnp.float32)
        normal, inverse = normal_rows(middle_ref[...])
        total = upstream + norm_pull(pulled, normal, inverse, gain_ref[...])
        grad_ref[...] = total
        branch = total.astype(low)
        branch_all[rows, :] = branch
        mixed_grad[rows, :] = nt(branch, mixing[...]).astype(low)

        @pl.when(step == 0)
        def _():
            sums_ref[...] = jnp.zeros_like(sums_ref)

        for row, value in enumerate((branch.astype(jnp.float32), pulled * normal, pulled, upstream)):
            sums_ref[row : row + 1, :] += jnp.sum(value, axis=0, keepdims=True)

    @pl.when(step == blocks - 1)
    def _():
        for core, target in ((1 - k, theirs), (k, jobs[2].total)):
            piece = outer_sum(mixed[...], branch_all[:, span(core * half, half)]).astype(low)
            target[...] = piece.reshape(target.shape)
        start(jobs[2].first)

    @pl.when(step >= blocks)
    def _():
        columns = span((step - blocks) * PAIR, PAIR)
        attend_back_pair(
            blocks, projected, mixed_grad.at[:, columns], lse_ref, back_ref, turned, key_sum,
            value_sum, lambda block: block > 0 and between(block),
        )

    pl.when(step == pl.num_programs(0) - 1)(close_all)


def attend_back(sizes, pulled, middle, upstream, mixed, mixing, gain, projected, lse, grads, quads, sent):
    tokens, model = upstream.shape
    pairs = model // PAIR
    blocks = tokens // BLK
    expand, shrink = grads
    depth, rows = sizes["z"], expand.shape[3]
    lead = (sizes["c"], sizes["z"], sizes["y"])
    half, grown, full = model // 2, expand.shape[-1] // 2, shrink.shape[-1]
    by_rows = pl.BlockSpec((BLK, model), lambda g: (jnp.minimum(g, blocks - 1), 0))

    def pair(g):
        return jnp.maximum(g - blocks, 0)

    triple = pl.BlockSpec((tokens, 3 * PAIR), lambda g: (0, pair(g)))
    scratch = [
        pltpu.VMEM((blocks, PAIR, BLK), low),
        pltpu.VMEM((blocks, BLK, PAIR), jnp.float32),
        pltpu.VMEM((blocks, BLK, PAIR), jnp.float32),
        pltpu.SemaphoreType.DMA((2, 32)),
        pltpu.VMEM((tokens, model), low),
        pltpu.VMEM((tokens, model), low),
        pltpu.VMEM((*lead, rows, half), low),
    ]
    for columns in (full, grown, half):
        scratch += ReduceNear.scratch(sizes, rows, columns, columns // 2)
    for columns in (grown, full):
        scratch += [pltpu.VMEM((depth - 1, rows, columns), low)]
    scratch += Finish.scratch(rows, grown)
    return pl.pallas_call(
        functools.partial(attend_back_kernel, sizes, blocks),
        grid=(blocks + pairs,),
        in_specs=[by_rows] * 3
        + [whole_vmem] * 3
        + [triple, pl.BlockSpec((None, 8, tokens), lambda g: (pair(g), 0, 0))]
        + [any_place] * 2
        + [whole_vmem] * 2
        + [any_place],
        out_specs=[triple, by_rows] + [whole_vmem] * 6 + [any_place],
        out_shape=[
            low_shape(*projected.shape),
            jax.ShapeDtypeStruct((tokens, model), jnp.float32),
            jax.ShapeDtypeStruct((8, model), jnp.float32),
            low_shape(depth, rows, half),
            low_shape(depth, rows, grown),
            low_shape(depth, rows, full),
            jax.ShapeDtypeStruct((2, rows // 2, grown), jnp.float32),
            jax.ShapeDtypeStruct((rows, full), jnp.float32),
            low_shape(BLK, model),
        ],
        scratch_shapes=scratch,
        compiler_params=params(5, 60),
        cost_estimate=small_cost,
        name="attend_back",
    )(pulled, middle, upstream, mixed, mixing, gain, projected, lse, *grads, *quads, sent)


def end_kernel(sizes, *refs):
    refs = Refs(refs)
    back_ref, back_far, low_far, joint_far, rows_far, middle_far = refs.take(6)
    gain_ref, vector, mixing_quad, expand_quad, shrink_quad, sent_out = refs.take(6)
    out, vector_out, mixing_out, expand_out, shrink_out, kept = refs.take(6)
    arrived_rows, far_out = refs.take(2)
    sems, steps, arrived = refs.take(3)
    grads, low_rows, turned, joint, rows_in, middle, sent = refs.take(7)
    spot = Spot(sizes)
    mover = Mover(spot, sems)
    width = joint.shape[-1] // 2
    part = width // 2
    tile = 256
    loads = [
        mover.local(far, near)
        for far, near in (
            (back_far, grads),
            (low_far, low_rows),
            (joint_far, joint),
            (rows_far, rows_in),
            (middle_far, middle),
        )
    ]
    jobs, deeps, ends, others_half = [], [], [], []
    for number in range(2):
        theirs, quad = refs.take(2)
        others_half.append(theirs)
        jobs.append(ReduceNear(mover, None, theirs, part // 2, quad, refs.take(6)))
        deeps.append(ReduceDeep(mover, quad, *refs.take(1)))
        ends.append(Finish(mover, *refs.take(2)))
    others = [
        ReduceDeep(mover, quad, *refs.take(1))
        for quad in (mixing_quad, expand_quad, shrink_quad)
    ]
    other_ends = [Finish(mover, *refs.take(2)) for _ in range(2)]
    hops = [
        mover.copy(steps.at[number], arrived.at[number], name)
        for number, name in enumerate(("k", "c", "y"))
    ]
    spread = [
        mover.copy(steps.at[3], arrived.at[2 + by], "z", by) for by in range(1, sizes["z"])
    ]
    rows_copy = mover.copy(sent, arrived_rows, "c")
    out_copy = mover.copy(sent_out.at[block_rows(1)], far_out, "c")

    def gradient(core, number, target):
        @pl.loop(0, part // tile)
        def _(t):
            columns = span(core * width + number * part + t * tile, tile)
            piece = nn(turned[...], grads[:, columns]).astype(low)
            target[..., span(t * tile, tile)] = piece.reshape(*target.shape[:-1], tile)

    sums = {}

    def pull_block(number):
        rows = block_rows(number)
        pulled = grads[rows, :]
        upstream = nt(pulled, joint[...])
        normal, inverse = normal_rows(rows_in[rows, :].astype(jnp.float32))
        middle[rows, :] += norm_pull(upstream, normal, inverse, gain_ref[...])
        for name, value in (
            ("gain", upstream * normal),
            ("shift", upstream),
            ("back", pulled.astype(jnp.float32)),
        ):
            value = jnp.sum(value, axis=0, keepdims=True)
            sums[name] = sums[name] + value if name in sums else value

    def hop(number):
        wait([hops[number]])
        steps[number + 1] = steps[number] + arrived[number]
        start([hops[number + 1]] if number < 2 else spread)

    start(loads[:2])
    spot.meet(all_axes)
    start([out_copy])
    wait(loads[:2])
    start(loads[2:])
    turned[...] = jnp.transpose(low_rows[...])
    for number, job in enumerate(jobs):
        gradient(1 - spot.k, number, others_half[number])
        start(job.first)
        gradient(spot.k, number, job.total)
        job.go_near()
    for job in others:
        start(job.copies)
    wait(loads[2:])
    pull_block(0)
    pull_block(1)
    jobs[0].go_far()
    pull_block(2)
    jobs[1].go_far()
    pull_block(3)
    for place in range(2):
        sent[block_rows(place), :] = chosen_block(back_ref[2 + place], middle).astype(low)
    start([rows_copy])
    for place in range(2):
        kept[block_rows(place), :] = chosen_block(back_ref[place], middle)
    steps[0] = vector[...]
    steps[0, 0:1, :] = sums["gain"]
    steps[0, 1:2, :] = sums["shift"]
    for pair in range(H // 2):
        for row, third in ((2, 0), (3, 2)):
            steps[0, row : row + 1, pair * PAIR : (pair + 1) * PAIR] = sums["back"][
                :, (3 * pair + third) * PAIR : (3 * pair + third + 1) * PAIR
            ]
    start(hops[:1])
    jobs[0].close()
    start(deeps[0].copies)
    hop(0)
    for job, ending in zip(others, other_ends):
        wait(job.copies)
        ending.summed[...] = job.result()
        start(ending.copies)
    wait(others[2].copies)
    shrink_out[...] = others[2].result()
    jobs[1].close()
    start(deeps[1].copies)
    hop(1)
    hop(2)
    for ending, target in zip(other_ends, (mixing_out, expand_out)):
        wait(ending.copies)
        ending.write(target)
    for deep, ending in zip(deeps, ends):
        wait(deep.copies)
        ending.summed[...] = deep.result()
        start(ending.copies)
    wait(spread)
    total = steps[3]
    for by in range(1, sizes["z"]):
        total = total + arrived[2 + by]
    vector_out[...] = total
    for number, ending in enumerate(ends):
        wait(ending.copies)
        ending.write(out, pl.ds(number * part, part))
    wait([rows_copy, out_copy])


def end(sizes, back, joint_back, first_low, joint, rows_in, middle_grad, gain, vector, quads, sent):
    tokens, model = rows_in.shape
    width = joint.shape[1] // 2
    lead = (sizes["c"], sizes["z"], sizes["y"])
    depth = sizes["z"]
    rows = model // (lead[0] * lead[1] * lead[2])
    part = width // 2
    half, grown, full = [quad.shape[-1] for quad in quads]
    scratch = [
        pltpu.SemaphoreType.DMA((2, 48)),
        pltpu.VMEM((4, *vector.shape), jnp.float32),
        pltpu.VMEM((2 + depth, *vector.shape), jnp.float32),
        pltpu.VMEM(joint_back.shape, low),
        pltpu.VMEM(first_low.shape, low),
        pltpu.VMEM(first_low.shape[::-1], low),
        pltpu.VMEM(joint.shape, low),
        pltpu.VMEM(rows_in.shape, low),
        pltpu.VMEM(middle_grad.shape, jnp.float32),
        pltpu.VMEM((tokens // 2, model), low),
    ]
    for number in range(2):
        scratch += [pltpu.VMEM((*lead, rows, part), low), pltpu.VMEM((depth, rows, part), low)]
        scratch += ReduceNear.scratch(sizes, rows, part, part // 2)
        scratch += [pltpu.VMEM((depth - 1, rows, part), low)]
        scratch += Finish.scratch(rows, part)
    scratch += [pltpu.VMEM((depth - 1, rows, columns), low) for columns in (half, grown, full)]
    for columns in (half, grown):
        scratch += Finish.scratch(rows, columns)
    own = rows // 2
    shapes = [(2, own, width), vector.shape, (2, own, half), (2, own, grown), (rows, full)]
    shapes.append((tokens // 2, model))
    return pl.pallas_call(
        functools.partial(end_kernel, sizes),
        in_specs=[pl.BlockSpec(memory_space=pltpu.SMEM)]
        + [any_place] * 5
        + [whole_vmem] * 5
        + [any_place],
        out_specs=[whole_vmem] * 6 + [any_place] * 2,
        out_shape=[jax.ShapeDtypeStruct(shape, jnp.float32) for shape in shapes]
        + [low_shape(tokens // 2, model), low_shape(BLK, model)],
        scratch_shapes=scratch,
        compiler_params=params(6, 60),
        cost_estimate=small_cost,
        name="end",
    )(back, joint_back, first_low, joint, rows_in, middle_grad, gain, vector, *quads, sent)


def last_kernel(ctx_ref, *refs):
    refs = Refs(refs)
    joint_part, mixing_part, expand_a, expand_b, shrink_a, shrink_b = refs.take(6)
    kept_grad, far_grad, kept_out, far_one, far_two = refs.take(5)
    states = [refs.take(3) for _ in range(4)]
    grad_out, block_out = refs.take(2)
    news = [refs.take(4) for _ in range(4)]
    here = ctx_ref[0]
    grad_out[here] = kept_grad[...]
    grad_out[1 - here] = far_grad[...].astype(jnp.float32)
    block_out[here] = kept_out[...]
    block_out[1 - here, :BLK, :] = far_one[...]
    block_out[1 - here, BLK:, :] = far_two[...]

    def update(number, where, gradient):
        weight, first, second = [ref[where] for ref in states[number]]
        results = adam_update(weight, first, second, gradient, 0.05, 0.1)
        for ref, value in zip(news[number], (*results, results[0].astype(low))):
            ref[where] = value

    every = slice(None)
    pairs = joint_part.shape[2] // (3 * PAIR)
    for core in range(2):
        for pair in range(pairs):
            for third in range(3):
                first = ((third * 2 + core) * pairs + pair) * PAIR
                source = (pair * 3 + third) * PAIR
                update(
                    0,
                    (every, pl.ds(first, PAIR)),
                    joint_part[core, :, source : source + PAIR],
                )
        half = mixing_part.shape[2]
        update(1, (every, pl.ds(core * half, half)), mixing_part[core])
        lane = lax.broadcasted_iota(jnp.int32, (1, PAIR), 1)
        for chip in range(0, expand_a.shape[2] // HD, 2):
            a = expand_a[core, :, chip * HD : chip * HD + PAIR]
            b = expand_b[core, :, chip * HD : chip * HD + PAIR]
            even = jnp.where(lane < HD, a, pltpu.roll(b, HD, 1))
            odd = jnp.where(lane < HD, pltpu.roll(a, HD, 1), b)
            for number, value in ((chip, even), (chip + 1, odd)):
                update(2, (every, pl.ds((number * 2 + core) * PAIR, PAIR)), value)
    rows = shrink_a.shape[0]
    update(3, (pl.ds(0, rows), every), shrink_a[...])
    update(3, (pl.ds(rows, rows), every), shrink_b[...])


def last(ctx, parts, kept_grad, far_grad, kept_out, far_outs, states):
    shapes = [jax.ShapeDtypeStruct((2, *kept_grad.shape), jnp.float32), low_shape(2, *kept_out.shape)]
    for weight, _, _ in states:
        shapes += [jax.ShapeDtypeStruct(weight.shape, jnp.float32)] * 3
        shapes.append(low_shape(*weight.shape))
    flat = [array for state in states for array in state]
    return pl.pallas_call(
        last_kernel,
        in_specs=[pl.BlockSpec(memory_space=pltpu.SMEM)] + [whole_vmem] * (11 + len(flat)),
        out_specs=[whole_vmem] * len(shapes),
        out_shape=shapes,
        compiler_params=pltpu.CompilerParams(vmem_limit_bytes=56 << 20),
        cost_estimate=small_cost,
        name="last",
    )(ctx, *parts, kept_grad, far_grad, kept_out, *far_outs, *flat)


def layer_norm(values, gain_row, shift_row):
    centered = values - jnp.mean(values, axis=-1, keepdims=True)
    variance = jnp.mean(centered * centered, axis=-1, keepdims=True)
    inverse = lax.rsqrt(variance + norm_eps)
    normal_part = centered * inverse
    return (normal_part * gain_row + shift_row, normal_part, inverse)


def norm_back(upstream, normal_part, inverse, gain_row):
    scaled = upstream * gain_row
    inner_sum = jnp.mean(scaled, axis=-1, keepdims=True)
    along_sum = jnp.mean(scaled * normal_part, axis=-1, keepdims=True)
    values_grad = inverse * (scaled - inner_sum - normal_part * along_sum)
    return (values_grad, jnp.sum(upstream * normal_part, axis=0), jnp.sum(upstream, axis=0))


def adam_update(weight, moment_one, moment_two, gradient, step_rate, decay_rate):
    first_new = 0.5 * moment_one + 0.5 * gradient
    second_new = 0.5 * moment_two + 0.5 * gradient * gradient
    correct = 1.0 - 0.5**STEP
    direction = first_new / correct / (jnp.sqrt(second_new / correct) + adam_eps)
    updated = weight - step_rate * (direction + decay_rate * weight)
    return (updated, first_new, second_new)


def to_groups(matrix):
    row_count = matrix.shape[0]
    return matrix.reshape(row_count, H // group_heads, group_heads, HD).transpose(1, 0, 2, 3)


def from_groups(stacked):
    return stacked.transpose(1, 0, 2, 3).reshape(stacked.shape[1], H * HD)


def tile_scores(queries, key_rows, allowed):
    products = jnp.einsum("rgd,lgd->grl", queries, key_rows, preferred_element_type=jnp.float32)
    return jnp.where(allowed[None], products * 0.125, -1e30)


def tile_forward(queries, key_rows, value_rows, allowed):
    scores = tile_scores(queries, key_rows, allowed)
    largest = jnp.max(scores, axis=-1, keepdims=True)
    exponent = jnp.exp(scores - largest)
    row_total = jnp.sum(exponent, axis=-1, keepdims=True)
    weights = (exponent / row_total).astype(low)
    mixed = jnp.einsum("grl,lgd->rgd", weights, value_rows, preferred_element_type=jnp.float32)
    return (mixed, (largest + jnp.log(row_total))[..., 0])


def tile_backward(queries, key_rows, value_rows, allowed, logsum, upstream):
    scores = tile_scores(queries, key_rows, allowed)
    recomputed = jnp.exp(scores - logsum[..., None])
    value_grad = jnp.einsum(
        "grl,rgd->lgd", recomputed.astype(low), upstream, preferred_element_type=jnp.float32
    )
    weight_grad = jnp.einsum(
        "rgd,lgd->grl", upstream, value_rows, preferred_element_type=jnp.float32
    )
    inner_sum = jnp.sum(recomputed * weight_grad, axis=-1, keepdims=True)
    score_grad = (recomputed * (weight_grad - inner_sum)).astype(low)
    query_grad = (
        jnp.einsum("grl,lgd->rgd", score_grad, key_rows, preferred_element_type=jnp.float32) * 0.125
    )
    key_grad = (
        jnp.einsum("grl,rgd->lgd", score_grad, queries, preferred_element_type=jnp.float32) * 0.125
    )
    return (query_grad, key_grad, value_grad)


def spread_forward(queries, key_value, allowed):
    def one_sequence(pieces):
        queries, key_value, allowed = pieces
        width = queries.shape[1]
        mixed, logsum = lax.map(
            lambda triple: tile_forward(triple[0], triple[1], triple[2], allowed),
            (to_groups(queries), to_groups(key_value[:, :width]), to_groups(key_value[:, width:])),
        )
        return (from_groups(mixed), logsum)

    return lax.map(one_sequence, (queries, key_value, allowed))


def spread_backward(queries, key_value, allowed, logsum, upstream):
    def one_sequence(pieces):
        queries, key_value, allowed, logsum, upstream = pieces
        width = queries.shape[1]
        query_grad, key_grad, value_grad = lax.map(
            lambda member: tile_backward(
                member[0], member[1], member[2], allowed, member[3], member[4]
            ),
            (
                to_groups(queries),
                to_groups(key_value[:, :width]),
                to_groups(key_value[:, width:]),
                logsum,
                to_groups(upstream),
            ),
        )
        return (
            from_groups(query_grad),
            jnp.concatenate([from_groups(key_grad), from_groups(value_grad)], axis=1),
        )

    return lax.map(one_sequence, (queries, key_value, allowed, logsum, upstream))


class Slice:
    def __init__(self, ctx_size, wshard_size):
        rest = wshard_size // 2
        self.sizes = {"c": ctx_size, "z": 4, "y": rest // 4, "k": 2}

    def here(self):
        flat = lax.axis_index(axes)
        found = {}
        for name in ("k", "y", "z", "c"):
            found[name] = flat % self.sizes[name]
            flat = flat // self.sizes[name]
        return found

    def shift(self, value, name, by):
        pairs = []
        sizes = self.sizes
        for c in range(sizes["c"]):
            for z in range(sizes["z"]):
                for y in range(sizes["y"]):
                    for k in range(sizes["k"]):
                        spot = {"c": c, "z": z, "y": y, "k": k}
                        goal = dict(spot)
                        goal[name] = (spot[name] + by) % sizes[name]
                        pairs.append((self.flat(spot), self.flat(goal)))
        return lax.ppermute(value, axes, pairs)

    def flat(self, spot):
        sizes = self.sizes
        return ((spot["c"] * sizes["z"] + spot["z"]) * sizes["y"] + spot["y"]) * sizes["k"] + spot[
            "k"
        ]

    def stack(self, array, name, here):
        size = self.sizes[name]
        parts = [array] + [self.shift(array, name, by) for by in range(1, size)]
        if size > 4:
            ordered = [parts[(-place) % size] for place in range(size)]
            return jnp.roll(jnp.stack(ordered), here[name], axis=0)
        return jnp.stack(
            [lax.select_n((here[name] - place) % size, *parts) if size > 2 else
             jnp.where(here[name] == place, parts[0], parts[1]) for place in range(size)]
        )

    def reach(self, pieces, name):
        grown = list(pieces)
        for by in range(1, self.sizes[name]):
            for array, place in pieces:
                moved = dict(place)
                moved[name] = (place[name] - by) % self.sizes[name]
                grown.append((self.shift(array, name, by), moved))
        return grown

    def gather_split(self, stacked, cut, here):
        sizes = self.sizes
        depth, rows, columns = stacked.shape
        out = jnp.zeros((sizes["c"], depth, sizes["y"], rows, columns), stacked.dtype)
        for low_column, high_column, order in ((0, cut, "cy"), (cut, columns, "yc")):
            pieces = [(stacked[:, :, low_column:high_column], here)]
            for name in order:
                pieces = self.reach(pieces, name)
            for array, place in pieces:
                out = lax.dynamic_update_slice(
                    out, array[None, :, None], (place["c"], 0, place["y"], 0, low_column)
                )
        return out.reshape(-1, columns)

    def send_terms(self, value, name, place, here):
        size = self.sizes[name]
        own = lax.dynamic_index_in_dim(value, here[name], place, False)
        moved = [
            self.shift(
                lax.dynamic_index_in_dim(value, (here[name] + by) % size, place, False), name, by
            )
            for by in range(1, size)
        ]
        return own, moved

    def add_terms(self, terms, kind=low):
        own, moved = terms
        total = own.astype(jnp.float32)
        for other in moved:
            total = total + other.astype(jnp.float32)
        return total.astype(kind)

    def everywhere(self, value):
        for name in ("k", "c", "y", "z"):
            total = value
            for by in range(1, self.sizes[name]):
                total = total + self.shift(value, name, by)
            value = total
        return value


def tie(value, *others):
    return lax.optimization_barrier((value, others))[0]


def by_core(core, first, second, axis):
    return jnp.where(
        core == 0,
        jnp.concatenate([first, second], axis=axis),
        jnp.concatenate([second, first], axis=axis),
    )


def pick(core, array, axis):
    return (
        lax.dynamic_index_in_dim(array, core, axis, False),
        lax.dynamic_index_in_dim(array, 1 - core, axis, False),
    )


def gather_far(grid, here, pieces):
    joint_halves, table, mixing_halves, expand_a, expand_b, shrink_a, shrink_b = pieces
    core = here["k"]

    def chip_rows(halves):
        own, other = pick(core, halves, 0)
        return by_core(core, own, grid.shift(other, "k", 1), 0)

    def everyone(block):
        width = block.shape[1]
        return grid.gather_split(grid.stack(block, "z", here), width // 2, here)

    def both(block, axis):
        own = everyone(block)
        return by_core(core, own, grid.shift(own, "k", 1), axis)

    return (
        both(chip_rows(joint_halves), 1),
        everyone(by_core(core, table, grid.shift(table, "k", 1), 0)),
        both(chip_rows(mixing_halves), 1),
        both(chip_rows(expand_a), 1),
        both(chip_rows(expand_b), 1),
        both(shrink_a, 0),
        both(shrink_b, 0),
    )


def reduce_far(grid, here, gradient, by_rows):
    core = here["k"]
    sizes = grid.sizes
    if by_rows:
        own, other = pick(core, gradient.reshape(2, -1, gradient.shape[1]), 0)
    else:
        own, other = pick(core, gradient.reshape(gradient.shape[0], 2, -1), 1)
    total = grid.add_terms((own, [grid.shift(other, "k", 1)]))
    total = total.reshape(sizes["c"], sizes["z"], sizes["y"], -1, own.shape[-1])
    for name, place in (("y", 2), ("c", 0)):
        total = grid.add_terms(grid.send_terms(total, name, place, here))
    total = grid.add_terms(grid.send_terms(total, "z", 0, here), jnp.float32)
    if by_rows:
        return total
    kept, other = pick(core, total.reshape(2, -1, total.shape[1]), 0)
    return by_core(core, kept[None], grid.shift(other, "k", 1)[None], 0)


def body(
    grid,
    block_input,
    block_order,
    cotangent,
    joint_weight,
    mixing_weight,
    expand_weight,
    shrink_weight,
    vectors,
    joint_first,
    mixing_first,
    expand_first,
    shrink_first,
    vectors_first,
    joint_second,
    mixing_second,
    expand_second,
    shrink_second,
    vectors_second,
):
    here = grid.here()
    sizes = grid.sizes
    ctx, ctx_size = here["c"], sizes["c"]
    seq_count, row_count, width = block_input.shape
    half = width // 2
    pairs = H // 2
    hidden_width = expand_weight.shape[1]
    own_rows = joint_weight.shape[0]
    slot = shrink_weight.shape[0]
    sub = slot // 2
    chips = hidden_width // (2 * slot)
    tokens = seq_count * row_count
    row_blocks = row_count // BLK
    near = ctx_size == 2 and seq_count == 2 and sizes["y"] == 2 and own_rows % 32 == 0

    def hidden_sets(shard):
        parts = shard.astype(low).reshape(own_rows, chips, 2, 2, sub)
        return [
            parts[:, :, :, number].transpose(2, 0, 1, 3).reshape(2, own_rows, chips * sub)
            for number in range(2)
        ]

    table = jnp.pad(vectors.T.astype(low), ((0, 0), (0, 128 - vectors.shape[0])))
    if near:
        joint, tables, *quads, far_input, far_upstream, next_half, next_shrink = begin(
            sizes,
            joint_weight,
            table,
            mixing_weight,
            expand_weight,
            shrink_weight,
            block_input,
            cotangent,
        )
    else:
        joint_halves = (
            joint_weight.astype(low)
            .reshape(own_rows, 3, 2, pairs // 2, PAIR)
            .transpose(2, 0, 3, 1, 4)
            .reshape(2, own_rows, 3 * half)
        )
        mixing_halves = mixing_weight.astype(low).reshape(own_rows, 2, half).transpose(1, 0, 2)
        shrink_low = shrink_weight.astype(low)
        pieces = [joint_halves, table, mixing_halves, *hidden_sets(expand_weight)]
        pieces += [shrink_low[:sub], shrink_low[sub:]]
        joint, tables, mixing, expand_a, expand_b, shrink_a, shrink_b = gather_far(
            grid, here, pieces
        )
    joint = joint.reshape(width, 3 * width)
    vector_values = (
        tables.reshape(width, -1)[:, : vectors.shape[0]].T.astype(jnp.float32)
    )

    if near:
        order = lax.dynamic_slice_in_dim(block_order, ctx, 1, 0)[0]
        blocks = order.shape[0]
        stored = jnp.arange(blocks, dtype=jnp.int32)
        moved = jnp.where(stored // row_blocks == ctx, 0, row_blocks) + stored % row_blocks
        place = jnp.sum(jnp.where(order[None, :] == stored[:, None], moved[None, :], 0), axis=1)
        back = jnp.sum(jnp.where(moved[None, :] == stored[:, None], order[None, :], 0), axis=1)
        place, back = place.astype(jnp.int32), back.astype(jnp.int32)
    joint_shift = jnp.stack(
        [
            vector_values[2].reshape(pairs, PAIR),
            jnp.zeros((pairs, PAIR), jnp.float32),
            vector_values[3].reshape(pairs, PAIR),
        ],
        axis=1,
    ).reshape(1, -1)
    lead = (sizes["c"], sizes["z"], sizes["y"])
    hidden_bias = vector_values[8:].reshape(chips, 2, 2, sub).transpose(2, 1, 0, 3).reshape(2, 1, -1)

    def by_device(expand_grad, shrink_grad):
        return (
            expand_grad.reshape(*lead, -1, expand_grad.shape[1]),
            shrink_grad.reshape(2, *lead, -1, width),
        )

    if near:
        mixed_low, logsum, input_low, first_low, projected, *gathered = attend(
            sizes,
            place,
            block_input,
            far_input,
            joint,
            vector_values[:2],
            joint_shift,
            cotangent,
            quads,
            next_half,
            next_shrink,
        )
        mixing, expand_a, shrink_a, *quads, last_upstream = gathered
        mixing = mixing.reshape(width, width)
        *before, expand_grad_a, shrink_grad_a, bias_a, middle, second_low, upstream, expand_b, shrink_b = mlp_gather(
            sizes,
            place,
            mixed_low,
            input_low,
            mixing,
            vector_values[:8],
            expand_a.reshape(width, -1),
            shrink_a.reshape(-1, width),
            hidden_bias[0],
            cotangent,
            far_upstream,
            last_upstream,
            quads,
        )
        second_grad, expand_grad_b, shrink_grad_b, bias_b, *quads, kept_out, sent_out = mlp_reduce(
            sizes,
            back,
            second_low,
            upstream,
            expand_b.reshape(width, -1),
            shrink_b.reshape(-1, width),
            hidden_bias[1],
            before,
            by_device(expand_grad_a, shrink_grad_a),
        )
    else:
        input_low = block_input.reshape(tokens, width)
        upstream = cotangent.reshape(tokens, width)
        input_rows = input_low.astype(jnp.float32)
        normed_first, normal_first, inverse_first = layer_norm(
            input_rows, vector_values[0], vector_values[1]
        )
        first_low = normed_first.astype(low)
        projected = (nn(first_low, joint) + joint_shift).astype(low)
        by_part = projected.reshape(seq_count, row_count, pairs, 3, PAIR)
        queries, keys, values = [
            by_part[:, :, :, part].reshape(seq_count, row_count, width) for part in range(3)
        ]
        key_value = lax.all_gather(
            jnp.concatenate([keys, values], axis=2), "ctx", axis=1, tiled=True
        )
        own_blocks = lax.dynamic_slice_in_dim(block_order, ctx * row_blocks, row_blocks, 1)
        query_block = jnp.repeat(own_blocks, BLK, axis=1, total_repeat_length=row_count)
        key_block = jnp.repeat(block_order, BLK, axis=1, total_repeat_length=key_value.shape[1])
        allowed = key_block[:, None, :] <= query_block[:, :, None]
        mixed, logsum = spread_forward(queries, key_value, allowed)
        mixed_low = mixed.astype(low).reshape(tokens, width)
        mixing = mixing.reshape(width, width)
        middle = input_rows + (nn(mixed_low, mixing) + vector_values[4])
        normed_second, normal_second, inverse_second = layer_norm(
            middle, vector_values[5], vector_values[6]
        )
        second_low = normed_second.astype(low)
        before = (middle + vector_values[7], jnp.zeros_like(middle))
        *before, expand_grad_a, shrink_grad_a, bias_a = mlp(
            second_low,
            upstream,
            expand_a.reshape(width, -1),
            shrink_a.reshape(-1, width),
            hidden_bias[0],
            before,
        )
        result, second_grad, expand_grad_b, shrink_grad_b, bias_b = mlp(
            second_low,
            upstream,
            expand_b.reshape(width, -1),
            shrink_b.reshape(-1, width),
            hidden_bias[1],
            before,
        )
        block_output = result.astype(low).reshape(block_input.shape)
    hidden_bias_grads = [
        bias.reshape(2, chips, 1, sub).transpose(1, 0, 2, 3) for bias in (bias_a, bias_b)
    ]

    if near:
        joint_back, middle_grad, sums, *last_quads, expand_part_a, shrink_part_a, far_one = attend_back(
            sizes,
            second_grad,
            middle,
            upstream,
            mixed_low,
            mixing,
            vector_values[5:6],
            projected,
            logsum,
            by_device(expand_grad_b, shrink_grad_b),
            quads,
            sent_out,
        )
    else:
        middle_part, gain_two, shift_two = norm_back(
            second_grad, normal_second, inverse_second, vector_values[5]
        )
        middle_grad = upstream.astype(jnp.float32) + middle_part
        branch_low = middle_grad.astype(low)
        mixing_grad = outer_sum(mixed_low, branch_low).astype(low)
        mixed_grad = nt(branch_low, mixing).astype(low)
        query_grad, key_value_grad = spread_backward(
            queries, key_value, allowed, logsum, mixed_grad.reshape(seq_count, row_count, width)
        )
        summed = lax.psum_scatter(
            key_value_grad.astype(low), "ctx", scatter_dimension=1, tiled=True
        )
        parts = [query_grad.astype(low), summed[..., :width], summed[..., width:]]
        joint_back = jnp.stack(
            [part.reshape(tokens, pairs, PAIR) for part in parts], axis=2
        ).reshape(tokens, 3 * width)
        mixing_part = reduce_far(grid, here, mixing_grad, False)
        expand_part_a, shrink_part_a, expand_part_b, shrink_part_b = [
            reduce_far(grid, here, grad, number % 2 == 1)
            for number, grad in enumerate(
                (expand_grad_a, shrink_grad_a, expand_grad_b, shrink_grad_b)
            )
        ]

    def column_sum(rows):
        return jnp.sum(rows.astype(jnp.float32), axis=0)

    hidden_bias_grad = jnp.concatenate(hidden_bias_grads, axis=2).reshape(-1, width)
    weights = (joint_weight, mixing_weight, expand_weight, shrink_weight)
    firsts = (joint_first, mixing_first, expand_first, shrink_first)
    seconds = (joint_second, mixing_second, expand_second, shrink_second)
    if near:
        rows = vectors.shape[0]
        vector_grad = jnp.concatenate(
            [jnp.zeros((4, width)), sums[:4], hidden_bias_grad, jnp.zeros((-rows % 8, width))],
            axis=0,
        )
        joint_part, vector_sum, mixing_part, expand_part_b, shrink_part_b, kept_grad, far_grad, far_two = end(
            sizes,
            back,
            joint_back,
            first_low,
            joint,
            input_low,
            middle_grad,
            vector_values[0:1],
            vector_grad,
            last_quads,
            sent_out,
        )
        input_gradient, block_output, *news = last(
            ctx.astype(jnp.int32).reshape(1),
            (joint_part, mixing_part, expand_part_a, expand_part_b, shrink_part_a, shrink_part_b),
            kept_grad,
            far_grad,
            kept_out,
            (far_one, far_two),
            list(zip(weights, firsts, seconds)),
        )
        updated, moments, squares, copies = [news[number::4] for number in range(4)]
    else:
        joint_grad = outer_sum(first_low, joint_back).astype(low)
        first_grad = nt(joint_back, joint)
        input_part, gain_one, shift_one = norm_back(
            first_grad, normal_first, inverse_first, vector_values[0]
        )
        input_gradient = (middle_grad + input_part).reshape(block_input.shape)
        joint_sums = column_sum(joint_back).reshape(pairs, 3, PAIR)
        vector_rows = [
            gain_one,
            shift_one,
            joint_sums[:, 0].reshape(-1),
            joint_sums[:, 2].reshape(-1),
            column_sum(branch_low),
            gain_two,
            shift_two,
            column_sum(upstream),
        ]
        joint_part = reduce_far(grid, here, joint_grad, False)
        vector_sum = grid.everywhere(
            jnp.concatenate([jnp.stack(vector_rows), hidden_bias_grad], axis=0)
        )
        joint_sum = (
            joint_part.reshape(2, own_rows, pairs // 2, 3, PAIR)
            .transpose(1, 3, 0, 2, 4)
            .reshape(joint_weight.shape)
        )
        mixing_sum = mixing_part.transpose(1, 0, 2).reshape(mixing_weight.shape)
        expand_sum = jnp.stack(
            [part.reshape(2, own_rows, chips, sub) for part in (expand_part_a, expand_part_b)]
        )
        expand_sum = expand_sum.transpose(2, 3, 1, 0, 4).reshape(expand_weight.shape)
        shrink_sum = jnp.concatenate([shrink_part_a, shrink_part_b], axis=0)
        updated, moments, squares = zip(
            *[
                adam_update(*terms, 0.05, 0.1)
                for terms in zip(
                    weights, firsts, seconds, (joint_sum, mixing_sum, expand_sum, shrink_sum)
                )
            ]
        )
        copies = [array.astype(low) for array in updated]
    vector_sum = lax.dynamic_slice(
        vector_sum, (0, lax.axis_index(axes) * vectors.shape[1]), vectors.shape
    )
    vectors_new, vectors_moment, vectors_square = adam_update(
        vectors, vectors_first, vectors_second, vector_sum, 0.5, 0.0
    )
    return (
        block_output,
        input_gradient,
        *updated,
        vectors_new,
        *moments,
        vectors_moment,
        *squares,
        vectors_square,
        *copies,
        vectors_new.astype(low),
    )


def solution(mesh):
    grid = Slice(mesh.shape["ctx"], mesh.shape["wshard"])
    rows = P("wshard", "ctx", None)
    matrix = P(axes, None)
    table = P(None, axes)
    parameters = (matrix, matrix, matrix, matrix, table)
    return jax.shard_map(
        functools.partial(body, grid),
        mesh=mesh,
        in_specs=(rows, P("wshard", None), rows) + parameters * 3,
        out_specs=(rows, rows) + parameters * 4,
        check_vma=False,
    )
```

```python
import functools

import jax
import jax.numpy as jnp
from jax import lax
from jax.experimental import pallas as pl
from jax.experimental.pallas import tpu as pltpu
from jax.sharding import PartitionSpec as P

H = 16
HD = 64
BLK = 256
STEP = 10
PAIR = 2 * HD

norm_eps = 1e-05
adam_eps = 1e-08
group_heads = 4
score_scale = 0.125 * 1.4426950408889634
gelu_root = 0.7978845608028654
gelu_cubic = 0.044715
low = jnp.bfloat16
axes = ("ctx", "wshard")
small_cost = pl.CostEstimate(flops=1024, bytes_accessed=1024, transcendentals=0)


def nt(left_side, right_side):
    return lax.dot_general(
        left_side, right_side, (((1,), (1,)), ((), ())), preferred_element_type=jnp.float32
    )


def nn(left_side, right_side):
    return jnp.dot(left_side, right_side, preferred_element_type=jnp.float32)


def outer_sum(left_side, right_side):
    return lax.dot_general(
        left_side, right_side, (((0,), (0,)), ((), ())), preferred_element_type=jnp.float32
    )


def block_rows(block):
    return pl.ds(block * BLK, BLK)


def thirds(ref):
    return [ref.at[:, pl.ds(part * PAIR, PAIR)] for part in range(3)]


def both_heads(rows):
    lane = lax.broadcasted_iota(jnp.int32, (1, PAIR), 1)
    empty = jnp.zeros_like(rows)
    return jnp.concatenate(
        [jnp.where(lane < HD, rows, empty), jnp.where(lane < HD, empty, rows)], axis=0
    )


def attend_pair(blocks, projected, o_ref, lse_ref, between):
    q_ref, k_ref, v_ref = thirds(projected)
    lane = lax.broadcasted_iota(jnp.int32, (1, PAIR), 1)
    for i in range(blocks):
        between(i)
        rows = block_rows(i)
        queries = both_heads(q_ref[rows, :])
        upto = pl.ds(0, (i + 1) * BLK)
        scores = nt(queries, k_ref[upto, :]) * score_scale
        top = jnp.max(scores, axis=1, keepdims=True)
        weights = jnp.exp2(scores - top)
        total = jnp.sum(weights, axis=1, keepdims=True)
        mixed = nn(weights.astype(low), v_ref[upto, :])
        mixed = mixed * (1.0 / total)
        o_ref[rows, :] = jnp.where(lane < HD, mixed[:BLK], mixed[BLK:]).astype(o_ref.dtype)
        logsum = jnp.transpose(jnp.broadcast_to(top + jnp.log2(total), (2 * BLK, PAIR)))
        for h in range(2):
            lse_ref[h : h + 1, rows] = logsum[0:1, h * BLK : (h + 1) * BLK]


def attend_back_pair(
    blocks, projected, do_ref, lse_ref, back_ref, turned, key_sum, value_sum, between
):
    q_ref, k_ref, v_ref = thirds(projected)
    dq_ref, dk_ref, dv_ref = thirds(back_ref)
    turned[...] = jnp.transpose(k_ref[...])
    for i in range(blocks):
        between(i)
        rows = block_rows(i)
        queries, upstream = both_heads(q_ref[rows, :]), both_heads(do_ref[rows, :])
        logsum = jnp.concatenate([lse_ref[0:1, rows], lse_ref[1:2, rows]], axis=1)
        upto = pl.ds(0, (i + 1) * BLK)
        weights = jnp.exp2(nt(k_ref[upto, :], queries) * score_scale - logsum)
        pulls = nt(v_ref[upto, :], upstream)
        inner = jnp.sum(weights * pulls, axis=0, keepdims=True)
        score_grad = (weights * (pulls - inner)).astype(low)
        value_grad = nn(weights.astype(low), upstream)
        key_grad = nn(score_grad, queries)
        query_grad = nn(turned[:, upto], score_grad)
        earlier, latest = pl.ds(0, i * BLK), block_rows(i)
        if i > 0:
            value_sum[earlier, :] += value_grad[: i * BLK]
            key_sum[earlier, :] += key_grad[: i * BLK]
        value_sum[latest, :] = value_grad[i * BLK :]
        key_sum[latest, :] = key_grad[i * BLK :]
        joined = jnp.concatenate([query_grad[:HD, :BLK], query_grad[HD:, BLK:]], axis=0)
        dq_ref[rows, :] = (jnp.transpose(joined) * 0.125).astype(dq_ref.dtype)
    dk_ref[...] = (key_sum[...] * 0.125).astype(dk_ref.dtype)
    dv_ref[...] = value_sum[...].astype(dv_ref.dtype)


def hooks(step, schedule):
    def between(block):
        for when, where, action in schedule:
            if where == block:
                pl.when(step == when)(action)

    return between


any_place = pl.BlockSpec(memory_space=pl.ANY)
whole_vmem = pl.BlockSpec(memory_space=pltpu.VMEM)


MESH = pl.DeviceIdType.MESH


class Spot:
    def __init__(self, sizes):
        self.sizes = sizes
        ctx, shard = lax.axis_index("ctx"), lax.axis_index("wshard")
        self.c = ctx
        self.k = shard % 2
        self.y = (shard // 2) % 2
        self.z = shard // 4

    def device(self, name, by=1):
        c, z, y, k = self.c, self.z, self.y, self.k
        if name == "c":
            c = 1 - c
        if name == "y":
            y = 1 - y
        if name == "k":
            k = 1 - k
        if name == "z":
            z = (z + by) % self.sizes["z"]
        return (c, (z * 2 + y) * 2 + k)

    def meet(self, names):
        barrier = pltpu.get_barrier_semaphore()
        partners = []
        for name in names:
            for by in range(1, self.sizes[name]):
                partners.append(self.device(name, by))
        for partner in partners:
            pl.semaphore_signal(barrier, inc=1, device_id=partner, device_id_type=MESH)
        pl.semaphore_wait(barrier, len(partners))


class Mover:
    def __init__(self, spot, sems):
        self.spot, self.sems, self.count = spot, sems, 0

    def copy(self, source, target, name, by=1):
        number = self.count
        self.count += 1
        return pltpu.make_async_remote_copy(
            src_ref=source,
            dst_ref=target,
            send_sem=self.sems.at[0, number],
            recv_sem=self.sems.at[1, number],
            device_id=self.spot.device(name, by),
            device_id_type=MESH,
        )

    def local(self, source, target):
        number = self.count
        self.count += 1
        return pltpu.make_async_copy(source, target, self.sems.at[0, number])


class Refs:
    def __init__(self, refs):
        self.refs = list(refs)

    def take(self, count):
        taken, self.refs = self.refs[:count], self.refs[count:]
        return taken


def start(copies):
    for copy in copies:
        copy.start()


def wait(copies):
    for copy in copies:
        copy.wait()


def span(first, size):
    return pl.ds(pl.multiple_of(first, 128), size)


class Deep:
    def __init__(self, mover, quad):
        z = mover.spot.z
        self.copies = [
            mover.copy(quad.at[z], quad.at[z], "z", by) for by in range(1, mover.spot.sizes["z"])
        ]


def first_rows(mover, halves, quad):
    spot = mover.spot
    rows = halves.shape[1]
    block = quad.at[spot.z, pl.ds(pl.multiple_of(spot.k * rows, rows), rows)]
    return [
        mover.local(halves.at[spot.k], block),
        mover.copy(halves.at[1 - spot.k], block, "k"),
    ]


class Near:
    def __init__(self, mover, quad, half, offset, cut, core=True):
        spot = mover.spot
        c, z, y = spot.c, spot.z, spot.y
        width = quad.shape[-1]
        every = slice(None)

        def part(ci, yi, first, size):
            return half.at[ci, every, yi, :, span(offset + first, size)]

        self.near, self.far = [mover.local(quad, part(c, y, 0, width))], []
        for first, size, one, two in ((0, cut, "c", "y"), (cut, width - cut, "y", "c")):
            if size == 0:
                continue
            source = quad.at[every, every, pl.ds(first, size)]
            self.near.append(mover.copy(source, part(c, y, first, size), one))
            self.near.append(mover.copy(source, part(c, y, first, size), two))
            block = part(1 - c if one == "c" else c, 1 - y if one == "y" else y, first, size)
            self.far.append(mover.copy(block, block, two))
        self.core = [[], [], []]
        if core:
            self.core[0].append(mover.copy(quad, part(c, y, 0, width), "k"))
            for stage, ci, yi in ((1, 1 - c, y), (1, c, 1 - y), (2, 1 - c, 1 - y)):
                block = part(ci, yi, 0, width)
                self.core[stage].append(mover.copy(block, block, "k"))

    def close(self):
        wait(self.far)
        start(self.core[2])

    def close_core(self):
        for stage in self.core:
            wait(stage)


class ReduceNear:
    def __init__(self, mover, mine, theirs, cut, quad, scratch):
        self.spot = spot = mover.spot
        self.cut, self.quad = cut, quad
        self.total, self.other, self.by_y, self.by_c, self.then_c, self.then_y = scratch
        self.width = width = self.total.shape[-1]
        c, y = spot.c, spot.y
        every, left, right = slice(None), pl.ds(0, cut), pl.ds(cut, width - cut)
        total = self.total
        self.first = [mover.copy(theirs, self.other, "k")]
        if mine is not None:
            self.first.append(mover.local(mine, total))
        self.near = [
            mover.copy(total.at[every, every, 1 - y, every, left], self.by_y, "y"),
            mover.copy(total.at[1 - c, every, every, every, right], self.by_c, "c"),
        ]
        self.far = [
            mover.copy(total.at[1 - c, every, y, every, left], self.then_c, "c"),
            mover.copy(total.at[c, every, 1 - y, every, right], self.then_y, "y"),
        ]

    @staticmethod
    def scratch(sizes, rows, width, cut):
        c, z, y = sizes["c"], sizes["z"], sizes["y"]
        shapes = [
            (c, z, y, rows, width),
            (c, z, y, rows, width),
            (c, z, rows, cut),
            (z, y, rows, width - cut),
            (z, rows, cut),
            (z, rows, width - cut),
        ]
        return [pltpu.VMEM(shape, low) for shape in shapes]

    def add(self, where, extra):
        total = self.total[where].astype(jnp.float32) + extra.astype(jnp.float32)
        return total.astype(low)

    def go_near(self):
        wait(self.first)
        sizes = self.spot.sizes
        for c in range(sizes["c"]):
            for y in range(sizes["y"]):

                @pl.loop(0, sizes["z"])
                def _(z):
                    self.total[c, z, y] = self.add((c, z, y), self.other[c, z, y])

        start(self.near)

    def go_far(self):
        wait(self.near)
        spot, cut = self.spot, self.cut
        left, right = pl.ds(0, cut), pl.ds(cut, self.width - cut)

        @pl.loop(0, spot.sizes["z"])
        def _(z):
            for c in range(spot.sizes["c"]):
                where = (c, z, spot.y, slice(None), left)
                self.total[where] = self.add(where, self.by_y[c, z])
            for y in range(spot.sizes["y"]):
                where = (spot.c, z, y, slice(None), right)
                self.total[where] = self.add(where, self.by_c[z, y])

        start(self.far)

    def close(self):
        wait(self.far)
        spot, cut = self.spot, self.cut
        left, right = pl.ds(0, cut), pl.ds(cut, self.width - cut)

        @pl.loop(0, spot.sizes["z"])
        def _(z):
            for columns, extra in ((left, self.then_c), (right, self.then_y)):
                where = (spot.c, z, spot.y, slice(None), columns)
                self.quad[z, :, columns] = self.add(where, extra[z])


class ReduceDeep:
    def __init__(self, mover, quad, by_z):
        self.spot = spot = mover.spot
        self.quad, self.by_z = quad, by_z
        depth = spot.sizes["z"]
        self.copies = [
            mover.copy(quad.at[(spot.z + by) % depth], by_z.at[by - 1], "z", by)
            for by in range(1, depth)
        ]

    def result(self):
        spot = self.spot
        value = self.quad[spot.z].astype(jnp.float32)
        for by in range(spot.sizes["z"] - 1):
            value = value + self.by_z[by].astype(jnp.float32)
        return value


class Finish:
    def __init__(self, mover, summed, arrived):
        self.k = mover.spot.k
        self.summed, self.arrived = summed, arrived
        rows = arrived.shape[0]
        self.rows = rows
        away = summed.at[pl.ds(pl.multiple_of((1 - self.k) * rows, rows), rows)]
        self.copies = [mover.copy(away, arrived, "k")]

    @staticmethod
    def scratch(rows, width):
        return [pltpu.VMEM((rows, width), jnp.float32), pltpu.VMEM((rows // 2, width), jnp.float32)]

    def write(self, out, columns=slice(None)):
        rows = self.rows
        kept = pl.ds(pl.multiple_of(self.k * rows, rows), rows)
        out[self.k, :, columns] = self.summed[kept, :]
        out[1 - self.k, :, columns] = self.arrived[...]


def core_halves(grad, k, width, first=0, size=None):
    size = width if size is None else size
    every = slice(None)
    return [
        grad.at[every, every, every, every, span(half * width + first, size)]
        for half in (k, 1 - k)
    ]


all_axes = ("k", "c", "y", "z")


def params(number, megabytes):
    return pltpu.CompilerParams(
        collective_id=number, has_side_effects=True, vmem_limit_bytes=megabytes << 20
    )


def cut_of(width):
    return max(5 * width // 8 // 128, 1) * 128


def low_shape(*dims):
    return jax.ShapeDtypeStruct(dims, low)


def begin_kernel(sizes, *refs):
    refs = Refs(refs)
    joint_weight, table, mixing_weight, expand_weight, shrink_weight = refs.take(5)
    rows_in, upstream = refs.take(2)
    joint, tables, mixing_quad, expand_quad, shrink_quad, far_rows, far_upstream = refs.take(7)
    next_expand, next_shrink = refs.take(2)
    joint_quad, table_quad, sems, joint_halves, mixing_halves, expand_halves, shrink = refs.take(7)
    spot = Spot(sizes)
    mover = Mover(spot, sems)
    width = joint_halves.shape[2]
    joint_first = first_rows(mover, joint_halves, joint_quad)
    rows = table.shape[0]
    spread = table_quad.at[spot.z, pl.ds(pl.multiple_of(spot.k * rows, rows), rows)]
    joint_first += [mover.local(table, spread), mover.copy(table, spread, "k")]
    later_first = first_rows(mover, mixing_halves, mixing_quad)
    later_first += first_rows(mover, expand_halves, expand_quad)
    later_first += [mover.local(shrink, shrink_quad.at[spot.z])]
    part = width // 2
    chunks = [joint_quad.at[:, :, pl.ds(first, part)] for first in (0, part)]
    now = [Deep(mover, chunk).copies for chunk in chunks]
    thin_deep = Deep(mover, table_quad).copies
    later = [Deep(mover, quad).copies for quad in (mixing_quad, shrink_quad, expand_quad)]
    jobs = [
        Near(mover, chunk, joint, spot.k * width + number * part, part)
        for number, chunk in enumerate(chunks)
    ]
    thin = Near(mover, table_quad, tables, 0, table.shape[1], core=False)
    rows_copies = [
        mover.copy(rows_in.at[1 - spot.c], far_rows, "c"),
        mover.copy(upstream.at[1 - spot.c, block_rows(0)], far_upstream, "c"),
    ]
    pairs = width // (3 * PAIR)
    for core in range(2):
        for pair in range(pairs):
            for third in range(3):
                source = ((third * 2 + core) * pairs + pair) * PAIR
                target = (pair * 3 + third) * PAIR
                joint_halves[core, :, target : target + PAIR] = joint_weight[
                    :, source : source + PAIR
                ].astype(low)
    spot.meet(all_axes)
    start(joint_first)
    start(rows_copies[:1])
    wait(joint_first)
    start(now[0] + thin_deep)
    half = mixing_halves.shape[2]
    for core in range(2):
        mixing_halves[core] = mixing_weight[:, core * half : (core + 1) * half].astype(low)
    sub = shrink.shape[0]
    shrink[...] = shrink_weight[:sub, :].astype(low)
    next_shrink[...] = shrink_weight[sub:, :].astype(low)
    lane = lax.broadcasted_iota(jnp.int32, (1, PAIR), 1)
    for core in range(2):
        for chip in range(0, expand_halves.shape[2] // HD, 2):
            one, two = [
                expand_weight[:, (number * 2 + core) * PAIR : (number * 2 + core + 1) * PAIR]
                for number in (chip, chip + 1)
            ]
            columns = pl.ds(chip * HD, PAIR)
            expand_halves[core, :, columns] = jnp.where(
                lane < HD, one, pltpu.roll(two, HD, 1)
            ).astype(low)
            next_expand[core, :, columns] = jnp.where(
                lane < HD, pltpu.roll(one, HD, 1), two
            ).astype(low)
    start(later_first)
    wait(now[0] + thin_deep)
    start(now[1])
    start(thin.near + jobs[0].near + jobs[0].core[0])
    wait(now[1])
    start(jobs[1].near + jobs[1].core[0])
    wait(later_first)
    for copies in later:
        start(copies)
    wait(thin.near + jobs[0].near)
    start(thin.far + jobs[0].far + jobs[0].core[1])
    wait(jobs[1].near)
    start(jobs[1].far + jobs[1].core[1])
    start(rows_copies[1:])
    wait(thin.far)
    for job in jobs:
        job.close()
    for copies in later:
        wait(copies)
    for job in jobs:
        job.close_core()
    wait(rows_copies)


def begin(sizes, joint_weight, table, mixing_weight, expand_weight, shrink_weight, rows_in, upstream):
    lead = (sizes["c"], sizes["z"], sizes["y"])
    own, model = mixing_weight.shape
    depth, rows = sizes["z"], 2 * own
    width, half, grown = 3 * model // 2, model // 2, expand_weight.shape[1] // 4
    sub = shrink_weight.shape[0] // 2
    return pl.pallas_call(
        functools.partial(begin_kernel, sizes),
        in_specs=[whole_vmem] * 5 + [any_place] * 2,
        out_specs=[any_place] * 7 + [whole_vmem] * 2,
        out_shape=[
            low_shape(*lead, rows, 2 * width),
            low_shape(*lead, rows, table.shape[1]),
            low_shape(depth, rows, half),
            low_shape(depth, rows, grown),
            low_shape(depth, sub, model),
            low_shape(*rows_in.shape[1:]),
            low_shape(BLK, model),
            low_shape(2, own, grown),
            low_shape(sub, model),
        ],
        scratch_shapes=[
            pltpu.VMEM((depth, rows, width), low),
            pltpu.VMEM((depth, rows, table.shape[1]), low),
            pltpu.SemaphoreType.DMA((2, 64)),
            pltpu.VMEM((2, own, width), low),
            pltpu.VMEM((2, own, half), low),
            pltpu.VMEM((2, own, grown), low),
            pltpu.VMEM((sub, model), low),
        ],
        compiler_params=params(1, 60),
        cost_estimate=small_cost,
        name="begin",
    )(joint_weight, table, mixing_weight, expand_weight, shrink_weight, rows_in, upstream)


def normal_rows(rows):
    centered = rows - jnp.mean(rows, axis=-1, keepdims=True)
    inverse = lax.rsqrt(jnp.mean(centered * centered, axis=-1, keepdims=True) + norm_eps)
    return centered * inverse, inverse


def norm_pull(upstream, normal, inverse, gain):
    scaled = upstream * gain
    inner = jnp.mean(scaled, axis=-1, keepdims=True)
    along = jnp.mean(scaled * normal, axis=-1, keepdims=True)
    return inverse * (scaled - inner - normal * along)


def chosen_block(number, source):
    chosen = jnp.full((1, source.shape[1]), number, jnp.int32)
    value = source[block_rows(0), :].astype(jnp.float32)
    for other in range(1, source.shape[0] // BLK):
        value = jnp.where(chosen == other, source[block_rows(other), :].astype(jnp.float32), value)
    return value


def attend_kernel(sizes, blocks, *refs):
    refs = Refs(refs)
    place_ref, rows_in, far_rows, joint, norm_ref, shift_ref, upstream = refs.take(7)
    mixing_quad, expand_quad, shrink_quad, expand_halves, shrink = refs.take(5)
    o_ref, lse_ref, rows_ref, low_ref, projected_ref = refs.take(5)
    mixing, expand, shrunk, next_expand, next_shrink, far_upstream = refs.take(6)
    sems, rows_all, joint_all, projected = refs.take(4)
    spot = Spot(sizes)
    mover = Mover(spot, sems)
    k = spot.k
    half, grown, width = mixing_quad.shape[-1], expand_quad.shape[-1], shrink_quad.shape[-1]
    loads = [
        mover.local(rows_in.at[spot.c], rows_all.at[pl.ds(0, 2 * BLK)]),
        mover.local(far_rows, rows_all.at[pl.ds(2 * BLK, 2 * BLK)]),
        mover.local(joint, joint_all),
    ]
    jobs = [
        Near(mover, mixing_quad, mixing, k * half, cut_of(half)),
        Near(mover, shrink_quad, shrunk.at[k], 0, cut_of(width)),
        Near(mover, expand_quad, expand, k * grown, cut_of(grown)),
    ]
    next_first = first_rows(mover, expand_halves, next_expand)
    next_first += [mover.local(shrink, next_shrink.at[spot.z])]
    deep = Deep(mover, next_expand).copies + Deep(mover, next_shrink).copies
    upstream_copy = [mover.copy(upstream.at[1 - spot.c, block_rows(1)], far_upstream, "c")]

    def open_all():
        start(loads)
        spot.meet(all_axes)
        start(next_first)
        for job in jobs:
            start(job.near + job.core[0])
        wait(loads)

    def next_deep():
        wait(next_first)
        start(deep)
        start(upstream_copy)

    def far(job):
        wait(job.near)
        start(job.far + job.core[1])

    def close_all():
        for job in jobs:
            job.close()
        wait(deep)
        for job in jobs:
            job.close_core()
        wait(upstream_copy)

    step = pl.program_id(0)
    between = hooks(
        step,
        [
            (0, 0, open_all),
            (2, 0, next_deep),
            (9, 0, lambda: far(jobs[0])),
            (10, 2, lambda: far(jobs[1])),
            (10, 3, lambda: far(jobs[2])),
        ],
    )
    between(0)

    @pl.when(step < blocks)
    def _():
        value = chosen_block(place_ref[step], rows_all)
        rows_ref[...] = value.astype(low)
        normal, _ = normal_rows(value)
        normed = (normal * norm_ref[0:1, :] + norm_ref[1:2, :]).astype(low)
        low_ref[...] = normed
        rows = pl.ds(pl.multiple_of(step * BLK, BLK), BLK)
        for first in range(0, joint_all.shape[1], 512):
            columns = pl.ds(first, 512)
            projected[rows, columns] = (nn(normed, joint_all[:, columns]) + shift_ref[:, columns]).astype(low)

    @pl.when(step >= blocks)
    def _():
        columns = span((step - blocks) * 3 * PAIR, 3 * PAIR)
        projected_ref[...] = projected[:, columns]
        attend_pair(blocks, projected_ref, o_ref, lse_ref, lambda block: block > 0 and between(block))

    pl.when(step == pl.num_programs(0) - 1)(close_all)


def attend(sizes, place, rows_in, far_rows, joint, norm, shift, upstream, quads, halves, shrink):
    model = rows_in.shape[2]
    blocks = place.shape[0]
    tokens = blocks * BLK
    pairs = model // PAIR
    lead = (sizes["c"], sizes["z"], sizes["y"])
    depth, rows, half = quads[0].shape
    grown, full = quads[1].shape[2], quads[2].shape[2]
    by_rows = pl.BlockSpec((BLK, model), lambda g: (jnp.minimum(g, blocks - 1), 0))

    def pair(g):
        return jnp.maximum(g - blocks, 0)

    return pl.pallas_call(
        functools.partial(attend_kernel, sizes, blocks),
        grid=(blocks + pairs,),
        in_specs=[pl.BlockSpec(memory_space=pltpu.SMEM)]
        + [any_place] * 3
        + [whole_vmem] * 2
        + [any_place]
        + [whole_vmem] * 5,
        out_specs=[
            pl.BlockSpec((tokens, PAIR), lambda g: (0, pair(g))),
            pl.BlockSpec((None, 8, tokens), lambda g: (pair(g), 0, 0)),
            by_rows,
            by_rows,
            pl.BlockSpec((tokens, 3 * PAIR), lambda g: (0, pair(g))),
        ]
        + [any_place] * 6,
        out_shape=[
            low_shape(tokens, model),
            jax.ShapeDtypeStruct((pairs, 8, tokens), jnp.float32),
            low_shape(tokens, model),
            low_shape(tokens, model),
            low_shape(tokens, 3 * model),
            low_shape(*lead, rows, 2 * half),
            low_shape(*lead, rows, 2 * grown),
            low_shape(2, *lead, rows, full),
            low_shape(depth, rows, grown),
            low_shape(depth, rows, full),
            low_shape(BLK, model),
        ],
        scratch_shapes=[
            pltpu.SemaphoreType.DMA((2, 64)),
            pltpu.VMEM((tokens, model), low),
            pltpu.VMEM((model, 3 * model), low),
            pltpu.VMEM((tokens, 3 * model), low),
        ],
        compiler_params=params(2, 56),
        cost_estimate=small_cost,
        name="attend",
    )(place, rows_in, far_rows, joint, norm, shift, upstream, *quads, halves, shrink)


def mlp_tile(rows_step, c_ref, dy_ref, we_ref, ws_ref, be_ref, outs, scratch, between):
    y_ref, dc_ref, gwe_ref, gws_ref, gbe_ref = outs
    turned, act_all, du_all = scratch
    tokens = c_ref.shape[0]
    we, ws = we_ref[...], ws_ref[...]
    total = None
    for part in range(tokens // rows_step):
        between(part)
        rows = pl.ds(part * rows_step, rows_step)
        hidden = nn(c_ref[rows, :], we) + be_ref[...]
        squared = hidden * hidden
        bent = jnp.tanh(gelu_root * hidden * (1.0 + gelu_cubic * squared))
        gate = 0.5 + 0.5 * bent
        act = (hidden * gate).astype(low)
        slope = gate + (0.5 * gelu_root) * hidden * (1.0 - bent * bent) * (
            1.0 + (3 * gelu_cubic) * squared
        )
        du = (nt(dy_ref[rows, :], ws) * slope).astype(low)
        act_all[rows, :] = act
        du_all[rows, :] = du
        y_ref[rows, :] += nn(act, ws)
        dc_ref[rows, :] += nt(du, we)
        added = jnp.sum(du.astype(jnp.float32), axis=0, keepdims=True)
        total = added if total is None else total + added
    gbe_ref[...] = total
    gwe_ref[...] = nn(turned[...], du_all[...]).astype(gwe_ref.dtype)
    gws_ref[...] = outer_sum(act_all[...], dy_ref[...]).astype(gws_ref.dtype)


def mlp_parts(tokens, width, hidden, tile):
    whole = pl.BlockSpec((tokens, width), lambda t: (0, 0), pipeline_mode=pl.Buffered(1))
    down = pl.BlockSpec((width, tile), lambda t: (0, t))
    across = pl.BlockSpec((tile, width), lambda t: (t, 0))
    thin = pl.BlockSpec((1, tile), lambda t: (0, t))
    return (
        [whole, whole, down, across, thin],
        [whole, whole, down, across, thin],
        [
            jax.ShapeDtypeStruct((tokens, width), jnp.float32),
            jax.ShapeDtypeStruct((tokens, width), jnp.float32),
            low_shape(width, hidden),
            low_shape(hidden, width),
            jax.ShapeDtypeStruct((1, hidden), jnp.float32),
        ],
        [
            pltpu.VMEM((width, tokens), low),
            pltpu.VMEM((tokens, tile), low),
            pltpu.VMEM((tokens, tile), low),
        ],
    )


def mlp_plain_kernel(rows_step, *refs):
    refs = Refs(refs)
    c_ref, dy_ref, we_ref, ws_ref, be_ref, y_in, dc_in = refs.take(7)
    outs, scratch, (sem,) = refs.take(5), refs.take(3), refs.take(1)

    @pl.when(pl.program_id(0) == 0)
    def _():
        scratch[0][...] = jnp.transpose(c_ref[...])
        copies = [
            pltpu.make_async_copy(y_in, outs[0], sem.at[0]),
            pltpu.make_async_copy(dc_in, outs[1], sem.at[1]),
        ]
        start(copies)
        wait(copies)

    mlp_tile(rows_step, c_ref, dy_ref, we_ref, ws_ref, be_ref, outs, scratch, lambda part: None)


def mlp(c, dy, we, ws, be, before, tile=512, rows_step=512):
    in_specs, out_specs, out_shape, scratch = mlp_parts(*c.shape, we.shape[1], tile)
    return pl.pallas_call(
        functools.partial(mlp_plain_kernel, rows_step),
        grid=(we.shape[1] // tile,),
        in_specs=in_specs + [any_place] * 2,
        out_specs=out_specs,
        out_shape=out_shape,
        scratch_shapes=scratch + [pltpu.SemaphoreType.DMA((2,))],
        compiler_params=pltpu.CompilerParams(vmem_limit_bytes=56 << 20),
        cost_estimate=small_cost,
        name="mlp",
    )(c, dy, we, ws, be, *before)


def mlp_gather_kernel(sizes, blocks, rows_step, *refs):
    refs = Refs(refs)
    place_ref, mixed_ref, rows_ref, mixing, vector_ref, we_ref, ws_ref, be_ref = refs.take(8)
    upstream, far_a, far_b, expand_quad, shrink_quad = refs.take(5)
    outs, (middle_ref, low_ref, upstream_ref) = refs.take(5), refs.take(3)
    expand, shrunk = refs.take(2)
    scratch, (sems, raw, c_all, dy_all) = refs.take(3), refs.take(4)
    spot = Spot(sizes)
    mover = Mover(spot, sems)
    grown, width = expand_quad.shape[-1], shrink_quad.shape[-1]
    loads = [
        mover.local(upstream.at[spot.c], raw.at[pl.ds(0, 2 * BLK)]),
        mover.local(far_a, raw.at[pl.ds(2 * BLK, BLK)]),
        mover.local(far_b, raw.at[pl.ds(3 * BLK, BLK)]),
    ]
    jobs = [
        Near(mover, shrink_quad, shrunk.at[spot.k], 0, width // 2),
        Near(mover, expand_quad, expand, spot.k * grown, grown // 2),
    ]

    def open_all():
        start(loads)
        spot.meet(all_axes)
        for job in jobs:
            start(job.near + job.core[0])
        wait(loads)

    def far(job):
        wait(job.near)
        start(job.far + job.core[1])

    def close_all():
        jobs[1].close()
        for job in jobs:
            job.close_core()

    step = pl.program_id(0)
    between = hooks(
        step,
        [
            (0, 0, open_all),
            (6, 0, lambda: far(jobs[0])),
            (6, 1, lambda: far(jobs[1])),
            (7, 1, jobs[0].close),
        ],
    )
    between(0)

    @pl.when(step < blocks)
    def _():
        rows = pl.ds(pl.multiple_of(step * BLK, BLK), BLK)
        dy = chosen_block(place_ref[step], raw).astype(low)
        upstream_ref[...] = dy
        dy_all[rows, :] = dy
        branch = nn(mixed_ref[...], mixing[...]) + vector_ref[4:5, :]
        middle = rows_ref[...].astype(jnp.float32) + branch
        middle_ref[...] = middle
        normal, _ = normal_rows(middle)
        second = (normal * vector_ref[5:6, :] + vector_ref[6:7, :]).astype(low)
        low_ref[...] = second
        c_all[rows, :] = second
        outs[0][rows, :] = middle + vector_ref[7:8, :]
        outs[1][rows, :] = jnp.zeros(middle.shape, jnp.float32)

    @pl.when(step == blocks)
    def _():
        scratch[0][...] = jnp.transpose(c_all[...])

    @pl.when(step >= blocks)
    def _():
        mlp_tile(
            rows_step, c_all, dy_all, we_ref, ws_ref, be_ref, outs, scratch,
            lambda part: part > 0 and between(part),
        )

    pl.when(step == pl.num_programs(0) - 1)(close_all)


def mlp_gather(sizes, place, mixed, rows_in, mixing, vectors, we, ws, be, upstream, far_a, far_b, quads, tile=512, rows_step=512):
    tokens, model = mixed.shape
    blocks = place.shape[0]
    hidden = we.shape[1]
    lead = (sizes["c"], sizes["z"], sizes["y"])
    rows, grown, full = quads[0].shape[1], quads[0].shape[2], quads[1].shape[2]
    by_rows = pl.BlockSpec((BLK, model), lambda g: (jnp.minimum(g, blocks - 1), 0))
    whole = pl.BlockSpec((tokens, model), lambda g: (0, 0), pipeline_mode=pl.Buffered(1))

    def at(g):
        return jnp.maximum(g - blocks, 0)

    down = pl.BlockSpec((model, tile), lambda g: (0, at(g)))
    across = pl.BlockSpec((tile, model), lambda g: (at(g), 0))
    thin = pl.BlockSpec((1, tile), lambda g: (0, at(g)))
    _, _, out_shape, scratch = mlp_parts(tokens, model, hidden, tile)
    return pl.pallas_call(
        functools.partial(mlp_gather_kernel, sizes, blocks, rows_step),
        grid=(blocks + hidden // tile,),
        in_specs=[pl.BlockSpec(memory_space=pltpu.SMEM), by_rows, by_rows, whole_vmem, whole_vmem]
        + [down, across, thin]
        + [any_place] * 3
        + [whole_vmem] * 2,
        out_specs=[whole, whole, down, across, thin] + [by_rows] * 3 + [any_place] * 2,
        out_shape=out_shape
        + [
            jax.ShapeDtypeStruct((tokens, model), jnp.float32),
            low_shape(tokens, model),
            low_shape(tokens, model),
            low_shape(*lead, rows, 2 * grown),
            low_shape(2, *lead, rows, full),
        ],
        scratch_shapes=scratch
        + [pltpu.SemaphoreType.DMA((2, 32))]
        + [pltpu.VMEM((tokens, model), low)] * 3,
        compiler_params=params(3, 60),
        cost_estimate=small_cost,
        name="mlp_gather",
    )(place, mixed, rows_in, mixing, vectors, we, ws, be, upstream, far_a, far_b, *quads)


def mlp_reduce_kernel(sizes, rows_step, *refs):
    refs = Refs(refs)
    back_ref, c_ref, dy_ref, we_ref, ws_ref, be_ref, y_in, dc_in, expand, shrink = refs.take(10)
    outs = refs.take(4)
    expand_quad, shrink_quad, kept, sent = refs.take(4)
    scratch, (sems, y_all) = refs.take(3), refs.take(2)
    outs = [y_all] + outs
    spot = Spot(sizes)
    mover = Mover(spot, sems)
    grown, width = expand_quad.shape[-1], shrink_quad.shape[-1]
    loads = [mover.local(y_in, y_all), mover.local(dc_in, outs[1])]
    jobs = [
        ReduceNear(
            mover, shrink.at[spot.k], shrink.at[1 - spot.k], width // 2, shrink_quad, refs.take(6)
        ),
        ReduceNear(
            mover, *core_halves(expand, spot.k, grown), grown // 2, expand_quad, refs.take(6)
        ),
    ]

    def open_all():
        start(loads)
        spot.meet(all_axes)
        start(jobs[0].first)
        scratch[0][...] = jnp.transpose(c_ref[...])
        wait(loads)

    def shrink_near():
        start(jobs[1].first)
        jobs[0].go_near()

    def close_all():
        for place in range(2):
            kept[block_rows(place), :] = chosen_block(back_ref[place], y_all).astype(low)
            sent[block_rows(place), :] = chosen_block(back_ref[2 + place], y_all).astype(low)
        for job in jobs:
            job.close()

    step = pl.program_id(0)
    schedule = [
        (0, 0, open_all),
        (0, 1, shrink_near),
        (1, 0, jobs[1].go_near),
        (3, 0, jobs[0].go_far),
        (3, 1, jobs[1].go_far),
    ]
    mlp_tile(
        rows_step, c_ref, dy_ref, we_ref, ws_ref, be_ref, outs, scratch, hooks(step, schedule)
    )
    pl.when(step == pl.num_programs(0) - 1)(close_all)


def mlp_reduce(sizes, back, c, dy, we, ws, be, before, grads, tile=512, rows_step=512):
    tokens, model = c.shape
    in_specs, out_specs, out_shape, scratch = mlp_parts(tokens, model, we.shape[1], tile)
    expand, shrink = grads
    depth, rows = sizes["z"], expand.shape[3]
    grown, full = expand.shape[-1] // 2, shrink.shape[-1]
    scratch = scratch + [pltpu.SemaphoreType.DMA((2, 16)), pltpu.VMEM((tokens, model), jnp.float32)]
    for columns in (full, grown):
        scratch += ReduceNear.scratch(sizes, rows, columns, columns // 2)
    return pl.pallas_call(
        functools.partial(mlp_reduce_kernel, sizes, rows_step),
        grid=(we.shape[1] // tile,),
        in_specs=[pl.BlockSpec(memory_space=pltpu.SMEM)] + in_specs + [any_place] * 4,
        out_specs=out_specs[1:] + [whole_vmem] * 4,
        out_shape=out_shape[1:]
        + [low_shape(depth, rows, grown), low_shape(depth, rows, full)]
        + [low_shape(tokens // 2, model)] * 2,
        scratch_shapes=scratch,
        compiler_params=params(4, 60),
        cost_estimate=small_cost,
        name="mlp_reduce",
    )(back, c, dy, we, ws, be, *before, *grads)


def attend_back_kernel(sizes, blocks, *refs):
    refs = Refs(refs)
    pulled_ref, middle_ref, upstream_ref, mixed, mixing, gain_ref = refs.take(6)
    projected, lse_ref, expand, shrink, done_expand, done_shrink, sent = refs.take(7)
    back_ref, grad_ref, sums_ref, mixing_quad, expand_quad, shrink_quad = refs.take(6)
    expand_out, shrink_out, far_out = refs.take(3)
    turned, key_sum, value_sum, sems, branch_all, mixed_grad, theirs = refs.take(7)
    spot = Spot(sizes)
    mover = Mover(spot, sems)
    k = spot.k
    half, grown, width = mixing_quad.shape[-1], expand_quad.shape[-1], shrink_quad.shape[-1]
    jobs = [
        ReduceNear(mover, shrink.at[k], shrink.at[1 - k], width // 2, shrink_quad, refs.take(6)),
        ReduceNear(mover, *core_halves(expand, k, grown), grown // 2, expand_quad, refs.take(6)),
        ReduceNear(mover, None, theirs, half // 2, mixing_quad, refs.take(6)),
    ]
    deep = [
        ReduceDeep(mover, done_expand, *refs.take(1)),
        ReduceDeep(mover, done_shrink, *refs.take(1)),
    ]
    ending = Finish(mover, *refs.take(2))
    rows_copy = [mover.copy(sent.at[block_rows(0)], far_out, "c")]

    def open_all():
        spot.meet(all_axes)
        for job in jobs[:2]:
            start(job.first)
        start(rows_copy)
        for job in deep:
            start(job.copies)

    def finish():
        wait(deep[0].copies)
        ending.summed[...] = deep[0].result()
        start(ending.copies)
        wait(deep[1].copies)
        shrink_out[...] = deep[1].result()

    def close_all():
        wait(ending.copies)
        ending.write(expand_out)
        jobs[1].close()
        jobs[2].close()
        wait(rows_copy)

    step = pl.program_id(0)
    between = hooks(
        step,
        [
            (0, 0, open_all),
            (3, 0, jobs[0].go_near),
            (4, 0, jobs[1].go_near),
            (4, 2, jobs[2].go_near),
            (7, 0, finish),
            (10, 0, jobs[0].go_far),
            (10, 2, jobs[1].go_far),
            (11, 0, jobs[2].go_far),
            (11, 3, jobs[0].close),
        ],
    )
    between(0)

    @pl.when(step < blocks)
    def _():
        rows = pl.ds(pl.multiple_of(step * BLK, BLK), BLK)
        pulled = pulled_ref[...]
        upstream = upstream_ref[...].astype(jnp.float32)
        normal, inverse = normal_rows(middle_ref[...])
        total = upstream + norm_pull(pulled, normal, inverse, gain_ref[...])
        grad_ref[...] = total
        branch = total.astype(low)
        branch_all[rows, :] = branch
        mixed_grad[rows, :] = nt(branch, mixing[...]).astype(low)

        @pl.when(step == 0)
        def _():
            sums_ref[...] = jnp.zeros_like(sums_ref)

        for row, value in enumerate((branch.astype(jnp.float32), pulled * normal, pulled, upstream)):
            sums_ref[row : row + 1, :] += jnp.sum(value, axis=0, keepdims=True)

    @pl.when(step == blocks - 1)
    def _():
        across = jnp.transpose(mixed[...])
        for core, target in ((1 - k, theirs), (k, jobs[2].total)):
            piece = nn(across, branch_all[:, span(core * half, half)]).astype(low)
            target[...] = piece.reshape(target.shape)
        start(jobs[2].first)

    @pl.when(step >= blocks)
    def _():
        columns = span((step - blocks) * PAIR, PAIR)
        attend_back_pair(
            blocks, projected, mixed_grad.at[:, columns], lse_ref, back_ref, turned, key_sum,
            value_sum, lambda block: block > 0 and between(block),
        )

    pl.when(step == pl.num_programs(0) - 1)(close_all)


def attend_back(sizes, pulled, middle, upstream, mixed, mixing, gain, projected, lse, grads, quads, sent):
    tokens, model = upstream.shape
    pairs = model // PAIR
    blocks = tokens // BLK
    expand, shrink = grads
    depth, rows = sizes["z"], expand.shape[3]
    lead = (sizes["c"], sizes["z"], sizes["y"])
    half, grown, full = model // 2, expand.shape[-1] // 2, shrink.shape[-1]
    by_rows = pl.BlockSpec((BLK, model), lambda g: (jnp.minimum(g, blocks - 1), 0))

    def pair(g):
        return jnp.maximum(g - blocks, 0)

    triple = pl.BlockSpec((tokens, 3 * PAIR), lambda g: (0, pair(g)))
    scratch = [
        pltpu.VMEM((PAIR, tokens), low),
        pltpu.VMEM((tokens, PAIR), jnp.float32),
        pltpu.VMEM((tokens, PAIR), jnp.float32),
        pltpu.SemaphoreType.DMA((2, 32)),
        pltpu.VMEM((tokens, model), low),
        pltpu.VMEM((tokens, model), low),
        pltpu.VMEM((*lead, rows, half), low),
    ]
    for columns in (full, grown, half):
        scratch += ReduceNear.scratch(sizes, rows, columns, columns // 2)
    for columns in (grown, full):
        scratch += [pltpu.VMEM((depth - 1, rows, columns), low)]
    scratch += Finish.scratch(rows, grown)
    return pl.pallas_call(
        functools.partial(attend_back_kernel, sizes, blocks),
        grid=(blocks + pairs,),
        in_specs=[by_rows] * 3
        + [whole_vmem] * 3
        + [triple, pl.BlockSpec((None, 8, tokens), lambda g: (pair(g), 0, 0))]
        + [any_place] * 2
        + [whole_vmem] * 2
        + [any_place],
        out_specs=[triple, by_rows] + [whole_vmem] * 6 + [any_place],
        out_shape=[
            low_shape(*projected.shape),
            jax.ShapeDtypeStruct((tokens, model), jnp.float32),
            jax.ShapeDtypeStruct((8, model), jnp.float32),
            low_shape(depth, rows, half),
            low_shape(depth, rows, grown),
            low_shape(depth, rows, full),
            jax.ShapeDtypeStruct((2, rows // 2, grown), jnp.float32),
            jax.ShapeDtypeStruct((rows, full), jnp.float32),
            low_shape(BLK, model),
        ],
        scratch_shapes=scratch,
        compiler_params=params(5, 60),
        cost_estimate=small_cost,
        name="attend_back",
    )(pulled, middle, upstream, mixed, mixing, gain, projected, lse, *grads, *quads, sent)


def end_kernel(sizes, *refs):
    refs = Refs(refs)
    back_ref, back_far, low_far, joint_far, rows_far, middle_far = refs.take(6)
    gain_ref, vector, mixing_quad, expand_quad, shrink_quad, sent_out = refs.take(6)
    out, vector_out, mixing_out, expand_out, shrink_out, kept = refs.take(6)
    arrived_rows, far_out = refs.take(2)
    sems, steps, arrived = refs.take(3)
    grads, low_rows, turned, joint, rows_in, middle, sent = refs.take(7)
    spot = Spot(sizes)
    mover = Mover(spot, sems)
    width = joint.shape[-1] // 2
    part = width // 2
    tile = 256
    loads = [
        mover.local(far, near)
        for far, near in (
            (back_far, grads),
            (low_far, low_rows),
            (joint_far, joint),
            (rows_far, rows_in),
            (middle_far, middle),
        )
    ]
    jobs, deeps, ends, others_half = [], [], [], []
    for number in range(2):
        theirs, quad = refs.take(2)
        others_half.append(theirs)
        jobs.append(ReduceNear(mover, None, theirs, part // 2, quad, refs.take(6)))
        deeps.append(ReduceDeep(mover, quad, *refs.take(1)))
        ends.append(Finish(mover, *refs.take(2)))
    others = [
        ReduceDeep(mover, quad, *refs.take(1))
        for quad in (mixing_quad, expand_quad, shrink_quad)
    ]
    other_ends = [Finish(mover, *refs.take(2)) for _ in range(2)]
    hops = [
        mover.copy(steps.at[number], arrived.at[number], name)
        for number, name in enumerate(("k", "c", "y"))
    ]
    spread = [
        mover.copy(steps.at[3], arrived.at[2 + by], "z", by) for by in range(1, sizes["z"])
    ]
    rows_copy = mover.copy(sent, arrived_rows, "c")
    out_copy = mover.copy(sent_out.at[block_rows(1)], far_out, "c")

    def gradient(core, number, target):
        @pl.loop(0, part // tile)
        def _(t):
            columns = span(core * width + number * part + t * tile, tile)
            piece = nn(turned[...], grads[:, columns]).astype(low)
            target[..., span(t * tile, tile)] = piece.reshape(*target.shape[:-1], tile)

    sums = {}

    def pull_block(number):
        rows = block_rows(number)
        pulled = grads[rows, :]
        upstream = nt(pulled, joint[...])
        normal, inverse = normal_rows(rows_in[rows, :].astype(jnp.float32))
        middle[rows, :] += norm_pull(upstream, normal, inverse, gain_ref[...])
        for name, value in (
            ("gain", upstream * normal),
            ("shift", upstream),
            ("back", pulled.astype(jnp.float32)),
        ):
            value = jnp.sum(value, axis=0, keepdims=True)
            sums[name] = sums[name] + value if name in sums else value

    def hop(number):
        wait([hops[number]])
        steps[number + 1] = steps[number] + arrived[number]
        start([hops[number + 1]] if number < 2 else spread)

    start(loads[:2])
    spot.meet(all_axes)
    start([out_copy])
    for job in others:
        start(job.copies)
    wait(loads[:2])
    start(loads[2:])
    turned[...] = jnp.transpose(low_rows[...])
    for number, job in enumerate(jobs):
        gradient(1 - spot.k, number, others_half[number])
        start(job.first)
        gradient(spot.k, number, job.total)
        job.go_near()
    wait(loads[2:])
    pull_block(0)
    pull_block(1)
    jobs[0].go_far()
    pull_block(2)
    jobs[1].go_far()
    pull_block(3)
    steps[0] = vector[...]
    steps[0, 0:1, :] = sums["gain"]
    steps[0, 1:2, :] = sums["shift"]
    for pair in range(H // 2):
        for row, third in ((2, 0), (3, 2)):
            steps[0, row : row + 1, pair * PAIR : (pair + 1) * PAIR] = sums["back"][
                :, (3 * pair + third) * PAIR : (3 * pair + third + 1) * PAIR
            ]
    start(hops[:1])
    for place in range(2):
        sent[block_rows(place), :] = chosen_block(back_ref[2 + place], middle).astype(low)
    hop(0)
    start([rows_copy])
    jobs[0].close()
    start(deeps[0].copies)
    for place in range(2):
        kept[block_rows(place), :] = chosen_block(back_ref[place], middle)
    for job, ending in zip(others, other_ends):
        wait(job.copies)
        ending.summed[...] = job.result()
        start(ending.copies)
    wait(others[2].copies)
    shrink_out[...] = others[2].result()
    jobs[1].close()
    start(deeps[1].copies)
    hop(1)
    hop(2)
    for ending, target in zip(other_ends, (mixing_out, expand_out)):
        wait(ending.copies)
        ending.write(target)
    for deep, ending in zip(deeps, ends):
        wait(deep.copies)
        ending.summed[...] = deep.result()
        start(ending.copies)
    wait(spread)
    total = steps[3]
    for by in range(1, sizes["z"]):
        total = total + arrived[2 + by]
    vector_out[...] = total
    for number, ending in enumerate(ends):
        wait(ending.copies)
        ending.write(out, pl.ds(number * part, part))
    wait([rows_copy, out_copy])


def end(sizes, back, joint_back, first_low, joint, rows_in, middle_grad, gain, vector, quads, sent):
    tokens, model = rows_in.shape
    width = joint.shape[1] // 2
    lead = (sizes["c"], sizes["z"], sizes["y"])
    depth = sizes["z"]
    rows = model // (lead[0] * lead[1] * lead[2])
    part = width // 2
    half, grown, full = [quad.shape[-1] for quad in quads]
    scratch = [
        pltpu.SemaphoreType.DMA((2, 48)),
        pltpu.VMEM((4, *vector.shape), jnp.float32),
        pltpu.VMEM((2 + depth, *vector.shape), jnp.float32),
        pltpu.VMEM(joint_back.shape, low),
        pltpu.VMEM(first_low.shape, low),
        pltpu.VMEM(first_low.shape[::-1], low),
        pltpu.VMEM(joint.shape, low),
        pltpu.VMEM(rows_in.shape, low),
        pltpu.VMEM(middle_grad.shape, jnp.float32),
        pltpu.VMEM((tokens // 2, model), low),
    ]
    for number in range(2):
        scratch += [pltpu.VMEM((*lead, rows, part), low), pltpu.VMEM((depth, rows, part), low)]
        scratch += ReduceNear.scratch(sizes, rows, part, part // 2)
        scratch += [pltpu.VMEM((depth - 1, rows, part), low)]
        scratch += Finish.scratch(rows, part)
    scratch += [pltpu.VMEM((depth - 1, rows, columns), low) for columns in (half, grown, full)]
    for columns in (half, grown):
        scratch += Finish.scratch(rows, columns)
    own = rows // 2
    shapes = [(2, own, width), vector.shape, (2, own, half), (2, own, grown), (rows, full)]
    shapes.append((tokens // 2, model))
    return pl.pallas_call(
        functools.partial(end_kernel, sizes),
        in_specs=[pl.BlockSpec(memory_space=pltpu.SMEM)]
        + [any_place] * 5
        + [whole_vmem] * 5
        + [any_place],
        out_specs=[whole_vmem] * 6 + [any_place] * 2,
        out_shape=[jax.ShapeDtypeStruct(shape, jnp.float32) for shape in shapes]
        + [low_shape(tokens // 2, model), low_shape(BLK, model)],
        scratch_shapes=scratch,
        compiler_params=params(6, 60),
        cost_estimate=small_cost,
        name="end",
    )(back, joint_back, first_low, joint, rows_in, middle_grad, gain, vector, *quads, sent)


def last_kernel(ctx_ref, *refs):
    refs = Refs(refs)
    joint_part, mixing_part, expand_a, expand_b, shrink_a, shrink_b = refs.take(6)
    kept_grad, far_grad, kept_out, far_one, far_two = refs.take(5)
    states = [refs.take(3) for _ in range(4)]
    grad_out, block_out = refs.take(2)
    news = [refs.take(4) for _ in range(4)]
    here = ctx_ref[0]
    grad_out[here] = kept_grad[...]
    grad_out[1 - here] = far_grad[...].astype(jnp.float32)
    block_out[here] = kept_out[...]
    block_out[1 - here, :BLK, :] = far_one[...]
    block_out[1 - here, BLK:, :] = far_two[...]

    def update(number, where, gradient):
        weight, first, second = [ref[where] for ref in states[number]]
        results = adam_update(weight, first, second, gradient, 0.05, 0.1)
        for ref, value in zip(news[number], (*results, results[0].astype(low))):
            ref[where] = value

    every = slice(None)
    pairs = joint_part.shape[2] // (3 * PAIR)
    for core in range(2):
        for pair in range(pairs):
            for third in range(3):
                first = ((third * 2 + core) * pairs + pair) * PAIR
                source = (pair * 3 + third) * PAIR
                update(
                    0,
                    (every, pl.ds(first, PAIR)),
                    joint_part[core, :, source : source + PAIR],
                )
        half = mixing_part.shape[2]
        update(1, (every, pl.ds(core * half, half)), mixing_part[core])
        lane = lax.broadcasted_iota(jnp.int32, (1, PAIR), 1)
        for chip in range(0, expand_a.shape[2] // HD, 2):
            a = expand_a[core, :, chip * HD : chip * HD + PAIR]
            b = expand_b[core, :, chip * HD : chip * HD + PAIR]
            even = jnp.where(lane < HD, a, pltpu.roll(b, HD, 1))
            odd = jnp.where(lane < HD, pltpu.roll(a, HD, 1), b)
            for number, value in ((chip, even), (chip + 1, odd)):
                update(2, (every, pl.ds((number * 2 + core) * PAIR, PAIR)), value)
    rows = shrink_a.shape[0]
    update(3, (pl.ds(0, rows), every), shrink_a[...])
    update(3, (pl.ds(rows, rows), every), shrink_b[...])


def last(ctx, parts, kept_grad, far_grad, kept_out, far_outs, states):
    shapes = [jax.ShapeDtypeStruct((2, *kept_grad.shape), jnp.float32), low_shape(2, *kept_out.shape)]
    for weight, _, _ in states:
        shapes += [jax.ShapeDtypeStruct(weight.shape, jnp.float32)] * 3
        shapes.append(low_shape(*weight.shape))
    flat = [array for state in states for array in state]
    return pl.pallas_call(
        last_kernel,
        in_specs=[pl.BlockSpec(memory_space=pltpu.SMEM)] + [whole_vmem] * (11 + len(flat)),
        out_specs=[whole_vmem] * len(shapes),
        out_shape=shapes,
        compiler_params=pltpu.CompilerParams(vmem_limit_bytes=56 << 20),
        cost_estimate=small_cost,
        name="last",
    )(ctx, *parts, kept_grad, far_grad, kept_out, *far_outs, *flat)


def layer_norm(values, gain_row, shift_row):
    centered = values - jnp.mean(values, axis=-1, keepdims=True)
    variance = jnp.mean(centered * centered, axis=-1, keepdims=True)
    inverse = lax.rsqrt(variance + norm_eps)
    normal_part = centered * inverse
    return (normal_part * gain_row + shift_row, normal_part, inverse)


def norm_back(upstream, normal_part, inverse, gain_row):
    scaled = upstream * gain_row
    inner_sum = jnp.mean(scaled, axis=-1, keepdims=True)
    along_sum = jnp.mean(scaled * normal_part, axis=-1, keepdims=True)
    values_grad = inverse * (scaled - inner_sum - normal_part * along_sum)
    return (values_grad, jnp.sum(upstream * normal_part, axis=0), jnp.sum(upstream, axis=0))


def adam_update(weight, moment_one, moment_two, gradient, step_rate, decay_rate):
    first_new = 0.5 * moment_one + 0.5 * gradient
    second_new = 0.5 * moment_two + 0.5 * gradient * gradient
    correct = 1.0 - 0.5**STEP
    direction = first_new / correct / (jnp.sqrt(second_new / correct) + adam_eps)
    updated = weight - step_rate * (direction + decay_rate * weight)
    return (updated, first_new, second_new)


def to_groups(matrix):
    row_count = matrix.shape[0]
    return matrix.reshape(row_count, H // group_heads, group_heads, HD).transpose(1, 0, 2, 3)


def from_groups(stacked):
    return stacked.transpose(1, 0, 2, 3).reshape(stacked.shape[1], H * HD)


def tile_scores(queries, key_rows, allowed):
    products = jnp.einsum("rgd,lgd->grl", queries, key_rows, preferred_element_type=jnp.float32)
    return jnp.where(allowed[None], products * 0.125, -1e30)


def tile_forward(queries, key_rows, value_rows, allowed):
    scores = tile_scores(queries, key_rows, allowed)
    largest = jnp.max(scores, axis=-1, keepdims=True)
    exponent = jnp.exp(scores - largest)
    row_total = jnp.sum(exponent, axis=-1, keepdims=True)
    weights = (exponent / row_total).astype(low)
    mixed = jnp.einsum("grl,lgd->rgd", weights, value_rows, preferred_element_type=jnp.float32)
    return (mixed, (largest + jnp.log(row_total))[..., 0])


def tile_backward(queries, key_rows, value_rows, allowed, logsum, upstream):
    scores = tile_scores(queries, key_rows, allowed)
    recomputed = jnp.exp(scores - logsum[..., None])
    value_grad = jnp.einsum(
        "grl,rgd->lgd", recomputed.astype(low), upstream, preferred_element_type=jnp.float32
    )
    weight_grad = jnp.einsum(
        "rgd,lgd->grl", upstream, value_rows, preferred_element_type=jnp.float32
    )
    inner_sum = jnp.sum(recomputed * weight_grad, axis=-1, keepdims=True)
    score_grad = (recomputed * (weight_grad - inner_sum)).astype(low)
    query_grad = (
        jnp.einsum("grl,lgd->rgd", score_grad, key_rows, preferred_element_type=jnp.float32) * 0.125
    )
    key_grad = (
        jnp.einsum("grl,rgd->lgd", score_grad, queries, preferred_element_type=jnp.float32) * 0.125
    )
    return (query_grad, key_grad, value_grad)


def spread_forward(queries, key_value, allowed):
    def one_sequence(pieces):
        queries, key_value, allowed = pieces
        width = queries.shape[1]
        mixed, logsum = lax.map(
            lambda triple: tile_forward(triple[0], triple[1], triple[2], allowed),
            (to_groups(queries), to_groups(key_value[:, :width]), to_groups(key_value[:, width:])),
        )
        return (from_groups(mixed), logsum)

    return lax.map(one_sequence, (queries, key_value, allowed))


def spread_backward(queries, key_value, allowed, logsum, upstream):
    def one_sequence(pieces):
        queries, key_value, allowed, logsum, upstream = pieces
        width = queries.shape[1]
        query_grad, key_grad, value_grad = lax.map(
            lambda member: tile_backward(
                member[0], member[1], member[2], allowed, member[3], member[4]
            ),
            (
                to_groups(queries),
                to_groups(key_value[:, :width]),
                to_groups(key_value[:, width:]),
                logsum,
                to_groups(upstream),
            ),
        )
        return (
            from_groups(query_grad),
            jnp.concatenate([from_groups(key_grad), from_groups(value_grad)], axis=1),
        )

    return lax.map(one_sequence, (queries, key_value, allowed, logsum, upstream))


class Slice:
    def __init__(self, ctx_size, wshard_size):
        rest = wshard_size // 2
        self.sizes = {"c": ctx_size, "z": 4, "y": rest // 4, "k": 2}

    def here(self):
        flat = lax.axis_index(axes)
        found = {}
        for name in ("k", "y", "z", "c"):
            found[name] = flat % self.sizes[name]
            flat = flat // self.sizes[name]
        return found

    def shift(self, value, name, by):
        pairs = []
        sizes = self.sizes
        for c in range(sizes["c"]):
            for z in range(sizes["z"]):
                for y in range(sizes["y"]):
                    for k in range(sizes["k"]):
                        spot = {"c": c, "z": z, "y": y, "k": k}
                        goal = dict(spot)
                        goal[name] = (spot[name] + by) % sizes[name]
                        pairs.append((self.flat(spot), self.flat(goal)))
        return lax.ppermute(value, axes, pairs)

    def flat(self, spot):
        sizes = self.sizes
        return ((spot["c"] * sizes["z"] + spot["z"]) * sizes["y"] + spot["y"]) * sizes["k"] + spot[
            "k"
        ]

    def stack(self, array, name, here):
        size = self.sizes[name]
        parts = [array] + [self.shift(array, name, by) for by in range(1, size)]
        if size > 4:
            ordered = [parts[(-place) % size] for place in range(size)]
            return jnp.roll(jnp.stack(ordered), here[name], axis=0)
        return jnp.stack(
            [lax.select_n((here[name] - place) % size, *parts) if size > 2 else
             jnp.where(here[name] == place, parts[0], parts[1]) for place in range(size)]
        )

    def reach(self, pieces, name):
        grown = list(pieces)
        for by in range(1, self.sizes[name]):
            for array, place in pieces:
                moved = dict(place)
                moved[name] = (place[name] - by) % self.sizes[name]
                grown.append((self.shift(array, name, by), moved))
        return grown

    def gather_split(self, stacked, cut, here):
        sizes = self.sizes
        depth, rows, columns = stacked.shape
        out = jnp.zeros((sizes["c"], depth, sizes["y"], rows, columns), stacked.dtype)
        for low_column, high_column, order in ((0, cut, "cy"), (cut, columns, "yc")):
            pieces = [(stacked[:, :, low_column:high_column], here)]
            for name in order:
                pieces = self.reach(pieces, name)
            for array, place in pieces:
                out = lax.dynamic_update_slice(
                    out, array[None, :, None], (place["c"], 0, place["y"], 0, low_column)
                )
        return out.reshape(-1, columns)

    def send_terms(self, value, name, place, here):
        size = self.sizes[name]
        own = lax.dynamic_index_in_dim(value, here[name], place, False)
        moved = [
            self.shift(
                lax.dynamic_index_in_dim(value, (here[name] + by) % size, place, False), name, by
            )
            for by in range(1, size)
        ]
        return own, moved

    def add_terms(self, terms, kind=low):
        own, moved = terms
        total = own.astype(jnp.float32)
        for other in moved:
            total = total + other.astype(jnp.float32)
        return total.astype(kind)

    def everywhere(self, value):
        for name in ("k", "c", "y", "z"):
            total = value
            for by in range(1, self.sizes[name]):
                total = total + self.shift(value, name, by)
            value = total
        return value


def tie(value, *others):
    return lax.optimization_barrier((value, others))[0]


def by_core(core, first, second, axis):
    return jnp.where(
        core == 0,
        jnp.concatenate([first, second], axis=axis),
        jnp.concatenate([second, first], axis=axis),
    )


def pick(core, array, axis):
    return (
        lax.dynamic_index_in_dim(array, core, axis, False),
        lax.dynamic_index_in_dim(array, 1 - core, axis, False),
    )


def gather_far(grid, here, pieces):
    joint_halves, table, mixing_halves, expand_a, expand_b, shrink_a, shrink_b = pieces
    core = here["k"]

    def chip_rows(halves):
        own, other = pick(core, halves, 0)
        return by_core(core, own, grid.shift(other, "k", 1), 0)

    def everyone(block):
        width = block.shape[1]
        return grid.gather_split(grid.stack(block, "z", here), width // 2, here)

    def both(block, axis):
        own = everyone(block)
        return by_core(core, own, grid.shift(own, "k", 1), axis)

    return (
        both(chip_rows(joint_halves), 1),
        everyone(by_core(core, table, grid.shift(table, "k", 1), 0)),
        both(chip_rows(mixing_halves), 1),
        both(chip_rows(expand_a), 1),
        both(chip_rows(expand_b), 1),
        both(shrink_a, 0),
        both(shrink_b, 0),
    )


def reduce_far(grid, here, gradient, by_rows):
    core = here["k"]
    sizes = grid.sizes
    if by_rows:
        own, other = pick(core, gradient.reshape(2, -1, gradient.shape[1]), 0)
    else:
        own, other = pick(core, gradient.reshape(gradient.shape[0], 2, -1), 1)
    total = grid.add_terms((own, [grid.shift(other, "k", 1)]))
    total = total.reshape(sizes["c"], sizes["z"], sizes["y"], -1, own.shape[-1])
    for name, place in (("y", 2), ("c", 0)):
        total = grid.add_terms(grid.send_terms(total, name, place, here))
    total = grid.add_terms(grid.send_terms(total, "z", 0, here), jnp.float32)
    if by_rows:
        return total
    kept, other = pick(core, total.reshape(2, -1, total.shape[1]), 0)
    return by_core(core, kept[None], grid.shift(other, "k", 1)[None], 0)


def body(
    grid,
    block_input,
    block_order,
    cotangent,
    joint_weight,
    mixing_weight,
    expand_weight,
    shrink_weight,
    vectors,
    joint_first,
    mixing_first,
    expand_first,
    shrink_first,
    vectors_first,
    joint_second,
    mixing_second,
    expand_second,
    shrink_second,
    vectors_second,
):
    here = grid.here()
    sizes = grid.sizes
    ctx, ctx_size = here["c"], sizes["c"]
    seq_count, row_count, width = block_input.shape
    half = width // 2
    pairs = H // 2
    hidden_width = expand_weight.shape[1]
    own_rows = joint_weight.shape[0]
    slot = shrink_weight.shape[0]
    sub = slot // 2
    chips = hidden_width // (2 * slot)
    tokens = seq_count * row_count
    row_blocks = row_count // BLK
    near = ctx_size == 2 and seq_count == 2 and sizes["y"] == 2 and own_rows % 32 == 0

    def hidden_sets(shard):
        parts = shard.astype(low).reshape(own_rows, chips, 2, 2, sub)
        return [
            parts[:, :, :, number].transpose(2, 0, 1, 3).reshape(2, own_rows, chips * sub)
            for number in range(2)
        ]

    table = jnp.pad(vectors.T.astype(low), ((0, 0), (0, 128 - vectors.shape[0])))
    if near:
        joint, tables, *quads, far_input, far_upstream, next_half, next_shrink = begin(
            sizes,
            joint_weight,
            table,
            mixing_weight,
            expand_weight,
            shrink_weight,
            block_input,
            cotangent,
        )
    else:
        joint_halves = (
            joint_weight.astype(low)
            .reshape(own_rows, 3, 2, pairs // 2, PAIR)
            .transpose(2, 0, 3, 1, 4)
            .reshape(2, own_rows, 3 * half)
        )
        mixing_halves = mixing_weight.astype(low).reshape(own_rows, 2, half).transpose(1, 0, 2)
        shrink_low = shrink_weight.astype(low)
        pieces = [joint_halves, table, mixing_halves, *hidden_sets(expand_weight)]
        pieces += [shrink_low[:sub], shrink_low[sub:]]
        joint, tables, mixing, expand_a, expand_b, shrink_a, shrink_b = gather_far(
            grid, here, pieces
        )
    joint = joint.reshape(width, 3 * width)
    vector_values = (
        tables.reshape(width, -1)[:, : vectors.shape[0]].T.astype(jnp.float32)
    )

    if near:
        order = lax.dynamic_slice_in_dim(block_order, ctx, 1, 0)[0]
        blocks = order.shape[0]
        stored = jnp.arange(blocks, dtype=jnp.int32)
        moved = jnp.where(stored // row_blocks == ctx, 0, row_blocks) + stored % row_blocks
        place = jnp.sum(jnp.where(order[None, :] == stored[:, None], moved[None, :], 0), axis=1)
        back = jnp.sum(jnp.where(moved[None, :] == stored[:, None], order[None, :], 0), axis=1)
        place, back = place.astype(jnp.int32), back.astype(jnp.int32)
    joint_shift = jnp.stack(
        [
            vector_values[2].reshape(pairs, PAIR),
            jnp.zeros((pairs, PAIR), jnp.float32),
            vector_values[3].reshape(pairs, PAIR),
        ],
        axis=1,
    ).reshape(1, -1)
    lead = (sizes["c"], sizes["z"], sizes["y"])
    hidden_bias = vector_values[8:].reshape(chips, 2, 2, sub).transpose(2, 1, 0, 3).reshape(2, 1, -1)

    def by_device(expand_grad, shrink_grad):
        return (
            expand_grad.reshape(*lead, -1, expand_grad.shape[1]),
            shrink_grad.reshape(2, *lead, -1, width),
        )

    if near:
        mixed_low, logsum, input_low, first_low, projected, *gathered = attend(
            sizes,
            place,
            block_input,
            far_input,
            joint,
            vector_values[:2],
            joint_shift,
            cotangent,
            quads,
            next_half,
            next_shrink,
        )
        mixing, expand_a, shrink_a, *quads, last_upstream = gathered
        mixing = mixing.reshape(width, width)
        *before, expand_grad_a, shrink_grad_a, bias_a, middle, second_low, upstream, expand_b, shrink_b = mlp_gather(
            sizes,
            place,
            mixed_low,
            input_low,
            mixing,
            vector_values[:8],
            expand_a.reshape(width, -1),
            shrink_a.reshape(-1, width),
            hidden_bias[0],
            cotangent,
            far_upstream,
            last_upstream,
            quads,
        )
        second_grad, expand_grad_b, shrink_grad_b, bias_b, *quads, kept_out, sent_out = mlp_reduce(
            sizes,
            back,
            second_low,
            upstream,
            expand_b.reshape(width, -1),
            shrink_b.reshape(-1, width),
            hidden_bias[1],
            before,
            by_device(expand_grad_a, shrink_grad_a),
        )
    else:
        input_low = block_input.reshape(tokens, width)
        upstream = cotangent.reshape(tokens, width)
        input_rows = input_low.astype(jnp.float32)
        normed_first, normal_first, inverse_first = layer_norm(
            input_rows, vector_values[0], vector_values[1]
        )
        first_low = normed_first.astype(low)
        projected = (nn(first_low, joint) + joint_shift).astype(low)
        by_part = projected.reshape(seq_count, row_count, pairs, 3, PAIR)
        queries, keys, values = [
            by_part[:, :, :, part].reshape(seq_count, row_count, width) for part in range(3)
        ]
        key_value = lax.all_gather(
            jnp.concatenate([keys, values], axis=2), "ctx", axis=1, tiled=True
        )
        own_blocks = lax.dynamic_slice_in_dim(block_order, ctx * row_blocks, row_blocks, 1)
        query_block = jnp.repeat(own_blocks, BLK, axis=1, total_repeat_length=row_count)
        key_block = jnp.repeat(block_order, BLK, axis=1, total_repeat_length=key_value.shape[1])
        allowed = key_block[:, None, :] <= query_block[:, :, None]
        mixed, logsum = spread_forward(queries, key_value, allowed)
        mixed_low = mixed.astype(low).reshape(tokens, width)
        mixing = mixing.reshape(width, width)
        middle = input_rows + (nn(mixed_low, mixing) + vector_values[4])
        normed_second, normal_second, inverse_second = layer_norm(
            middle, vector_values[5], vector_values[6]
        )
        second_low = normed_second.astype(low)
        before = (middle + vector_values[7], jnp.zeros_like(middle))
        *before, expand_grad_a, shrink_grad_a, bias_a = mlp(
            second_low,
            upstream,
            expand_a.reshape(width, -1),
            shrink_a.reshape(-1, width),
            hidden_bias[0],
            before,
        )
        result, second_grad, expand_grad_b, shrink_grad_b, bias_b = mlp(
            second_low,
            upstream,
            expand_b.reshape(width, -1),
            shrink_b.reshape(-1, width),
            hidden_bias[1],
            before,
        )
        block_output = result.astype(low).reshape(block_input.shape)
    hidden_bias_grads = [
        bias.reshape(2, chips, 1, sub).transpose(1, 0, 2, 3) for bias in (bias_a, bias_b)
    ]

    if near:
        joint_back, middle_grad, sums, *last_quads, expand_part_a, shrink_part_a, far_one = attend_back(
            sizes,
            second_grad,
            middle,
            upstream,
            mixed_low,
            mixing,
            vector_values[5:6],
            projected,
            logsum,
            by_device(expand_grad_b, shrink_grad_b),
            quads,
            sent_out,
        )
    else:
        middle_part, gain_two, shift_two = norm_back(
            second_grad, normal_second, inverse_second, vector_values[5]
        )
        middle_grad = upstream.astype(jnp.float32) + middle_part
        branch_low = middle_grad.astype(low)
        mixing_grad = outer_sum(mixed_low, branch_low).astype(low)
        mixed_grad = nt(branch_low, mixing).astype(low)
        query_grad, key_value_grad = spread_backward(
            queries, key_value, allowed, logsum, mixed_grad.reshape(seq_count, row_count, width)
        )
        summed = lax.psum_scatter(
            key_value_grad.astype(low), "ctx", scatter_dimension=1, tiled=True
        )
        parts = [query_grad.astype(low), summed[..., :width], summed[..., width:]]
        joint_back = jnp.stack(
            [part.reshape(tokens, pairs, PAIR) for part in parts], axis=2
        ).reshape(tokens, 3 * width)
        mixing_part = reduce_far(grid, here, mixing_grad, False)
        expand_part_a, shrink_part_a, expand_part_b, shrink_part_b = [
            reduce_far(grid, here, grad, number % 2 == 1)
            for number, grad in enumerate(
                (expand_grad_a, shrink_grad_a, expand_grad_b, shrink_grad_b)
            )
        ]

    def column_sum(rows):
        return jnp.sum(rows.astype(jnp.float32), axis=0)

    hidden_bias_grad = jnp.concatenate(hidden_bias_grads, axis=2).reshape(-1, width)
    weights = (joint_weight, mixing_weight, expand_weight, shrink_weight)
    firsts = (joint_first, mixing_first, expand_first, shrink_first)
    seconds = (joint_second, mixing_second, expand_second, shrink_second)
    if near:
        rows = vectors.shape[0]
        vector_grad = jnp.concatenate(
            [jnp.zeros((4, width)), sums[:4], hidden_bias_grad, jnp.zeros((-rows % 8, width))],
            axis=0,
        )
        joint_part, vector_sum, mixing_part, expand_part_b, shrink_part_b, kept_grad, far_grad, far_two = end(
            sizes,
            back,
            joint_back,
            first_low,
            joint,
            input_low,
            middle_grad,
            vector_values[0:1],
            vector_grad,
            last_quads,
            sent_out,
        )
        input_gradient, block_output, *news = last(
            ctx.astype(jnp.int32).reshape(1),
            (joint_part, mixing_part, expand_part_a, expand_part_b, shrink_part_a, shrink_part_b),
            kept_grad,
            far_grad,
            kept_out,
            (far_one, far_two),
            list(zip(weights, firsts, seconds)),
        )
        updated, moments, squares, copies = [news[number::4] for number in range(4)]
    else:
        joint_grad = outer_sum(first_low, joint_back).astype(low)
        first_grad = nt(joint_back, joint)
        input_part, gain_one, shift_one = norm_back(
            first_grad, normal_first, inverse_first, vector_values[0]
        )
        input_gradient = (middle_grad + input_part).reshape(block_input.shape)
        joint_sums = column_sum(joint_back).reshape(pairs, 3, PAIR)
        vector_rows = [
            gain_one,
            shift_one,
            joint_sums[:, 0].reshape(-1),
            joint_sums[:, 2].reshape(-1),
            column_sum(branch_low),
            gain_two,
            shift_two,
            column_sum(upstream),
        ]
        joint_part = reduce_far(grid, here, joint_grad, False)
        vector_sum = grid.everywhere(
            jnp.concatenate([jnp.stack(vector_rows), hidden_bias_grad], axis=0)
        )
        joint_sum = (
            joint_part.reshape(2, own_rows, pairs // 2, 3, PAIR)
            .transpose(1, 3, 0, 2, 4)
            .reshape(joint_weight.shape)
        )
        mixing_sum = mixing_part.transpose(1, 0, 2).reshape(mixing_weight.shape)
        expand_sum = jnp.stack(
            [part.reshape(2, own_rows, chips, sub) for part in (expand_part_a, expand_part_b)]
        )
        expand_sum = expand_sum.transpose(2, 3, 1, 0, 4).reshape(expand_weight.shape)
        shrink_sum = jnp.concatenate([shrink_part_a, shrink_part_b], axis=0)
        updated, moments, squares = zip(
            *[
                adam_update(*terms, 0.05, 0.1)
                for terms in zip(
                    weights, firsts, seconds, (joint_sum, mixing_sum, expand_sum, shrink_sum)
                )
            ]
        )
        copies = [array.astype(low) for array in updated]
    vector_sum = lax.dynamic_slice(
        vector_sum, (0, lax.axis_index(axes) * vectors.shape[1]), vectors.shape
    )
    vectors_new, vectors_moment, vectors_square = adam_update(
        vectors, vectors_first, vectors_second, vector_sum, 0.5, 0.0
    )
    return (
        block_output,
        input_gradient,
        *updated,
        vectors_new,
        *moments,
        vectors_moment,
        *squares,
        vectors_square,
        *copies,
        vectors_new.astype(low),
    )


def solution(mesh):
    grid = Slice(mesh.shape["ctx"], mesh.shape["wshard"])
    rows = P("wshard", "ctx", None)
    matrix = P(axes, None)
    table = P(None, axes)
    parameters = (matrix, matrix, matrix, matrix, table)
    return jax.shard_map(
        functools.partial(body, grid),
        mesh=mesh,
        in_specs=(rows, P("wshard", None), rows) + parameters * 3,
        out_specs=(rows, rows) + parameters * 4,
        check_vma=False,
    )
```

```python
import functools

import jax
import jax.numpy as jnp
from jax import lax
from jax.experimental import pallas as pl
from jax.experimental.pallas import tpu as pltpu
from jax.sharding import PartitionSpec as P

H = 16
HD = 64
BLK = 256
STEP = 10
PAIR = 2 * HD

norm_eps = 1e-05
adam_eps = 1e-08
group_heads = 4
score_scale = 0.125 * 1.4426950408889634
gelu_root = 0.7978845608028654
gelu_cubic = 0.044715
low = jnp.bfloat16
axes = ("ctx", "wshard")
small_cost = pl.CostEstimate(flops=1024, bytes_accessed=1024, transcendentals=0)


def nt(left_side, right_side):
    return lax.dot_general(
        left_side, right_side, (((1,), (1,)), ((), ())), preferred_element_type=jnp.float32
    )


def nn(left_side, right_side):
    return jnp.dot(left_side, right_side, preferred_element_type=jnp.float32)


def outer_sum(left_side, right_side):
    return lax.dot_general(
        left_side, right_side, (((0,), (0,)), ((), ())), preferred_element_type=jnp.float32
    )


def block_rows(block):
    return pl.ds(block * BLK, BLK)


def thirds(ref):
    return [ref.at[:, pl.ds(part * PAIR, PAIR)] for part in range(3)]


def both_heads(rows):
    lane = lax.broadcasted_iota(jnp.int32, (1, PAIR), 1)
    empty = jnp.zeros_like(rows)
    return jnp.concatenate(
        [jnp.where(lane < HD, rows, empty), jnp.where(lane < HD, empty, rows)], axis=0
    )


def attend_pair(blocks, projected, o_ref, lse_ref, between):
    q_ref, k_ref, v_ref = thirds(projected)
    lane = lax.broadcasted_iota(jnp.int32, (1, PAIR), 1)
    for i in range(blocks):
        between(i)
        rows = block_rows(i)
        queries = both_heads(q_ref[rows, :])
        upto = pl.ds(0, (i + 1) * BLK)
        scores = nt(queries, k_ref[upto, :]) * score_scale
        top = jnp.max(scores, axis=1, keepdims=True)
        weights = jnp.exp2(scores - top)
        total = jnp.sum(weights, axis=1, keepdims=True)
        mixed = nn(weights.astype(low), v_ref[upto, :])
        mixed = mixed * (1.0 / total)
        o_ref[rows, :] = jnp.where(lane < HD, mixed[:BLK], mixed[BLK:]).astype(o_ref.dtype)
        logsum = jnp.transpose(jnp.broadcast_to(top + jnp.log2(total), (2 * BLK, PAIR)))
        for h in range(2):
            lse_ref[h : h + 1, rows] = logsum[0:1, h * BLK : (h + 1) * BLK]


def attend_back_pair(
    blocks, projected, do_ref, lse_ref, back_ref, turned, key_sum, value_sum, between
):
    q_ref, k_ref, v_ref = thirds(projected)
    dq_ref, dk_ref, dv_ref = thirds(back_ref)
    turned[...] = jnp.transpose(k_ref[...])
    for i in range(blocks):
        between(i)
        rows = block_rows(i)
        queries, upstream = both_heads(q_ref[rows, :]), both_heads(do_ref[rows, :])
        logsum = jnp.concatenate([lse_ref[0:1, rows], lse_ref[1:2, rows]], axis=1)
        upto = pl.ds(0, (i + 1) * BLK)
        weights = jnp.exp2(nt(k_ref[upto, :], queries) * score_scale - logsum)
        pulls = nt(v_ref[upto, :], upstream)
        inner = jnp.sum(weights * pulls, axis=0, keepdims=True)
        score_grad = (weights * (pulls - inner)).astype(low)
        value_grad = nn(weights.astype(low), upstream)
        key_grad = nn(score_grad, queries)
        query_grad = nn(turned[:, upto], score_grad)
        earlier, latest = pl.ds(0, i * BLK), block_rows(i)
        if i > 0:
            value_sum[earlier, :] += value_grad[: i * BLK]
            key_sum[earlier, :] += key_grad[: i * BLK]
        value_sum[latest, :] = value_grad[i * BLK :]
        key_sum[latest, :] = key_grad[i * BLK :]
        joined = jnp.concatenate([query_grad[:HD, :BLK], query_grad[HD:, BLK:]], axis=0)
        dq_ref[rows, :] = (jnp.transpose(joined) * 0.125).astype(dq_ref.dtype)
    dk_ref[...] = (key_sum[...] * 0.125).astype(dk_ref.dtype)
    dv_ref[...] = value_sum[...].astype(dv_ref.dtype)


def hooks(step, schedule):
    def between(block):
        for when, where, action in schedule:
            if where == block:
                pl.when(step == when)(action)

    return between


any_place = pl.BlockSpec(memory_space=pl.ANY)
whole_vmem = pl.BlockSpec(memory_space=pltpu.VMEM)


MESH = pl.DeviceIdType.MESH


class Spot:
    def __init__(self, sizes):
        self.sizes = sizes
        ctx, shard = lax.axis_index("ctx"), lax.axis_index("wshard")
        self.c = ctx
        self.k = shard % 2
        self.y = (shard // 2) % 2
        self.z = shard // 4

    def device(self, name, by=1):
        c, z, y, k = self.c, self.z, self.y, self.k
        if name == "c":
            c = 1 - c
        if name == "y":
            y = 1 - y
        if name == "k":
            k = 1 - k
        if name == "z":
            z = (z + by) % self.sizes["z"]
        return (c, (z * 2 + y) * 2 + k)

    def meet(self, names):
        barrier = pltpu.get_barrier_semaphore()
        partners = []
        for name in names:
            for by in range(1, self.sizes[name]):
                partners.append(self.device(name, by))
        for partner in partners:
            pl.semaphore_signal(barrier, inc=1, device_id=partner, device_id_type=MESH)
        pl.semaphore_wait(barrier, len(partners))


class Mover:
    def __init__(self, spot, sems):
        self.spot, self.sems, self.count = spot, sems, 0

    def copy(self, source, target, name, by=1):
        number = self.count
        self.count += 1
        return pltpu.make_async_remote_copy(
            src_ref=source,
            dst_ref=target,
            send_sem=self.sems.at[0, number],
            recv_sem=self.sems.at[1, number],
            device_id=self.spot.device(name, by),
            device_id_type=MESH,
        )

    def local(self, source, target):
        number = self.count
        self.count += 1
        return pltpu.make_async_copy(source, target, self.sems.at[0, number])


class Refs:
    def __init__(self, refs):
        self.refs = list(refs)

    def take(self, count):
        taken, self.refs = self.refs[:count], self.refs[count:]
        return taken


def start(copies):
    for copy in copies:
        copy.start()


def wait(copies):
    for copy in copies:
        copy.wait()


def span(first, size):
    return pl.ds(pl.multiple_of(first, 128), size)


class Deep:
    def __init__(self, mover, quad):
        z = mover.spot.z
        self.copies = [
            mover.copy(quad.at[z], quad.at[z], "z", by) for by in range(1, mover.spot.sizes["z"])
        ]


def first_rows(mover, halves, quad):
    spot = mover.spot
    rows = halves.shape[1]
    block = quad.at[spot.z, pl.ds(pl.multiple_of(spot.k * rows, rows), rows)]
    return [
        mover.local(halves.at[spot.k], block),
        mover.copy(halves.at[1 - spot.k], block, "k"),
    ]


class Near:
    def __init__(self, mover, quad, half, offset, cut, core=True):
        spot = mover.spot
        c, z, y = spot.c, spot.z, spot.y
        width = quad.shape[-1]
        every = slice(None)

        def part(ci, yi, first, size):
            return half.at[ci, every, yi, :, span(offset + first, size)]

        self.near, self.far = [mover.local(quad, part(c, y, 0, width))], []
        for first, size, one, two in ((0, cut, "c", "y"), (cut, width - cut, "y", "c")):
            if size == 0:
                continue
            source = quad.at[every, every, pl.ds(first, size)]
            self.near.append(mover.copy(source, part(c, y, first, size), one))
            self.near.append(mover.copy(source, part(c, y, first, size), two))
            block = part(1 - c if one == "c" else c, 1 - y if one == "y" else y, first, size)
            self.far.append(mover.copy(block, block, two))
        self.core = [[], [], []]
        if core:
            self.core[0].append(mover.copy(quad, part(c, y, 0, width), "k"))
            for stage, ci, yi in ((1, 1 - c, y), (1, c, 1 - y), (2, 1 - c, 1 - y)):
                block = part(ci, yi, 0, width)
                self.core[stage].append(mover.copy(block, block, "k"))

    def close(self):
        wait(self.far)
        start(self.core[2])

    def close_core(self):
        for stage in self.core:
            wait(stage)


class ReduceNear:
    def __init__(self, mover, mine, theirs, cut, quad, scratch):
        self.spot = spot = mover.spot
        self.cut, self.quad = cut, quad
        self.total, self.other, self.by_y, self.by_c, self.then_c, self.then_y = scratch
        self.width = width = self.total.shape[-1]
        c, y = spot.c, spot.y
        every, left, right = slice(None), pl.ds(0, cut), pl.ds(cut, width - cut)
        total = self.total
        self.first = [mover.copy(theirs, self.other, "k")]
        if mine is not None:
            self.first.append(mover.local(mine, total))
        self.near = [
            mover.copy(total.at[every, every, 1 - y, every, left], self.by_y, "y"),
            mover.copy(total.at[1 - c, every, every, every, right], self.by_c, "c"),
        ]
        self.far = [
            mover.copy(total.at[1 - c, every, y, every, left], self.then_c, "c"),
            mover.copy(total.at[c, every, 1 - y, every, right], self.then_y, "y"),
        ]

    @staticmethod
    def scratch(sizes, rows, width, cut):
        c, z, y = sizes["c"], sizes["z"], sizes["y"]
        shapes = [
            (c, z, y, rows, width),
            (c, z, y, rows, width),
            (c, z, rows, cut),
            (z, y, rows, width - cut),
            (z, rows, cut),
            (z, rows, width - cut),
        ]
        return [pltpu.VMEM(shape, low) for shape in shapes]

    def add(self, where, extra):
        total = self.total[where].astype(jnp.float32) + extra.astype(jnp.float32)
        return total.astype(low)

    def go_near(self):
        wait(self.first)
        sizes = self.spot.sizes
        for c in range(sizes["c"]):
            for y in range(sizes["y"]):

                @pl.loop(0, sizes["z"])
                def _(z):
                    self.total[c, z, y] = self.add((c, z, y), self.other[c, z, y])

        start(self.near)

    def go_far(self):
        wait(self.near)
        spot, cut = self.spot, self.cut
        left, right = pl.ds(0, cut), pl.ds(cut, self.width - cut)

        @pl.loop(0, spot.sizes["z"])
        def _(z):
            for c in range(spot.sizes["c"]):
                where = (c, z, spot.y, slice(None), left)
                self.total[where] = self.add(where, self.by_y[c, z])
            for y in range(spot.sizes["y"]):
                where = (spot.c, z, y, slice(None), right)
                self.total[where] = self.add(where, self.by_c[z, y])

        start(self.far)

    def close(self):
        wait(self.far)
        spot, cut = self.spot, self.cut
        left, right = pl.ds(0, cut), pl.ds(cut, self.width - cut)

        @pl.loop(0, spot.sizes["z"])
        def _(z):
            for columns, extra in ((left, self.then_c), (right, self.then_y)):
                where = (spot.c, z, spot.y, slice(None), columns)
                self.quad[z, :, columns] = self.add(where, extra[z])


class ReduceDeep:
    def __init__(self, mover, quad, by_z):
        self.spot = spot = mover.spot
        self.quad, self.by_z = quad, by_z
        depth = spot.sizes["z"]
        self.copies = [
            mover.copy(quad.at[(spot.z + by) % depth], by_z.at[by - 1], "z", by)
            for by in range(1, depth)
        ]

    def result(self):
        spot = self.spot
        value = self.quad[spot.z].astype(jnp.float32)
        for by in range(spot.sizes["z"] - 1):
            value = value + self.by_z[by].astype(jnp.float32)
        return value


class Finish:
    def __init__(self, mover, summed, arrived):
        self.k = mover.spot.k
        self.summed, self.arrived = summed, arrived
        rows = arrived.shape[0]
        self.rows = rows
        away = summed.at[pl.ds(pl.multiple_of((1 - self.k) * rows, rows), rows)]
        self.copies = [mover.copy(away, arrived, "k")]

    @staticmethod
    def scratch(rows, width):
        return [pltpu.VMEM((rows, width), jnp.float32), pltpu.VMEM((rows // 2, width), jnp.float32)]

    def write(self, out, columns=slice(None)):
        rows = self.rows
        kept = pl.ds(pl.multiple_of(self.k * rows, rows), rows)
        out[self.k, :, columns] = self.summed[kept, :]
        out[1 - self.k, :, columns] = self.arrived[...]


def core_halves(grad, k, width, first=0, size=None):
    size = width if size is None else size
    every = slice(None)
    return [
        grad.at[every, every, every, every, span(half * width + first, size)]
        for half in (k, 1 - k)
    ]


all_axes = ("k", "c", "y", "z")


def params(number, megabytes):
    return pltpu.CompilerParams(
        collective_id=number, has_side_effects=True, vmem_limit_bytes=megabytes << 20
    )


def cut_of(width):
    return max(5 * width // 8 // 128, 1) * 128


def low_shape(*dims):
    return jax.ShapeDtypeStruct(dims, low)


def begin_kernel(sizes, *refs):
    refs = Refs(refs)
    joint_weight, table, mixing_weight, expand_weight, shrink_weight = refs.take(5)
    rows_in, upstream = refs.take(2)
    joint, tables, mixing_quad, expand_quad, shrink_quad, far_rows, far_upstream = refs.take(7)
    next_expand, next_shrink = refs.take(2)
    joint_quad, table_quad, sems, joint_halves, mixing_halves, expand_halves, shrink = refs.take(7)
    spot = Spot(sizes)
    mover = Mover(spot, sems)
    width = joint_halves.shape[2]
    joint_first = first_rows(mover, joint_halves, joint_quad)
    rows = table.shape[0]
    spread = table_quad.at[spot.z, pl.ds(pl.multiple_of(spot.k * rows, rows), rows)]
    joint_first += [mover.local(table, spread), mover.copy(table, spread, "k")]
    later_first = first_rows(mover, mixing_halves, mixing_quad)
    later_first += first_rows(mover, expand_halves, expand_quad)
    later_first += [mover.local(shrink, shrink_quad.at[spot.z])]
    part = width // 2
    chunks = [joint_quad.at[:, :, pl.ds(first, part)] for first in (0, part)]
    now = [Deep(mover, chunk).copies for chunk in chunks]
    thin_deep = Deep(mover, table_quad).copies
    later = [Deep(mover, quad).copies for quad in (mixing_quad, shrink_quad, expand_quad)]
    jobs = [
        Near(mover, chunk, joint, spot.k * width + number * part, part)
        for number, chunk in enumerate(chunks)
    ]
    thin = Near(mover, table_quad, tables, 0, table.shape[1], core=False)
    rows_copies = [
        mover.copy(rows_in.at[1 - spot.c, block_rows(0)], far_rows.at[block_rows(0)], "c"),
        mover.copy(rows_in.at[1 - spot.c, block_rows(1)], far_rows.at[block_rows(1)], "c"),
        mover.copy(upstream.at[1 - spot.c, block_rows(0)], far_upstream, "c"),
    ]
    pairs = width // (3 * PAIR)
    for core in range(2):
        for pair in range(pairs):
            for third in range(3):
                source = ((third * 2 + core) * pairs + pair) * PAIR
                target = (pair * 3 + third) * PAIR
                joint_halves[core, :, target : target + PAIR] = joint_weight[
                    :, source : source + PAIR
                ].astype(low)
    spot.meet(all_axes)
    start(joint_first)
    start(rows_copies[:1])
    wait(joint_first)
    start(now[0] + thin_deep)
    half = mixing_halves.shape[2]
    for core in range(2):
        mixing_halves[core] = mixing_weight[:, core * half : (core + 1) * half].astype(low)
    sub = shrink.shape[0]
    shrink[...] = shrink_weight[:sub, :].astype(low)
    next_shrink[...] = shrink_weight[sub:, :].astype(low)
    lane = lax.broadcasted_iota(jnp.int32, (1, PAIR), 1)
    for core in range(2):
        for chip in range(0, expand_halves.shape[2] // HD, 2):
            one, two = [
                expand_weight[:, (number * 2 + core) * PAIR : (number * 2 + core + 1) * PAIR]
                for number in (chip, chip + 1)
            ]
            columns = pl.ds(chip * HD, PAIR)
            expand_halves[core, :, columns] = jnp.where(
                lane < HD, one, pltpu.roll(two, HD, 1)
            ).astype(low)
            next_expand[core, :, columns] = jnp.where(
                lane < HD, pltpu.roll(one, HD, 1), two
            ).astype(low)
    start(later_first)
    wait(now[0] + thin_deep)
    start(now[1])
    start(thin.near + jobs[0].near + jobs[0].core[0])
    wait(now[1])
    start(jobs[1].near + jobs[1].core[0])
    wait(later_first)
    for copies in later:
        start(copies)
    wait(thin.near + jobs[0].near)
    start(thin.far + jobs[0].far + jobs[0].core[1])
    start(rows_copies[1:2])
    wait(jobs[1].near)
    start(jobs[1].far + jobs[1].core[1])
    start(rows_copies[2:])
    wait(thin.far)
    for job in jobs:
        job.close()
    for copies in later:
        wait(copies)
    for job in jobs:
        job.close_core()
    wait(rows_copies)


def begin(sizes, joint_weight, table, mixing_weight, expand_weight, shrink_weight, rows_in, upstream):
    lead = (sizes["c"], sizes["z"], sizes["y"])
    own, model = mixing_weight.shape
    depth, rows = sizes["z"], 2 * own
    width, half, grown = 3 * model // 2, model // 2, expand_weight.shape[1] // 4
    sub = shrink_weight.shape[0] // 2
    return pl.pallas_call(
        functools.partial(begin_kernel, sizes),
        in_specs=[whole_vmem] * 5 + [any_place] * 2,
        out_specs=[any_place] * 7 + [whole_vmem] * 2,
        out_shape=[
            low_shape(*lead, rows, 2 * width),
            low_shape(*lead, rows, table.shape[1]),
            low_shape(depth, rows, half),
            low_shape(depth, rows, grown),
            low_shape(depth, sub, model),
            low_shape(*rows_in.shape[1:]),
            low_shape(BLK, model),
            low_shape(2, own, grown),
            low_shape(sub, model),
        ],
        scratch_shapes=[
            pltpu.VMEM((depth, rows, width), low),
            pltpu.VMEM((depth, rows, table.shape[1]), low),
            pltpu.SemaphoreType.DMA((2, 64)),
            pltpu.VMEM((2, own, width), low),
            pltpu.VMEM((2, own, half), low),
            pltpu.VMEM((2, own, grown), low),
            pltpu.VMEM((sub, model), low),
        ],
        compiler_params=params(1, 60),
        cost_estimate=small_cost,
        name="begin",
    )(joint_weight, table, mixing_weight, expand_weight, shrink_weight, rows_in, upstream)


def normal_rows(rows):
    centered = rows - jnp.mean(rows, axis=-1, keepdims=True)
    inverse = lax.rsqrt(jnp.mean(centered * centered, axis=-1, keepdims=True) + norm_eps)
    return centered * inverse, inverse


def norm_pull(upstream, normal, inverse, gain):
    scaled = upstream * gain
    inner = jnp.mean(scaled, axis=-1, keepdims=True)
    along = jnp.mean(scaled * normal, axis=-1, keepdims=True)
    return inverse * (scaled - inner - normal * along)


def chosen_block(number, source):
    chosen = jnp.full((1, source.shape[1]), number, jnp.int32)
    value = source[block_rows(0), :].astype(jnp.float32)
    for other in range(1, source.shape[0] // BLK):
        value = jnp.where(chosen == other, source[block_rows(other), :].astype(jnp.float32), value)
    return value


def hidden_pairs(width, columns):
    chips = columns // 2 // HD
    for core in range(2):
        for chip in range(0, chips, 2):
            places = []
            for number in (chip, chip + 1):
                row, first = divmod((number * 2 + core) * PAIR, width)
                places.append((slice(8 + row, 9 + row), slice(first, first + PAIR)))
            first = core * (columns // 2) + chip * HD
            yield places, slice(first, first + PAIR)


def attend_kernel(sizes, blocks, *refs):
    refs = Refs(refs)
    place_ref, rows_in, far_rows, joint, table, upstream = refs.take(6)
    mixing_quad, expand_quad, shrink_quad, expand_halves, shrink = refs.take(5)
    o_ref, lse_ref, rows_ref, low_ref, projected_ref, vectors, bias_a, bias_b = refs.take(8)
    mixing, expand, shrunk, next_expand, next_shrink, far_upstream = refs.take(6)
    sems, rows_all, joint_all, projected, shift_ref = refs.take(5)
    spot = Spot(sizes)
    mover = Mover(spot, sems)
    k = spot.k
    half, grown, width = mixing_quad.shape[-1], expand_quad.shape[-1], shrink_quad.shape[-1]
    loads = [
        mover.local(rows_in.at[spot.c], rows_all.at[pl.ds(0, 2 * BLK)]),
        mover.local(far_rows, rows_all.at[pl.ds(2 * BLK, 2 * BLK)]),
        mover.local(joint, joint_all),
    ]
    jobs = [
        Near(mover, mixing_quad, mixing, k * half, cut_of(half)),
        Near(mover, shrink_quad, shrunk.at[k], 0, cut_of(width)),
        Near(mover, expand_quad, expand, k * grown, cut_of(grown)),
    ]
    next_first = first_rows(mover, expand_halves, next_expand)
    next_first += [mover.local(shrink, next_shrink.at[spot.z])]
    deep = Deep(mover, next_expand).copies + Deep(mover, next_shrink).copies
    upstream_copy = [mover.copy(upstream.at[1 - spot.c, block_rows(1)], far_upstream, "c")]

    def open_all():
        start(loads)
        spot.meet(all_axes)
        start(next_first)
        for job in jobs:
            start(job.near + job.core[0])
        vector_rows()
        wait(loads)

    def next_deep():
        wait(next_first)
        start(deep)
        start(upstream_copy)

    def vector_rows():
        vectors[...] = jnp.transpose(table[...].astype(jnp.float32))[: vectors.shape[0]]
        shift_ref[...] = jnp.zeros_like(shift_ref)
        for pair in range(H // 2):
            for row, third in ((2, 0), (3, 2)):
                columns = pl.ds((3 * pair + third) * PAIR, PAIR)
                shift_ref[:, columns] = vectors[row : row + 1, pair * PAIR : (pair + 1) * PAIR]
        lane = lax.broadcasted_iota(jnp.int32, (1, PAIR), 1)
        for (one, two), target in hidden_pairs(vectors.shape[1], bias_a.shape[1]):
            one, two = vectors[one], vectors[two]
            bias_a[:, target] = jnp.where(lane < HD, one, pltpu.roll(two, HD, 1))
            bias_b[:, target] = jnp.where(lane < HD, pltpu.roll(one, HD, 1), two)

    def far(job):
        wait(job.near)
        start(job.far + job.core[1])

    def close_all():
        for job in jobs:
            job.close()
        wait(deep)
        for job in jobs:
            job.close_core()
        wait(upstream_copy)

    step = pl.program_id(0)
    between = hooks(
        step,
        [
            (0, 0, open_all),
            (2, 0, next_deep),
            (9, 0, lambda: far(jobs[0])),
            (10, 2, lambda: far(jobs[1])),
            (10, 3, lambda: far(jobs[2])),
        ],
    )
    between(0)

    @pl.when(step < blocks)
    def _():
        value = chosen_block(place_ref[step], rows_all)
        rows_ref[...] = value.astype(low)
        normal, _ = normal_rows(value)
        normed = (normal * vectors[0:1, :] + vectors[1:2, :]).astype(low)
        low_ref[...] = normed
        rows = pl.ds(pl.multiple_of(step * BLK, BLK), BLK)
        for first in range(0, joint_all.shape[1], 512):
            columns = pl.ds(first, 512)
            projected[rows, columns] = (nn(normed, joint_all[:, columns]) + shift_ref[:, columns]).astype(low)

    @pl.when(step >= blocks)
    def _():
        columns = span((step - blocks) * 3 * PAIR, 3 * PAIR)
        projected_ref[...] = projected[:, columns]
        attend_pair(blocks, projected_ref, o_ref, lse_ref, lambda block: block > 0 and between(block))

    pl.when(step == pl.num_programs(0) - 1)(close_all)


def attend(sizes, place, rows_in, far_rows, joint, table, upstream, quads, halves, shrink):
    model = rows_in.shape[2]
    blocks = place.shape[0]
    tokens = blocks * BLK
    pairs = model // PAIR
    lead = (sizes["c"], sizes["z"], sizes["y"])
    depth, rows, half = quads[0].shape
    grown, full = quads[1].shape[2], quads[2].shape[2]
    by_rows = pl.BlockSpec((BLK, model), lambda g: (jnp.minimum(g, blocks - 1), 0))

    def pair(g):
        return jnp.maximum(g - blocks, 0)

    return pl.pallas_call(
        functools.partial(attend_kernel, sizes, blocks),
        grid=(blocks + pairs,),
        in_specs=[pl.BlockSpec(memory_space=pltpu.SMEM)]
        + [any_place] * 3
        + [whole_vmem, any_place]
        + [whole_vmem] * 5,
        out_specs=[
            pl.BlockSpec((tokens, PAIR), lambda g: (0, pair(g))),
            pl.BlockSpec((None, 8, tokens), lambda g: (pair(g), 0, 0)),
            by_rows,
            by_rows,
            pl.BlockSpec((tokens, 3 * PAIR), lambda g: (0, pair(g))),
        ]
        + [whole_vmem] * 3
        + [any_place] * 6,
        out_shape=[
            low_shape(tokens, model),
            jax.ShapeDtypeStruct((pairs, 8, tokens), jnp.float32),
            low_shape(tokens, model),
            low_shape(tokens, model),
            low_shape(tokens, 3 * model),
            jax.ShapeDtypeStruct((16, model), jnp.float32),
            jax.ShapeDtypeStruct((1, 2 * grown), jnp.float32),
            jax.ShapeDtypeStruct((1, 2 * grown), jnp.float32),
            low_shape(*lead, rows, 2 * half),
            low_shape(*lead, rows, 2 * grown),
            low_shape(2, *lead, rows, full),
            low_shape(depth, rows, grown),
            low_shape(depth, rows, full),
            low_shape(BLK, model),
        ],
        scratch_shapes=[
            pltpu.SemaphoreType.DMA((2, 64)),
            pltpu.VMEM((tokens, model), low),
            pltpu.VMEM((model, 3 * model), low),
            pltpu.VMEM((tokens, 3 * model), low),
            pltpu.VMEM((1, 3 * model), jnp.float32),
        ],
        compiler_params=params(2, 60),
        cost_estimate=small_cost,
        name="attend",
    )(place, rows_in, far_rows, joint, table, upstream, *quads, halves, shrink)


def mlp_tile(rows_step, c_ref, dy_ref, we_ref, ws_ref, be_ref, outs, scratch, between):
    y_ref, dc_ref, gwe_ref, gws_ref, gbe_ref = outs
    turned, act_all, du_all = scratch
    tokens = c_ref.shape[0]
    we, ws = we_ref[...], ws_ref[...]
    total = None
    for part in range(tokens // rows_step):
        between(part)
        rows = pl.ds(part * rows_step, rows_step)
        hidden = nn(c_ref[rows, :], we) + be_ref[...]
        squared = hidden * hidden
        bent = jnp.tanh(gelu_root * hidden * (1.0 + gelu_cubic * squared))
        gate = 0.5 + 0.5 * bent
        act = (hidden * gate).astype(low)
        slope = gate + (0.5 * gelu_root) * hidden * (1.0 - bent * bent) * (
            1.0 + (3 * gelu_cubic) * squared
        )
        du = (nt(dy_ref[rows, :], ws) * slope).astype(low)
        act_all[rows, :] = act
        du_all[rows, :] = du
        y_ref[rows, :] += nn(act, ws)
        dc_ref[rows, :] += nt(du, we)
        added = jnp.sum(du.astype(jnp.float32), axis=0, keepdims=True)
        total = added if total is None else total + added
    gbe_ref[...] = total
    gwe_ref[...] = nn(turned[...], du_all[...]).astype(gwe_ref.dtype)
    gws_ref[...] = outer_sum(act_all[...], dy_ref[...]).astype(gws_ref.dtype)


def mlp_parts(tokens, width, hidden, tile):
    whole = pl.BlockSpec((tokens, width), lambda t: (0, 0), pipeline_mode=pl.Buffered(1))
    down = pl.BlockSpec((width, tile), lambda t: (0, t))
    across = pl.BlockSpec((tile, width), lambda t: (t, 0))
    thin = pl.BlockSpec((1, tile), lambda t: (0, t))
    return (
        [whole, whole, down, across, thin],
        [whole, whole, down, across, thin],
        [
            jax.ShapeDtypeStruct((tokens, width), jnp.float32),
            jax.ShapeDtypeStruct((tokens, width), jnp.float32),
            low_shape(width, hidden),
            low_shape(hidden, width),
            jax.ShapeDtypeStruct((1, hidden), jnp.float32),
        ],
        [
            pltpu.VMEM((width, tokens), low),
            pltpu.VMEM((tokens, tile), low),
            pltpu.VMEM((tokens, tile), low),
        ],
    )


def mlp_plain_kernel(rows_step, *refs):
    refs = Refs(refs)
    c_ref, dy_ref, we_ref, ws_ref, be_ref, y_in, dc_in = refs.take(7)
    outs, scratch, (sem,) = refs.take(5), refs.take(3), refs.take(1)

    @pl.when(pl.program_id(0) == 0)
    def _():
        scratch[0][...] = jnp.transpose(c_ref[...])
        copies = [
            pltpu.make_async_copy(y_in, outs[0], sem.at[0]),
            pltpu.make_async_copy(dc_in, outs[1], sem.at[1]),
        ]
        start(copies)
        wait(copies)

    mlp_tile(rows_step, c_ref, dy_ref, we_ref, ws_ref, be_ref, outs, scratch, lambda part: None)


def mlp(c, dy, we, ws, be, before, tile=512, rows_step=512):
    in_specs, out_specs, out_shape, scratch = mlp_parts(*c.shape, we.shape[1], tile)
    return pl.pallas_call(
        functools.partial(mlp_plain_kernel, rows_step),
        grid=(we.shape[1] // tile,),
        in_specs=in_specs + [any_place] * 2,
        out_specs=out_specs,
        out_shape=out_shape,
        scratch_shapes=scratch + [pltpu.SemaphoreType.DMA((2,))],
        compiler_params=pltpu.CompilerParams(vmem_limit_bytes=56 << 20),
        cost_estimate=small_cost,
        name="mlp",
    )(c, dy, we, ws, be, *before)


def mlp_gather_kernel(sizes, blocks, rows_step, *refs):
    refs = Refs(refs)
    place_ref, mixed_ref, rows_ref, mixing, vector_ref, we_ref, ws_ref, be_ref = refs.take(8)
    upstream, far_a, far_b, expand_quad, shrink_quad = refs.take(5)
    outs, (middle_ref, low_ref, upstream_ref) = refs.take(5), refs.take(3)
    expand, shrunk = refs.take(2)
    scratch, (sems, raw, c_all, dy_all) = refs.take(3), refs.take(4)
    spot = Spot(sizes)
    mover = Mover(spot, sems)
    grown, width = expand_quad.shape[-1], shrink_quad.shape[-1]
    loads = [
        mover.local(upstream.at[spot.c], raw.at[pl.ds(0, 2 * BLK)]),
        mover.local(far_a, raw.at[pl.ds(2 * BLK, BLK)]),
        mover.local(far_b, raw.at[pl.ds(3 * BLK, BLK)]),
    ]
    jobs = [
        Near(mover, shrink_quad, shrunk.at[spot.k], 0, width // 2),
        Near(mover, expand_quad, expand, spot.k * grown, grown // 2),
    ]

    def open_all():
        start(loads)
        spot.meet(all_axes)
        for job in jobs:
            start(job.near + job.core[0])
        wait(loads)

    def far(job):
        wait(job.near)
        start(job.far + job.core[1])

    def close_all():
        jobs[1].close()
        for job in jobs:
            job.close_core()

    step = pl.program_id(0)
    between = hooks(
        step,
        [
            (0, 0, open_all),
            (6, 0, lambda: far(jobs[0])),
            (6, 1, lambda: far(jobs[1])),
            (7, 1, jobs[0].close),
        ],
    )
    between(0)

    @pl.when(step < blocks)
    def _():
        rows = pl.ds(pl.multiple_of(step * BLK, BLK), BLK)
        dy = chosen_block(place_ref[step], raw).astype(low)
        upstream_ref[...] = dy
        dy_all[rows, :] = dy
        branch = nn(mixed_ref[...], mixing[...]) + vector_ref[4:5, :]
        middle = rows_ref[...].astype(jnp.float32) + branch
        middle_ref[...] = middle
        normal, _ = normal_rows(middle)
        second = (normal * vector_ref[5:6, :] + vector_ref[6:7, :]).astype(low)
        low_ref[...] = second
        c_all[rows, :] = second
        outs[0][rows, :] = middle + vector_ref[7:8, :]
        outs[1][rows, :] = jnp.zeros(middle.shape, jnp.float32)

    @pl.when(step == blocks)
    def _():
        scratch[0][...] = jnp.transpose(c_all[...])

    @pl.when(step >= blocks)
    def _():
        mlp_tile(
            rows_step, c_all, dy_all, we_ref, ws_ref, be_ref, outs, scratch,
            lambda part: part > 0 and between(part),
        )

    pl.when(step == pl.num_programs(0) - 1)(close_all)


def mlp_gather(sizes, place, mixed, rows_in, mixing, vectors, we, ws, be, upstream, far_a, far_b, quads, tile=512, rows_step=512):
    tokens, model = mixed.shape
    blocks = place.shape[0]
    hidden = we.shape[1]
    lead = (sizes["c"], sizes["z"], sizes["y"])
    rows, grown, full = quads[0].shape[1], quads[0].shape[2], quads[1].shape[2]
    by_rows = pl.BlockSpec((BLK, model), lambda g: (jnp.minimum(g, blocks - 1), 0))
    whole = pl.BlockSpec((tokens, model), lambda g: (0, 0), pipeline_mode=pl.Buffered(1))

    def at(g):
        return jnp.maximum(g - blocks, 0)

    down = pl.BlockSpec((model, tile), lambda g: (0, at(g)))
    across = pl.BlockSpec((tile, model), lambda g: (at(g), 0))
    thin = pl.BlockSpec((1, tile), lambda g: (0, at(g)))
    _, _, out_shape, scratch = mlp_parts(tokens, model, hidden, tile)
    return pl.pallas_call(
        functools.partial(mlp_gather_kernel, sizes, blocks, rows_step),
        grid=(blocks + hidden // tile,),
        in_specs=[pl.BlockSpec(memory_space=pltpu.SMEM), by_rows, by_rows, whole_vmem, whole_vmem]
        + [down, across, thin]
        + [any_place] * 3
        + [whole_vmem] * 2,
        out_specs=[whole, whole, down, across, thin] + [by_rows] * 3 + [any_place] * 2,
        out_shape=out_shape
        + [
            jax.ShapeDtypeStruct((tokens, model), jnp.float32),
            low_shape(tokens, model),
            low_shape(tokens, model),
            low_shape(*lead, rows, 2 * grown),
            low_shape(2, *lead, rows, full),
        ],
        scratch_shapes=scratch
        + [pltpu.SemaphoreType.DMA((2, 32))]
        + [pltpu.VMEM((tokens, model), low)] * 3,
        compiler_params=params(3, 60),
        cost_estimate=small_cost,
        name="mlp_gather",
    )(place, mixed, rows_in, mixing, vectors, we, ws, be, upstream, far_a, far_b, *quads)


def mlp_reduce_kernel(sizes, rows_step, *refs):
    refs = Refs(refs)
    back_ref, c_ref, dy_ref, we_ref, ws_ref, be_ref, y_in, dc_in, expand, shrink = refs.take(10)
    outs = refs.take(4)
    expand_quad, shrink_quad, kept, sent = refs.take(4)
    scratch, (sems, y_all) = refs.take(3), refs.take(2)
    outs = [y_all] + outs
    spot = Spot(sizes)
    mover = Mover(spot, sems)
    grown, width = expand_quad.shape[-1], shrink_quad.shape[-1]
    loads = [mover.local(y_in, y_all), mover.local(dc_in, outs[1])]
    jobs = [
        ReduceNear(
            mover, shrink.at[spot.k], shrink.at[1 - spot.k], width // 2, shrink_quad, refs.take(6)
        ),
        ReduceNear(
            mover, *core_halves(expand, spot.k, grown), grown // 2, expand_quad, refs.take(6)
        ),
    ]

    def open_all():
        start(loads)
        spot.meet(all_axes)
        start(jobs[0].first)
        scratch[0][...] = jnp.transpose(c_ref[...])
        wait(loads)

    def shrink_near():
        start(jobs[1].first)
        jobs[0].go_near()

    def close_all():
        for place in range(2):
            kept[block_rows(place), :] = chosen_block(back_ref[place], y_all).astype(low)
            sent[block_rows(place), :] = chosen_block(back_ref[2 + place], y_all).astype(low)
        for job in jobs:
            job.close()

    step = pl.program_id(0)
    schedule = [
        (0, 0, open_all),
        (0, 1, shrink_near),
        (1, 0, jobs[1].go_near),
        (3, 0, jobs[0].go_far),
        (3, 1, jobs[1].go_far),
    ]
    mlp_tile(
        rows_step, c_ref, dy_ref, we_ref, ws_ref, be_ref, outs, scratch, hooks(step, schedule)
    )
    pl.when(step == pl.num_programs(0) - 1)(close_all)


def mlp_reduce(sizes, back, c, dy, we, ws, be, before, grads, tile=512, rows_step=512):
    tokens, model = c.shape
    in_specs, out_specs, out_shape, scratch = mlp_parts(tokens, model, we.shape[1], tile)
    expand, shrink = grads
    depth, rows = sizes["z"], expand.shape[3]
    grown, full = expand.shape[-1] // 2, shrink.shape[-1]
    scratch = scratch + [pltpu.SemaphoreType.DMA((2, 16)), pltpu.VMEM((tokens, model), jnp.float32)]
    for columns in (full, grown):
        scratch += ReduceNear.scratch(sizes, rows, columns, columns // 2)
    return pl.pallas_call(
        functools.partial(mlp_reduce_kernel, sizes, rows_step),
        grid=(we.shape[1] // tile,),
        in_specs=[pl.BlockSpec(memory_space=pltpu.SMEM)] + in_specs + [any_place] * 4,
        out_specs=out_specs[1:] + [whole_vmem] * 4,
        out_shape=out_shape[1:]
        + [low_shape(depth, rows, grown), low_shape(depth, rows, full)]
        + [low_shape(tokens // 2, model)] * 2,
        scratch_shapes=scratch,
        compiler_params=params(4, 60),
        cost_estimate=small_cost,
        name="mlp_reduce",
    )(back, c, dy, we, ws, be, *before, *grads)


def attend_back_kernel(sizes, blocks, *refs):
    refs = Refs(refs)
    pulled_ref, middle_ref, upstream_ref, mixed, mixing, gain_ref = refs.take(6)
    projected, lse_ref, expand, shrink, done_expand, done_shrink, sent = refs.take(7)
    back_ref, grad_ref, sums_ref, mixing_quad, expand_quad, shrink_quad = refs.take(6)
    expand_out, shrink_out, far_out = refs.take(3)
    turned, key_sum, value_sum, sems, branch_all, mixed_grad, theirs = refs.take(7)
    spot = Spot(sizes)
    mover = Mover(spot, sems)
    k = spot.k
    half, grown, width = mixing_quad.shape[-1], expand_quad.shape[-1], shrink_quad.shape[-1]
    jobs = [
        ReduceNear(mover, shrink.at[k], shrink.at[1 - k], width // 2, shrink_quad, refs.take(6)),
        ReduceNear(mover, *core_halves(expand, k, grown), grown // 2, expand_quad, refs.take(6)),
        ReduceNear(mover, None, theirs, half // 2, mixing_quad, refs.take(6)),
    ]
    deep = [
        ReduceDeep(mover, done_expand, *refs.take(1)),
        ReduceDeep(mover, done_shrink, *refs.take(1)),
    ]
    ending = Finish(mover, *refs.take(2))
    rows_copy = [mover.copy(sent.at[block_rows(0)], far_out, "c")]

    def open_all():
        spot.meet(all_axes)
        start(jobs[0].first)
        start(rows_copy)
        for job in deep:
            start(job.copies)

    def finish():
        wait(deep[0].copies)
        ending.summed[...] = deep[0].result()
        start(ending.copies)
        wait(deep[1].copies)
        shrink_out[...] = deep[1].result()

    def close_all():
        wait(ending.copies)
        ending.write(expand_out)
        jobs[1].close()
        jobs[2].close()
        wait(rows_copy)

    step = pl.program_id(0)
    between = hooks(
        step,
        [
            (0, 0, open_all),
            (1, 0, lambda: start(jobs[1].first)),
            (2, 0, jobs[0].go_near),
            (4, 0, jobs[1].go_near),
            (4, 2, jobs[2].go_near),
            (7, 0, finish),
            (10, 0, jobs[0].go_far),
            (10, 2, jobs[1].go_far),
            (11, 0, jobs[2].go_far),
            (11, 3, jobs[0].close),
        ],
    )
    between(0)

    @pl.when(step < blocks)
    def _():
        rows = pl.ds(pl.multiple_of(step * BLK, BLK), BLK)
        pulled = pulled_ref[...]
        upstream = upstream_ref[...].astype(jnp.float32)
        normal, inverse = normal_rows(middle_ref[...])
        total = upstream + norm_pull(pulled, normal, inverse, gain_ref[5:6, :])
        grad_ref[...] = total
        branch = total.astype(low)
        branch_all[rows, :] = branch
        mixed_grad[rows, :] = nt(branch, mixing[...]).astype(low)

        @pl.when(step == 0)
        def _():
            sums_ref[...] = jnp.zeros_like(sums_ref)

        for row, value in enumerate((branch.astype(jnp.float32), pulled * normal, pulled, upstream)):
            sums_ref[row : row + 1, :] += jnp.sum(value, axis=0, keepdims=True)

    @pl.when(step == blocks - 1)
    def _():
        across = jnp.transpose(mixed[...])
        for core, target in ((1 - k, theirs), (k, jobs[2].total)):
            piece = nn(across, branch_all[:, span(core * half, half)]).astype(low)
            target[...] = piece.reshape(target.shape)
        start(jobs[2].first)

    @pl.when(step >= blocks)
    def _():
        columns = span((step - blocks) * PAIR, PAIR)
        attend_back_pair(
            blocks, projected, mixed_grad.at[:, columns], lse_ref, back_ref, turned, key_sum,
            value_sum, lambda block: block > 0 and between(block),
        )

    pl.when(step == pl.num_programs(0) - 1)(close_all)


def attend_back(sizes, pulled, middle, upstream, mixed, mixing, gain, projected, lse, grads, quads, sent):
    tokens, model = upstream.shape
    pairs = model // PAIR
    blocks = tokens // BLK
    expand, shrink = grads
    depth, rows = sizes["z"], expand.shape[3]
    lead = (sizes["c"], sizes["z"], sizes["y"])
    half, grown, full = model // 2, expand.shape[-1] // 2, shrink.shape[-1]
    by_rows = pl.BlockSpec((BLK, model), lambda g: (jnp.minimum(g, blocks - 1), 0))

    def pair(g):
        return jnp.maximum(g - blocks, 0)

    triple = pl.BlockSpec((tokens, 3 * PAIR), lambda g: (0, pair(g)))
    scratch = [
        pltpu.VMEM((PAIR, tokens), low),
        pltpu.VMEM((tokens, PAIR), jnp.float32),
        pltpu.VMEM((tokens, PAIR), jnp.float32),
        pltpu.SemaphoreType.DMA((2, 32)),
        pltpu.VMEM((tokens, model), low),
        pltpu.VMEM((tokens, model), low),
        pltpu.VMEM((*lead, rows, half), low),
    ]
    for columns in (full, grown, half):
        scratch += ReduceNear.scratch(sizes, rows, columns, columns // 2)
    for columns in (grown, full):
        scratch += [pltpu.VMEM((depth - 1, rows, columns), low)]
    scratch += Finish.scratch(rows, grown)
    return pl.pallas_call(
        functools.partial(attend_back_kernel, sizes, blocks),
        grid=(blocks + pairs,),
        in_specs=[by_rows] * 3
        + [whole_vmem] * 3
        + [triple, pl.BlockSpec((None, 8, tokens), lambda g: (pair(g), 0, 0))]
        + [any_place] * 2
        + [whole_vmem] * 2
        + [any_place],
        out_specs=[triple, by_rows] + [whole_vmem] * 6 + [any_place],
        out_shape=[
            low_shape(*projected.shape),
            jax.ShapeDtypeStruct((tokens, model), jnp.float32),
            jax.ShapeDtypeStruct((8, model), jnp.float32),
            low_shape(depth, rows, half),
            low_shape(depth, rows, grown),
            low_shape(depth, rows, full),
            jax.ShapeDtypeStruct((2, rows // 2, grown), jnp.float32),
            jax.ShapeDtypeStruct((rows, full), jnp.float32),
            low_shape(BLK, model),
        ],
        scratch_shapes=scratch,
        compiler_params=params(5, 60),
        cost_estimate=small_cost,
        name="attend_back",
    )(pulled, middle, upstream, mixed, mixing, gain, projected, lse, *grads, *quads, sent)


end_chunks = 4


def end_kernel(sizes, *refs):
    refs = Refs(refs)
    back_ref, back_far, low_far, joint_far, rows_far, middle_far = refs.take(6)
    gain_ref, row_sums, bias_a, bias_b, mixing_quad, expand_quad, shrink_quad, sent_out = refs.take(8)
    out, vector_out, mixing_out, expand_out, shrink_out, kept = refs.take(6)
    arrived_rows, far_out = refs.take(2)
    sems, steps, arrived = refs.take(3)
    grads, low_rows, turned, joint, rows_in, middle, sent = refs.take(7)
    spot = Spot(sizes)
    mover = Mover(spot, sems)
    width, tokens = joint.shape[-1] // 2, rows_in.shape[0]
    part = width // end_chunks
    tile = 384
    loads = [
        mover.local(far, near)
        for far, near in (
            (back_far, grads),
            (low_far, low_rows),
            (joint_far, joint),
            (rows_far, rows_in),
            (middle_far, middle),
        )
    ]
    jobs, deeps, ends, others_half = [], [], [], []
    for number in range(end_chunks):
        theirs, quad = refs.take(2)
        others_half.append(theirs)
        jobs.append(ReduceNear(mover, None, theirs, 2 * part // 3, quad, refs.take(6)))
        deeps.append(ReduceDeep(mover, quad, *refs.take(1)))
        ends.append(Finish(mover, *refs.take(2)))
    others = [
        ReduceDeep(mover, quad, *refs.take(1))
        for quad in (mixing_quad, expand_quad, shrink_quad)
    ]
    other_ends = [Finish(mover, *refs.take(2)) for _ in range(2)]
    hops = [
        mover.copy(steps.at[number], arrived.at[number], name)
        for number, name in enumerate(("k", "c", "y"))
    ]
    spread = [
        mover.copy(steps.at[3], arrived.at[2 + by], "z", by) for by in range(1, sizes["z"])
    ]
    rows_copy = mover.copy(sent, arrived_rows, "c")
    out_copy = mover.copy(sent_out.at[block_rows(1)], far_out, "c")

    def gradient(core, number, target):
        @pl.loop(0, part // tile)
        def _(t):
            columns = span(core * width + number * part + t * tile, tile)
            piece = nn(turned[...], grads[:, columns]).astype(low)
            target[..., span(t * tile, tile)] = piece.reshape(*target.shape[:-1], tile)

    sums = {}

    def pull_block(number):
        rows = block_rows(number)
        pulled = grads[rows, :]
        upstream = nt(pulled, joint[...])
        normal, inverse = normal_rows(rows_in[rows, :].astype(jnp.float32))
        middle[rows, :] += norm_pull(upstream, normal, inverse, gain_ref[0:1, :])
        for name, value in (
            ("gain", upstream * normal),
            ("shift", upstream),
            ("back", pulled.astype(jnp.float32)),
        ):
            value = jnp.sum(value, axis=0, keepdims=True)
            sums[name] = sums[name] + value if name in sums else value

    def hop(number):
        wait([hops[number]])
        steps[number + 1] = steps[number] + arrived[number]
        start([hops[number + 1]] if number < 2 else spread)

    start(loads[:2])
    spot.meet(all_axes)
    start([out_copy])
    for job in others:
        start(job.copies)
    wait(loads[:2])
    start(loads[2:])
    turned[...] = jnp.transpose(low_rows[...])
    for number, job in enumerate(jobs):
        gradient(1 - spot.k, number, others_half[number])
        start(job.first)
        gradient(spot.k, number, job.total)
        job.go_near()
    wait(loads[2:])
    for number in range(tokens // BLK):
        pull_block(number)
        jobs[number].go_far()
    steps[0] = jnp.zeros(steps.shape[1:], jnp.float32)
    steps[0, 4:8, :] = row_sums[:4, :]
    lane = lax.broadcasted_iota(jnp.int32, (1, PAIR), 1)
    for (one, two), source in hidden_pairs(steps.shape[2], bias_a.shape[1]):
        a, b = bias_a[:, source], bias_b[:, source]
        steps[(0, *one)] = jnp.where(lane < HD, a, pltpu.roll(b, HD, 1))
        steps[(0, *two)] = jnp.where(lane < HD, pltpu.roll(a, HD, 1), b)
    steps[0, 0:1, :] = sums["gain"]
    steps[0, 1:2, :] = sums["shift"]
    for pair in range(H // 2):
        for row, third in ((2, 0), (3, 2)):
            steps[0, row : row + 1, pair * PAIR : (pair + 1) * PAIR] = sums["back"][
                :, (3 * pair + third) * PAIR : (3 * pair + third + 1) * PAIR
            ]
    start(hops[:1])
    for place in range(2):
        sent[block_rows(place), :] = chosen_block(back_ref[2 + place], middle).astype(low)
    hop(0)
    start([rows_copy])
    for job, deep in zip(jobs[:2], deeps[:2]):
        job.close()
        start(deep.copies)
    for place in range(2):
        kept[block_rows(place), :] = chosen_block(back_ref[place], middle)
    for job, ending in zip(others, other_ends):
        wait(job.copies)
        ending.summed[...] = job.result()
        start(ending.copies)
    wait(others[2].copies)
    shrink_out[...] = others[2].result()
    for job, deep in zip(jobs[2:], deeps[2:]):
        job.close()
        start(deep.copies)
    hop(1)
    hop(2)
    for ending, target in zip(other_ends, (mixing_out, expand_out)):
        wait(ending.copies)
        ending.write(target)
    for deep, ending in zip(deeps, ends):
        wait(deep.copies)
        ending.summed[...] = deep.result()
        start(ending.copies)
    wait(spread)
    total = steps[3]
    for by in range(1, sizes["z"]):
        total = total + arrived[2 + by]
    vector_out[...] = total
    for number, ending in enumerate(ends):
        wait(ending.copies)
        ending.write(out, pl.ds(number * part, part))
    wait([rows_copy, out_copy])


def end(sizes, back, joint_back, first_low, joint, rows_in, middle_grad, gain, row_sums, bias_a, bias_b, quads, sent):
    tokens, model = rows_in.shape
    width = joint.shape[1] // 2
    lead = (sizes["c"], sizes["z"], sizes["y"])
    depth = sizes["z"]
    rows = model // (lead[0] * lead[1] * lead[2])
    part = width // end_chunks
    half, grown, full = [quad.shape[-1] for quad in quads]
    scratch = [
        pltpu.SemaphoreType.DMA((2, 80)),
        pltpu.VMEM((4, *gain.shape), jnp.float32),
        pltpu.VMEM((2 + depth, *gain.shape), jnp.float32),
        pltpu.VMEM(joint_back.shape, low),
        pltpu.VMEM(first_low.shape, low),
        pltpu.VMEM(first_low.shape[::-1], low),
        pltpu.VMEM(joint.shape, low),
        pltpu.VMEM(rows_in.shape, low),
        pltpu.VMEM(middle_grad.shape, jnp.float32),
        pltpu.VMEM((tokens // 2, model), low),
    ]
    for number in range(end_chunks):
        scratch += [pltpu.VMEM((*lead, rows, part), low), pltpu.VMEM((depth, rows, part), low)]
        scratch += ReduceNear.scratch(sizes, rows, part, 2 * part // 3)
        scratch += [pltpu.VMEM((depth - 1, rows, part), low)]
        scratch += Finish.scratch(rows, part)
    scratch += [pltpu.VMEM((depth - 1, rows, columns), low) for columns in (half, grown, full)]
    for columns in (half, grown):
        scratch += Finish.scratch(rows, columns)
    own = rows // 2
    shapes = [(2, own, width), gain.shape, (2, own, half), (2, own, grown), (rows, full)]
    shapes.append((tokens // 2, model))
    return pl.pallas_call(
        functools.partial(end_kernel, sizes),
        in_specs=[pl.BlockSpec(memory_space=pltpu.SMEM)]
        + [any_place] * 5
        + [whole_vmem] * 7
        + [any_place],
        out_specs=[whole_vmem] * 6 + [any_place] * 2,
        out_shape=[jax.ShapeDtypeStruct(shape, jnp.float32) for shape in shapes]
        + [low_shape(tokens // 2, model), low_shape(BLK, model)],
        scratch_shapes=scratch,
        compiler_params=params(6, 60),
        cost_estimate=small_cost,
        name="end",
    )(back, joint_back, first_low, joint, rows_in, middle_grad, gain, row_sums, bias_a, bias_b, *quads, sent)


def last_kernel(ctx_ref, *refs):
    refs = Refs(refs)
    joint_part, mixing_part, expand_a, expand_b, shrink_a, shrink_b = refs.take(6)
    kept_grad, far_grad, kept_out, far_one, far_two = refs.take(5)
    (vector_sum,) = refs.take(1)
    states = [refs.take(3) for _ in range(5)]
    grad_out, block_out = refs.take(2)
    news = [refs.take(4) for _ in range(5)]
    here = ctx_ref[0]
    grad_out[here] = kept_grad[...]
    grad_out[1 - here] = far_grad[...].astype(jnp.float32)
    block_out[here] = kept_out[...]
    block_out[1 - here, :BLK, :] = far_one[...]
    block_out[1 - here, BLK:, :] = far_two[...]

    def update(number, where, gradient, rate=0.05, decay=0.1):
        weight, first, second = [ref[where] for ref in states[number]]
        results = adam_update(weight, first, second, gradient, rate, decay)
        for ref, value in zip(news[number], (*results, results[0].astype(low))):
            ref[where] = value

    every = slice(None)
    pairs = joint_part.shape[2] // (3 * PAIR)
    for core in range(2):
        for pair in range(pairs):
            for third in range(3):
                first = ((third * 2 + core) * pairs + pair) * PAIR
                source = (pair * 3 + third) * PAIR
                update(
                    0,
                    (every, pl.ds(first, PAIR)),
                    joint_part[core, :, source : source + PAIR],
                )
        half = mixing_part.shape[2]
        update(1, (every, pl.ds(core * half, half)), mixing_part[core])
        lane = lax.broadcasted_iota(jnp.int32, (1, PAIR), 1)
        for chip in range(0, expand_a.shape[2] // HD, 2):
            a = expand_a[core, :, chip * HD : chip * HD + PAIR]
            b = expand_b[core, :, chip * HD : chip * HD + PAIR]
            even = jnp.where(lane < HD, a, pltpu.roll(b, HD, 1))
            odd = jnp.where(lane < HD, pltpu.roll(a, HD, 1), b)
            for number, value in ((chip, even), (chip + 1, odd)):
                update(2, (every, pl.ds((number * 2 + core) * PAIR, PAIR)), value)
    rows = shrink_a.shape[0]
    update(3, (pl.ds(0, rows), every), shrink_a[...])
    update(3, (pl.ds(rows, rows), every), shrink_b[...])
    table_rows, columns = states[4][0].shape
    moved = pltpu.roll(vector_sum[...], vector_sum.shape[1] - ctx_ref[1] * columns, 1)
    update(4, (every, every), moved[:table_rows, :columns], 0.5, 0.0)


def last(ctx, parts, kept_grad, far_grad, kept_out, far_outs, vector_sum, states):
    shapes = [jax.ShapeDtypeStruct((2, *kept_grad.shape), jnp.float32), low_shape(2, *kept_out.shape)]
    for weight, _, _ in states:
        shapes += [jax.ShapeDtypeStruct(weight.shape, jnp.float32)] * 3
        shapes.append(low_shape(*weight.shape))
    flat = [array for state in states for array in state]
    return pl.pallas_call(
        last_kernel,
        in_specs=[pl.BlockSpec(memory_space=pltpu.SMEM)] + [whole_vmem] * (12 + len(flat)),
        out_specs=[whole_vmem] * len(shapes),
        out_shape=shapes,
        compiler_params=pltpu.CompilerParams(vmem_limit_bytes=56 << 20),
        cost_estimate=small_cost,
        name="last",
    )(ctx, *parts, kept_grad, far_grad, kept_out, *far_outs, vector_sum, *flat)


def layer_norm(values, gain_row, shift_row):
    centered = values - jnp.mean(values, axis=-1, keepdims=True)
    variance = jnp.mean(centered * centered, axis=-1, keepdims=True)
    inverse = lax.rsqrt(variance + norm_eps)
    normal_part = centered * inverse
    return (normal_part * gain_row + shift_row, normal_part, inverse)


def norm_back(upstream, normal_part, inverse, gain_row):
    scaled = upstream * gain_row
    inner_sum = jnp.mean(scaled, axis=-1, keepdims=True)
    along_sum = jnp.mean(scaled * normal_part, axis=-1, keepdims=True)
    values_grad = inverse * (scaled - inner_sum - normal_part * along_sum)
    return (values_grad, jnp.sum(upstream * normal_part, axis=0), jnp.sum(upstream, axis=0))


def adam_update(weight, moment_one, moment_two, gradient, step_rate, decay_rate):
    first_new = 0.5 * moment_one + 0.5 * gradient
    second_new = 0.5 * moment_two + 0.5 * gradient * gradient
    correct = 1.0 - 0.5**STEP
    direction = first_new / correct / (jnp.sqrt(second_new / correct) + adam_eps)
    updated = weight - step_rate * (direction + decay_rate * weight)
    return (updated, first_new, second_new)


def to_groups(matrix):
    row_count = matrix.shape[0]
    return matrix.reshape(row_count, H // group_heads, group_heads, HD).transpose(1, 0, 2, 3)


def from_groups(stacked):
    return stacked.transpose(1, 0, 2, 3).reshape(stacked.shape[1], H * HD)


def tile_scores(queries, key_rows, allowed):
    products = jnp.einsum("rgd,lgd->grl", queries, key_rows, preferred_element_type=jnp.float32)
    return jnp.where(allowed[None], products * 0.125, -1e30)


def tile_forward(queries, key_rows, value_rows, allowed):
    scores = tile_scores(queries, key_rows, allowed)
    largest = jnp.max(scores, axis=-1, keepdims=True)
    exponent = jnp.exp(scores - largest)
    row_total = jnp.sum(exponent, axis=-1, keepdims=True)
    weights = (exponent / row_total).astype(low)
    mixed = jnp.einsum("grl,lgd->rgd", weights, value_rows, preferred_element_type=jnp.float32)
    return (mixed, (largest + jnp.log(row_total))[..., 0])


def tile_backward(queries, key_rows, value_rows, allowed, logsum, upstream):
    scores = tile_scores(queries, key_rows, allowed)
    recomputed = jnp.exp(scores - logsum[..., None])
    value_grad = jnp.einsum(
        "grl,rgd->lgd", recomputed.astype(low), upstream, preferred_element_type=jnp.float32
    )
    weight_grad = jnp.einsum(
        "rgd,lgd->grl", upstream, value_rows, preferred_element_type=jnp.float32
    )
    inner_sum = jnp.sum(recomputed * weight_grad, axis=-1, keepdims=True)
    score_grad = (recomputed * (weight_grad - inner_sum)).astype(low)
    query_grad = (
        jnp.einsum("grl,lgd->rgd", score_grad, key_rows, preferred_element_type=jnp.float32) * 0.125
    )
    key_grad = (
        jnp.einsum("grl,rgd->lgd", score_grad, queries, preferred_element_type=jnp.float32) * 0.125
    )
    return (query_grad, key_grad, value_grad)


def spread_forward(queries, key_value, allowed):
    def one_sequence(pieces):
        queries, key_value, allowed = pieces
        width = queries.shape[1]
        mixed, logsum = lax.map(
            lambda triple: tile_forward(triple[0], triple[1], triple[2], allowed),
            (to_groups(queries), to_groups(key_value[:, :width]), to_groups(key_value[:, width:])),
        )
        return (from_groups(mixed), logsum)

    return lax.map(one_sequence, (queries, key_value, allowed))


def spread_backward(queries, key_value, allowed, logsum, upstream):
    def one_sequence(pieces):
        queries, key_value, allowed, logsum, upstream = pieces
        width = queries.shape[1]
        query_grad, key_grad, value_grad = lax.map(
            lambda member: tile_backward(
                member[0], member[1], member[2], allowed, member[3], member[4]
            ),
            (
                to_groups(queries),
                to_groups(key_value[:, :width]),
                to_groups(key_value[:, width:]),
                logsum,
                to_groups(upstream),
            ),
        )
        return (
            from_groups(query_grad),
            jnp.concatenate([from_groups(key_grad), from_groups(value_grad)], axis=1),
        )

    return lax.map(one_sequence, (queries, key_value, allowed, logsum, upstream))


class Slice:
    def __init__(self, ctx_size, wshard_size):
        rest = wshard_size // 2
        self.sizes = {"c": ctx_size, "z": 4, "y": rest // 4, "k": 2}

    def here(self):
        flat = lax.axis_index(axes)
        found = {}
        for name in ("k", "y", "z", "c"):
            found[name] = flat % self.sizes[name]
            flat = flat // self.sizes[name]
        return found

    def shift(self, value, name, by):
        pairs = []
        sizes = self.sizes
        for c in range(sizes["c"]):
            for z in range(sizes["z"]):
                for y in range(sizes["y"]):
                    for k in range(sizes["k"]):
                        spot = {"c": c, "z": z, "y": y, "k": k}
                        goal = dict(spot)
                        goal[name] = (spot[name] + by) % sizes[name]
                        pairs.append((self.flat(spot), self.flat(goal)))
        return lax.ppermute(value, axes, pairs)

    def flat(self, spot):
        sizes = self.sizes
        return ((spot["c"] * sizes["z"] + spot["z"]) * sizes["y"] + spot["y"]) * sizes["k"] + spot[
            "k"
        ]

    def stack(self, array, name, here):
        size = self.sizes[name]
        parts = [array] + [self.shift(array, name, by) for by in range(1, size)]
        if size > 4:
            ordered = [parts[(-place) % size] for place in range(size)]
            return jnp.roll(jnp.stack(ordered), here[name], axis=0)
        return jnp.stack(
            [lax.select_n((here[name] - place) % size, *parts) if size > 2 else
             jnp.where(here[name] == place, parts[0], parts[1]) for place in range(size)]
        )

    def reach(self, pieces, name):
        grown = list(pieces)
        for by in range(1, self.sizes[name]):
            for array, place in pieces:
                moved = dict(place)
                moved[name] = (place[name] - by) % self.sizes[name]
                grown.append((self.shift(array, name, by), moved))
        return grown

    def gather_split(self, stacked, cut, here):
        sizes = self.sizes
        depth, rows, columns = stacked.shape
        out = jnp.zeros((sizes["c"], depth, sizes["y"], rows, columns), stacked.dtype)
        for low_column, high_column, order in ((0, cut, "cy"), (cut, columns, "yc")):
            pieces = [(stacked[:, :, low_column:high_column], here)]
            for name in order:
                pieces = self.reach(pieces, name)
            for array, place in pieces:
                out = lax.dynamic_update_slice(
                    out, array[None, :, None], (place["c"], 0, place["y"], 0, low_column)
                )
        return out.reshape(-1, columns)

    def send_terms(self, value, name, place, here):
        size = self.sizes[name]
        own = lax.dynamic_index_in_dim(value, here[name], place, False)
        moved = [
            self.shift(
                lax.dynamic_index_in_dim(value, (here[name] + by) % size, place, False), name, by
            )
            for by in range(1, size)
        ]
        return own, moved

    def add_terms(self, terms, kind=low):
        own, moved = terms
        total = own.astype(jnp.float32)
        for other in moved:
            total = total + other.astype(jnp.float32)
        return total.astype(kind)

    def everywhere(self, value):
        for name in ("k", "c", "y", "z"):
            total = value
            for by in range(1, self.sizes[name]):
                total = total + self.shift(value, name, by)
            value = total
        return value


def tie(value, *others):
    return lax.optimization_barrier((value, others))[0]


def by_core(core, first, second, axis):
    return jnp.where(
        core == 0,
        jnp.concatenate([first, second], axis=axis),
        jnp.concatenate([second, first], axis=axis),
    )


def pick(core, array, axis):
    return (
        lax.dynamic_index_in_dim(array, core, axis, False),
        lax.dynamic_index_in_dim(array, 1 - core, axis, False),
    )


def gather_far(grid, here, pieces):
    joint_halves, table, mixing_halves, expand_a, expand_b, shrink_a, shrink_b = pieces
    core = here["k"]

    def chip_rows(halves):
        own, other = pick(core, halves, 0)
        return by_core(core, own, grid.shift(other, "k", 1), 0)

    def everyone(block):
        width = block.shape[1]
        return grid.gather_split(grid.stack(block, "z", here), width // 2, here)

    def both(block, axis):
        own = everyone(block)
        return by_core(core, own, grid.shift(own, "k", 1), axis)

    return (
        both(chip_rows(joint_halves), 1),
        everyone(by_core(core, table, grid.shift(table, "k", 1), 0)),
        both(chip_rows(mixing_halves), 1),
        both(chip_rows(expand_a), 1),
        both(chip_rows(expand_b), 1),
        both(shrink_a, 0),
        both(shrink_b, 0),
    )


def reduce_far(grid, here, gradient, by_rows):
    core = here["k"]
    sizes = grid.sizes
    if by_rows:
        own, other = pick(core, gradient.reshape(2, -1, gradient.shape[1]), 0)
    else:
        own, other = pick(core, gradient.reshape(gradient.shape[0], 2, -1), 1)
    total = grid.add_terms((own, [grid.shift(other, "k", 1)]))
    total = total.reshape(sizes["c"], sizes["z"], sizes["y"], -1, own.shape[-1])
    for name, place in (("y", 2), ("c", 0)):
        total = grid.add_terms(grid.send_terms(total, name, place, here))
    total = grid.add_terms(grid.send_terms(total, "z", 0, here), jnp.float32)
    if by_rows:
        return total
    kept, other = pick(core, total.reshape(2, -1, total.shape[1]), 0)
    return by_core(core, kept[None], grid.shift(other, "k", 1)[None], 0)


def body(
    grid,
    block_input,
    block_order,
    cotangent,
    joint_weight,
    mixing_weight,
    expand_weight,
    shrink_weight,
    vectors,
    joint_first,
    mixing_first,
    expand_first,
    shrink_first,
    vectors_first,
    joint_second,
    mixing_second,
    expand_second,
    shrink_second,
    vectors_second,
):
    here = grid.here()
    sizes = grid.sizes
    ctx, ctx_size = here["c"], sizes["c"]
    seq_count, row_count, width = block_input.shape
    half = width // 2
    pairs = H // 2
    hidden_width = expand_weight.shape[1]
    own_rows = joint_weight.shape[0]
    slot = shrink_weight.shape[0]
    sub = slot // 2
    chips = hidden_width // (2 * slot)
    tokens = seq_count * row_count
    row_blocks = row_count // BLK
    near = ctx_size == 2 and seq_count == 2 and sizes["y"] == 2 and own_rows % 32 == 0

    def hidden_sets(shard):
        parts = shard.astype(low).reshape(own_rows, chips, 2, 2, sub)
        return [
            parts[:, :, :, number].transpose(2, 0, 1, 3).reshape(2, own_rows, chips * sub)
            for number in range(2)
        ]

    table = jnp.pad(vectors.T.astype(low), ((0, 0), (0, 128 - vectors.shape[0])))
    if near:
        joint, tables, *quads, far_input, far_upstream, next_half, next_shrink = begin(
            sizes,
            joint_weight,
            table,
            mixing_weight,
            expand_weight,
            shrink_weight,
            block_input,
            cotangent,
        )
    else:
        joint_halves = (
            joint_weight.astype(low)
            .reshape(own_rows, 3, 2, pairs // 2, PAIR)
            .transpose(2, 0, 3, 1, 4)
            .reshape(2, own_rows, 3 * half)
        )
        mixing_halves = mixing_weight.astype(low).reshape(own_rows, 2, half).transpose(1, 0, 2)
        shrink_low = shrink_weight.astype(low)
        pieces = [joint_halves, table, mixing_halves, *hidden_sets(expand_weight)]
        pieces += [shrink_low[:sub], shrink_low[sub:]]
        joint, tables, mixing, expand_a, expand_b, shrink_a, shrink_b = gather_far(
            grid, here, pieces
        )
    joint = joint.reshape(width, 3 * width)
    if near:
        order = lax.dynamic_slice_in_dim(block_order, ctx, 1, 0)[0]
        blocks = order.shape[0]
        stored = jnp.arange(blocks, dtype=jnp.int32)
        moved = jnp.where(stored // row_blocks == ctx, 0, row_blocks) + stored % row_blocks
        place = jnp.sum(jnp.where(order[None, :] == stored[:, None], moved[None, :], 0), axis=1)
        back = jnp.sum(jnp.where(moved[None, :] == stored[:, None], order[None, :], 0), axis=1)
        place, back = place.astype(jnp.int32), back.astype(jnp.int32)
    lead = (sizes["c"], sizes["z"], sizes["y"])
    def by_device(expand_grad, shrink_grad):
        return (
            expand_grad.reshape(*lead, -1, expand_grad.shape[1]),
            shrink_grad.reshape(2, *lead, -1, width),
        )

    if near:
        mixed_low, logsum, input_low, first_low, projected, vector_values, hidden_a, hidden_b, *gathered = attend(
            sizes,
            place,
            block_input,
            far_input,
            joint,
            tables.reshape(width, -1),
            cotangent,
            quads,
            next_half,
            next_shrink,
        )
        mixing, expand_a, shrink_a, *quads, last_upstream = gathered
        mixing = mixing.reshape(width, width)
        *before, expand_grad_a, shrink_grad_a, bias_a, middle, second_low, upstream, expand_b, shrink_b = mlp_gather(
            sizes,
            place,
            mixed_low,
            input_low,
            mixing,
            vector_values,
            expand_a.reshape(width, -1),
            shrink_a.reshape(-1, width),
            hidden_a,
            cotangent,
            far_upstream,
            last_upstream,
            quads,
        )
        second_grad, expand_grad_b, shrink_grad_b, bias_b, *quads, kept_out, sent_out = mlp_reduce(
            sizes,
            back,
            second_low,
            upstream,
            expand_b.reshape(width, -1),
            shrink_b.reshape(-1, width),
            hidden_b,
            before,
            by_device(expand_grad_a, shrink_grad_a),
        )
    else:
        vector_values = (
            tables.reshape(width, -1)[:, : vectors.shape[0]].T.astype(jnp.float32)
        )
        joint_shift = jnp.stack(
            [
                vector_values[2].reshape(pairs, PAIR),
                jnp.zeros((pairs, PAIR), jnp.float32),
                vector_values[3].reshape(pairs, PAIR),
            ],
            axis=1,
        ).reshape(1, -1)
        hidden_bias = vector_values[8:].reshape(chips, 2, 2, sub).transpose(2, 1, 0, 3).reshape(2, 1, -1)
        input_low = block_input.reshape(tokens, width)
        upstream = cotangent.reshape(tokens, width)
        input_rows = input_low.astype(jnp.float32)
        normed_first, normal_first, inverse_first = layer_norm(
            input_rows, vector_values[0], vector_values[1]
        )
        first_low = normed_first.astype(low)
        projected = (nn(first_low, joint) + joint_shift).astype(low)
        by_part = projected.reshape(seq_count, row_count, pairs, 3, PAIR)
        queries, keys, values = [
            by_part[:, :, :, part].reshape(seq_count, row_count, width) for part in range(3)
        ]
        key_value = lax.all_gather(
            jnp.concatenate([keys, values], axis=2), "ctx", axis=1, tiled=True
        )
        own_blocks = lax.dynamic_slice_in_dim(block_order, ctx * row_blocks, row_blocks, 1)
        query_block = jnp.repeat(own_blocks, BLK, axis=1, total_repeat_length=row_count)
        key_block = jnp.repeat(block_order, BLK, axis=1, total_repeat_length=key_value.shape[1])
        allowed = key_block[:, None, :] <= query_block[:, :, None]
        mixed, logsum = spread_forward(queries, key_value, allowed)
        mixed_low = mixed.astype(low).reshape(tokens, width)
        mixing = mixing.reshape(width, width)
        middle = input_rows + (nn(mixed_low, mixing) + vector_values[4])
        normed_second, normal_second, inverse_second = layer_norm(
            middle, vector_values[5], vector_values[6]
        )
        second_low = normed_second.astype(low)
        before = (middle + vector_values[7], jnp.zeros_like(middle))
        *before, expand_grad_a, shrink_grad_a, bias_a = mlp(
            second_low,
            upstream,
            expand_a.reshape(width, -1),
            shrink_a.reshape(-1, width),
            hidden_bias[0],
            before,
        )
        result, second_grad, expand_grad_b, shrink_grad_b, bias_b = mlp(
            second_low,
            upstream,
            expand_b.reshape(width, -1),
            shrink_b.reshape(-1, width),
            hidden_bias[1],
            before,
        )
        block_output = result.astype(low).reshape(block_input.shape)
    if near:
        joint_back, middle_grad, sums, *last_quads, expand_part_a, shrink_part_a, far_one = attend_back(
            sizes,
            second_grad,
            middle,
            upstream,
            mixed_low,
            mixing,
            vector_values,
            projected,
            logsum,
            by_device(expand_grad_b, shrink_grad_b),
            quads,
            sent_out,
        )
    else:
        middle_part, gain_two, shift_two = norm_back(
            second_grad, normal_second, inverse_second, vector_values[5]
        )
        middle_grad = upstream.astype(jnp.float32) + middle_part
        branch_low = middle_grad.astype(low)
        mixing_grad = outer_sum(mixed_low, branch_low).astype(low)
        mixed_grad = nt(branch_low, mixing).astype(low)
        query_grad, key_value_grad = spread_backward(
            queries, key_value, allowed, logsum, mixed_grad.reshape(seq_count, row_count, width)
        )
        summed = lax.psum_scatter(
            key_value_grad.astype(low), "ctx", scatter_dimension=1, tiled=True
        )
        parts = [query_grad.astype(low), summed[..., :width], summed[..., width:]]
        joint_back = jnp.stack(
            [part.reshape(tokens, pairs, PAIR) for part in parts], axis=2
        ).reshape(tokens, 3 * width)
        mixing_part = reduce_far(grid, here, mixing_grad, False)
        expand_part_a, shrink_part_a, expand_part_b, shrink_part_b = [
            reduce_far(grid, here, grad, number % 2 == 1)
            for number, grad in enumerate(
                (expand_grad_a, shrink_grad_a, expand_grad_b, shrink_grad_b)
            )
        ]

    def column_sum(rows):
        return jnp.sum(rows.astype(jnp.float32), axis=0)

    weights = (joint_weight, mixing_weight, expand_weight, shrink_weight)
    firsts = (joint_first, mixing_first, expand_first, shrink_first)
    seconds = (joint_second, mixing_second, expand_second, shrink_second)
    if near:
        joint_part, vector_sum, mixing_part, expand_part_b, shrink_part_b, kept_grad, far_grad, far_two = end(
            sizes,
            back,
            joint_back,
            first_low,
            joint,
            input_low,
            middle_grad,
            vector_values,
            sums,
            bias_a,
            bias_b,
            last_quads,
            sent_out,
        )
        input_gradient, block_output, *news = last(
            jnp.stack([ctx, lax.axis_index(axes)]).astype(jnp.int32),
            (joint_part, mixing_part, expand_part_a, expand_part_b, shrink_part_a, shrink_part_b),
            kept_grad,
            far_grad,
            kept_out,
            (far_one, far_two),
            vector_sum,
            list(
                zip(
                    (*weights, vectors), (*firsts, vectors_first), (*seconds, vectors_second)
                )
            ),
        )
        updated, moments, squares, copies = [news[number::4] for number in range(4)]
    else:
        hidden_bias_grads = [
            bias.reshape(2, chips, 1, sub).transpose(1, 0, 2, 3) for bias in (bias_a, bias_b)
        ]
        hidden_bias_grad = jnp.concatenate(hidden_bias_grads, axis=2).reshape(-1, width)
        joint_grad = outer_sum(first_low, joint_back).astype(low)
        first_grad = nt(joint_back, joint)
        input_part, gain_one, shift_one = norm_back(
            first_grad, normal_first, inverse_first, vector_values[0]
        )
        input_gradient = (middle_grad + input_part).reshape(block_input.shape)
        joint_sums = column_sum(joint_back).reshape(pairs, 3, PAIR)
        vector_rows = [
            gain_one,
            shift_one,
            joint_sums[:, 0].reshape(-1),
            joint_sums[:, 2].reshape(-1),
            column_sum(branch_low),
            gain_two,
            shift_two,
            column_sum(upstream),
        ]
        joint_part = reduce_far(grid, here, joint_grad, False)
        vector_sum = grid.everywhere(
            jnp.concatenate([jnp.stack(vector_rows), hidden_bias_grad], axis=0)
        )
        joint_sum = (
            joint_part.reshape(2, own_rows, pairs // 2, 3, PAIR)
            .transpose(1, 3, 0, 2, 4)
            .reshape(joint_weight.shape)
        )
        mixing_sum = mixing_part.transpose(1, 0, 2).reshape(mixing_weight.shape)
        expand_sum = jnp.stack(
            [part.reshape(2, own_rows, chips, sub) for part in (expand_part_a, expand_part_b)]
        )
        expand_sum = expand_sum.transpose(2, 3, 1, 0, 4).reshape(expand_weight.shape)
        shrink_sum = jnp.concatenate([shrink_part_a, shrink_part_b], axis=0)
        updated, moments, squares = zip(
            *[
                adam_update(*terms, 0.05, 0.1)
                for terms in zip(
                    weights, firsts, seconds, (joint_sum, mixing_sum, expand_sum, shrink_sum)
                )
            ]
        )
        copies = [array.astype(low) for array in updated]
        vector_sum = lax.dynamic_slice(
            vector_sum, (0, lax.axis_index(axes) * vectors.shape[1]), vectors.shape
        )
        vectors_new, vectors_moment, vectors_square = adam_update(
            vectors, vectors_first, vectors_second, vector_sum, 0.5, 0.0
        )
        updated, moments, squares = [
            (*arrays, array)
            for arrays, array in (
                (updated, vectors_new),
                (moments, vectors_moment),
                (squares, vectors_square),
            )
        ]
        copies.append(vectors_new.astype(low))
    return (block_output, input_gradient, *updated, *moments, *squares, *copies)


def solution(mesh):
    grid = Slice(mesh.shape["ctx"], mesh.shape["wshard"])
    rows = P("wshard", "ctx", None)
    matrix = P(axes, None)
    table = P(None, axes)
    parameters = (matrix, matrix, matrix, matrix, table)
    return jax.shard_map(
        functools.partial(body, grid),
        mesh=mesh,
        in_specs=(rows, P("wshard", None), rows) + parameters * 3,
        out_specs=(rows, rows) + parameters * 4,
        check_vma=False,
    )
```

```python
import functools

import jax
import jax.numpy as jnp
from jax import lax
from jax.experimental import pallas as pl
from jax.experimental.pallas import tpu as pltpu
from jax.sharding import PartitionSpec as P

H = 16
HD = 64
BLK = 256
STEP = 10
PAIR = 2 * HD

norm_eps = 1e-05
adam_eps = 1e-08
group_heads = 4
score_scale = 0.125 * 1.4426950408889634
gelu_root = 0.7978845608028654
gelu_cubic = 0.044715
low = jnp.bfloat16
axes = ("ctx", "wshard")
small_cost = pl.CostEstimate(flops=1024, bytes_accessed=1024, transcendentals=0)


def nt(left_side, right_side):
    return lax.dot_general(
        left_side, right_side, (((1,), (1,)), ((), ())), preferred_element_type=jnp.float32
    )


def nn(left_side, right_side):
    return jnp.dot(left_side, right_side, preferred_element_type=jnp.float32)


def outer_sum(left_side, right_side):
    return lax.dot_general(
        left_side, right_side, (((0,), (0,)), ((), ())), preferred_element_type=jnp.float32
    )


def block_rows(block):
    return pl.ds(block * BLK, BLK)


def thirds(ref):
    return [ref.at[:, pl.ds(part * PAIR, PAIR)] for part in range(3)]


def both_heads(rows):
    lane = lax.broadcasted_iota(jnp.int32, (1, PAIR), 1)
    empty = jnp.zeros_like(rows)
    return jnp.concatenate(
        [jnp.where(lane < HD, rows, empty), jnp.where(lane < HD, empty, rows)], axis=0
    )


def attend_pair(blocks, projected, o_ref, lse_ref, between):
    q_ref, k_ref, v_ref = thirds(projected)
    lane = lax.broadcasted_iota(jnp.int32, (1, PAIR), 1)
    for i in range(blocks):
        between(i)
        rows = block_rows(i)
        queries = both_heads(q_ref[rows, :])
        upto = pl.ds(0, (i + 1) * BLK)
        scores = nt(queries, k_ref[upto, :]) * score_scale
        top = jnp.max(scores, axis=1, keepdims=True)
        weights = jnp.exp2(scores - top)
        total = jnp.sum(weights, axis=1, keepdims=True)
        mixed = nn(weights.astype(low), v_ref[upto, :])
        mixed = mixed * (1.0 / total)
        o_ref[rows, :] = jnp.where(lane < HD, mixed[:BLK], mixed[BLK:]).astype(o_ref.dtype)
        logsum = jnp.transpose(jnp.broadcast_to(top + jnp.log2(total), (2 * BLK, PAIR)))
        for h in range(2):
            lse_ref[h : h + 1, rows] = logsum[0:1, h * BLK : (h + 1) * BLK]


def attend_back_pair(
    blocks, projected, do_ref, lse_ref, back_ref, turned, key_sum, value_sum, between
):
    q_ref, k_ref, v_ref = thirds(projected)
    dq_ref, dk_ref, dv_ref = thirds(back_ref)
    turned[...] = jnp.transpose(k_ref[...])
    for i in range(blocks):
        between(i)
        rows = block_rows(i)
        queries, upstream = both_heads(q_ref[rows, :]), both_heads(do_ref[rows, :])
        logsum = jnp.concatenate([lse_ref[0:1, rows], lse_ref[1:2, rows]], axis=1)
        upto = pl.ds(0, (i + 1) * BLK)
        weights = jnp.exp2(nt(k_ref[upto, :], queries) * score_scale - logsum)
        pulls = nt(v_ref[upto, :], upstream)
        inner = jnp.sum(weights * pulls, axis=0, keepdims=True)
        score_grad = (weights * (pulls - inner)).astype(low)
        value_grad = nn(weights.astype(low), upstream)
        key_grad = nn(score_grad, queries)
        query_grad = nn(turned[:, upto], score_grad)
        earlier, latest = pl.ds(0, i * BLK), block_rows(i)
        if i > 0:
            value_sum[earlier, :] += value_grad[: i * BLK]
            key_sum[earlier, :] += key_grad[: i * BLK]
        value_sum[latest, :] = value_grad[i * BLK :]
        key_sum[latest, :] = key_grad[i * BLK :]
        joined = jnp.concatenate([query_grad[:HD, :BLK], query_grad[HD:, BLK:]], axis=0)
        dq_ref[rows, :] = (jnp.transpose(joined) * 0.125).astype(dq_ref.dtype)
    dk_ref[...] = (key_sum[...] * 0.125).astype(dk_ref.dtype)
    dv_ref[...] = value_sum[...].astype(dv_ref.dtype)


def hooks(step, schedule):
    def between(block):
        for when, where, action in schedule:
            if where == block:
                pl.when(step == when)(action)

    return between


any_place = pl.BlockSpec(memory_space=pl.ANY)
whole_vmem = pl.BlockSpec(memory_space=pltpu.VMEM)


MESH = pl.DeviceIdType.MESH


class Spot:
    def __init__(self, sizes):
        self.sizes = sizes
        ctx, shard = lax.axis_index("ctx"), lax.axis_index("wshard")
        self.c = ctx
        self.k = shard % 2
        self.y = (shard // 2) % 2
        self.z = shard // 4

    def device(self, name, by=1):
        c, z, y, k = self.c, self.z, self.y, self.k
        if name == "c":
            c = 1 - c
        if name == "y":
            y = 1 - y
        if name == "k":
            k = 1 - k
        if name == "z":
            z = (z + by) % self.sizes["z"]
        return (c, (z * 2 + y) * 2 + k)

    def meet(self, names):
        barrier = pltpu.get_barrier_semaphore()
        partners = []
        for name in names:
            for by in range(1, self.sizes[name]):
                partners.append(self.device(name, by))
        for partner in partners:
            pl.semaphore_signal(barrier, inc=1, device_id=partner, device_id_type=MESH)
        pl.semaphore_wait(barrier, len(partners))


class Mover:
    def __init__(self, spot, sems):
        self.spot, self.sems, self.count = spot, sems, 0

    def copy(self, source, target, name, by=1):
        number = self.count
        self.count += 1
        return pltpu.make_async_remote_copy(
            src_ref=source,
            dst_ref=target,
            send_sem=self.sems.at[0, number],
            recv_sem=self.sems.at[1, number],
            device_id=self.spot.device(name, by),
            device_id_type=MESH,
        )

    def local(self, source, target):
        number = self.count
        self.count += 1
        return pltpu.make_async_copy(source, target, self.sems.at[0, number])


class Refs:
    def __init__(self, refs):
        self.refs = list(refs)

    def take(self, count):
        taken, self.refs = self.refs[:count], self.refs[count:]
        return taken


def start(copies):
    for copy in copies:
        copy.start()


def wait(copies):
    for copy in copies:
        copy.wait()


def span(first, size):
    return pl.ds(pl.multiple_of(first, 128), size)


class Deep:
    def __init__(self, mover, quad):
        z = mover.spot.z
        self.copies = [
            mover.copy(quad.at[z], quad.at[z], "z", by) for by in range(1, mover.spot.sizes["z"])
        ]


def first_rows(mover, halves, quad):
    spot = mover.spot
    rows = halves.shape[1]
    block = quad.at[spot.z, pl.ds(pl.multiple_of(spot.k * rows, rows), rows)]
    return [
        mover.local(halves.at[spot.k], block),
        mover.copy(halves.at[1 - spot.k], block, "k"),
    ]


class Near:
    def __init__(self, mover, quad, half, offset, cut, core=True):
        spot = mover.spot
        c, z, y = spot.c, spot.z, spot.y
        width = quad.shape[-1]
        every = slice(None)

        def part(ci, yi, first, size):
            return half.at[ci, every, yi, :, span(offset + first, size)]

        self.near, self.far = [mover.local(quad, part(c, y, 0, width))], []
        for first, size, one, two in ((0, cut, "c", "y"), (cut, width - cut, "y", "c")):
            if size == 0:
                continue
            source = quad.at[every, every, pl.ds(first, size)]
            self.near.append(mover.copy(source, part(c, y, first, size), one))
            self.near.append(mover.copy(source, part(c, y, first, size), two))
            block = part(1 - c if one == "c" else c, 1 - y if one == "y" else y, first, size)
            self.far.append(mover.copy(block, block, two))
        self.core = [[], [], []]
        if core:
            self.core[0].append(mover.copy(quad, part(c, y, 0, width), "k"))
            for stage, ci, yi in ((1, 1 - c, y), (1, c, 1 - y), (2, 1 - c, 1 - y)):
                block = part(ci, yi, 0, width)
                self.core[stage].append(mover.copy(block, block, "k"))

    def close(self):
        wait(self.far)
        start(self.core[2])

    def close_core(self):
        for stage in self.core:
            wait(stage)


class ReduceNear:
    def __init__(self, mover, mine, theirs, cut, quad, scratch):
        self.spot = spot = mover.spot
        self.cut, self.quad = cut, quad
        self.total, self.other, self.by_y, self.by_c, self.then_c, self.then_y = scratch
        self.width = width = self.total.shape[-1]
        c, y = spot.c, spot.y
        every, left, right = slice(None), pl.ds(0, cut), pl.ds(cut, width - cut)
        total = self.total
        self.first = [mover.copy(theirs, self.other, "k")]
        if mine is not None:
            self.first.append(mover.local(mine, total))
        self.near = [
            mover.copy(total.at[every, every, 1 - y, every, left], self.by_y, "y"),
            mover.copy(total.at[1 - c, every, every, every, right], self.by_c, "c"),
        ]
        self.far = [
            mover.copy(total.at[1 - c, every, y, every, left], self.then_c, "c"),
            mover.copy(total.at[c, every, 1 - y, every, right], self.then_y, "y"),
        ]

    @staticmethod
    def scratch(sizes, rows, width, cut):
        c, z, y = sizes["c"], sizes["z"], sizes["y"]
        shapes = [
            (c, z, y, rows, width),
            (c, z, y, rows, width),
            (c, z, rows, cut),
            (z, y, rows, width - cut),
            (z, rows, cut),
            (z, rows, width - cut),
        ]
        return [pltpu.VMEM(shape, low) for shape in shapes]

    def add(self, where, extra):
        total = self.total[where].astype(jnp.float32) + extra.astype(jnp.float32)
        return total.astype(low)

    def go_near(self):
        wait(self.first)
        sizes = self.spot.sizes
        for c in range(sizes["c"]):
            for y in range(sizes["y"]):

                @pl.loop(0, sizes["z"])
                def _(z):
                    self.total[c, z, y] = self.add((c, z, y), self.other[c, z, y])

        start(self.near)

    def go_far(self):
        wait(self.near)
        spot, cut = self.spot, self.cut
        left, right = pl.ds(0, cut), pl.ds(cut, self.width - cut)

        @pl.loop(0, spot.sizes["z"])
        def _(z):
            for c in range(spot.sizes["c"]):
                where = (c, z, spot.y, slice(None), left)
                self.total[where] = self.add(where, self.by_y[c, z])
            for y in range(spot.sizes["y"]):
                where = (spot.c, z, y, slice(None), right)
                self.total[where] = self.add(where, self.by_c[z, y])

        start(self.far)

    def close(self):
        wait(self.far)
        spot, cut = self.spot, self.cut
        left, right = pl.ds(0, cut), pl.ds(cut, self.width - cut)

        @pl.loop(0, spot.sizes["z"])
        def _(z):
            for columns, extra in ((left, self.then_c), (right, self.then_y)):
                where = (spot.c, z, spot.y, slice(None), columns)
                self.quad[z, :, columns] = self.add(where, extra[z])


class ReduceDeep:
    def __init__(self, mover, quad, by_z):
        self.spot = spot = mover.spot
        self.quad, self.by_z = quad, by_z
        depth = spot.sizes["z"]
        self.copies = [
            mover.copy(quad.at[(spot.z + by) % depth], by_z.at[by - 1], "z", by)
            for by in range(1, depth)
        ]

    def result(self):
        spot = self.spot
        value = self.quad[spot.z].astype(jnp.float32)
        for by in range(spot.sizes["z"] - 1):
            value = value + self.by_z[by].astype(jnp.float32)
        return value


class Finish:
    def __init__(self, mover, summed, arrived):
        self.k = mover.spot.k
        self.summed, self.arrived = summed, arrived
        rows = arrived.shape[0]
        self.rows = rows
        away = summed.at[pl.ds(pl.multiple_of((1 - self.k) * rows, rows), rows)]
        self.copies = [mover.copy(away, arrived, "k")]

    @staticmethod
    def scratch(rows, width):
        return [pltpu.VMEM((rows, width), jnp.float32), pltpu.VMEM((rows // 2, width), jnp.float32)]

    def write(self, out, columns=slice(None)):
        rows = self.rows
        kept = pl.ds(pl.multiple_of(self.k * rows, rows), rows)
        out[self.k, :, columns] = self.summed[kept, :]
        out[1 - self.k, :, columns] = self.arrived[...]


def core_halves(grad, k, width, first=0, size=None):
    size = width if size is None else size
    every = slice(None)
    return [
        grad.at[every, every, every, every, span(half * width + first, size)]
        for half in (k, 1 - k)
    ]


all_axes = ("k", "c", "y", "z")


def params(number, megabytes):
    return pltpu.CompilerParams(
        collective_id=number, has_side_effects=True, vmem_limit_bytes=megabytes << 20
    )


def cut_of(width):
    return max(5 * width // 8 // 128, 1) * 128


def low_shape(*dims):
    return jax.ShapeDtypeStruct(dims, low)


def begin_kernel(sizes, *refs):
    refs = Refs(refs)
    joint_weight, table, mixing_weight, expand_weight, shrink_weight = refs.take(5)
    rows_in, upstream = refs.take(2)
    joint, tables, mixing_quad, expand_quad, shrink_quad, far_rows, far_upstream = refs.take(7)
    next_expand, next_shrink = refs.take(2)
    joint_quad, table_quad, sems, joint_halves, mixing_halves, expand_halves, shrink = refs.take(7)
    spot = Spot(sizes)
    mover = Mover(spot, sems)
    width = joint_halves.shape[2]
    joint_first = first_rows(mover, joint_halves, joint_quad)
    rows = table.shape[0]
    spread = table_quad.at[spot.z, pl.ds(pl.multiple_of(spot.k * rows, rows), rows)]
    joint_first += [mover.local(table, spread), mover.copy(table, spread, "k")]
    later_first = first_rows(mover, mixing_halves, mixing_quad)
    later_first += first_rows(mover, expand_halves, expand_quad)
    later_first += [mover.local(shrink, shrink_quad.at[spot.z])]
    part = width // 2
    chunks = [joint_quad.at[:, :, pl.ds(first, part)] for first in (0, part)]
    now = [Deep(mover, chunk).copies for chunk in chunks]
    thin_deep = Deep(mover, table_quad).copies
    later = [Deep(mover, quad).copies for quad in (mixing_quad, shrink_quad, expand_quad)]
    jobs = [
        Near(mover, chunk, joint, spot.k * width + number * part, part)
        for number, chunk in enumerate(chunks)
    ]
    thin = Near(mover, table_quad, tables, 0, table.shape[1], core=False)
    rows_copies = [
        mover.copy(rows_in.at[1 - spot.c, block_rows(0)], far_rows.at[block_rows(0)], "c"),
        mover.copy(rows_in.at[1 - spot.c, block_rows(1)], far_rows.at[block_rows(1)], "c"),
        mover.copy(upstream.at[1 - spot.c, block_rows(0)], far_upstream, "c"),
    ]
    pairs = width // (3 * PAIR)
    for core in range(2):
        for pair in range(pairs):
            for third in range(3):
                source = ((third * 2 + core) * pairs + pair) * PAIR
                target = (pair * 3 + third) * PAIR
                joint_halves[core, :, target : target + PAIR] = joint_weight[
                    :, source : source + PAIR
                ].astype(low)
    spot.meet(all_axes)
    start(joint_first)
    start(rows_copies[:1])
    wait(joint_first)
    start(now[0] + thin_deep)
    half = mixing_halves.shape[2]
    for core in range(2):
        mixing_halves[core] = mixing_weight[:, core * half : (core + 1) * half].astype(low)
    sub = shrink.shape[0]
    shrink[...] = shrink_weight[:sub, :].astype(low)
    next_shrink[...] = shrink_weight[sub:, :].astype(low)
    lane = lax.broadcasted_iota(jnp.int32, (1, PAIR), 1)
    for core in range(2):
        for chip in range(0, expand_halves.shape[2] // HD, 2):
            one, two = [
                expand_weight[:, (number * 2 + core) * PAIR : (number * 2 + core + 1) * PAIR]
                for number in (chip, chip + 1)
            ]
            columns = pl.ds(chip * HD, PAIR)
            expand_halves[core, :, columns] = jnp.where(
                lane < HD, one, pltpu.roll(two, HD, 1)
            ).astype(low)
            next_expand[core, :, columns] = jnp.where(
                lane < HD, pltpu.roll(one, HD, 1), two
            ).astype(low)
    start(later_first)
    wait(now[0] + thin_deep)
    start(now[1])
    start(thin.near + jobs[0].near + jobs[0].core[0])
    wait(now[1])
    start(jobs[1].near + jobs[1].core[0])
    wait(later_first)
    for copies in later:
        start(copies)
    wait(thin.near + jobs[0].near)
    start(thin.far + jobs[0].far + jobs[0].core[1])
    start(rows_copies[1:2])
    wait(jobs[1].near)
    start(jobs[1].far + jobs[1].core[1])
    start(rows_copies[2:])
    wait(thin.far)
    for job in jobs:
        job.close()
    for copies in later:
        wait(copies)
    for job in jobs:
        job.close_core()
    wait(rows_copies)


def begin(sizes, joint_weight, table, mixing_weight, expand_weight, shrink_weight, rows_in, upstream):
    lead = (sizes["c"], sizes["z"], sizes["y"])
    own, model = mixing_weight.shape
    depth, rows = sizes["z"], 2 * own
    width, half, grown = 3 * model // 2, model // 2, expand_weight.shape[1] // 4
    sub = shrink_weight.shape[0] // 2
    return pl.pallas_call(
        functools.partial(begin_kernel, sizes),
        in_specs=[whole_vmem] * 5 + [any_place] * 2,
        out_specs=[any_place] * 7 + [whole_vmem] * 2,
        out_shape=[
            low_shape(*lead, rows, 2 * width),
            low_shape(*lead, rows, table.shape[1]),
            low_shape(depth, rows, half),
            low_shape(depth, rows, grown),
            low_shape(depth, sub, model),
            low_shape(*rows_in.shape[1:]),
            low_shape(BLK, model),
            low_shape(2, own, grown),
            low_shape(sub, model),
        ],
        scratch_shapes=[
            pltpu.VMEM((depth, rows, width), low),
            pltpu.VMEM((depth, rows, table.shape[1]), low),
            pltpu.SemaphoreType.DMA((2, 64)),
            pltpu.VMEM((2, own, width), low),
            pltpu.VMEM((2, own, half), low),
            pltpu.VMEM((2, own, grown), low),
            pltpu.VMEM((sub, model), low),
        ],
        compiler_params=params(1, 60),
        cost_estimate=small_cost,
        name="begin",
    )(joint_weight, table, mixing_weight, expand_weight, shrink_weight, rows_in, upstream)


def normal_rows(rows):
    centered = rows - jnp.mean(rows, axis=-1, keepdims=True)
    inverse = lax.rsqrt(jnp.mean(centered * centered, axis=-1, keepdims=True) + norm_eps)
    return centered * inverse, inverse


def norm_pull(upstream, normal, inverse, gain):
    scaled = upstream * gain
    inner = jnp.mean(scaled, axis=-1, keepdims=True)
    along = jnp.mean(scaled * normal, axis=-1, keepdims=True)
    return inverse * (scaled - inner - normal * along)


def chosen_block(number, source):
    chosen = jnp.full((1, source.shape[1]), number, jnp.int32)
    value = source[block_rows(0), :].astype(jnp.float32)
    for other in range(1, source.shape[0] // BLK):
        value = jnp.where(chosen == other, source[block_rows(other), :].astype(jnp.float32), value)
    return value


def hidden_pairs(width, columns):
    chips = columns // 2 // HD
    for core in range(2):
        for chip in range(0, chips, 2):
            places = []
            for number in (chip, chip + 1):
                row, first = divmod((number * 2 + core) * PAIR, width)
                places.append((slice(8 + row, 9 + row), slice(first, first + PAIR)))
            first = core * (columns // 2) + chip * HD
            yield places, slice(first, first + PAIR)


def attend_kernel(sizes, blocks, *refs):
    refs = Refs(refs)
    place_ref, rows_in, far_rows, joint, table, upstream = refs.take(6)
    mixing_quad, expand_quad, shrink_quad, expand_halves, shrink = refs.take(5)
    o_ref, lse_ref, rows_ref, low_ref, projected_ref, vectors, bias_a, bias_b = refs.take(8)
    mixing, expand, shrunk, next_expand, next_shrink, far_upstream = refs.take(6)
    sems, rows_all, joint_all, projected, shift_ref = refs.take(5)
    spot = Spot(sizes)
    mover = Mover(spot, sems)
    k = spot.k
    half, grown, width = mixing_quad.shape[-1], expand_quad.shape[-1], shrink_quad.shape[-1]
    loads = [
        mover.local(rows_in.at[spot.c], rows_all.at[pl.ds(0, 2 * BLK)]),
        mover.local(far_rows, rows_all.at[pl.ds(2 * BLK, 2 * BLK)]),
        mover.local(joint, joint_all),
    ]
    jobs = [
        Near(mover, mixing_quad, mixing, k * half, cut_of(half)),
        Near(mover, shrink_quad, shrunk.at[k], 0, cut_of(width)),
        Near(mover, expand_quad, expand, k * grown, cut_of(grown)),
    ]
    next_first = first_rows(mover, expand_halves, next_expand)
    next_first += [mover.local(shrink, next_shrink.at[spot.z])]
    deep = Deep(mover, next_expand).copies + Deep(mover, next_shrink).copies
    upstream_copy = [mover.copy(upstream.at[1 - spot.c, block_rows(1)], far_upstream, "c")]

    def open_all():
        start(loads)
        spot.meet(all_axes)
        start(next_first)
        for job in jobs:
            start(job.near + job.core[0])
        vector_rows()
        wait(loads)

    def next_deep():
        wait(next_first)
        start(deep)
        start(upstream_copy)

    def vector_rows():
        vectors[...] = jnp.transpose(table[...].astype(jnp.float32))[: vectors.shape[0]]
        shift_ref[...] = jnp.zeros_like(shift_ref)
        for pair in range(H // 2):
            for row, third in ((2, 0), (3, 2)):
                columns = pl.ds((3 * pair + third) * PAIR, PAIR)
                shift_ref[:, columns] = vectors[row : row + 1, pair * PAIR : (pair + 1) * PAIR]
        lane = lax.broadcasted_iota(jnp.int32, (1, PAIR), 1)
        for (one, two), target in hidden_pairs(vectors.shape[1], bias_a.shape[1]):
            one, two = vectors[one], vectors[two]
            bias_a[:, target] = jnp.where(lane < HD, one, pltpu.roll(two, HD, 1))
            bias_b[:, target] = jnp.where(lane < HD, pltpu.roll(one, HD, 1), two)

    def far(job):
        wait(job.near)
        start(job.far + job.core[1])

    def close_all():
        for job in jobs:
            job.close()
        wait(deep)
        for job in jobs:
            job.close_core()
        wait(upstream_copy)

    step = pl.program_id(0)
    between = hooks(
        step,
        [
            (0, 0, open_all),
            (2, 0, next_deep),
            (7, 2, lambda: far(jobs[0])),
            (8, 2, lambda: far(jobs[1])),
            (9, 2, lambda: far(jobs[2])),
        ],
    )
    between(0)

    @pl.when(step < blocks)
    def _():
        value = chosen_block(place_ref[step], rows_all)
        rows_ref[...] = value.astype(low)
        normal, _ = normal_rows(value)
        normed = (normal * vectors[0:1, :] + vectors[1:2, :]).astype(low)
        low_ref[...] = normed
        rows = pl.ds(pl.multiple_of(step * BLK, BLK), BLK)
        for first in range(0, joint_all.shape[1], 512):
            columns = pl.ds(first, 512)
            projected[rows, columns] = (nn(normed, joint_all[:, columns]) + shift_ref[:, columns]).astype(low)

    @pl.when(step >= blocks)
    def _():
        columns = span((step - blocks) * 3 * PAIR, 3 * PAIR)
        projected_ref[...] = projected[:, columns]
        attend_pair(blocks, projected_ref, o_ref, lse_ref, lambda block: block > 0 and between(block))

    pl.when(step == pl.num_programs(0) - 1)(close_all)


def attend(sizes, place, rows_in, far_rows, joint, table, upstream, quads, halves, shrink):
    model = rows_in.shape[2]
    blocks = place.shape[0]
    tokens = blocks * BLK
    pairs = model // PAIR
    lead = (sizes["c"], sizes["z"], sizes["y"])
    depth, rows, half = quads[0].shape
    grown, full = quads[1].shape[2], quads[2].shape[2]
    by_rows = pl.BlockSpec((BLK, model), lambda g: (jnp.minimum(g, blocks - 1), 0))

    def pair(g):
        return jnp.maximum(g - blocks, 0)

    return pl.pallas_call(
        functools.partial(attend_kernel, sizes, blocks),
        grid=(blocks + pairs,),
        in_specs=[pl.BlockSpec(memory_space=pltpu.SMEM)]
        + [any_place] * 3
        + [whole_vmem, any_place]
        + [whole_vmem] * 5,
        out_specs=[
            pl.BlockSpec((tokens, PAIR), lambda g: (0, pair(g))),
            pl.BlockSpec((None, 8, tokens), lambda g: (pair(g), 0, 0)),
            by_rows,
            by_rows,
            pl.BlockSpec((tokens, 3 * PAIR), lambda g: (0, pair(g))),
        ]
        + [whole_vmem] * 3
        + [any_place] * 6,
        out_shape=[
            low_shape(tokens, model),
            jax.ShapeDtypeStruct((pairs, 8, tokens), jnp.float32),
            low_shape(tokens, model),
            low_shape(tokens, model),
            low_shape(tokens, 3 * model),
            jax.ShapeDtypeStruct((16, model), jnp.float32),
            jax.ShapeDtypeStruct((1, 2 * grown), jnp.float32),
            jax.ShapeDtypeStruct((1, 2 * grown), jnp.float32),
            low_shape(*lead, rows, 2 * half),
            low_shape(*lead, rows, 2 * grown),
            low_shape(2, *lead, rows, full),
            low_shape(depth, rows, grown),
            low_shape(depth, rows, full),
            low_shape(BLK, model),
        ],
        scratch_shapes=[
            pltpu.SemaphoreType.DMA((2, 64)),
            pltpu.VMEM((tokens, model), low),
            pltpu.VMEM((model, 3 * model), low),
            pltpu.VMEM((tokens, 3 * model), low),
            pltpu.VMEM((1, 3 * model), jnp.float32),
        ],
        compiler_params=params(2, 60),
        cost_estimate=small_cost,
        name="attend",
    )(place, rows_in, far_rows, joint, table, upstream, *quads, halves, shrink)


def mlp_tile(rows_step, c_ref, dy_ref, we_ref, ws_ref, be_ref, outs, scratch, between):
    y_ref, dc_ref, gwe_ref, gws_ref, gbe_ref = outs
    turned, act_all, du_all = scratch
    tokens = c_ref.shape[0]
    we, ws = we_ref[...], ws_ref[...]
    total = None
    for part in range(tokens // rows_step):
        between(part)
        rows = pl.ds(part * rows_step, rows_step)
        hidden = nn(c_ref[rows, :], we) + be_ref[...]
        squared = hidden * hidden
        bent = jnp.tanh(gelu_root * hidden * (1.0 + gelu_cubic * squared))
        gate = 0.5 + 0.5 * bent
        act = (hidden * gate).astype(low)
        slope = gate + (0.5 * gelu_root) * hidden * (1.0 - bent * bent) * (
            1.0 + (3 * gelu_cubic) * squared
        )
        du = (nt(dy_ref[rows, :], ws) * slope).astype(low)
        act_all[rows, :] = act
        du_all[rows, :] = du
        y_ref[rows, :] += nn(act, ws)
        dc_ref[rows, :] += nt(du, we)
        added = jnp.sum(du.astype(jnp.float32), axis=0, keepdims=True)
        total = added if total is None else total + added
    gbe_ref[...] = total
    gwe_ref[...] = nn(turned[...], du_all[...]).astype(gwe_ref.dtype)
    gws_ref[...] = outer_sum(act_all[...], dy_ref[...]).astype(gws_ref.dtype)


def mlp_parts(tokens, width, hidden, tile):
    whole = pl.BlockSpec((tokens, width), lambda t: (0, 0), pipeline_mode=pl.Buffered(1))
    down = pl.BlockSpec((width, tile), lambda t: (0, t))
    across = pl.BlockSpec((tile, width), lambda t: (t, 0))
    thin = pl.BlockSpec((1, tile), lambda t: (0, t))
    return (
        [whole, whole, down, across, thin],
        [whole, whole, down, across, thin],
        [
            jax.ShapeDtypeStruct((tokens, width), jnp.float32),
            jax.ShapeDtypeStruct((tokens, width), jnp.float32),
            low_shape(width, hidden),
            low_shape(hidden, width),
            jax.ShapeDtypeStruct((1, hidden), jnp.float32),
        ],
        [
            pltpu.VMEM((width, tokens), low),
            pltpu.VMEM((tokens, tile), low),
            pltpu.VMEM((tokens, tile), low),
        ],
    )


def mlp_plain_kernel(rows_step, *refs):
    refs = Refs(refs)
    c_ref, dy_ref, we_ref, ws_ref, be_ref, y_in, dc_in = refs.take(7)
    outs, scratch, (sem,) = refs.take(5), refs.take(3), refs.take(1)

    @pl.when(pl.program_id(0) == 0)
    def _():
        scratch[0][...] = jnp.transpose(c_ref[...])
        copies = [
            pltpu.make_async_copy(y_in, outs[0], sem.at[0]),
            pltpu.make_async_copy(dc_in, outs[1], sem.at[1]),
        ]
        start(copies)
        wait(copies)

    mlp_tile(rows_step, c_ref, dy_ref, we_ref, ws_ref, be_ref, outs, scratch, lambda part: None)


def mlp(c, dy, we, ws, be, before, tile=512, rows_step=512):
    in_specs, out_specs, out_shape, scratch = mlp_parts(*c.shape, we.shape[1], tile)
    return pl.pallas_call(
        functools.partial(mlp_plain_kernel, rows_step),
        grid=(we.shape[1] // tile,),
        in_specs=in_specs + [any_place] * 2,
        out_specs=out_specs,
        out_shape=out_shape,
        scratch_shapes=scratch + [pltpu.SemaphoreType.DMA((2,))],
        compiler_params=pltpu.CompilerParams(vmem_limit_bytes=56 << 20),
        cost_estimate=small_cost,
        name="mlp",
    )(c, dy, we, ws, be, *before)


def mlp_gather_kernel(sizes, blocks, rows_step, *refs):
    refs = Refs(refs)
    place_ref, mixed_ref, rows_ref, mixing, vector_ref, we_ref, ws_ref, be_ref = refs.take(8)
    upstream, far_a, far_b, expand_quad, shrink_quad = refs.take(5)
    outs, (middle_ref, low_ref, upstream_ref) = refs.take(5), refs.take(3)
    expand, shrunk = refs.take(2)
    scratch, (sems, raw, c_all, dy_all) = refs.take(3), refs.take(4)
    spot = Spot(sizes)
    mover = Mover(spot, sems)
    grown, width = expand_quad.shape[-1], shrink_quad.shape[-1]
    loads = [
        mover.local(upstream.at[spot.c], raw.at[pl.ds(0, 2 * BLK)]),
        mover.local(far_a, raw.at[pl.ds(2 * BLK, BLK)]),
        mover.local(far_b, raw.at[pl.ds(3 * BLK, BLK)]),
    ]
    jobs = [
        Near(mover, shrink_quad, shrunk.at[spot.k], 0, width // 2),
        Near(mover, expand_quad, expand, spot.k * grown, grown // 2),
    ]

    def open_all():
        start(loads)
        spot.meet(all_axes)
        for job in jobs:
            start(job.near + job.core[0])
        wait(loads)

    def far(job):
        wait(job.near)
        start(job.far + job.core[1])

    def close_all():
        jobs[1].close()
        for job in jobs:
            job.close_core()

    step = pl.program_id(0)
    between = hooks(
        step,
        [
            (0, 0, open_all),
            (6, 0, lambda: far(jobs[0])),
            (6, 1, lambda: far(jobs[1])),
            (7, 1, jobs[0].close),
        ],
    )
    between(0)

    @pl.when(step < blocks)
    def _():
        rows = pl.ds(pl.multiple_of(step * BLK, BLK), BLK)
        dy = chosen_block(place_ref[step], raw).astype(low)
        upstream_ref[...] = dy
        dy_all[rows, :] = dy
        branch = nn(mixed_ref[...], mixing[...]) + vector_ref[4:5, :]
        middle = rows_ref[...].astype(jnp.float32) + branch
        middle_ref[...] = middle
        normal, _ = normal_rows(middle)
        second = (normal * vector_ref[5:6, :] + vector_ref[6:7, :]).astype(low)
        low_ref[...] = second
        c_all[rows, :] = second
        outs[0][rows, :] = middle + vector_ref[7:8, :]
        outs[1][rows, :] = jnp.zeros(middle.shape, jnp.float32)

    @pl.when(step == blocks)
    def _():
        scratch[0][...] = jnp.transpose(c_all[...])

    @pl.when(step >= blocks)
    def _():
        mlp_tile(
            rows_step, c_all, dy_all, we_ref, ws_ref, be_ref, outs, scratch,
            lambda part: part > 0 and between(part),
        )

    pl.when(step == pl.num_programs(0) - 1)(close_all)


def mlp_gather(sizes, place, mixed, rows_in, mixing, vectors, we, ws, be, upstream, far_a, far_b, quads, tile=512, rows_step=512):
    tokens, model = mixed.shape
    blocks = place.shape[0]
    hidden = we.shape[1]
    lead = (sizes["c"], sizes["z"], sizes["y"])
    rows, grown, full = quads[0].shape[1], quads[0].shape[2], quads[1].shape[2]
    by_rows = pl.BlockSpec((BLK, model), lambda g: (jnp.minimum(g, blocks - 1), 0))
    whole = pl.BlockSpec((tokens, model), lambda g: (0, 0), pipeline_mode=pl.Buffered(1))

    def at(g):
        return jnp.maximum(g - blocks, 0)

    down = pl.BlockSpec((model, tile), lambda g: (0, at(g)))
    across = pl.BlockSpec((tile, model), lambda g: (at(g), 0))
    thin = pl.BlockSpec((1, tile), lambda g: (0, at(g)))
    _, _, out_shape, scratch = mlp_parts(tokens, model, hidden, tile)
    return pl.pallas_call(
        functools.partial(mlp_gather_kernel, sizes, blocks, rows_step),
        grid=(blocks + hidden // tile,),
        in_specs=[pl.BlockSpec(memory_space=pltpu.SMEM), by_rows, by_rows, whole_vmem, whole_vmem]
        + [down, across, thin]
        + [any_place] * 3
        + [whole_vmem] * 2,
        out_specs=[whole, whole, down, across, thin] + [by_rows] * 3 + [any_place] * 2,
        out_shape=out_shape
        + [
            jax.ShapeDtypeStruct((tokens, model), jnp.float32),
            low_shape(tokens, model),
            low_shape(tokens, model),
            low_shape(*lead, rows, 2 * grown),
            low_shape(2, *lead, rows, full),
        ],
        scratch_shapes=scratch
        + [pltpu.SemaphoreType.DMA((2, 32))]
        + [pltpu.VMEM((tokens, model), low)] * 3,
        compiler_params=params(3, 60),
        cost_estimate=small_cost,
        name="mlp_gather",
    )(place, mixed, rows_in, mixing, vectors, we, ws, be, upstream, far_a, far_b, *quads)


def mlp_reduce_kernel(sizes, rows_step, *refs):
    refs = Refs(refs)
    back_ref, c_ref, dy_ref, we_ref, ws_ref, be_ref, y_in, dc_in, expand, shrink = refs.take(10)
    outs = refs.take(4)
    expand_quad, shrink_quad, kept, sent = refs.take(4)
    scratch, (sems, y_all) = refs.take(3), refs.take(2)
    outs = [y_all] + outs
    spot = Spot(sizes)
    mover = Mover(spot, sems)
    grown, width = expand_quad.shape[-1], shrink_quad.shape[-1]
    loads = [mover.local(y_in, y_all), mover.local(dc_in, outs[1])]
    jobs = [
        ReduceNear(
            mover, shrink.at[spot.k], shrink.at[1 - spot.k], width // 2, shrink_quad, refs.take(6)
        ),
        ReduceNear(
            mover, *core_halves(expand, spot.k, grown), grown // 2, expand_quad, refs.take(6)
        ),
    ]

    def open_all():
        start(loads)
        spot.meet(all_axes)
        start(jobs[0].first)
        scratch[0][...] = jnp.transpose(c_ref[...])
        wait(loads)

    def shrink_near():
        start(jobs[1].first)
        jobs[0].go_near()

    def close_all():
        for place in range(2):
            kept[block_rows(place), :] = chosen_block(back_ref[place], y_all).astype(low)
            sent[block_rows(place), :] = chosen_block(back_ref[2 + place], y_all).astype(low)
        for job in jobs:
            job.close()

    step = pl.program_id(0)
    schedule = [
        (0, 0, open_all),
        (0, 1, shrink_near),
        (1, 0, jobs[1].go_near),
        (3, 0, jobs[0].go_far),
        (3, 1, jobs[1].go_far),
    ]
    mlp_tile(
        rows_step, c_ref, dy_ref, we_ref, ws_ref, be_ref, outs, scratch, hooks(step, schedule)
    )
    pl.when(step == pl.num_programs(0) - 1)(close_all)


def mlp_reduce(sizes, back, c, dy, we, ws, be, before, grads, tile=512, rows_step=512):
    tokens, model = c.shape
    in_specs, out_specs, out_shape, scratch = mlp_parts(tokens, model, we.shape[1], tile)
    expand, shrink = grads
    depth, rows = sizes["z"], expand.shape[3]
    grown, full = expand.shape[-1] // 2, shrink.shape[-1]
    scratch = scratch + [pltpu.SemaphoreType.DMA((2, 16)), pltpu.VMEM((tokens, model), jnp.float32)]
    for columns in (full, grown):
        scratch += ReduceNear.scratch(sizes, rows, columns, columns // 2)
    return pl.pallas_call(
        functools.partial(mlp_reduce_kernel, sizes, rows_step),
        grid=(we.shape[1] // tile,),
        in_specs=[pl.BlockSpec(memory_space=pltpu.SMEM)] + in_specs + [any_place] * 4,
        out_specs=out_specs[1:] + [whole_vmem] * 4,
        out_shape=out_shape[1:]
        + [low_shape(depth, rows, grown), low_shape(depth, rows, full)]
        + [low_shape(tokens // 2, model)] * 2,
        scratch_shapes=scratch,
        compiler_params=params(4, 60),
        cost_estimate=small_cost,
        name="mlp_reduce",
    )(back, c, dy, we, ws, be, *before, *grads)


def attend_back_kernel(sizes, blocks, *refs):
    refs = Refs(refs)
    pulled_ref, middle_ref, upstream_ref, mixed, mixing, gain_ref = refs.take(6)
    projected, lse_ref, expand, shrink, done_expand, done_shrink, sent = refs.take(7)
    back_ref, grad_ref, sums_ref, mixing_quad, expand_quad, shrink_quad = refs.take(6)
    expand_out, shrink_out, far_out = refs.take(3)
    turned, key_sum, value_sum, sems, branch_all, mixed_grad, theirs = refs.take(7)
    spot = Spot(sizes)
    mover = Mover(spot, sems)
    k = spot.k
    half, grown, width = mixing_quad.shape[-1], expand_quad.shape[-1], shrink_quad.shape[-1]
    jobs = [
        ReduceNear(mover, shrink.at[k], shrink.at[1 - k], width // 2, shrink_quad, refs.take(6)),
        ReduceNear(mover, *core_halves(expand, k, grown), grown // 2, expand_quad, refs.take(6)),
        ReduceNear(mover, None, theirs, half // 2, mixing_quad, refs.take(6)),
    ]
    deep = [
        ReduceDeep(mover, done_expand, *refs.take(1)),
        ReduceDeep(mover, done_shrink, *refs.take(1)),
    ]
    ending = Finish(mover, *refs.take(2))
    rows_copy = [mover.copy(sent.at[block_rows(0)], far_out, "c")]

    def open_all():
        spot.meet(all_axes)
        start(jobs[0].first)
        start(rows_copy)
        for job in deep:
            start(job.copies)

    def finish():
        wait(deep[0].copies)
        ending.summed[...] = deep[0].result()
        start(ending.copies)
        wait(deep[1].copies)
        shrink_out[...] = deep[1].result()

    def close_all():
        wait(ending.copies)
        ending.write(expand_out)
        jobs[1].close()
        jobs[2].close()
        wait(rows_copy)

    step = pl.program_id(0)
    between = hooks(
        step,
        [
            (0, 0, open_all),
            (1, 0, lambda: start(jobs[1].first)),
            (2, 0, jobs[0].go_near),
            (4, 0, jobs[1].go_near),
            (4, 2, jobs[2].go_near),
            (7, 0, finish),
            (8, 2, jobs[0].go_far),
            (9, 1, jobs[1].go_far),
            (9, 3, jobs[2].go_far),
            (11, 0, jobs[0].close),
        ],
    )
    between(0)

    @pl.when(step < blocks)
    def _():
        rows = pl.ds(pl.multiple_of(step * BLK, BLK), BLK)
        pulled = pulled_ref[...]
        upstream = upstream_ref[...].astype(jnp.float32)
        normal, inverse = normal_rows(middle_ref[...])
        total = upstream + norm_pull(pulled, normal, inverse, gain_ref[5:6, :])
        grad_ref[...] = total
        branch = total.astype(low)
        branch_all[rows, :] = branch
        mixed_grad[rows, :] = nt(branch, mixing[...]).astype(low)

        @pl.when(step == 0)
        def _():
            sums_ref[...] = jnp.zeros_like(sums_ref)

        for row, value in enumerate((branch.astype(jnp.float32), pulled * normal, pulled, upstream)):
            sums_ref[row : row + 1, :] += jnp.sum(value, axis=0, keepdims=True)

    @pl.when(step == blocks - 1)
    def _():
        across = jnp.transpose(mixed[...])
        for core, target in ((1 - k, theirs), (k, jobs[2].total)):
            piece = nn(across, branch_all[:, span(core * half, half)]).astype(low)
            target[...] = piece.reshape(target.shape)
        start(jobs[2].first)

    @pl.when(step >= blocks)
    def _():
        columns = span((step - blocks) * PAIR, PAIR)
        attend_back_pair(
            blocks, projected, mixed_grad.at[:, columns], lse_ref, back_ref, turned, key_sum,
            value_sum, lambda block: block > 0 and between(block),
        )

    pl.when(step == pl.num_programs(0) - 1)(close_all)


def attend_back(sizes, pulled, middle, upstream, mixed, mixing, gain, projected, lse, grads, quads, sent):
    tokens, model = upstream.shape
    pairs = model // PAIR
    blocks = tokens // BLK
    expand, shrink = grads
    depth, rows = sizes["z"], expand.shape[3]
    lead = (sizes["c"], sizes["z"], sizes["y"])
    half, grown, full = model // 2, expand.shape[-1] // 2, shrink.shape[-1]
    by_rows = pl.BlockSpec((BLK, model), lambda g: (jnp.minimum(g, blocks - 1), 0))

    def pair(g):
        return jnp.maximum(g - blocks, 0)

    triple = pl.BlockSpec((tokens, 3 * PAIR), lambda g: (0, pair(g)))
    scratch = [
        pltpu.VMEM((PAIR, tokens), low),
        pltpu.VMEM((tokens, PAIR), jnp.float32),
        pltpu.VMEM((tokens, PAIR), jnp.float32),
        pltpu.SemaphoreType.DMA((2, 32)),
        pltpu.VMEM((tokens, model), low),
        pltpu.VMEM((tokens, model), low),
        pltpu.VMEM((*lead, rows, half), low),
    ]
    for columns in (full, grown, half):
        scratch += ReduceNear.scratch(sizes, rows, columns, columns // 2)
    for columns in (grown, full):
        scratch += [pltpu.VMEM((depth - 1, rows, columns), low)]
    scratch += Finish.scratch(rows, grown)
    return pl.pallas_call(
        functools.partial(attend_back_kernel, sizes, blocks),
        grid=(blocks + pairs,),
        in_specs=[by_rows] * 3
        + [whole_vmem] * 3
        + [triple, pl.BlockSpec((None, 8, tokens), lambda g: (pair(g), 0, 0))]
        + [any_place] * 2
        + [whole_vmem] * 2
        + [any_place],
        out_specs=[triple, by_rows] + [whole_vmem] * 6 + [any_place],
        out_shape=[
            low_shape(*projected.shape),
            jax.ShapeDtypeStruct((tokens, model), jnp.float32),
            jax.ShapeDtypeStruct((8, model), jnp.float32),
            low_shape(depth, rows, half),
            low_shape(depth, rows, grown),
            low_shape(depth, rows, full),
            jax.ShapeDtypeStruct((2, rows // 2, grown), jnp.float32),
            jax.ShapeDtypeStruct((rows, full), jnp.float32),
            low_shape(BLK, model),
        ],
        scratch_shapes=scratch,
        compiler_params=params(5, 60),
        cost_estimate=small_cost,
        name="attend_back",
    )(pulled, middle, upstream, mixed, mixing, gain, projected, lse, *grads, *quads, sent)


end_chunks = 4


def end_kernel(sizes, *refs):
    refs = Refs(refs)
    back_ref, back_far, low_far, joint_far, rows_far, middle_far = refs.take(6)
    gain_ref, row_sums, bias_a, bias_b, mixing_quad, expand_quad, shrink_quad, sent_out = refs.take(8)
    out, vector_out, mixing_out, expand_out, shrink_out, kept = refs.take(6)
    arrived_rows, far_out = refs.take(2)
    sems, steps, arrived = refs.take(3)
    grads, low_rows, turned, joint, rows_in, middle, sent = refs.take(7)
    spot = Spot(sizes)
    mover = Mover(spot, sems)
    width, tokens = joint.shape[-1] // 2, rows_in.shape[0]
    part = width // end_chunks
    tile = 384
    loads = [
        mover.local(far, near)
        for far, near in (
            (back_far, grads),
            (low_far, low_rows),
            (joint_far, joint),
            (rows_far, rows_in),
            (middle_far, middle),
        )
    ]
    jobs, deeps, ends, others_half = [], [], [], []
    for number in range(end_chunks):
        theirs, quad = refs.take(2)
        others_half.append(theirs)
        jobs.append(ReduceNear(mover, None, theirs, 2 * part // 3, quad, refs.take(6)))
        deeps.append(ReduceDeep(mover, quad, *refs.take(1)))
        ends.append(Finish(mover, *refs.take(2)))
    others = [
        ReduceDeep(mover, quad, *refs.take(1))
        for quad in (mixing_quad, expand_quad, shrink_quad)
    ]
    other_ends = [Finish(mover, *refs.take(2)) for _ in range(2)]
    hops = [
        mover.copy(steps.at[number], arrived.at[number], name)
        for number, name in enumerate(("k", "c", "y"))
    ]
    spread = [
        mover.copy(steps.at[3], arrived.at[2 + by], "z", by) for by in range(1, sizes["z"])
    ]
    rows_copy = mover.copy(sent, arrived_rows, "c")
    out_copy = mover.copy(sent_out.at[block_rows(1)], far_out, "c")

    def gradient(core, number, target):
        @pl.loop(0, part // tile)
        def _(t):
            columns = span(core * width + number * part + t * tile, tile)
            piece = nn(turned[...], grads[:, columns]).astype(low)
            target[..., span(t * tile, tile)] = piece.reshape(*target.shape[:-1], tile)

    sums = {}

    def pull_block(number):
        rows = block_rows(number)
        pulled = grads[rows, :]
        upstream = nt(pulled, joint[...])
        normal, inverse = normal_rows(rows_in[rows, :].astype(jnp.float32))
        middle[rows, :] += norm_pull(upstream, normal, inverse, gain_ref[0:1, :])
        for name, value in (
            ("gain", upstream * normal),
            ("shift", upstream),
            ("back", pulled.astype(jnp.float32)),
        ):
            value = jnp.sum(value, axis=0, keepdims=True)
            sums[name] = sums[name] + value if name in sums else value

    def hop(number):
        wait([hops[number]])
        steps[number + 1] = steps[number] + arrived[number]
        start([hops[number + 1]] if number < 2 else spread)

    start(loads[:2])
    spot.meet(all_axes)
    start([out_copy])
    for job in others:
        start(job.copies)
    wait(loads[:2])
    start(loads[2:])
    turned[...] = jnp.transpose(low_rows[...])
    for number, job in enumerate(jobs):
        gradient(1 - spot.k, number, others_half[number])
        start(job.first)
        gradient(spot.k, number, job.total)
        job.go_near()
    wait(loads[2:])
    for number in range(tokens // BLK):
        pull_block(number)
        jobs[number].go_far()
    steps[0] = jnp.zeros(steps.shape[1:], jnp.float32)
    steps[0, 4:8, :] = row_sums[:4, :]
    lane = lax.broadcasted_iota(jnp.int32, (1, PAIR), 1)
    for (one, two), source in hidden_pairs(steps.shape[2], bias_a.shape[1]):
        a, b = bias_a[:, source], bias_b[:, source]
        steps[(0, *one)] = jnp.where(lane < HD, a, pltpu.roll(b, HD, 1))
        steps[(0, *two)] = jnp.where(lane < HD, pltpu.roll(a, HD, 1), b)
    steps[0, 0:1, :] = sums["gain"]
    steps[0, 1:2, :] = sums["shift"]
    for pair in range(H // 2):
        for row, third in ((2, 0), (3, 2)):
            steps[0, row : row + 1, pair * PAIR : (pair + 1) * PAIR] = sums["back"][
                :, (3 * pair + third) * PAIR : (3 * pair + third + 1) * PAIR
            ]
    start(hops[:1])
    for place in range(2):
        sent[block_rows(place), :] = chosen_block(back_ref[2 + place], middle).astype(low)
    hop(0)
    start([rows_copy])
    for job, deep in zip(jobs[:2], deeps[:2]):
        job.close()
        start(deep.copies)
    for place in range(2):
        kept[block_rows(place), :] = chosen_block(back_ref[place], middle)
    for job, ending in zip(others, other_ends):
        wait(job.copies)
        ending.summed[...] = job.result()
        start(ending.copies)
    wait(others[2].copies)
    shrink_out[...] = others[2].result()
    for job, deep in zip(jobs[2:], deeps[2:]):
        job.close()
        start(deep.copies)
    hop(1)
    hop(2)
    for ending, target in zip(other_ends, (mixing_out, expand_out)):
        wait(ending.copies)
        ending.write(target)
    for deep, ending in zip(deeps, ends):
        wait(deep.copies)
        ending.summed[...] = deep.result()
        start(ending.copies)
    wait(spread)
    total = steps[3]
    for by in range(1, sizes["z"]):
        total = total + arrived[2 + by]
    vector_out[...] = total
    for number, ending in enumerate(ends):
        wait(ending.copies)
        ending.write(out, pl.ds(number * part, part))
    wait([rows_copy, out_copy])


def end(sizes, back, joint_back, first_low, joint, rows_in, middle_grad, gain, row_sums, bias_a, bias_b, quads, sent):
    tokens, model = rows_in.shape
    width = joint.shape[1] // 2
    lead = (sizes["c"], sizes["z"], sizes["y"])
    depth = sizes["z"]
    rows = model // (lead[0] * lead[1] * lead[2])
    part = width // end_chunks
    half, grown, full = [quad.shape[-1] for quad in quads]
    scratch = [
        pltpu.SemaphoreType.DMA((2, 80)),
        pltpu.VMEM((4, *gain.shape), jnp.float32),
        pltpu.VMEM((2 + depth, *gain.shape), jnp.float32),
        pltpu.VMEM(joint_back.shape, low),
        pltpu.VMEM(first_low.shape, low),
        pltpu.VMEM(first_low.shape[::-1], low),
        pltpu.VMEM(joint.shape, low),
        pltpu.VMEM(rows_in.shape, low),
        pltpu.VMEM(middle_grad.shape, jnp.float32),
        pltpu.VMEM((tokens // 2, model), low),
    ]
    for number in range(end_chunks):
        scratch += [pltpu.VMEM((*lead, rows, part), low), pltpu.VMEM((depth, rows, part), low)]
        scratch += ReduceNear.scratch(sizes, rows, part, 2 * part // 3)
        scratch += [pltpu.VMEM((depth - 1, rows, part), low)]
        scratch += Finish.scratch(rows, part)
    scratch += [pltpu.VMEM((depth - 1, rows, columns), low) for columns in (half, grown, full)]
    for columns in (half, grown):
        scratch += Finish.scratch(rows, columns)
    own = rows // 2
    shapes = [(2, own, width), gain.shape, (2, own, half), (2, own, grown), (rows, full)]
    shapes.append((tokens // 2, model))
    return pl.pallas_call(
        functools.partial(end_kernel, sizes),
        in_specs=[pl.BlockSpec(memory_space=pltpu.SMEM)]
        + [any_place] * 5
        + [whole_vmem] * 7
        + [any_place],
        out_specs=[whole_vmem] * 6 + [any_place] * 2,
        out_shape=[jax.ShapeDtypeStruct(shape, jnp.float32) for shape in shapes]
        + [low_shape(tokens // 2, model), low_shape(BLK, model)],
        scratch_shapes=scratch,
        compiler_params=params(6, 60),
        cost_estimate=small_cost,
        name="end",
    )(back, joint_back, first_low, joint, rows_in, middle_grad, gain, row_sums, bias_a, bias_b, *quads, sent)


def last_kernel(ctx_ref, *refs):
    refs = Refs(refs)
    joint_part, mixing_part, expand_a, expand_b, shrink_a, shrink_b = refs.take(6)
    kept_grad, far_grad, kept_out, far_one, far_two = refs.take(5)
    (vector_sum,) = refs.take(1)
    states = [refs.take(3) for _ in range(5)]
    grad_out, block_out = refs.take(2)
    news = [refs.take(4) for _ in range(5)]
    here = ctx_ref[0]
    grad_out[here] = kept_grad[...]
    grad_out[1 - here] = far_grad[...].astype(jnp.float32)
    block_out[here] = kept_out[...]
    block_out[1 - here, :BLK, :] = far_one[...]
    block_out[1 - here, BLK:, :] = far_two[...]

    def update(number, where, gradient, rate=0.05, decay=0.1):
        weight, first, second = [ref[where] for ref in states[number]]
        results = adam_update(weight, first, second, gradient, rate, decay)
        for ref, value in zip(news[number], (*results, results[0].astype(low))):
            ref[where] = value

    every = slice(None)
    pairs = joint_part.shape[2] // (3 * PAIR)
    for core in range(2):
        for pair in range(pairs):
            for third in range(3):
                first = ((third * 2 + core) * pairs + pair) * PAIR
                source = (pair * 3 + third) * PAIR
                update(
                    0,
                    (every, pl.ds(first, PAIR)),
                    joint_part[core, :, source : source + PAIR],
                )
        half = mixing_part.shape[2]
        update(1, (every, pl.ds(core * half, half)), mixing_part[core])
        lane = lax.broadcasted_iota(jnp.int32, (1, PAIR), 1)
        for chip in range(0, expand_a.shape[2] // HD, 2):
            a = expand_a[core, :, chip * HD : chip * HD + PAIR]
            b = expand_b[core, :, chip * HD : chip * HD + PAIR]
            even = jnp.where(lane < HD, a, pltpu.roll(b, HD, 1))
            odd = jnp.where(lane < HD, pltpu.roll(a, HD, 1), b)
            for number, value in ((chip, even), (chip + 1, odd)):
                update(2, (every, pl.ds((number * 2 + core) * PAIR, PAIR)), value)
    rows = shrink_a.shape[0]
    update(3, (pl.ds(0, rows), every), shrink_a[...])
    update(3, (pl.ds(rows, rows), every), shrink_b[...])
    table_rows, columns = states[4][0].shape
    moved = pltpu.roll(vector_sum[...], vector_sum.shape[1] - ctx_ref[1] * columns, 1)
    update(4, (every, every), moved[:table_rows, :columns], 0.5, 0.0)


def last(ctx, parts, kept_grad, far_grad, kept_out, far_outs, vector_sum, states):
    shapes = [jax.ShapeDtypeStruct((2, *kept_grad.shape), jnp.float32), low_shape(2, *kept_out.shape)]
    for weight, _, _ in states:
        shapes += [jax.ShapeDtypeStruct(weight.shape, jnp.float32)] * 3
        shapes.append(low_shape(*weight.shape))
    flat = [array for state in states for array in state]
    return pl.pallas_call(
        last_kernel,
        in_specs=[pl.BlockSpec(memory_space=pltpu.SMEM)] + [whole_vmem] * (12 + len(flat)),
        out_specs=[whole_vmem] * len(shapes),
        out_shape=shapes,
        compiler_params=pltpu.CompilerParams(vmem_limit_bytes=56 << 20),
        cost_estimate=small_cost,
        name="last",
    )(ctx, *parts, kept_grad, far_grad, kept_out, *far_outs, vector_sum, *flat)


def layer_norm(values, gain_row, shift_row):
    centered = values - jnp.mean(values, axis=-1, keepdims=True)
    variance = jnp.mean(centered * centered, axis=-1, keepdims=True)
    inverse = lax.rsqrt(variance + norm_eps)
    normal_part = centered * inverse
    return (normal_part * gain_row + shift_row, normal_part, inverse)


def norm_back(upstream, normal_part, inverse, gain_row):
    scaled = upstream * gain_row
    inner_sum = jnp.mean(scaled, axis=-1, keepdims=True)
    along_sum = jnp.mean(scaled * normal_part, axis=-1, keepdims=True)
    values_grad = inverse * (scaled - inner_sum - normal_part * along_sum)
    return (values_grad, jnp.sum(upstream * normal_part, axis=0), jnp.sum(upstream, axis=0))


def adam_update(weight, moment_one, moment_two, gradient, step_rate, decay_rate):
    first_new = 0.5 * moment_one + 0.5 * gradient
    second_new = 0.5 * moment_two + 0.5 * gradient * gradient
    correct = 1.0 - 0.5**STEP
    direction = first_new / correct / (jnp.sqrt(second_new / correct) + adam_eps)
    updated = weight - step_rate * (direction + decay_rate * weight)
    return (updated, first_new, second_new)


def to_groups(matrix):
    row_count = matrix.shape[0]
    return matrix.reshape(row_count, H // group_heads, group_heads, HD).transpose(1, 0, 2, 3)


def from_groups(stacked):
    return stacked.transpose(1, 0, 2, 3).reshape(stacked.shape[1], H * HD)


def tile_scores(queries, key_rows, allowed):
    products = jnp.einsum("rgd,lgd->grl", queries, key_rows, preferred_element_type=jnp.float32)
    return jnp.where(allowed[None], products * 0.125, -1e30)


def tile_forward(queries, key_rows, value_rows, allowed):
    scores = tile_scores(queries, key_rows, allowed)
    largest = jnp.max(scores, axis=-1, keepdims=True)
    exponent = jnp.exp(scores - largest)
    row_total = jnp.sum(exponent, axis=-1, keepdims=True)
    weights = (exponent / row_total).astype(low)
    mixed = jnp.einsum("grl,lgd->rgd", weights, value_rows, preferred_element_type=jnp.float32)
    return (mixed, (largest + jnp.log(row_total))[..., 0])


def tile_backward(queries, key_rows, value_rows, allowed, logsum, upstream):
    scores = tile_scores(queries, key_rows, allowed)
    recomputed = jnp.exp(scores - logsum[..., None])
    value_grad = jnp.einsum(
        "grl,rgd->lgd", recomputed.astype(low), upstream, preferred_element_type=jnp.float32
    )
    weight_grad = jnp.einsum(
        "rgd,lgd->grl", upstream, value_rows, preferred_element_type=jnp.float32
    )
    inner_sum = jnp.sum(recomputed * weight_grad, axis=-1, keepdims=True)
    score_grad = (recomputed * (weight_grad - inner_sum)).astype(low)
    query_grad = (
        jnp.einsum("grl,lgd->rgd", score_grad, key_rows, preferred_element_type=jnp.float32) * 0.125
    )
    key_grad = (
        jnp.einsum("grl,rgd->lgd", score_grad, queries, preferred_element_type=jnp.float32) * 0.125
    )
    return (query_grad, key_grad, value_grad)


def spread_forward(queries, key_value, allowed):
    def one_sequence(pieces):
        queries, key_value, allowed = pieces
        width = queries.shape[1]
        mixed, logsum = lax.map(
            lambda triple: tile_forward(triple[0], triple[1], triple[2], allowed),
            (to_groups(queries), to_groups(key_value[:, :width]), to_groups(key_value[:, width:])),
        )
        return (from_groups(mixed), logsum)

    return lax.map(one_sequence, (queries, key_value, allowed))


def spread_backward(queries, key_value, allowed, logsum, upstream):
    def one_sequence(pieces):
        queries, key_value, allowed, logsum, upstream = pieces
        width = queries.shape[1]
        query_grad, key_grad, value_grad = lax.map(
            lambda member: tile_backward(
                member[0], member[1], member[2], allowed, member[3], member[4]
            ),
            (
                to_groups(queries),
                to_groups(key_value[:, :width]),
                to_groups(key_value[:, width:]),
                logsum,
                to_groups(upstream),
            ),
        )
        return (
            from_groups(query_grad),
            jnp.concatenate([from_groups(key_grad), from_groups(value_grad)], axis=1),
        )

    return lax.map(one_sequence, (queries, key_value, allowed, logsum, upstream))


class Slice:
    def __init__(self, ctx_size, wshard_size):
        rest = wshard_size // 2
        self.sizes = {"c": ctx_size, "z": 4, "y": rest // 4, "k": 2}

    def here(self):
        flat = lax.axis_index(axes)
        found = {}
        for name in ("k", "y", "z", "c"):
            found[name] = flat % self.sizes[name]
            flat = flat // self.sizes[name]
        return found

    def shift(self, value, name, by):
        pairs = []
        sizes = self.sizes
        for c in range(sizes["c"]):
            for z in range(sizes["z"]):
                for y in range(sizes["y"]):
                    for k in range(sizes["k"]):
                        spot = {"c": c, "z": z, "y": y, "k": k}
                        goal = dict(spot)
                        goal[name] = (spot[name] + by) % sizes[name]
                        pairs.append((self.flat(spot), self.flat(goal)))
        return lax.ppermute(value, axes, pairs)

    def flat(self, spot):
        sizes = self.sizes
        return ((spot["c"] * sizes["z"] + spot["z"]) * sizes["y"] + spot["y"]) * sizes["k"] + spot[
            "k"
        ]

    def stack(self, array, name, here):
        size = self.sizes[name]
        parts = [array] + [self.shift(array, name, by) for by in range(1, size)]
        if size > 4:
            ordered = [parts[(-place) % size] for place in range(size)]
            return jnp.roll(jnp.stack(ordered), here[name], axis=0)
        return jnp.stack(
            [lax.select_n((here[name] - place) % size, *parts) if size > 2 else
             jnp.where(here[name] == place, parts[0], parts[1]) for place in range(size)]
        )

    def reach(self, pieces, name):
        grown = list(pieces)
        for by in range(1, self.sizes[name]):
            for array, place in pieces:
                moved = dict(place)
                moved[name] = (place[name] - by) % self.sizes[name]
                grown.append((self.shift(array, name, by), moved))
        return grown

    def gather_split(self, stacked, cut, here):
        sizes = self.sizes
        depth, rows, columns = stacked.shape
        out = jnp.zeros((sizes["c"], depth, sizes["y"], rows, columns), stacked.dtype)
        for low_column, high_column, order in ((0, cut, "cy"), (cut, columns, "yc")):
            pieces = [(stacked[:, :, low_column:high_column], here)]
            for name in order:
                pieces = self.reach(pieces, name)
            for array, place in pieces:
                out = lax.dynamic_update_slice(
                    out, array[None, :, None], (place["c"], 0, place["y"], 0, low_column)
                )
        return out.reshape(-1, columns)

    def send_terms(self, value, name, place, here):
        size = self.sizes[name]
        own = lax.dynamic_index_in_dim(value, here[name], place, False)
        moved = [
            self.shift(
                lax.dynamic_index_in_dim(value, (here[name] + by) % size, place, False), name, by
            )
            for by in range(1, size)
        ]
        return own, moved

    def add_terms(self, terms, kind=low):
        own, moved = terms
        total = own.astype(jnp.float32)
        for other in moved:
            total = total + other.astype(jnp.float32)
        return total.astype(kind)

    def everywhere(self, value):
        for name in ("k", "c", "y", "z"):
            total = value
            for by in range(1, self.sizes[name]):
                total = total + self.shift(value, name, by)
            value = total
        return value


def tie(value, *others):
    return lax.optimization_barrier((value, others))[0]


def by_core(core, first, second, axis):
    return jnp.where(
        core == 0,
        jnp.concatenate([first, second], axis=axis),
        jnp.concatenate([second, first], axis=axis),
    )


def pick(core, array, axis):
    return (
        lax.dynamic_index_in_dim(array, core, axis, False),
        lax.dynamic_index_in_dim(array, 1 - core, axis, False),
    )


def gather_far(grid, here, pieces):
    joint_halves, table, mixing_halves, expand_a, expand_b, shrink_a, shrink_b = pieces
    core = here["k"]

    def chip_rows(halves):
        own, other = pick(core, halves, 0)
        return by_core(core, own, grid.shift(other, "k", 1), 0)

    def everyone(block):
        width = block.shape[1]
        return grid.gather_split(grid.stack(block, "z", here), width // 2, here)

    def both(block, axis):
        own = everyone(block)
        return by_core(core, own, grid.shift(own, "k", 1), axis)

    return (
        both(chip_rows(joint_halves), 1),
        everyone(by_core(core, table, grid.shift(table, "k", 1), 0)),
        both(chip_rows(mixing_halves), 1),
        both(chip_rows(expand_a), 1),
        both(chip_rows(expand_b), 1),
        both(shrink_a, 0),
        both(shrink_b, 0),
    )


def reduce_far(grid, here, gradient, by_rows):
    core = here["k"]
    sizes = grid.sizes
    if by_rows:
        own, other = pick(core, gradient.reshape(2, -1, gradient.shape[1]), 0)
    else:
        own, other = pick(core, gradient.reshape(gradient.shape[0], 2, -1), 1)
    total = grid.add_terms((own, [grid.shift(other, "k", 1)]))
    total = total.reshape(sizes["c"], sizes["z"], sizes["y"], -1, own.shape[-1])
    for name, place in (("y", 2), ("c", 0)):
        total = grid.add_terms(grid.send_terms(total, name, place, here))
    total = grid.add_terms(grid.send_terms(total, "z", 0, here), jnp.float32)
    if by_rows:
        return total
    kept, other = pick(core, total.reshape(2, -1, total.shape[1]), 0)
    return by_core(core, kept[None], grid.shift(other, "k", 1)[None], 0)


def body(
    grid,
    block_input,
    block_order,
    cotangent,
    joint_weight,
    mixing_weight,
    expand_weight,
    shrink_weight,
    vectors,
    joint_first,
    mixing_first,
    expand_first,
    shrink_first,
    vectors_first,
    joint_second,
    mixing_second,
    expand_second,
    shrink_second,
    vectors_second,
):
    here = grid.here()
    sizes = grid.sizes
    ctx, ctx_size = here["c"], sizes["c"]
    seq_count, row_count, width = block_input.shape
    half = width // 2
    pairs = H // 2
    hidden_width = expand_weight.shape[1]
    own_rows = joint_weight.shape[0]
    slot = shrink_weight.shape[0]
    sub = slot // 2
    chips = hidden_width // (2 * slot)
    tokens = seq_count * row_count
    row_blocks = row_count // BLK
    near = ctx_size == 2 and seq_count == 2 and sizes["y"] == 2 and own_rows % 32 == 0

    def hidden_sets(shard):
        parts = shard.astype(low).reshape(own_rows, chips, 2, 2, sub)
        return [
            parts[:, :, :, number].transpose(2, 0, 1, 3).reshape(2, own_rows, chips * sub)
            for number in range(2)
        ]

    table = jnp.pad(vectors.T.astype(low), ((0, 0), (0, 128 - vectors.shape[0])))
    if near:
        joint, tables, *quads, far_input, far_upstream, next_half, next_shrink = begin(
            sizes,
            joint_weight,
            table,
            mixing_weight,
            expand_weight,
            shrink_weight,
            block_input,
            cotangent,
        )
    else:
        joint_halves = (
            joint_weight.astype(low)
            .reshape(own_rows, 3, 2, pairs // 2, PAIR)
            .transpose(2, 0, 3, 1, 4)
            .reshape(2, own_rows, 3 * half)
        )
        mixing_halves = mixing_weight.astype(low).reshape(own_rows, 2, half).transpose(1, 0, 2)
        shrink_low = shrink_weight.astype(low)
        pieces = [joint_halves, table, mixing_halves, *hidden_sets(expand_weight)]
        pieces += [shrink_low[:sub], shrink_low[sub:]]
        joint, tables, mixing, expand_a, expand_b, shrink_a, shrink_b = gather_far(
            grid, here, pieces
        )
    joint = joint.reshape(width, 3 * width)
    if near:
        order = lax.dynamic_slice_in_dim(block_order, ctx, 1, 0)[0]
        blocks = order.shape[0]
        stored = jnp.arange(blocks, dtype=jnp.int32)
        moved = jnp.where(stored // row_blocks == ctx, 0, row_blocks) + stored % row_blocks
        place = jnp.sum(jnp.where(order[None, :] == stored[:, None], moved[None, :], 0), axis=1)
        back = jnp.sum(jnp.where(moved[None, :] == stored[:, None], order[None, :], 0), axis=1)
        place, back = place.astype(jnp.int32), back.astype(jnp.int32)
    lead = (sizes["c"], sizes["z"], sizes["y"])
    def by_device(expand_grad, shrink_grad):
        return (
            expand_grad.reshape(*lead, -1, expand_grad.shape[1]),
            shrink_grad.reshape(2, *lead, -1, width),
        )

    if near:
        mixed_low, logsum, input_low, first_low, projected, vector_values, hidden_a, hidden_b, *gathered = attend(
            sizes,
            place,
            block_input,
            far_input,
            joint,
            tables.reshape(width, -1),
            cotangent,
            quads,
            next_half,
            next_shrink,
        )
        mixing, expand_a, shrink_a, *quads, last_upstream = gathered
        mixing = mixing.reshape(width, width)
        *before, expand_grad_a, shrink_grad_a, bias_a, middle, second_low, upstream, expand_b, shrink_b = mlp_gather(
            sizes,
            place,
            mixed_low,
            input_low,
            mixing,
            vector_values,
            expand_a.reshape(width, -1),
            shrink_a.reshape(-1, width),
            hidden_a,
            cotangent,
            far_upstream,
            last_upstream,
            quads,
        )
        second_grad, expand_grad_b, shrink_grad_b, bias_b, *quads, kept_out, sent_out = mlp_reduce(
            sizes,
            back,
            second_low,
            upstream,
            expand_b.reshape(width, -1),
            shrink_b.reshape(-1, width),
            hidden_b,
            before,
            by_device(expand_grad_a, shrink_grad_a),
        )
    else:
        vector_values = (
            tables.reshape(width, -1)[:, : vectors.shape[0]].T.astype(jnp.float32)
        )
        joint_shift = jnp.stack(
            [
                vector_values[2].reshape(pairs, PAIR),
                jnp.zeros((pairs, PAIR), jnp.float32),
                vector_values[3].reshape(pairs, PAIR),
            ],
            axis=1,
        ).reshape(1, -1)
        hidden_bias = vector_values[8:].reshape(chips, 2, 2, sub).transpose(2, 1, 0, 3).reshape(2, 1, -1)
        input_low = block_input.reshape(tokens, width)
        upstream = cotangent.reshape(tokens, width)
        input_rows = input_low.astype(jnp.float32)
        normed_first, normal_first, inverse_first = layer_norm(
            input_rows, vector_values[0], vector_values[1]
        )
        first_low = normed_first.astype(low)
        projected = (nn(first_low, joint) + joint_shift).astype(low)
        by_part = projected.reshape(seq_count, row_count, pairs, 3, PAIR)
        queries, keys, values = [
            by_part[:, :, :, part].reshape(seq_count, row_count, width) for part in range(3)
        ]
        key_value = lax.all_gather(
            jnp.concatenate([keys, values], axis=2), "ctx", axis=1, tiled=True
        )
        own_blocks = lax.dynamic_slice_in_dim(block_order, ctx * row_blocks, row_blocks, 1)
        query_block = jnp.repeat(own_blocks, BLK, axis=1, total_repeat_length=row_count)
        key_block = jnp.repeat(block_order, BLK, axis=1, total_repeat_length=key_value.shape[1])
        allowed = key_block[:, None, :] <= query_block[:, :, None]
        mixed, logsum = spread_forward(queries, key_value, allowed)
        mixed_low = mixed.astype(low).reshape(tokens, width)
        mixing = mixing.reshape(width, width)
        middle = input_rows + (nn(mixed_low, mixing) + vector_values[4])
        normed_second, normal_second, inverse_second = layer_norm(
            middle, vector_values[5], vector_values[6]
        )
        second_low = normed_second.astype(low)
        before = (middle + vector_values[7], jnp.zeros_like(middle))
        *before, expand_grad_a, shrink_grad_a, bias_a = mlp(
            second_low,
            upstream,
            expand_a.reshape(width, -1),
            shrink_a.reshape(-1, width),
            hidden_bias[0],
            before,
        )
        result, second_grad, expand_grad_b, shrink_grad_b, bias_b = mlp(
            second_low,
            upstream,
            expand_b.reshape(width, -1),
            shrink_b.reshape(-1, width),
            hidden_bias[1],
            before,
        )
        block_output = result.astype(low).reshape(block_input.shape)
    if near:
        joint_back, middle_grad, sums, *last_quads, expand_part_a, shrink_part_a, far_one = attend_back(
            sizes,
            second_grad,
            middle,
            upstream,
            mixed_low,
            mixing,
            vector_values,
            projected,
            logsum,
            by_device(expand_grad_b, shrink_grad_b),
            quads,
            sent_out,
        )
    else:
        middle_part, gain_two, shift_two = norm_back(
            second_grad, normal_second, inverse_second, vector_values[5]
        )
        middle_grad = upstream.astype(jnp.float32) + middle_part
        branch_low = middle_grad.astype(low)
        mixing_grad = outer_sum(mixed_low, branch_low).astype(low)
        mixed_grad = nt(branch_low, mixing).astype(low)
        query_grad, key_value_grad = spread_backward(
            queries, key_value, allowed, logsum, mixed_grad.reshape(seq_count, row_count, width)
        )
        summed = lax.psum_scatter(
            key_value_grad.astype(low), "ctx", scatter_dimension=1, tiled=True
        )
        parts = [query_grad.astype(low), summed[..., :width], summed[..., width:]]
        joint_back = jnp.stack(
            [part.reshape(tokens, pairs, PAIR) for part in parts], axis=2
        ).reshape(tokens, 3 * width)
        mixing_part = reduce_far(grid, here, mixing_grad, False)
        expand_part_a, shrink_part_a, expand_part_b, shrink_part_b = [
            reduce_far(grid, here, grad, number % 2 == 1)
            for number, grad in enumerate(
                (expand_grad_a, shrink_grad_a, expand_grad_b, shrink_grad_b)
            )
        ]

    def column_sum(rows):
        return jnp.sum(rows.astype(jnp.float32), axis=0)

    weights = (joint_weight, mixing_weight, expand_weight, shrink_weight)
    firsts = (joint_first, mixing_first, expand_first, shrink_first)
    seconds = (joint_second, mixing_second, expand_second, shrink_second)
    if near:
        joint_part, vector_sum, mixing_part, expand_part_b, shrink_part_b, kept_grad, far_grad, far_two = end(
            sizes,
            back,
            joint_back,
            first_low,
            joint,
            input_low,
            middle_grad,
            vector_values,
            sums,
            bias_a,
            bias_b,
            last_quads,
            sent_out,
        )
        input_gradient, block_output, *news = last(
            jnp.stack([ctx, lax.axis_index(axes)]).astype(jnp.int32),
            (joint_part, mixing_part, expand_part_a, expand_part_b, shrink_part_a, shrink_part_b),
            kept_grad,
            far_grad,
            kept_out,
            (far_one, far_two),
            vector_sum,
            list(
                zip(
                    (*weights, vectors), (*firsts, vectors_first), (*seconds, vectors_second)
                )
            ),
        )
        updated, moments, squares, copies = [news[number::4] for number in range(4)]
    else:
        hidden_bias_grads = [
            bias.reshape(2, chips, 1, sub).transpose(1, 0, 2, 3) for bias in (bias_a, bias_b)
        ]
        hidden_bias_grad = jnp.concatenate(hidden_bias_grads, axis=2).reshape(-1, width)
        joint_grad = outer_sum(first_low, joint_back).astype(low)
        first_grad = nt(joint_back, joint)
        input_part, gain_one, shift_one = norm_back(
            first_grad, normal_first, inverse_first, vector_values[0]
        )
        input_gradient = (middle_grad + input_part).reshape(block_input.shape)
        joint_sums = column_sum(joint_back).reshape(pairs, 3, PAIR)
        vector_rows = [
            gain_one,
            shift_one,
            joint_sums[:, 0].reshape(-1),
            joint_sums[:, 2].reshape(-1),
            column_sum(branch_low),
            gain_two,
            shift_two,
            column_sum(upstream),
        ]
        joint_part = reduce_far(grid, here, joint_grad, False)
        vector_sum = grid.everywhere(
            jnp.concatenate([jnp.stack(vector_rows), hidden_bias_grad], axis=0)
        )
        joint_sum = (
            joint_part.reshape(2, own_rows, pairs // 2, 3, PAIR)
            .transpose(1, 3, 0, 2, 4)
            .reshape(joint_weight.shape)
        )
        mixing_sum = mixing_part.transpose(1, 0, 2).reshape(mixing_weight.shape)
        expand_sum = jnp.stack(
            [part.reshape(2, own_rows, chips, sub) for part in (expand_part_a, expand_part_b)]
        )
        expand_sum = expand_sum.transpose(2, 3, 1, 0, 4).reshape(expand_weight.shape)
        shrink_sum = jnp.concatenate([shrink_part_a, shrink_part_b], axis=0)
        updated, moments, squares = zip(
            *[
                adam_update(*terms, 0.05, 0.1)
                for terms in zip(
                    weights, firsts, seconds, (joint_sum, mixing_sum, expand_sum, shrink_sum)
                )
            ]
        )
        copies = [array.astype(low) for array in updated]
        vector_sum = lax.dynamic_slice(
            vector_sum, (0, lax.axis_index(axes) * vectors.shape[1]), vectors.shape
        )
        vectors_new, vectors_moment, vectors_square = adam_update(
            vectors, vectors_first, vectors_second, vector_sum, 0.5, 0.0
        )
        updated, moments, squares = [
            (*arrays, array)
            for arrays, array in (
                (updated, vectors_new),
                (moments, vectors_moment),
                (squares, vectors_square),
            )
        ]
        copies.append(vectors_new.astype(low))
    return (block_output, input_gradient, *updated, *moments, *squares, *copies)


def solution(mesh):
    grid = Slice(mesh.shape["ctx"], mesh.shape["wshard"])
    rows = P("wshard", "ctx", None)
    matrix = P(axes, None)
    table = P(None, axes)
    parameters = (matrix, matrix, matrix, matrix, table)
    return jax.shard_map(
        functools.partial(body, grid),
        mesh=mesh,
        in_specs=(rows, P("wshard", None), rows) + parameters * 3,
        out_specs=(rows, rows) + parameters * 4,
        check_vma=False,
    )
```
